32 devices in a mesh: sys: 4 (over y, x), edge: 8 (over z, core).
Axes of the slice: x: 2, y: 2, z: 4, core: 2. Of those that a mesh axis runs over, the one named last changes fastest.
Arguments:
- positions: float32 [3, 4096], P(None, ('sys', 'edge')), may hold values from 0 to 2.5
- velocities: float32 [3, 4096], P(None, ('sys', 'edge')), may hold values from -3 to 3
- species: int32 [4096], P(('sys', 'edge')), may hold values from 0 to 3
- senders: int32 [3, 32768], P(None, ('sys', 'edge')), may hold values from 0 to 127, as said below
- receivers: int32 [3, 32768], P(None, ('sys', 'edge')), may hold values from 0 to 127, as said below
- edge_mask: int32 [3, 32768], P(None, ('sys', 'edge')), may hold values 0 or 1
- embedding: float32 [4, 64], replicated, may hold values from -4 to 4
- radial_in: float32 [2, 8, 64], replicated, may hold values from -4 to 4
- radial_out: float32 [2, 64, 192], replicated, may hold values from -0.75 to 0.75
- mix_first: float32 [64, 192], replicated, may hold values from -0.75 to 0.75
- mix_square: float32 [3, 64, 64], replicated, may hold values from -0.75 to 0.75
- readout: float32 [64], replicated, may hold values from -0.75 to 0.75
- embedding_rows: float32 [4], replicated, may hold values from 1e-05 to 0.01
- embedding_cols: float32 [64], replicated, may hold values from 1e-05 to 0.01
- radial_in_rows: float32 [2, 8], replicated, may hold values from 1e-05 to 0.01
- radial_in_cols: float32 [2, 64], replicated, may hold values from 1e-05 to 0.01
- radial_out_rows: float32 [2, 64], replicated, may hold values from 1e-05 to 0.01
- radial_out_cols: float32 [2, 192], replicated, may hold values from 1e-05 to 0.01
- mix_first_rows: float32 [64], replicated, may hold values from 1e-05 to 0.01
- mix_first_cols: float32 [192], replicated, may hold values from 1e-05 to 0.01
- mix_square_rows: float32 [3, 64], replicated, may hold values from 1e-05 to 0.01
- mix_square_cols: float32 [3, 64], replicated, may hold values from 1e-05 to 0.01
- readout_second: float32 [64], replicated, may hold values from 1e-05 to 0.01
Outputs:
- loss_total: float32 [], replicated
- embedding_grad: float32 [4, 64], replicated
- embedding_rows_new: float32 [4], replicated
- embedding_cols_new: float32 [64], replicated
- embedding_new: float32 [4, 64], replicated
- embedding_half: bfloat16 [4, 64], replicated
- radial_in_grad: float32 [2, 8, 64], replicated
- radial_in_rows_new: float32 [2, 8], replicated
- radial_in_cols_new: float32 [2, 64], replicated
- radial_in_new: float32 [2, 8, 64], replicated
- radial_in_half: bfloat16 [2, 8, 64], replicated
- radial_out_grad: float32 [2, 64, 192], replicated
- radial_out_rows_new: float32 [2, 64], replicated
- radial_out_cols_new: float32 [2, 192], replicated
- radial_out_new: float32 [2, 64, 192], replicated
- radial_out_half: bfloat16 [2, 64, 192], replicated
- mix_first_grad: float32 [64, 192], replicated
- mix_first_rows_new: float32 [64], replicated
- mix_first_cols_new: float32 [192], replicated
- mix_first_new: float32 [64, 192], replicated
- mix_first_half: bfloat16 [64, 192], replicated
- mix_square_grad: float32 [3, 64, 64], replicated
- mix_square_rows_new: float32 [3, 64], replicated
- mix_square_cols_new: float32 [3, 64], replicated
- mix_square_new: float32 [3, 64, 64], replicated
- mix_square_half: bfloat16 [3, 64, 64], replicated
- readout_grad: float32 [64], replicated
- readout_second_new: float32 [64], replicated
- readout_new: float32 [64], replicated
- readout_half: bfloat16 [64], replicated
The draws below stay inside these ranges and needn't reach their ends.
Inputs may be any that keep to these rules, and one draw needn't show every extreme that they name: `senders`: A sender is an atom of the device that holds the edge slot. receivers[k, s] // 64 == senders[k, s] // 64: an edge joins two atoms of one system.
All inputs are finite; a program needn't handle non-finite values. No bound on the sum of `edge_mask` on one device may be relied on, other than what follows from the above.
Results may differ from the reference program's by a relative error of at most 0.001.
Values sent between devices are 32-bit elements; how exact they have to be, the bound alone decides.
A program may use at most 256 MiB of HBM per device.

```python
import math
import jax
import jax.numpy as jnp
from jax import lax

C = 64
NB = 8
RH = 64
NT = 4
AT_DEV = 64
SYS_LOC = 2
EDGE_DEV = 1024
STEPS = 2
STEP_NUM = 10
EVALS = 3
A_LOC = 128
SLOT = 128
SYS_ATOMS = 512
ATOMS = 4096
EDGES = 32768
N_SYS = 4
N_EDGE = 8


def edge_pairs(key):
    first_key, second_key = jax.random.split(key)
    sender = jax.random.randint(first_key, (EVALS, EDGES), 0, A_LOC)
    partner = jax.random.randint(second_key, (EVALS, EDGES), 0, AT_DEV)
    return (sender, sender // AT_DEV * AT_DEV + partner)


def draw_senders(key, part):
    return edge_pairs(key)[0]


def draw_receivers(key, part):
    return edge_pairs(key)[1]


def place_ends(entries, key, least, largest):
    index_at = [jax.random.randint(jax.random.fold_in(key, axis), (), 0, length) for axis, length in enumerate(entries.shape)]
    main_axis = entries.shape.index(max(entries.shape))
    next_to = index_at[:main_axis] + [(index_at[main_axis] + 1) % entries.shape[main_axis]] + index_at[main_axis + 1:]
    return entries.at[tuple(index_at)].set(least).at[tuple(next_to)].set(largest)


def block_scale(own_key, dims, pieces, low, high):
    loudness, own = 1.0, jax.random.fold_in(own_key, 6)
    for dim, shards_of in pieces:
        draws = jnp.exp(jax.random.uniform(jax.random.fold_in(own, dim), (shards_of,), jnp.float32, low / len(pieces), high / len(pieces)))
        loudness = loudness * jnp.repeat(draws, dims[dim] // shards_of).reshape([-1 if axis == dim else 1 for axis in range(len(dims))])
    return loudness


def bell_draw(stream_key, shape, scale, most, cuts=(), kind=jnp.bfloat16):
    factor_of = block_scale(stream_key, shape, cuts, -0.22, 0.18) if cuts else 1.0
    array = jax.random.normal(stream_key, shape, jnp.float32) * scale * factor_of
    return jnp.minimum(jnp.maximum(array, -most), most).astype(kind)


def setup_inputs(seed: int = 0) -> dict:
    seeds = jax.random.split(jax.random.key(seed), 24)
    return {
        "positions": jnp.clip(2.5 * jax.random.uniform(seeds[0], (3, ATOMS), jnp.float32) ** block_scale(seeds[0], (3, ATOMS), ((1, 32),), -0.2, 0.2), 0.0, 2.5),
        "velocities": bell_draw(seeds[1], (3, ATOMS), 0.5, 3.0, ((1, 32),), jnp.float32),
        "species": place_ends(jax.random.randint(seeds[2], (ATOMS,), 0, NT), jax.random.fold_in(seeds[2], 1), 0, NT - 1).astype(jnp.int32),
        "senders": draw_senders(jax.random.fold_in(seeds[23], 71), 0),
        "receivers": draw_receivers(jax.random.fold_in(seeds[23], 71), 0),
        "edge_mask": place_ends((jax.random.randint(seeds[5], (EVALS, EDGES), 0, 5) < 4).astype(jnp.int32), jax.random.fold_in(seeds[5], 1), 0, 1),
        "embedding": bell_draw(seeds[6], (NT, C), 1.0, 4.0, (), jnp.float32),
        "radial_in": bell_draw(seeds[7], (2, NB, RH), (NB // 4) ** -0.5, 4.0, (), jnp.float32),
        "radial_out": bell_draw(seeds[8], (2, RH, 3 * C), RH ** -0.5, 0.75, (), jnp.float32),
        "mix_first": bell_draw(seeds[9], (C, 3 * C), C ** -0.5, 0.75, (), jnp.float32),
        "mix_square": bell_draw(seeds[10], (3, C, C), C ** -0.5, 0.75, (), jnp.float32),
        "readout": bell_draw(seeds[11], (C,), C ** -0.5, 0.75, (), jnp.float32),
        "embedding_rows": jnp.clip(jnp.exp(jax.random.uniform(seeds[12], (NT,), jnp.float32, math.log(9.999999747378752e-06), math.log(0.01))), 9.999999747378752e-06, 0.01),
        "embedding_cols": jnp.clip(jnp.exp(jax.random.uniform(seeds[13], (C,), jnp.float32, math.log(9.999999747378752e-06), math.log(0.01))), 9.999999747378752e-06, 0.01),
        "radial_in_rows": jnp.clip(jnp.exp(jax.random.uniform(seeds[14], (2, NB), jnp.float32, math.log(9.999999747378752e-06), math.log(0.01))), 9.999999747378752e-06, 0.01),
        "radial_in_cols": jnp.clip(jnp.exp(jax.random.uniform(seeds[15], (2, RH), jnp.float32, math.log(9.999999747378752e-06), math.log(0.01))), 9.999999747378752e-06, 0.01),
        "radial_out_rows": jnp.clip(jnp.exp(jax.random.uniform(seeds[16], (2, RH), jnp.float32, math.log(9.999999747378752e-06), math.log(0.01))), 9.999999747378752e-06, 0.01),
        "radial_out_cols": jnp.clip(jnp.exp(jax.random.uniform(seeds[17], (2, 3 * C), jnp.float32, math.log(9.999999747378752e-06), math.log(0.01))), 9.999999747378752e-06, 0.01),
        "mix_first_rows": jnp.clip(jnp.exp(jax.random.uniform(seeds[18], (C,), jnp.float32, math.log(9.999999747378752e-06), math.log(0.01))), 9.999999747378752e-06, 0.01),
        "mix_first_cols": jnp.clip(jnp.exp(jax.random.uniform(seeds[19], (3 * C,), jnp.float32, math.log(9.999999747378752e-06), math.log(0.01))), 9.999999747378752e-06, 0.01),
        "mix_square_rows": jnp.clip(jnp.exp(jax.random.uniform(seeds[20], (3, C), jnp.float32, math.log(9.999999747378752e-06), math.log(0.01))), 9.999999747378752e-06, 0.01),
        "mix_square_cols": jnp.clip(jnp.exp(jax.random.uniform(seeds[21], (3, C), jnp.float32, math.log(9.999999747378752e-06), math.log(0.01))), 9.999999747378752e-06, 0.01),
        "readout_second": jnp.clip(jnp.exp(jax.random.uniform(seeds[22], (C,), jnp.float32, math.log(9.999999747378752e-06), math.log(0.01))), 9.999999747378752e-06, 0.01),
    }


@jax.custom_vjp
def low(v):
    return lax.optimization_barrier(v.astype(jnp.bfloat16)).astype(jnp.float32)

@jax.custom_vjp
def low_back(v):
    return v

def low_keep(v):
    return (low(v), None)

def low_pass(kept, grad):
    return (grad,)

def back_keep(v):
    return (v, None)

def back_low(kept, grad):
    return (low(grad),)
low.defvjp(low_keep, low_pass)
low_back.defvjp(back_keep, back_low)
PRECISE = lax.Precision.HIGHEST
SOFTEN = 0.25
CUTOFF = 5.0
INV_NEIGH = 0.2
STEP_DT = 0.5
RELATIVE = 0.3
EPS_SQUARE = 1e-30
ROOT3 = math.sqrt(3.0)
ROOT5 = math.sqrt(5.0)

def geometry(sender_pos, receiver_pos):
    offset_vec = sender_pos - receiver_pos
    radius = jnp.sqrt(lax.optimization_barrier(jnp.sum(offset_vec * offset_vec, axis=0)) + SOFTEN)
    direction = offset_vec / radius
    unit_x, unit_y, unit_z = (direction[0], direction[1], direction[2])
    first_harm = ROOT3 * direction
    second_harm = ROOT5 * jnp.stack([ROOT3 * unit_x * unit_y, ROOT3 * unit_y * unit_z, 0.5 * (3.0 * unit_z * unit_z - 1.0), ROOT3 * unit_x * unit_z, 0.5 * ROOT3 * (unit_x * unit_x - unit_y * unit_y)])
    scaled = radius / CUTOFF
    envelope = 1.0 - 28.0 * scaled ** 6 + 48.0 * scaled ** 7 - 21.0 * scaled ** 8
    orders = jnp.arange(1, bessel_count() + 1).astype(jnp.float32)[:, None]
    bessel = math.sqrt(2.0 / CUTOFF) * jnp.sin(orders * math.pi * scaled[None, :]) / radius[None, :] * envelope[None, :]
    return (first_harm, second_harm, bessel)

def bessel_count():
    return NB

def radial(bessel, weight_in, weight_out):
    hidden = jax.nn.silu(jnp.einsum('nr,ne->re', weight_in, bessel, precision=PRECISE))
    return jnp.einsum('rk,re->ke', weight_out, hidden, precision=PRECISE)

def first_messages(first_harm, second_harm, bessel, sender_feat, edge_weight, weight_in, weight_out):
    channels = sender_feat.shape[0]
    edge_weights = radial(bessel, weight_in, weight_out)
    scalar_part = (edge_weights[:channels] * sender_feat)[None]
    vector_part = (edge_weights[channels:2 * channels] * sender_feat)[None] * first_harm[:, None, :]
    tensor_part = (edge_weights[2 * channels:] * sender_feat)[None] * second_harm[:, None, :]
    return jnp.concatenate([scalar_part, vector_part, tensor_part], axis=0) * edge_weight

def node_first(summed, scalar_prev, mix_first, mix_square):
    gathered = summed * INV_NEIGH
    channels = scalar_prev.shape[0]
    mixed = jnp.einsum('cd,ca->da', mix_first, gathered[0], precision=PRECISE)
    vectors = jnp.einsum('mca,cd->mda', gathered[1:4], mix_square[0], precision=PRECISE)
    tensors = jnp.einsum('mca,cd->mda', gathered[4:9], mix_square[1], precision=PRECISE)
    scalars = scalar_prev + jax.nn.silu(mixed[:channels])
    vectors = jax.nn.sigmoid(mixed[channels:2 * channels])[None] * vectors
    tensors = jax.nn.sigmoid(mixed[2 * channels:])[None] * tensors
    return jnp.concatenate([scalars[None], vectors, tensors], axis=0)

def second_messages(first_harm, second_harm, bessel, sender_feat, edge_weight, weight_in, weight_out):
    channels = sender_feat.shape[1]
    edge_weights = radial(bessel, weight_in, weight_out)
    along_first = jnp.einsum('kce,ke->ce', sender_feat[1:4], first_harm, precision=PRECISE)
    along_second = jnp.einsum('kce,ke->ce', sender_feat[4:9], second_harm, precision=PRECISE)
    combined = edge_weights[:channels] * sender_feat[0] + edge_weights[channels:2 * channels] * along_first + edge_weights[2 * channels:] * along_second
    return combined * edge_weight

def node_second(features, summed, mix_square, readout):
    scalars = features[0] + jax.nn.silu(jnp.einsum('cd,ca->da', mix_square[2], summed * INV_NEIGH, precision=PRECISE))
    return jnp.einsum('c,ca->a', readout, scalars, precision=PRECISE)

def factored(gradient, weight, row_state, col_state):
    decay_rate = 1.0 - STEP_NUM ** (-0.8)
    squares = gradient * gradient + EPS_SQUARE
    row_new = decay_rate * row_state + (1.0 - decay_rate) * lax.optimization_barrier(jnp.mean(squares, axis=-1))
    col_new = decay_rate * col_state + (1.0 - decay_rate) * lax.optimization_barrier(jnp.mean(squares, axis=-2))
    second = row_new[..., :, None] * col_new[..., None, :] / lax.optimization_barrier(jnp.mean(row_new, axis=-1, keepdims=True))[..., None]
    weight_rms = jnp.sqrt(lax.optimization_barrier(jnp.mean(weight * weight, axis=(-2, -1), keepdims=True)) + 1e-06)
    weight_new = weight - RELATIVE * weight_rms * gradient * lax.rsqrt(second)
    return (gradient, row_new, col_new, weight_new, weight_new.astype(jnp.bfloat16))

def unfactored(gradient, weight, second):
    decay_rate = 1.0 - STEP_NUM ** (-0.8)
    second_new = decay_rate * second + (1.0 - decay_rate) * (gradient * gradient + EPS_SQUARE)
    weight_rms = jnp.sqrt(jnp.mean(weight * weight) + 1e-06)
    weight_new = weight - RELATIVE * weight_rms * gradient * lax.rsqrt(second_new)
    return (gradient, second_new, weight_new, weight_new.astype(jnp.bfloat16))

def segment(values, segment_ids, segments):
    moved_axis = jnp.moveaxis(values, -1, 0)
    return jnp.moveaxis(jax.ops.segment_sum(moved_axis, segment_ids, num_segments=segments), 0, -1)

def atom_energies(coords, params, spec_hot, send_glob, recv_glob, edge_weight):
    embedding, radial_in, radial_out, mix_first, mix_square, readout = params
    atom_count = coords.shape[1]
    scalar_start = jnp.einsum('tc,ta->ca', embedding, spec_hot, precision=PRECISE)
    first_harm, second_harm, bessel = geometry(coords[:, send_glob], coords[:, recv_glob])
    first = first_messages(first_harm, second_harm, bessel, scalar_start[:, send_glob], edge_weight, radial_in[0], radial_out[0])
    features = node_first(segment(first, recv_glob, atom_count), scalar_start, mix_first, mix_square)
    second = second_messages(first_harm, second_harm, bessel, features[:, :, send_glob], edge_weight, radial_in[1], radial_out[1])
    return node_second(features, segment(second, recv_glob, atom_count), mix_square, readout)

def per_system(values):
    return values.reshape(N_EDGE, SYS_LOC, AT_DEV).sum(axis=(0, 2))

def group_loss(params, coords, speeds, spec_hot, send_glob, recv_glob, edge_weight):

    def evaluate(position, number):
        energies, pullback = jax.vjp(lambda place_now: atom_energies(place_now, params, spec_hot, send_glob[number], recv_glob[number], edge_weight[number]), position)
        return (energies, -pullback(jnp.ones_like(energies))[0])
    first_energy, forces = evaluate(coords, 0)
    position = coords
    moving = speeds
    energies = first_energy
    for number in range(STEPS):
        half_speed = moving + 0.5 * STEP_DT * forces
        position = position + STEP_DT * half_speed
        energies, forces = evaluate(position, number + 1)
        moving = half_speed + 0.5 * STEP_DT * forces
    start = per_system(first_energy) + per_system(0.5 * lax.optimization_barrier(jnp.sum(speeds * speeds, axis=0)))
    finish = per_system(energies) + per_system(0.5 * lax.optimization_barrier(jnp.sum(moving * moving, axis=0)))
    drift = finish - start
    return jnp.sum(drift * drift) / SYS_ATOMS

def reference(positions, velocities, species, senders, receivers, edge_mask, embedding, radial_in, radial_out, mix_first, mix_square, readout, embedding_rows, embedding_cols, radial_in_rows, radial_in_cols, radial_out_rows, radial_out_cols, mix_first_rows, mix_first_cols, mix_square_rows, mix_square_cols, readout_second):
    params = (embedding, radial_in, radial_out, mix_first, mix_square, readout)
    group_atoms = N_EDGE * A_LOC
    group_edges = N_EDGE * EDGE_DEV
    coords = positions.reshape(3, N_SYS, group_atoms).transpose(1, 0, 2)
    speeds = velocities.reshape(3, N_SYS, group_atoms).transpose(1, 0, 2)
    group_species = species.reshape(N_SYS, group_atoms)
    slot_ids = jnp.arange(group_edges).astype(jnp.int32)
    holder = (slot_ids // EDGE_DEV * A_LOC).astype(jnp.int32)
    owner = (slot_ids % EDGE_DEV // SLOT * A_LOC).astype(jnp.int32)
    send_glob = senders.reshape(EVALS, N_SYS, group_edges).transpose(1, 0, 2) + holder[None, None, :]
    recv_glob = receivers.reshape(EVALS, N_SYS, group_edges).transpose(1, 0, 2) + owner[None, None, :]
    weights_all = edge_mask.reshape(EVALS, N_SYS, group_edges).transpose(1, 0, 2).astype(jnp.float32)

    def one_group(group_items):
        coords_g, speeds_g, species_g, send_g, recv_g, weight_g = group_items
        spec_hot = (species_g[None, :] == jnp.arange(NT)[:, None]).astype(jnp.float32)
        value, pullback = jax.vjp(lambda weights: group_loss(weights, coords_g, speeds_g, spec_hot, send_g, recv_g, weight_g), params)
        return (value, pullback(jnp.ones((), jnp.float32))[0])
    losses, gradients = lax.map(one_group, (coords, speeds, group_species, send_glob, recv_glob, weights_all))
    loss_total = jnp.sum(losses)
    gradients = jax.tree.map(lambda stacked: lax.optimization_barrier(jnp.sum(stacked, axis=0)), gradients)
    emb = factored(gradients[0], embedding, embedding_rows, embedding_cols)
    rin = factored(gradients[1], radial_in, radial_in_rows, radial_in_cols)
    rout = factored(gradients[2], radial_out, radial_out_rows, radial_out_cols)
    mfirst = factored(gradients[3], mix_first, mix_first_rows, mix_first_cols)
    msquare = factored(gradients[4], mix_square, mix_square_rows, mix_square_cols)
    rdout = unfactored(gradients[5], readout, readout_second)
    return (loss_total, emb[0], emb[1], emb[2], emb[3], emb[4], rin[0], rin[1], rin[2], rin[3], rin[4], rout[0], rout[1], rout[2], rout[3], rout[4], mfirst[0], mfirst[1], mfirst[2], mfirst[3], mfirst[4], msquare[0], msquare[1], msquare[2], msquare[3], msquare[4], rdout[0], rdout[1], rdout[2], rdout[3])
```

```python
from functools import reduce
import math

import jax
import jax.numpy as jnp
from jax import lax
from jax.experimental import pallas as pl
from jax.experimental.pallas import tpu as pltpu
from jax.sharding import PartitionSpec as P

NB = 8
SYS_LOC = 2
STEPS = 2
STEP_NUM = 10
EVALS = 3


PRECISE = lax.Precision.HIGHEST
SOFTEN = 0.25
CUTOFF = 5.0
INV_NEIGH = 0.2
STEP_DT = 0.5
RELATIVE = 0.3
EPS_SQUARE = 1e-30
ROOT3 = math.sqrt(3.0)
ROOT5 = math.sqrt(5.0)


def geometry(sender_pos, receiver_pos):
    offset_vec = sender_pos - receiver_pos
    radius = jnp.sqrt(jnp.sum(offset_vec * offset_vec, axis=0) + SOFTEN)
    direction = offset_vec / radius
    unit_x, unit_y, unit_z = (direction[0], direction[1], direction[2])
    first_harm = ROOT3 * direction
    second_harm = ROOT5 * jnp.stack(
        [
            ROOT3 * unit_x * unit_y,
            ROOT3 * unit_y * unit_z,
            0.5 * (3.0 * unit_z * unit_z - 1.0),
            ROOT3 * unit_x * unit_z,
            0.5 * ROOT3 * (unit_x * unit_x - unit_y * unit_y),
        ]
    )
    scaled = radius / CUTOFF
    envelope = 1.0 - 28.0 * scaled**6 + 48.0 * scaled**7 - 21.0 * scaled**8
    orders = jnp.arange(1, NB + 1).astype(jnp.float32)[:, None]
    bessel = (
        math.sqrt(2.0 / CUTOFF)
        * jnp.sin(orders * math.pi * scaled[None, :])
        / radius[None, :]
        * envelope[None, :]
    )
    return (first_harm, second_harm, bessel)


def radial(bessel, weight_in, weight_out):
    hidden = jax.nn.silu(jnp.einsum("nr,ne->re", weight_in, bessel, precision=PRECISE))
    return jnp.einsum("rk,re->ke", weight_out, hidden, precision=PRECISE)


def first_messages(
    first_harm, second_harm, bessel, sender_feat, edge_weight, weight_in, weight_out
):
    channels = sender_feat.shape[0]
    edge_weights = radial(bessel, weight_in, weight_out)
    scalar_part = (edge_weights[:channels] * sender_feat)[None]
    vector_part = (edge_weights[channels : 2 * channels] * sender_feat)[None] * first_harm[
        :, None, :
    ]
    tensor_part = (edge_weights[2 * channels :] * sender_feat)[None] * second_harm[:, None, :]
    return jnp.concatenate([scalar_part, vector_part, tensor_part], axis=0) * edge_weight


def node_first(summed, scalar_prev, mix_first, mix_square):
    gathered = summed * INV_NEIGH
    channels = scalar_prev.shape[0]
    mixed = jnp.einsum("cd,ca->da", mix_first, gathered[0], precision=PRECISE)
    vectors = jnp.einsum("mca,cd->mda", gathered[1:4], mix_square[0], precision=PRECISE)
    tensors = jnp.einsum("mca,cd->mda", gathered[4:9], mix_square[1], precision=PRECISE)
    scalars = scalar_prev + jax.nn.silu(mixed[:channels])
    vectors = jax.nn.sigmoid(mixed[channels : 2 * channels])[None] * vectors
    tensors = jax.nn.sigmoid(mixed[2 * channels :])[None] * tensors
    return jnp.concatenate([scalars[None], vectors, tensors], axis=0)


def second_messages(
    first_harm, second_harm, bessel, sender_feat, edge_weight, weight_in, weight_out
):
    channels = sender_feat.shape[1]
    edge_weights = radial(bessel, weight_in, weight_out)
    along_first = jnp.einsum("kce,ke->ce", sender_feat[1:4], first_harm, precision=PRECISE)
    along_second = jnp.einsum("kce,ke->ce", sender_feat[4:9], second_harm, precision=PRECISE)
    combined = (
        edge_weights[:channels] * sender_feat[0]
        + edge_weights[channels : 2 * channels] * along_first
        + edge_weights[2 * channels :] * along_second
    )
    return combined * edge_weight


def node_second(features, summed, mix_square, readout):
    scalars = features[0] + jax.nn.silu(
        jnp.einsum("cd,ca->da", mix_square[2], summed * INV_NEIGH, precision=PRECISE)
    )
    return jnp.einsum("c,ca->a", readout, scalars, precision=PRECISE)


def factored(gradient, weight, row_state, col_state):
    decay_rate = 1.0 - STEP_NUM ** (-0.8)
    squares = gradient * gradient + EPS_SQUARE
    row_new = decay_rate * row_state + (1.0 - decay_rate) * jnp.mean(squares, axis=-1)
    col_new = decay_rate * col_state + (1.0 - decay_rate) * jnp.mean(squares, axis=-2)
    second = (
        row_new[..., :, None]
        * col_new[..., None, :]
        / jnp.mean(row_new, axis=-1, keepdims=True)[..., None]
    )
    weight_rms = jnp.sqrt(jnp.mean(weight * weight, axis=(-2, -1), keepdims=True) + 1e-06)
    weight_new = weight - RELATIVE * weight_rms * gradient * lax.rsqrt(second)
    return (gradient, row_new, col_new, weight_new, weight_new.astype(jnp.bfloat16))


def unfactored(gradient, weight, second):
    decay_rate = 1.0 - STEP_NUM ** (-0.8)
    second_new = decay_rate * second + (1.0 - decay_rate) * (gradient * gradient + EPS_SQUARE)
    weight_rms = jnp.sqrt(jnp.mean(weight * weight) + 1e-06)
    weight_new = weight - RELATIVE * weight_rms * gradient * lax.rsqrt(second_new)
    return (gradient, second_new, weight_new, weight_new.astype(jnp.bfloat16))


def add_trees(trees):
    return reduce(lambda left, right: jax.tree.map(jnp.add, left, right), trees)


def per_system(values):
    return values.reshape(SYS_LOC, -1).sum(axis=1)


def build(send_row, arrived_lists, mask_row, atom_count, spec_hot):
    edge_weight = mask_row.astype(jnp.float32)
    arrived_row = arrived_lists[0]
    send_hot = (send_row[None, :] == jnp.arange(atom_count)[:, None]).astype(jnp.float32)
    inc_hot = (arrived_row[None, :] == jnp.arange(atom_count)[:, None]).astype(jnp.float32)

    def fetch_positions(coords):
        return lax.all_to_all(
            jnp.dot(coords, inc_hot, precision=PRECISE),
            "edge",
            split_axis=1,
            concat_axis=1,
            tiled=True,
        )

    def return_positions(cotangent):
        arrived = lax.all_to_all(cotangent, "edge", split_axis=1, concat_axis=1, tiled=True)
        return jnp.einsum("de,ae->da", arrived, inc_hot, precision=PRECISE)

    def collect(values):
        arrived = lax.all_to_all(values, "edge", split_axis=2, concat_axis=2, tiled=True)
        return jnp.einsum("mce,ae->mca", arrived, inc_hot, precision=PRECISE)

    def spread(values):
        per_slot = jnp.einsum("mca,ae->mce", values, inc_hot, precision=PRECISE)
        return lax.all_to_all(per_slot, "edge", split_axis=2, concat_axis=2, tiled=True)

    def scalar_start(params):
        return jnp.einsum("tc,ta->ca", params[0], spec_hot, precision=PRECISE)

    def give_back(aux_cot, recv_cot):
        return return_positions(aux_cot + recv_cot)

    def edge_first(coords, recv_pos, params):
        first_harm, second_harm, bessel = geometry(
            jnp.dot(coords, send_hot, precision=PRECISE), recv_pos
        )
        sender_feat = jnp.dot(scalar_start(params), send_hot, precision=PRECISE)
        return first_messages(
            first_harm, second_harm, bessel, sender_feat, edge_weight, params[1][0], params[2][0]
        )

    def collect_first(values):
        return collect(values)

    def spread_first(values):
        return spread(values)

    def node_one(summed, params):
        return node_first(summed, scalar_start(params), params[3], params[4])

    def edge_second(coords, recv_pos, features, params):
        first_harm, second_harm, bessel = geometry(
            jnp.dot(coords, send_hot, precision=PRECISE), recv_pos
        )
        sender_feat = jnp.einsum("mca,ae->mce", features, send_hot, precision=PRECISE)
        return second_messages(
            first_harm, second_harm, bessel, sender_feat, edge_weight, params[1][1], params[2][1]
        )[None]

    def node_two(features, summed, params):
        return node_second(features, summed[0], params[4], params[5])

    def back_node_two(features, summed, params):
        _, pullback = jax.vjp(
            lambda feature_in, summed_in: node_two(feature_in, summed_in, params), features, summed
        )
        return pullback(jnp.ones((atom_count,), jnp.float32))

    def back_edge_two(coords, recv_pos, features, params, cotangent):
        _, pullback = jax.vjp(
            lambda where_at, recv_at, feature_in: edge_second(
                where_at, recv_at, feature_in, params
            ),
            coords,
            recv_pos,
            features,
        )
        return pullback(cotangent)

    def back_node_one(summed, params, cotangent):
        _, pullback = jax.vjp(lambda summed_in: node_one(summed_in, params), summed)
        return pullback(cotangent)[0]

    def back_edge_one(coords, aux_pos, params, cotangent):
        _, pullback = jax.vjp(
            lambda where_at, aux_at: edge_first(where_at, aux_at, params), coords, aux_pos
        )
        return pullback(cotangent)

    def evaluate(coords, params):
        recv_pos = fetch_positions(coords)
        summed_one = collect_first(edge_first(coords, recv_pos, params))
        features = node_one(summed_one, params)
        summed_two = collect(edge_second(coords, recv_pos, features, params))
        energies = node_two(features, summed_two, params)
        feature_node, summed_two_bar = back_node_two(features, summed_two, params)
        second_bar = spread(summed_two_bar)
        coord_second, recv_second, feature_edge = back_edge_two(
            coords, recv_pos, features, params, second_bar
        )
        feature_bar = feature_node + feature_edge
        first_bar = spread_first(back_node_one(summed_one, params, feature_bar))
        coord_first, aux_first = back_edge_one(coords, recv_pos, params, first_bar)
        forces = -(coord_first + coord_second + give_back(aux_first, recv_second))
        stored = (
            coords,
            recv_pos,
            recv_pos,
            summed_one,
            features,
            summed_two,
            second_bar,
            feature_bar,
            first_bar,
        )
        return (energies, forces, stored)

    def reverse(stored, params, energy_bar, force_bar):
        (
            coords,
            recv_pos,
            aux_pos,
            summed_one,
            features,
            summed_two,
            second_bar,
            feature_bar,
            first_bar,
        ) = stored
        coord_cot = -force_bar
        recv_cot = fetch_positions(coord_cot)
        _, pullback = jax.vjp(back_edge_one, coords, aux_pos, params, first_bar)
        coord_one, aux_one, param_one, first_cot = pullback((coord_cot, recv_cot))
        _, pullback = jax.vjp(back_node_one, summed_one, params, feature_bar)
        summed_one_a, param_two, feature_cot = pullback(collect_first(first_cot))
        _, pullback = jax.vjp(back_edge_two, coords, recv_pos, features, params, second_bar)
        coord_two, recv_two, feature_one, param_three, second_cot = pullback(
            (coord_cot, recv_cot, feature_cot)
        )
        _, pullback = jax.vjp(back_node_two, features, summed_two, params)
        feature_two, summed_two_a, param_four = pullback((feature_cot, collect(second_cot)))
        _, pullback = jax.vjp(node_two, features, summed_two, params)
        feature_three, summed_two_b, param_five = pullback(energy_bar)
        _, pullback = jax.vjp(edge_second, coords, recv_pos, features, params)
        coord_three, recv_three, feature_four, param_six = pullback(
            spread(summed_two_a + summed_two_b)
        )
        _, pullback = jax.vjp(node_one, summed_one, params)
        summed_one_b, param_seven = pullback(
            feature_one + feature_two + feature_three + feature_four
        )
        _, pullback = jax.vjp(edge_first, coords, aux_pos, params)
        coord_four, aux_four, param_eight = pullback(spread_first(summed_one_a + summed_one_b))
        coord_total = (
            coord_one
            + coord_two
            + coord_three
            + coord_four
            + give_back(aux_one + aux_four, recv_two + recv_three)
        )
        param_total = add_trees(
            [
                param_one,
                param_two,
                param_three,
                param_four,
                param_five,
                param_six,
                param_seven,
                param_eight,
            ]
        )
        return (coord_total, param_total)

    return (evaluate, reverse)


def update(summed, params, states):
    embedding, radial_in, radial_out, mix_first, mix_square, readout = params
    (
        embedding_rows,
        embedding_cols,
        radial_in_rows,
        radial_in_cols,
        radial_out_rows,
        radial_out_cols,
        mix_first_rows,
        mix_first_cols,
        mix_square_rows,
        mix_square_cols,
        readout_second,
    ) = states
    emb = factored(summed[0], embedding, embedding_rows, embedding_cols)
    rin = factored(summed[1], radial_in, radial_in_rows, radial_in_cols)
    rout = factored(summed[2], radial_out, radial_out_rows, radial_out_cols)
    mfirst = factored(summed[3], mix_first, mix_first_rows, mix_first_cols)
    msquare = factored(summed[4], mix_square, mix_square_rows, mix_square_cols)
    rdout = unfactored(summed[5], readout, readout_second)
    return (
        summed[6],
        emb[0],
        emb[1],
        emb[2],
        emb[3],
        emb[4],
        rin[0],
        rin[1],
        rin[2],
        rin[3],
        rin[4],
        rout[0],
        rout[1],
        rout[2],
        rout[3],
        rout[4],
        mfirst[0],
        mfirst[1],
        mfirst[2],
        mfirst[3],
        mfirst[4],
        msquare[0],
        msquare[1],
        msquare[2],
        msquare[3],
        msquare[4],
        rdout[0],
        rdout[1],
        rdout[2],
        rdout[3],
    )


F32 = jnp.float32
BF = jnp.bfloat16
MESH = pl.DeviceIdType.MESH
ROOT15 = math.sqrt(15.0)
TILE_GROUPS = 2
CHUNK = 16
N_COMP = 9
KIND_INIT, KIND_EDGES, KIND_MSG, KIND_COT, KIND_FORCE = 0, 1, 2, 3, 4
KIND_TMSG, KIND_TCOT, KIND_TFORCE, KIND_SCATTER, KIND_GATHER, KIND_SYS = 5, 6, 7, 8, 9, 10
KINDS = 11


def dot_nn(left, right):
    return lax.dot_general(left, right, (((1,), (0,)), ((), ())), preferred_element_type=F32)


def dot_nt(left, right):
    return lax.dot_general(left, right, (((1,), (1,)), ((), ())), preferred_element_type=F32)


def two_parts(value):
    high = value.astype(BF)
    return high, (value - high.astype(F32)).astype(BF)


def two_parts_f32(value):
    high = value.astype(BF).astype(F32)
    return high, value - high


def three_parts_f32(value):
    high = value.astype(BF).astype(F32)
    rest = value - high
    middle = rest.astype(BF).astype(F32)
    return high, middle, rest - middle


def left_three(weight):
    high, low = two_parts_f32(weight)
    return jnp.concatenate([high, high, low], axis=1).astype(BF)


def right_three(value):
    high, low = two_parts(value)
    return jnp.concatenate([high, low, high], axis=0)


def right_three_small(value):
    high, low = two_parts_f32(value)
    return jnp.concatenate([high, low, high, jnp.zeros_like(high)], axis=0).astype(BF)


def stack_three(value):
    high, middle, low = three_parts_f32(value)
    return jnp.concatenate([high, middle, low, jnp.zeros_like(high)], axis=0).astype(BF)


def join_three(value):
    return value[0:8] + value[8:16] + value[16:24]


def outer_three(left, right):
    left_high, left_low = two_parts(left)
    right_high, right_low = two_parts(right)
    return (
        dot_nt(left_high, right_high)
        + dot_nt(left_low, right_high)
        + dot_nt(left_high, right_low)
    )


def logistic(value):
    return 1.0 / (1.0 + jnp.exp(jnp.minimum(-value, 80.0)))


def silu_slope(value, gate):
    return gate * (1.0 + value * (1.0 - gate))


def silu_bend(value, gate):
    return gate * (1.0 - gate) * (2.0 + value * (1.0 - 2.0 * gate))


def sin_cos_pi(turns):
    whole = jnp.floor(turns + 0.5)
    part = turns - whole
    sign = 1.0 - 2.0 * (whole - 2.0 * jnp.floor(0.5 * whole))
    square = part * part
    sine = 0.0
    for order in range(15, 0, -2):
        sine = sine * square + (-1.0) ** (order // 2) * math.pi**order / math.factorial(order)
    cosine = 0.0
    for order in range(16, -1, -2):
        cosine = cosine * square + (-1.0) ** (order // 2) * math.pi**order / math.factorial(order)
    return sign * (part * sine), sign * cosine


def sin_cos_multiples(sine, cosine):
    sines, cosines = [None, sine], [None, cosine]
    for order in range(2, 9):
        half, rest = order // 2, order - order // 2
        sines.append(sines[half] * cosines[rest] + cosines[half] * sines[rest])
        cosines.append(cosines[half] * cosines[rest] - sines[half] * sines[rest])
    return sines[1:], cosines[1:]


def second_slope(one, two, three, given):
    return (
        ROOT15 * (two * given[0] + three * given[3] + one * given[4]),
        ROOT15 * (one * given[0] + three * given[1] - two * given[4]),
        ROOT15 * (two * given[1] + one * given[3]) + 3.0 * ROOT5 * three * given[2],
    )


def rows_of(value, first, count):
    return [value[first + number : first + number + 1] for number in range(count)]


def step_kernel(
    n_edge,
    n_sys,
    pos_ref,
    vel_ref,
    spec_ref,
    send_ref,
    recv_ref,
    mask_ref,
    emb_ref,
    rin_ref,
    rout_ref,
    mfirst_ref,
    msquare_ref,
    readout_ref,
    total_ref,
    scratch,
):
    s = scratch
    channels = emb_ref.shape[1]
    wide = N_COMP * channels
    atoms = pos_ref.shape[1]
    group = TILE_GROUPS
    tiles = n_edge // group
    lanes = group * atoms
    chunks = channels // CHUNK
    me = lax.axis_index("edge")
    my_sys = lax.axis_index("sys")
    half_atoms = atoms // SYS_LOC

    def peer(distance):
        return lax.rem(me + distance, n_edge)

    def remote(source, target, kind, other):
        return pltpu.make_async_remote_copy(
            src_ref=source,
            dst_ref=target,
            send_sem=s.send_sem.at[kind, other],
            recv_sem=s.recv_sem.at[kind, me],
            device_id={"edge": other},
            device_id_type=MESH,
        )

    def landed(target, kind, other):
        pltpu.make_async_remote_copy(
            src_ref=target,
            dst_ref=target,
            send_sem=s.send_sem.at[kind, other],
            recv_sem=s.recv_sem.at[kind, other],
            device_id={"edge": other},
            device_id_type=MESH,
        ).wait_recv()

    def each_peer(action):
        def body(distance, carry):
            action(peer(distance))
            return carry

        lax.fori_loop(1, n_edge, body, 0)

    def loop(count, action):
        def body(index, carry):
            action(index)
            return carry

        lax.fori_loop(0, count, body, 0)

    def chunk_at(base, index):
        return pl.ds(pl.multiple_of(base + index * CHUNK, CHUNK), CHUNK)

    barrier = pltpu.get_barrier_semaphore()

    def greet(other):
        pl.semaphore_signal(barrier, inc=1, device_id={"edge": other}, device_id_type=MESH)

    each_peer(greet)

    def greet_sys(distance, carry):
        other = lax.rem(my_sys + distance, n_sys)
        pl.semaphore_signal(barrier, inc=1, device_id={"sys": other}, device_id_type=MESH)
        return carry

    lax.fori_loop(1, n_sys, greet_sys, 0)

    s.start_float[me] = jnp.concatenate([pos_ref[...], vel_ref[...], pos_ref[0:2]], axis=0)
    for number in range(EVALS):
        s.lists_out[:, 3 * number, :] = send_ref[number]
        s.lists_out[:, 3 * number + 1, :] = recv_ref[number]
        s.lists_out[:, 3 * number + 2, :] = mask_ref[number]
    species_row = jnp.broadcast_to(spec_ref[...], (n_edge, atoms))
    for row in range(3 * EVALS, 16):
        s.lists_out[:, row, :] = species_row

    pl.semaphore_wait(barrier, n_edge - 1 + n_sys - 1)

    def start_first(other):
        remote(s.start_float.at[me], s.start_float.at[me], KIND_INIT, other).start()
        remote(s.lists_out.at[other], s.lists_in.at[me], KIND_EDGES, other).start()

    each_peer(start_first)
    s.lists_in[me] = s.lists_out[me]

    for layer in range(2):
        w_in = rin_ref[layer]
        high, low = two_parts_f32(w_in)
        zero = jnp.zeros_like(high)
        s.w_in_left[layer] = jnp.concatenate([high, high, low, zero], axis=0).T.astype(BF)
        s.w_in_back[layer] = jnp.concatenate(
            [left_three(w_in), jnp.zeros((8, 3 * channels), BF)], axis=0
        )
        w_out = rout_ref[layer]
        s.w_out_left[layer] = left_three(w_out.T)
        s.w_out_back[layer] = left_three(w_out)
    s.mf_left[...] = left_three(mfirst_ref[...].T)
    s.mf_back[...] = left_three(mfirst_ref[...])
    for number in range(3):
        s.ms_left[number] = left_three(msquare_ref[number].T)
        s.ms_back[number] = left_three(msquare_ref[number])
    emb_pad = jnp.concatenate(
        [emb_ref[...], jnp.zeros((16 - emb_ref.shape[0], channels), F32)], axis=0
    )
    s.emb_left[...] = jnp.concatenate(list(three_parts_f32(emb_pad)), axis=0).T.astype(BF)
    s.readout_col[...] = jnp.broadcast_to(readout_ref[...], (atoms, channels)).T
    for ref in (
        s.grad_emb,
        s.grad_in,
        s.grad_out,
        s.grad_mf,
        s.grad_ms,
        s.grad_ro,
    ):
        ref[...] = jnp.zeros_like(ref)

    own_species = (lax.broadcasted_iota(jnp.int32, (16, atoms), 0) == spec_ref[...]).astype(F32)
    own_species = own_species.astype(BF)

    def species_values(hot):
        return dot_nn(s.emb_left[...], jnp.concatenate([hot, hot, hot], axis=0))

    s.start_scalar[...] = species_values(own_species)

    def first_landed(other):
        landed(s.start_float.at[other], KIND_INIT, other)
        landed(s.lists_in.at[other], KIND_EDGES, other)

    each_peer(first_landed)

    def first_sent(other):
        remote(s.start_float.at[me], s.start_float.at[me], KIND_INIT, other).wait_send()
        remote(s.lists_out.at[other], s.lists_in.at[me], KIND_EDGES, other).wait_send()

    each_peer(first_sent)
    for axis in range(3):
        s.place[axis] = s.start_float[:, axis, :]
        s.speed[axis] = s.start_float[:, 3 + axis, :]

    def one_hots(number):
        atom_row = lax.broadcasted_iota(jnp.int32, (atoms, atoms), 0)

        def hot(row):
            return (atom_row == row).astype(F32).astype(BF)

        def body(index):
            for part in range(group):
                other = index * group + part
                at = pl.ds(part * atoms, atoms)
                out_list = s.lists_out.at[other]
                in_list = s.lists_in.at[other]
                sender = out_list[pl.ds(3 * number, 1), :]
                receiver = out_list[pl.ds(3 * number + 1, 1), :]
                mask = out_list[pl.ds(3 * number + 2, 1), :]
                s.own_hot[number, index, :, at] = hot(sender)
                s.far_hot[number, index, :, at] = hot(jnp.where(mask == 0, -1, receiver))
                sender = in_list[pl.ds(3 * number, 1), :]
                receiver = in_list[pl.ds(3 * number + 1, 1), :]
                mask = in_list[pl.ds(3 * number + 2, 1), :]
                sender_hot = hot(sender)
                s.own_hot[number, tiles + index, :, at] = hot(jnp.where(mask == 0, -1, receiver))
                s.far_hot[number, tiles + index, :, at] = sender_hot
                species = in_list[pl.ds(3 * EVALS, 1), :]
                kinds = lax.broadcasted_iota(jnp.int32, (16, atoms), 0)
                species_hot = (kinds == species).astype(F32).astype(BF)
                s.kind_hot[number, index, :, at] = dot_nn(species_hot, sender_hot).astype(BF)
            s.kind_value[number, index] = species_values(s.kind_hot[number, index])

        loop(tiles, body)

    def table(rows):
        for axis in range(3):
            s.rows[:, axis, :] = rows[axis]
        for axis in range(3, 8):
            s.rows[:, axis, :] = jnp.zeros((n_edge, atoms), F32)

        def body(other):
            s.pieces[other] = stack_three(s.rows[other])

        loop(n_edge, body)

    def edge_difference(number, index):
        sign = jnp.where(index < tiles, 1.0, -1.0)
        own = dot_nn(s.pieces[me], s.own_hot[number, index])
        first = lax.rem(index, tiles) * group
        far = [
            dot_nn(s.pieces[first + part], s.far_hot[number, index, :, part * atoms : (part + 1) * atoms])
            for part in range(group)
        ]
        return sign * join_three(own - jnp.concatenate(far, axis=1))

    def scatter_rows(number, target):
        s.row_sums[...] = jnp.zeros_like(s.row_sums)

        def body(index):
            sign = jnp.where(index < tiles, 1.0, -1.0)
            parts = stack_three(s.edge_rows[index])
            s.row_sums[me] += sign * dot_nt(parts, s.own_hot[number, index])
            first = lax.rem(index, tiles) * group
            for part in range(group):
                at = slice(part * atoms, (part + 1) * atoms)
                s.row_sums[first + part] -= sign * dot_nt(
                    parts[:, at], s.far_hot[number, index, :, at]
                )

        loop(2 * tiles, body)
        for other in range(n_edge):
            total = join_three(s.row_sums[other])
            for axis in range(3):
                target[axis, other : other + 1, :] = total[axis : axis + 1]

    def geometry(number, index):
        offset = edge_difference(number, index)
        geo = s.geo.at[number, index]
        radius = jnp.sqrt(jnp.sum(offset * offset, axis=0, keepdims=True) + SOFTEN)
        inverse = 1.0 / radius
        unit = offset * inverse
        one, two, three = rows_of(unit, 0, 3)
        geo[0:3, :] = ROOT3 * unit[0:3]
        geo[3:4, :] = ROOT15 * one * two
        geo[4:5, :] = ROOT15 * two * three
        geo[5:6, :] = 0.5 * ROOT5 * (3.0 * three * three - 1.0)
        geo[6:7, :] = ROOT15 * one * three
        geo[7:8, :] = 0.5 * ROOT15 * (one * one - two * two)
        t = radius * (1.0 / CUTOFF)
        sines, cosines = sin_cos_multiples(*sin_cos_pi(t))
        sines = jnp.concatenate(sines, axis=0)
        cosines = jnp.concatenate(cosines, axis=0)
        t2 = t * t
        t4 = t2 * t2
        amount = math.sqrt(2.0 / CUTOFF) * inverse
        env = 1.0 - t4 * t2 * (28.0 - 48.0 * t + 21.0 * t2)
        env_one = -168.0 / CUTOFF * t4 * t * (1.0 - t) * (1.0 - t)
        env_two = -168.0 / CUTOFF**2 * t4 * (1.0 - t) * (5.0 - 7.0 * t)
        front = amount * env
        front_one = amount * (env_one - env * inverse)
        front_two = amount * (env_two - 2.0 * inverse * (env_one - env * inverse))
        waves = (lax.broadcasted_iota(jnp.int32, (NB, 1), 0) + 1).astype(F32) * (
            math.pi / CUTOFF
        )
        geo[8:16, :] = front * sines
        geo[16:24, :] = front_one * sines + front * waves * cosines
        geo[24:32, :] = (
            front_two * sines + 2.0 * front_one * waves * cosines - front * waves * waves * sines
        )
        geo[32:35, :] = unit[0:3]
        geo[35:36, :] = inverse

    def first_back(number, index):
        geo = s.geo.at[number, index]
        bars = s.geo_bar.at[number, index]
        ybar = rows_of(bars[0:8, :], 0, 8)
        slope = jnp.sum(bars[8:16, :] * geo[16:24, :], axis=0, keepdims=True)
        units = rows_of(geo[32:40, :], 0, 3)
        inverse = geo[35:36, :]
        extra = second_slope(*units, ybar[3:])
        back = [ROOT3 * ybar[axis] + extra[axis] for axis in range(3)]
        along = back[0] * units[0] + back[1] * units[1] + back[2] * units[2]
        rest = slope - along * inverse
        for axis in range(3):
            bars[16 + axis : 17 + axis, :] = back[axis]
            s.edge_rows[index, axis : axis + 1, :] = back[axis] * inverse + rest * units[axis]
        bars[19:20, :] = rest

    def geometry_tangent(number, index):
        move = edge_difference(number, index)
        geo = s.geo.at[number, index]
        out = s.geo_dot.at[index]
        inverse = geo[35:36, :]
        one, two, three = rows_of(geo[32:40, :], 0, 3)
        moves = rows_of(move, 0, 3)
        speed = one * moves[0] + two * moves[1] + three * moves[2]
        d_one, d_two, d_three = [
            (amount - unit * speed) * inverse for amount, unit in zip(moves, (one, two, three))
        ]
        out[0:1, :] = ROOT3 * d_one
        out[1:2, :] = ROOT3 * d_two
        out[2:3, :] = ROOT3 * d_three
        out[3:4, :] = ROOT15 * (d_one * two + one * d_two)
        out[4:5, :] = ROOT15 * (d_two * three + two * d_three)
        out[5:6, :] = 3.0 * ROOT5 * three * d_three
        out[6:7, :] = ROOT15 * (d_one * three + one * d_three)
        out[7:8, :] = ROOT15 * (one * d_one - two * d_two)
        out[8:16, :] = geo[16:24, :] * speed
        out[16:17, :] = d_one
        out[17:18, :] = d_two
        out[18:19, :] = d_three
        out[19:20, :] = speed
        out[20:23, :] = move[0:3]

    def second_back(number, index, hats):
        geo = s.geo.at[number, index]
        bars = s.geo_bar.at[number, index]
        dots = s.geo_dot.at[index]
        units = rows_of(geo[32:40, :], 0, 3)
        inverse = geo[35:36, :]
        turns = rows_of(dots[16:24, :], 0, 3)
        speed = dots[19:20, :]
        moves = rows_of(dots[16:24, :], 4, 3)
        back = rows_of(bars[16:24, :], 0, 3)
        rest = bars[19:20, :]
        yhat = rows_of(hats, 0, 8)
        ybar = rows_of(bars[0:8, :], 0, 8)
        extra = second_slope(*units, yhat[3:])
        more = second_slope(*turns, ybar[3:])
        radial_hat = jnp.sum(
            hats[8:16] * geo[16:24, :] + speed * (bars[8:16, :] * geo[24:32, :]),
            axis=0,
            keepdims=True,
        ) - inverse * (turns[0] * back[0] + turns[1] * back[1] + turns[2] * back[2])
        unit_hat = [
            ROOT3 * yhat[axis]
            + extra[axis]
            + more[axis]
            - speed * inverse * back[axis]
            + rest * moves[axis]
            for axis in range(3)
        ]
        along = unit_hat[0] * units[0] + unit_hat[1] * units[1] + unit_hat[2] * units[2]
        left = radial_hat - along * inverse
        for axis in range(3):
            s.edge_rows[index, axis : axis + 1, :] = unit_hat[axis] * inverse + left * units[axis]

    def radial_forward(layer, number, index, basis):
        before = dot_nn(s.w_in_left[layer], right_three_small(basis))
        s.hidden[layer, number, index] = before
        gate = logistic(before)
        s.radial[layer, number, index] = dot_nn(
            s.w_out_left[layer], right_three(before * gate)
        )

    def radial_tangent(layer, number, index, basis_dot):
        before = s.hidden[layer, number, index]
        before_dot = dot_nn(s.w_in_left[layer], right_three_small(basis_dot))
        s.hidden_dot[layer, index] = before_dot
        gate = logistic(before)
        s.radial_dot[layer, index] = dot_nn(
            s.w_out_left[layer], right_three(silu_slope(before, gate) * before_dot)
        )

    def radial_back(layer, number, index, high_ref, low_ref):
        high, low = high_ref[...], low_ref[...]
        hidden_bar = dot_nn(s.w_out_back[layer], jnp.concatenate([high, low, high], axis=0))
        s.hidden_bar[layer, number, index] = hidden_bar
        before = s.hidden[layer, number, index]
        before_bar = silu_slope(before, logistic(before)) * hidden_bar
        return dot_nn(s.w_in_back[layer], right_three(before_bar))[0:8]

    def radial_second(layer, number, index, basis, basis_dot):
        first_high, first_low = s.r_high[...], s.r_low[...]
        next_high, next_low = s.h_high[...], s.h_low[...]
        hidden_hat = dot_nn(
            s.w_out_back[layer], jnp.concatenate([next_high, next_low, next_high], axis=0)
        )
        before = s.hidden[layer, number, index]
        before_dot = s.hidden_dot[layer, index]
        hidden_bar = s.hidden_bar[layer, number, index]
        gate = logistic(before)
        slope = silu_slope(before, gate)
        before_hat = slope * hidden_hat + silu_bend(before, gate) * before_dot * hidden_bar
        before_bar = slope * hidden_bar
        out_high, out_low = two_parts(before * gate)
        dot_high, dot_low = two_parts(slope * before_dot)
        s.grad_out[layer] += (
            dot_nt(out_high, next_high)
            + dot_nt(out_low, next_high)
            + dot_nt(out_high, next_low)
            + dot_nt(dot_high, first_high)
            + dot_nt(dot_low, first_high)
            + dot_nt(dot_high, first_low)
        )
        s.grad_in[layer] += outer_three(basis, before_hat) + outer_three(basis_dot, before_bar)
        return dot_nn(s.w_in_back[layer], right_three(before_hat))[0:8]

    def put_pieces(high_ref, low_ref, at, value):
        high, low = two_parts(value)
        high_ref[at, :] = high
        low_ref[at, :] = low

    def add_scatter(total, hot):
        total[...] += dot_nt(s.m_high[...], hot) + dot_nt(s.m_low[...], hot)

    def harmonic_rows(ref):
        return [ref[row : row + 1, :] for row in range(8)]

    def fold(value):
        return value[0:8] + value[8:16]

    def sum_rows(parts):
        return jnp.concatenate([jnp.sum(part, axis=0, keepdims=True) for part in parts], axis=0)

    def first_forward(number, index):
        tile = tiles + index
        geo = s.geo.at[number, tile]
        radial_forward(0, number, index, geo[8:16, :])
        rad = s.radial.at[0, number, index]
        kind = s.kind_value.at[number, index]

        def body(c):
            value = kind[chunk_at(0, c), :]
            y = harmonic_rows(geo)
            put_pieces(s.m_high, s.m_low, chunk_at(0, c), rad[chunk_at(0, c), :] * value)
            vector = rad[chunk_at(channels, c), :] * value
            tensor = rad[chunk_at(2 * channels, c), :] * value
            for k in range(8):
                part = (vector if k < 3 else tensor) * y[k]
                put_pieces(s.m_high, s.m_low, chunk_at((k + 1) * channels, c), part)

        loop(chunks, body)
        add_scatter(s.sum_wide, s.own_hot[number, tile])

    def first_tangent(number, index):
        tile = tiles + index
        geo = s.geo.at[number, tile]
        dots = s.geo_dot.at[tile]
        radial_tangent(0, number, index, dots[8:16, :])
        rad = s.radial.at[0, number, index]
        rad_dot = s.radial_dot.at[0, index]
        kind = s.kind_value.at[number, index]

        def body(c):
            value = kind[chunk_at(0, c), :]
            y = harmonic_rows(geo)
            y_dot = harmonic_rows(dots)
            put_pieces(s.m_high, s.m_low, chunk_at(0, c), rad_dot[chunk_at(0, c), :] * value)
            vector = rad[chunk_at(channels, c), :] * value
            tensor = rad[chunk_at(2 * channels, c), :] * value
            vector_dot = rad_dot[chunk_at(channels, c), :] * value
            tensor_dot = rad_dot[chunk_at(2 * channels, c), :] * value
            for k in range(8):
                base, move = (vector, vector_dot) if k < 3 else (tensor, tensor_dot)
                part = move * y[k] + base * y_dot[k]
                put_pieces(s.m_high, s.m_low, chunk_at((k + 1) * channels, c), part)

        loop(chunks, body)
        add_scatter(s.sum_wide, s.own_hot[number, tile])

    def gather_wide(hot):
        return dot_nn(s.a_high[...], hot) + dot_nn(s.a_low[...], hot)

    def first_reverse(number, index):
        tile = tiles + index
        geo = s.geo.at[number, tile]
        s.first_cot[number, index] = gather_wide(s.own_hot[number, tile])
        cot = s.first_cot.at[number, index]
        rad = s.radial.at[0, number, index]
        kind = s.kind_value.at[number, index]

        def body(c, sums):
            value = kind[chunk_at(0, c), :]
            y = harmonic_rows(geo)
            put_pieces(s.r_high, s.r_low, chunk_at(0, c), cot[chunk_at(0, c), :] * value)
            sums = list(sums)
            for first, last, path in ((0, 3, 1), (3, 8, 2)):
                base = rad[chunk_at(path * channels, c), :] * value
                total = 0.0
                for k in range(first, last):
                    given = cot[chunk_at((k + 1) * channels, c), :]
                    total = total + given * y[k]
                    sums[k] = sums[k] + fold(base * given)
                put_pieces(s.r_high, s.r_low, chunk_at(path * channels, c), total * value)
            return tuple(sums)

        sums = lax.fori_loop(0, chunks, body, (jnp.zeros((8, lanes), F32),) * 8)
        s.geo_bar[number, tile, 0:8, :] = sum_rows(sums)
        s.geo_bar[number, tile, 8:16, :] = radial_back(0, number, index, s.r_high, s.r_low)
        first_back(number, tile)

    def first_second(number, index):
        tile = tiles + index
        geo = s.geo.at[number, tile]
        dots = s.geo_dot.at[tile]
        s.wide_tile[...] = gather_wide(s.own_hot[number, tile])
        hat = s.wide_tile
        cot = s.first_cot.at[number, index]
        rad = s.radial.at[0, number, index]
        rad_dot = s.radial_dot.at[0, index]
        kind = s.kind_value.at[number, index]

        def body(c, sums):
            value = kind[chunk_at(0, c), :]
            y = harmonic_rows(geo)
            y_dot = harmonic_rows(dots)
            sums = list(sums)
            total = cot[chunk_at(0, c), :]
            total_hat = hat[chunk_at(0, c), :]
            put_pieces(s.r_high, s.r_low, chunk_at(0, c), total * value)
            put_pieces(s.h_high, s.h_low, chunk_at(0, c), total_hat * value)
            value_hat = rad[chunk_at(0, c), :] * total_hat + rad_dot[chunk_at(0, c), :] * total
            for first, last, path in ((0, 3, 1), (3, 8, 2)):
                rad_here = rad[chunk_at(path * channels, c), :]
                rad_move = rad_dot[chunk_at(path * channels, c), :]
                base = rad_here * value
                move = rad_move * value
                total = 0.0
                total_hat = 0.0
                for k in range(first, last):
                    given = cot[chunk_at((k + 1) * channels, c), :]
                    given_hat = hat[chunk_at((k + 1) * channels, c), :]
                    total = total + given * y[k]
                    total_hat = total_hat + (given_hat * y[k] + given * y_dot[k])
                    sums[k] = sums[k] + fold(base * given_hat + move * given)
                put_pieces(s.r_high, s.r_low, chunk_at(path * channels, c), total * value)
                put_pieces(s.h_high, s.h_low, chunk_at(path * channels, c), total_hat * value)
                value_hat = value_hat + rad_here * total_hat + rad_move * total
            put_pieces(s.v_high, s.v_low, chunk_at(0, c), value_hat)
            return tuple(sums)

        sums = lax.fori_loop(0, chunks, body, (jnp.zeros((8, lanes), F32),) * 8)
        kinds = s.kind_hot[number, index]
        s.grad_emb[...] += dot_nt(kinds, s.v_high[...]) + dot_nt(kinds, s.v_low[...])
        basis_hat = radial_second(0, number, index, geo[8:16, :], dots[8:16, :])
        second_back(number, tile, jnp.concatenate([sum_rows(sums), basis_hat], axis=0))

    def gather_far(ref, number, index):
        found = []
        for part in range(group):
            high, low = two_parts(ref[index * group + part])
            hot = s.far_hot[number, index, :, part * atoms : (part + 1) * atoms]
            found.append(dot_nn(high, hot) + dot_nn(low, hot))
        return jnp.concatenate(found, axis=1)

    def send_messages(number, index, kind):
        for part in range(group):
            other = index * group + part
            at = slice(part * atoms, (part + 1) * atoms)
            hot = s.far_hot[number, index, :, at]
            s.msg_out[other] = dot_nt(s.v_high[:, at], hot) + dot_nt(s.v_low[:, at], hot)

            @pl.when(other != me)
            def _():
                remote(s.msg_out.at[other], s.msg_in.at[me], kind, other).start()

    def second_forward(number, index):
        geo = s.geo.at[number, index]
        radial_forward(1, number, index, geo[8:16, :])
        s.feat[number, index] = gather_wide(s.own_hot[number, index])
        feat = s.feat.at[number, index]
        rad = s.radial.at[1, number, index]

        def body(c):
            y = harmonic_rows(geo)
            total = rad[chunk_at(0, c), :] * feat[chunk_at(0, c), :]
            for first, last, path in ((0, 3, 1), (3, 8, 2)):
                along = 0.0
                for k in range(first, last):
                    along = along + feat[chunk_at((k + 1) * channels, c), :] * y[k]
                s.along[number, index, chunk_at((path - 1) * channels, c), :] = along
                total = total + rad[chunk_at(path * channels, c), :] * along
            put_pieces(s.v_high, s.v_low, chunk_at(0, c), total)

        loop(chunks, body)
        send_messages(number, index, KIND_MSG)

    def second_tangent(number, index):
        geo = s.geo.at[number, index]
        dots = s.geo_dot.at[index]
        radial_tangent(1, number, index, dots[8:16, :])
        s.feat_dot[index] = gather_wide(s.own_hot[number, index])
        feat = s.feat.at[number, index]
        feat_dot = s.feat_dot.at[index]
        rad = s.radial.at[1, number, index]
        rad_dot = s.radial_dot.at[1, index]

        def body(c):
            y = harmonic_rows(geo)
            y_dot = harmonic_rows(dots)
            at = chunk_at(0, c)
            total = rad_dot[at, :] * feat[at, :] + rad[at, :] * feat_dot[at, :]
            for first, last, path in ((0, 3, 1), (3, 8, 2)):
                move = 0.0
                for k in range(first, last):
                    here = chunk_at((k + 1) * channels, c)
                    move = move + (feat_dot[here, :] * y[k] + feat[here, :] * y_dot[k])
                here = chunk_at((path - 1) * channels, c)
                s.along_dot[index, here, :] = move
                here_rad = chunk_at(path * channels, c)
                total = total + (
                    rad_dot[here_rad, :] * s.along[number, index, here, :]
                    + rad[here_rad, :] * move
                )
            put_pieces(s.v_high, s.v_low, at, total)

        loop(chunks, body)
        send_messages(number, index, KIND_TMSG)

    def second_reverse(number, index):
        geo = s.geo.at[number, index]
        s.msg_cot[number, index] = gather_far(s.cot_all, number, index)
        cot = s.msg_cot.at[number, index]
        feat = s.feat.at[number, index]
        rad = s.radial.at[1, number, index]

        def body(c, sums):
            y = harmonic_rows(geo)
            at = chunk_at(0, c)
            given = cot[at, :]
            sums = list(sums)
            put_pieces(s.r_high, s.r_low, at, feat[at, :] * given)
            put_pieces(s.m_high, s.m_low, at, rad[at, :] * given)
            for first, last, path in ((0, 3, 1), (3, 8, 2)):
                here = chunk_at(path * channels, c)
                along = s.along[number, index, chunk_at((path - 1) * channels, c), :]
                put_pieces(s.r_high, s.r_low, here, along * given)
                base = rad[here, :] * given
                for k in range(first, last):
                    wide_at = chunk_at((k + 1) * channels, c)
                    put_pieces(s.m_high, s.m_low, wide_at, base * y[k])
                    sums[k] = sums[k] + fold(base * feat[wide_at, :])
            return tuple(sums)

        sums = lax.fori_loop(0, chunks, body, (jnp.zeros((8, lanes), F32),) * 8)
        s.geo_bar[number, index, 0:8, :] = sum_rows(sums)
        s.geo_bar[number, index, 8:16, :] = radial_back(1, number, index, s.r_high, s.r_low)
        first_back(number, index)
        add_scatter(s.sum_wide, s.own_hot[number, index])

    def second_second(number, index):
        geo = s.geo.at[number, index]
        dots = s.geo_dot.at[index]
        s.msg_hat[...] = gather_far(s.cot_all, number, index)
        cot = s.msg_cot.at[number, index]
        feat = s.feat.at[number, index]
        feat_dot = s.feat_dot.at[index]
        rad = s.radial.at[1, number, index]
        rad_dot = s.radial_dot.at[1, index]

        def body(c, sums):
            y = harmonic_rows(geo)
            y_dot = harmonic_rows(dots)
            at = chunk_at(0, c)
            given = cot[at, :]
            given_hat = s.msg_hat[at, :]
            sums = list(sums)
            put_pieces(s.r_high, s.r_low, at, feat[at, :] * given)
            put_pieces(s.h_high, s.h_low, at, feat[at, :] * given_hat + feat_dot[at, :] * given)
            put_pieces(s.m_high, s.m_low, at, rad[at, :] * given_hat + rad_dot[at, :] * given)
            for first, last, path in ((0, 3, 1), (3, 8, 2)):
                here = chunk_at(path * channels, c)
                along_at = chunk_at((path - 1) * channels, c)
                along = s.along[number, index, along_at, :]
                along_dot = s.along_dot[index, along_at, :]
                put_pieces(s.r_high, s.r_low, here, along * given)
                put_pieces(s.h_high, s.h_low, here, along * given_hat + along_dot * given)
                base = rad[here, :] * given
                base_hat = rad[here, :] * given_hat + rad_dot[here, :] * given
                for k in range(first, last):
                    wide_at = chunk_at((k + 1) * channels, c)
                    put_pieces(s.m_high, s.m_low, wide_at, base_hat * y[k] + base * y_dot[k])
                    sums[k] = sums[k] + fold(
                        base_hat * feat[wide_at, :] + base * feat_dot[wide_at, :]
                    )
            return tuple(sums)

        sums = lax.fori_loop(0, chunks, body, (jnp.zeros((8, lanes), F32),) * 8)
        basis_hat = radial_second(1, number, index, geo[8:16, :], dots[8:16, :])
        second_back(number, index, jnp.concatenate([sum_rows(sums), basis_hat], axis=0))
        add_scatter(s.sum_wide, s.own_hot[number, index])

    def part_of(ref, component):
        return ref[component * channels : (component + 1) * channels, :]

    def linear(left, value):
        return dot_nn(left, right_three(value))

    def keep_wide(component, value):
        high, low = two_parts(value)
        s.a_high[component * channels : (component + 1) * channels, :] = high
        s.a_low[component * channels : (component + 1) * channels, :] = low

    def node_first_forward(number):
        s.agg[number] = INV_NEIGH * s.sum_wide[...]
        agg = s.agg.at[number]
        mixed = linear(s.mf_left[...], part_of(agg, 0))
        s.mixed[number] = mixed
        before, gate_one, gate_two = [mixed[i * channels : (i + 1) * channels] for i in range(3)]
        scalar = s.start_scalar[...] + before * logistic(before)
        s.scalar[number] = scalar
        keep_wide(0, scalar)
        gates = (logistic(gate_one), logistic(gate_two))
        for k in range(8):
            path = 0 if k < 3 else 1
            raw = linear(s.ms_left[path], part_of(agg, k + 1))
            s.raw[number, k * channels : (k + 1) * channels, :] = raw
            keep_wide(k + 1, gates[path] * raw)

    def node_first_tangent(number):
        s.agg_dot[...] = INV_NEIGH * s.sum_wide[...]
        mixed = s.mixed.at[number]
        mixed_dot = linear(s.mf_left[...], part_of(s.agg_dot, 0))
        s.mixed_dot[...] = mixed_dot
        before = part_of(mixed, 0)
        scalar_dot = silu_slope(before, logistic(before)) * mixed_dot[0:channels]
        s.scalar_dot[...] = scalar_dot
        keep_wide(0, scalar_dot)
        for first, last, path in ((0, 3, 0), (3, 8, 1)):
            gate = logistic(part_of(mixed, path + 1))
            move = gate * (1.0 - gate) * mixed_dot[(path + 1) * channels : (path + 2) * channels]
            for k in range(first, last):
                raw_dot = linear(s.ms_left[path], part_of(s.agg_dot, k + 1))
                s.raw_dot[k * channels : (k + 1) * channels, :] = raw_dot
                raw = s.raw[number, k * channels : (k + 1) * channels, :]
                keep_wide(k + 1, move * raw + gate * raw_dot)

    def node_first_reverse(number):
        s.feat_bar[number] = s.sum_wide[...]
        s.feat_bar[number, 0:channels, :] += s.readout_col[...]
        bar = s.feat_bar.at[number]
        mixed = s.mixed.at[number]
        before = part_of(mixed, 0)
        s.mixed_bar[number, 0:channels, :] = silu_slope(before, logistic(before)) * part_of(bar, 0)
        for first, last, path in ((0, 3, 0), (3, 8, 1)):
            gate = logistic(part_of(mixed, path + 1))
            total = 0.0
            for k in range(first, last):
                given = part_of(bar, k + 1)
                total = total + given * s.raw[number, k * channels : (k + 1) * channels, :]
                raw_bar = gate * given
                s.raw_bar[number, k * channels : (k + 1) * channels, :] = raw_bar
                keep_wide(k + 1, INV_NEIGH * linear(s.ms_back[path], raw_bar))
            s.mixed_bar[number, (path + 1) * channels : (path + 2) * channels, :] = (
                gate * (1.0 - gate) * total
            )
        keep_wide(0, INV_NEIGH * linear(s.mf_back[...], s.mixed_bar[number]))

    def node_first_second(number, energy_bar):
        s.sum_wide[0:channels, :] += s.readout_col[...] * energy_bar
        hat = s.sum_wide
        bar = s.feat_bar.at[number]
        mixed = s.mixed.at[number]
        before = part_of(mixed, 0)
        gate = logistic(before)
        scalar_hat = part_of(hat, 0)
        s.mixed_hat[0:channels, :] = silu_slope(before, gate) * scalar_hat + silu_bend(
            before, gate
        ) * s.mixed_dot[0:channels, :] * part_of(bar, 0)
        s.grad_emb[...] += dot_nt(own_species, two_parts(scalar_hat)[0]) + dot_nt(
            own_species, two_parts(scalar_hat)[1]
        )
        for first, last, path in ((0, 3, 0), (3, 8, 1)):
            gate = logistic(part_of(mixed, path + 1))
            slope = gate * (1.0 - gate)
            bend = slope * (1.0 - 2.0 * gate)
            mixed_dot = s.mixed_dot[(path + 1) * channels : (path + 2) * channels, :]
            one = 0.0
            two = 0.0
            grad = 0.0
            for k in range(first, last):
                at = slice(k * channels, (k + 1) * channels)
                given = part_of(bar, k + 1)
                given_hat = part_of(hat, k + 1)
                raw = s.raw[number, at, :]
                one = one + (given_hat * raw + given * s.raw_dot[at, :])
                two = two + given * raw
                raw_hat = gate * given_hat + slope * mixed_dot * given
                keep_wide(k + 1, INV_NEIGH * linear(s.ms_back[path], raw_hat))
                grad = grad + outer_three(part_of(s.agg.at[number], k + 1), raw_hat)
                grad = grad + outer_three(part_of(s.agg_dot, k + 1), s.raw_bar[number, at, :])
            s.grad_ms[path] += grad
            s.mixed_hat[(path + 1) * channels : (path + 2) * channels, :] = (
                slope * one + bend * mixed_dot * two
            )
        keep_wide(0, INV_NEIGH * linear(s.mf_back[...], s.mixed_hat[...]))
        s.grad_mf[...] += outer_three(part_of(s.agg.at[number], 0), s.mixed_hat[...])
        s.grad_mf[...] += outer_three(part_of(s.agg_dot, 0), s.mixed_bar[number])

    def collect_messages(kind):
        s.msg_in[me] = s.msg_out[me]

        def wait_message(other):
            landed(s.msg_in.at[other], kind, other)
            remote(s.msg_out.at[other], s.msg_in.at[me], kind, other).wait_send()

        each_peer(wait_message)
        total = s.msg_in[0]
        for other in range(1, n_edge):
            total = total + s.msg_in[other]
        return INV_NEIGH * total

    def share_cotangent(value, kind):
        s.cot_all[me] = value

        def start(other):
            remote(s.cot_all.at[me], s.cot_all.at[me], kind, other).start()

        each_peer(start)

    def wait_cotangent(index, kind):
        for part in range(group):
            other = index * group + part

            @pl.when(other != me)
            def _():
                landed(s.cot_all.at[other], kind, other)

    def sent_cotangent(kind):
        def wait(other):
            remote(s.cot_all.at[me], s.cot_all.at[me], kind, other).wait_send()

        each_peer(wait)

    def node_second_forward(number):
        agg = collect_messages(KIND_MSG)
        s.agg_two[number] = agg
        before = linear(s.ms_left[2], agg)
        s.last[number] = before
        gate = logistic(before)
        s.energy_row[...] = jnp.sum(
            s.readout_col[...] * (s.scalar[number] + before * gate), axis=0, keepdims=True
        )
        before_bar = s.readout_col[...] * silu_slope(before, gate)
        share_cotangent(INV_NEIGH * linear(s.ms_back[2], before_bar), KIND_COT)

    def node_second_second(number, energy_bar):
        agg_dot = collect_messages(KIND_TMSG)
        agg = s.agg_two[number]
        before = s.last[number]
        before_dot = linear(s.ms_left[2], agg_dot)
        gate = logistic(before)
        slope = silu_slope(before, gate)
        before_hat = s.readout_col[...] * (
            energy_bar * slope + silu_bend(before, gate) * before_dot
        )
        share_cotangent(INV_NEIGH * linear(s.ms_back[2], before_hat), KIND_TCOT)
        before_bar = s.readout_col[...] * slope
        s.grad_ms[2] += outer_three(agg, before_hat) + outer_three(agg_dot, before_bar)
        s.grad_ro[...] += energy_bar * (s.scalar[number] + before * gate) + (
            s.scalar_dot[...] + slope * before_dot
        )

    def far_first(action):
        mine = lax.div(me, group)
        loop(tiles, lambda step: action(lax.rem(mine + 1 + step, tiles)))

    def near_first(action):
        mine = lax.div(me, group)
        loop(tiles, lambda step: action(lax.rem(mine + step, tiles)))

    def share_rows(out_ref, in_ref, kind):
        def start(other):
            remote(out_ref, in_ref.at[me], kind, other).start()

        each_peer(start)
        in_ref[me] = out_ref[...]

        def wait(other):
            landed(in_ref.at[other], kind, other)
            remote(out_ref, in_ref.at[me], kind, other).wait_send()

        each_peer(wait)
        total = in_ref[0]
        for other in range(1, n_edge):
            total = total + in_ref[other]
        return total

    def evaluate(number):
        one_hots(number)
        table(s.place)
        loop(2 * tiles, lambda index: geometry(number, index))
        s.sum_wide[...] = jnp.zeros_like(s.sum_wide)
        loop(tiles, lambda index: first_forward(number, index))
        node_first_forward(number)
        far_first(lambda index: second_forward(number, index))
        node_second_forward(number)
        s.sum_wide[...] = jnp.zeros_like(s.sum_wide)

        def back(index):
            wait_cotangent(index, KIND_COT)
            second_reverse(number, index)

        near_first(back)
        sent_cotangent(KIND_COT)
        node_first_reverse(number)
        loop(tiles, lambda index: first_reverse(number, index))
        scatter_rows(number, s.force_out)
        s.force_out[3] = jnp.zeros((n_edge, atoms), F32)
        s.force_out[3, pl.ds(me, 1), :] = s.energy_row[...]
        total = share_rows(s.force_out, s.force_in, KIND_FORCE)
        force = -total[0:3]
        s.energy[number] = total[3]
        half_kick = 0.5 * STEP_DT * force

        @pl.when(number > 0)
        def _():
            s.speed[...] = s.speed[...] + half_kick

        @pl.when(number == 0)
        def _():
            s.start_kinetic[...] = 0.5 * jnp.sum(s.speed[...] * s.speed[...], axis=0)

        @pl.when(number < EVALS - 1)
        def _():
            s.speed[...] = s.speed[...] + half_kick
            s.place[...] = s.place[...] + STEP_DT * s.speed[...]

    loop(EVALS, evaluate)

    kinetic = 0.5 * jnp.sum(s.speed[...] * s.speed[...], axis=0)
    change = (s.energy[EVALS - 1] + kinetic) - (s.energy[0] + s.start_kinetic[...])
    system_of = lax.broadcasted_iota(jnp.int32, (n_edge, atoms), 1) // half_atoms
    system_atoms = float(half_atoms * n_edge)
    loss = jnp.zeros((1, 1), F32)
    drift_grad = jnp.zeros((n_edge, atoms), F32)
    for number in range(SYS_LOC):
        mine = system_of == number
        drift = jnp.sum(jnp.where(mine, change, 0.0), axis=(0, 1), keepdims=True)
        loss = loss + drift * drift / system_atoms
        drift_grad = drift_grad + jnp.where(mine, 2.0 * drift / system_atoms, 0.0)
    s.drift_grad[...] = drift_grad
    s.place_bar[...] = jnp.zeros_like(s.place_bar)
    s.speed_bar[...] = drift_grad[None] * s.speed[...]
    loss = loss * jnp.where(me == 0, 1.0, 0.0)

    def reverse(step):
        number = EVALS - 1 - step
        sides = jnp.where(jnp.logical_or(number == 0, number == EVALS - 1), 1.0, 2.0)
        ends = jnp.where(number == 0, -1.0, jnp.where(number == EVALS - 1, 1.0, 0.0))
        s.move[...] = (-0.5 * STEP_DT * sides) * s.speed_bar[...]
        table(s.move)
        loop(2 * tiles, lambda index: geometry_tangent(number, index))
        energy_bar = ends * s.drift_grad[pl.ds(me, 1), :]
        s.sum_wide[...] = jnp.zeros_like(s.sum_wide)
        loop(tiles, lambda index: first_tangent(number, index))
        node_first_tangent(number)
        far_first(lambda index: second_tangent(number, index))
        node_second_second(number, energy_bar)
        s.sum_wide[...] = jnp.zeros_like(s.sum_wide)

        def back(index):
            wait_cotangent(index, KIND_TCOT)
            second_second(number, index)

        near_first(back)
        sent_cotangent(KIND_TCOT)
        node_first_second(number, energy_bar)
        loop(tiles, lambda index: first_second(number, index))

        @pl.when(number > 0)
        def _():
            scatter_rows(number, s.place_out)
            total = share_rows(s.place_out, s.place_in, KIND_TFORCE)
            s.place_bar[...] = s.place_bar[...] + total
            s.speed_bar[...] = s.speed_bar[...] + STEP_DT * s.place_bar[...]

    loop(EVALS, reverse)

    out = s.grad_all
    rows_each = out.shape[0] // n_edge
    blocks = []
    for layer in range(2):
        for path in range(3):
            blocks.append(s.grad_out[layer, :, path * channels : (path + 1) * channels])
    for path in range(3):
        blocks.append(s.grad_mf[:, path * channels : (path + 1) * channels])
    for number in range(3):
        blocks.append(s.grad_ms[number])
    for pair in range(6):
        out[pair * channels : (pair + 1) * channels, :] = jnp.concatenate(
            [blocks[2 * pair], blocks[2 * pair + 1]], axis=1
        )
    base = 6 * channels
    out[base : base + 8, :] = jnp.concatenate([s.grad_in[0], s.grad_in[1]], axis=1)
    ones = jnp.ones((8, atoms), BF)
    high, middle, low = three_parts_f32(s.grad_ro[...])
    ro_rows = (
        dot_nt(ones, high.astype(BF)) + dot_nt(ones, middle.astype(BF)) + dot_nt(ones, low.astype(BF))
    )
    row_of = lax.broadcasted_iota(jnp.int32, (8, channels), 0)
    ro_rows = jnp.where(row_of == 0, ro_rows, jnp.where(row_of == 1, loss, 0.0))
    out[base + 8 : base + 16, :] = jnp.concatenate([s.grad_emb[0:8, :], ro_rows], axis=1)
    rest = out.shape[0] - (base + 16)
    out[base + 16 :, :] = jnp.zeros((rest, out.shape[1]), F32)

    def part_rows(ref, other):
        return ref.at[pl.ds(pl.multiple_of(other * rows_each, 8), rows_each)]

    def start_scatter(other):
        remote(part_rows(out, other), s.part_in.at[me], KIND_SCATTER, other).start()

    each_peer(start_scatter)
    s.part_in[me] = part_rows(out, me)[...]

    def wait_scatter(other):
        landed(s.part_in.at[other], KIND_SCATTER, other)
        remote(part_rows(out, other), s.part_in.at[me], KIND_SCATTER, other).wait_send()

    each_peer(wait_scatter)
    total = s.part_in[0]
    for other in range(1, n_edge):
        total = total + s.part_in[other]
    s.sys_in[my_sys] = total

    def sys_copy(other):
        return pltpu.make_async_remote_copy(
            src_ref=s.sys_in.at[my_sys],
            dst_ref=s.sys_in.at[my_sys],
            send_sem=s.send_sem.at[KIND_SYS, other],
            recv_sem=s.recv_sem.at[KIND_SYS, my_sys],
            device_id={"sys": other},
            device_id_type=MESH,
        )

    def each_sys(action):
        def body(distance, carry):
            action(lax.rem(my_sys + distance, n_sys))
            return carry

        lax.fori_loop(1, n_sys, body, 0)

    each_sys(lambda other: sys_copy(other).start())

    def wait_sys(other):
        pltpu.make_async_remote_copy(
            src_ref=s.sys_in.at[other],
            dst_ref=s.sys_in.at[other],
            send_sem=s.send_sem.at[KIND_SYS, other],
            recv_sem=s.recv_sem.at[KIND_SYS, other],
            device_id={"sys": other},
            device_id_type=MESH,
        ).wait_recv()
        sys_copy(other).wait_send()

    each_sys(wait_sys)
    total = s.sys_in[0]
    for other in range(1, n_sys):
        total = total + s.sys_in[other]
    mine = part_rows(s.summed, me)
    mine[...] = total
    each_peer(lambda other: remote(mine, mine, KIND_GATHER, other).start())

    def wait_gather(other):
        landed(part_rows(s.summed, other), KIND_GATHER, other)
        remote(mine, mine, KIND_GATHER, other).wait_send()

    each_peer(wait_gather)
    total_ref[...] = s.summed[...]


class Scratch:
    pass


def step_scratch(n_edge, n_sys, channels, atoms, grad_rows):
    tiles = n_edge // TILE_GROUPS
    lanes = TILE_GROUPS * atoms
    wide = N_COMP * channels
    vm = lambda *shape: pltpu.VMEM(shape, F32)
    vb = lambda *shape: pltpu.VMEM(shape, BF)
    vi = lambda *shape: pltpu.VMEM(shape, jnp.int32)
    return {
        "send_sem": pltpu.SemaphoreType.DMA((KINDS, n_edge)),
        "recv_sem": pltpu.SemaphoreType.DMA((KINDS, n_edge)),
        "start_float": vm(n_edge, 8, atoms),
        "lists_out": vi(n_edge, 16, atoms),
        "lists_in": vi(n_edge, 16, atoms),
        "w_in_left": vb(2, channels, 32),
        "w_in_back": vb(2, 16, 3 * channels),
        "w_out_left": vb(2, 3 * channels, 3 * channels),
        "w_out_back": vb(2, channels, 9 * channels),
        "mf_left": vb(3 * channels, 3 * channels),
        "mf_back": vb(channels, 9 * channels),
        "ms_left": vb(3, channels, 3 * channels),
        "ms_back": vb(3, channels, 3 * channels),
        "emb_left": vb(channels, 48),
        "readout_col": vm(channels, atoms),
        "start_scalar": vm(channels, atoms),
        "place": vm(3, n_edge, atoms),
        "speed": vm(3, n_edge, atoms),
        "energy_row": vm(1, atoms),
        "energy": vm(EVALS, n_edge, atoms),
        "start_kinetic": vm(n_edge, atoms),
        "drift_grad": vm(n_edge, atoms),
        "place_bar": vm(3, n_edge, atoms),
        "speed_bar": vm(3, n_edge, atoms),
        "move": vm(3, n_edge, atoms),
        "own_hot": vb(EVALS, 2 * tiles, atoms, lanes),
        "far_hot": vb(EVALS, 2 * tiles, atoms, lanes),
        "kind_hot": vb(EVALS, tiles, 16, lanes),
        "kind_value": vm(EVALS, tiles, channels, lanes),
        "rows": vm(n_edge, 8, atoms),
        "pieces": vb(n_edge, 32, atoms),
        "row_sums": vm(n_edge, 32, atoms),
        "edge_rows": vm(2 * tiles, 8, lanes),
        "geo": vm(EVALS, 2 * tiles, 40, lanes),
        "geo_bar": vm(EVALS, 2 * tiles, 24, lanes),
        "geo_dot": vm(2 * tiles, 24, lanes),
        "hidden": vm(2, EVALS, tiles, channels, lanes),
        "hidden_bar": vm(2, EVALS, tiles, channels, lanes),
        "hidden_dot": vm(2, tiles, channels, lanes),
        "radial": vm(2, EVALS, tiles, 3 * channels, lanes),
        "radial_dot": vm(2, tiles, 3 * channels, lanes),
        "m_high": vb(wide, lanes),
        "m_low": vb(wide, lanes),
        "r_high": vb(3 * channels, lanes),
        "r_low": vb(3 * channels, lanes),
        "h_high": vb(3 * channels, lanes),
        "h_low": vb(3 * channels, lanes),
        "v_high": vb(channels, lanes),
        "v_low": vb(channels, lanes),
        "a_high": vb(wide, atoms),
        "a_low": vb(wide, atoms),
        "sum_wide": vm(wide, atoms),
        "wide_tile": vm(wide, lanes),
        "first_cot": vm(EVALS, tiles, wide, lanes),
        "feat": vm(EVALS, tiles, wide, lanes),
        "feat_dot": vm(tiles, wide, lanes),
        "along": vm(EVALS, tiles, 2 * channels, lanes),
        "along_dot": vm(tiles, 2 * channels, lanes),
        "msg_cot": vm(EVALS, tiles, channels, lanes),
        "msg_hat": vm(channels, lanes),
        "agg": vm(EVALS, wide, atoms),
        "agg_dot": vm(wide, atoms),
        "mixed": vm(EVALS, 3 * channels, atoms),
        "mixed_dot": vm(3 * channels, atoms),
        "mixed_bar": vm(EVALS, 3 * channels, atoms),
        "mixed_hat": vm(3 * channels, atoms),
        "raw": vm(EVALS, 8 * channels, atoms),
        "raw_dot": vm(8 * channels, atoms),
        "raw_bar": vm(EVALS, 8 * channels, atoms),
        "scalar": vm(EVALS, channels, atoms),
        "scalar_dot": vm(channels, atoms),
        "feat_bar": vm(EVALS, wide, atoms),
        "agg_two": vm(EVALS, channels, atoms),
        "last": vm(EVALS, channels, atoms),
        "msg_out": vm(n_edge, channels, atoms),
        "msg_in": vm(n_edge, channels, atoms),
        "cot_all": vm(n_edge, channels, atoms),
        "force_out": vm(4, n_edge, atoms),
        "force_in": vm(n_edge, 4, n_edge, atoms),
        "place_out": vm(3, n_edge, atoms),
        "place_in": vm(n_edge, 3, n_edge, atoms),
        "grad_emb": vm(16, channels),
        "grad_in": vm(2, NB, channels),
        "grad_out": vm(2, channels, 3 * channels),
        "grad_mf": vm(channels, 3 * channels),
        "grad_ms": vm(3, channels, channels),
        "grad_ro": vm(channels, atoms),
        "grad_all": vm(grad_rows, 2 * channels),
        "part_in": vm(n_edge, grad_rows // n_edge, 2 * channels),
        "sys_in": vm(n_sys, grad_rows // n_edge, 2 * channels),
        "summed": vm(grad_rows, 2 * channels),
    }


def whole_step(positions, velocities, species, senders, receivers, edge_mask, params):
    n_edge, n_sys = lax.axis_size("edge"), lax.axis_size("sys")
    atoms = positions.shape[1]
    channels = params[0].shape[1]
    unit = 8 * n_edge
    grad_rows = -(-(6 * channels + 16) // unit) * unit
    shapes = step_scratch(n_edge, n_sys, channels, atoms, grad_rows)
    names = tuple(shapes)

    def kernel(*refs):
        scratch = Scratch()
        for name, ref in zip(names, refs[13:]):
            setattr(scratch, name, ref)
        step_kernel(n_edge, n_sys, *refs[:13], scratch)

    lists = [entry.reshape(EVALS, n_edge, atoms) for entry in (senders, receivers, edge_mask)]
    embedding, radial_in, radial_out, mix_first, mix_square, readout = params
    operands = (
        positions,
        velocities,
        species[None],
        *lists,
        embedding,
        radial_in,
        radial_out,
        mix_first,
        mix_square,
        readout[None],
    )
    return pl.pallas_call(
        kernel,
        out_shape=jax.ShapeDtypeStruct((grad_rows, 2 * channels), F32),
        in_specs=[pl.BlockSpec(memory_space=pltpu.VMEM)] * len(operands),
        out_specs=pl.BlockSpec(memory_space=pltpu.VMEM),
        scratch_shapes=list(shapes.values()),
        compiler_params=pltpu.CompilerParams(
            collective_id=0, has_side_effects=True, vmem_limit_bytes=56 * 1024 * 1024
        ),
    )(*operands)


def fits_kernel(senders, atom_count):
    n_edge = lax.axis_size("edge")
    slots = senders.shape[1] // n_edge
    return slots == atom_count and atom_count % 128 == 0 and n_edge % TILE_GROUPS == 0


def unpack(total, params):
    embedding = params[0]
    kinds, channels = embedding.shape
    blocks = [
        total[
            pair * channels : (pair + 1) * channels, side * channels : (side + 1) * channels
        ]
        for pair in range(6)
        for side in range(2)
    ]
    base = 6 * channels
    return (
        total[base + 8 : base + 8 + kinds, :channels],
        jnp.stack([total[base : base + 8, :channels], total[base : base + 8, channels:]]),
        jnp.stack([jnp.concatenate(blocks[0:3], axis=1), jnp.concatenate(blocks[3:6], axis=1)]),
        jnp.concatenate(blocks[6:9], axis=1),
        jnp.stack(blocks[9:12]),
        total[base + 8, channels:],
        total[base + 9, channels],
    )


def on_device(
    positions,
    velocities,
    species,
    senders,
    receivers,
    edge_mask,
    embedding,
    radial_in,
    radial_out,
    mix_first,
    mix_square,
    readout,
    embedding_rows,
    embedding_cols,
    radial_in_rows,
    radial_in_cols,
    radial_out_rows,
    radial_out_cols,
    mix_first_rows,
    mix_first_cols,
    mix_square_rows,
    mix_square_cols,
    readout_second,
):
    params = (embedding, radial_in, radial_out, mix_first, mix_square, readout)
    atom_count = positions.shape[1]
    states = (
        embedding_rows,
        embedding_cols,
        radial_in_rows,
        radial_in_cols,
        radial_out_rows,
        radial_out_cols,
        mix_first_rows,
        mix_first_cols,
        mix_square_rows,
        mix_square_cols,
        readout_second,
    )
    if fits_kernel(senders, atom_count):
        summed = unpack(
            whole_step(positions, velocities, species, senders, receivers, edge_mask, params),
            params,
        )
        return update(summed, params, states)
    spec_hot = (species[None, :] == jnp.arange(embedding.shape[0])[:, None]).astype(jnp.float32)
    edge_lists = receivers[None]
    arrived = lax.all_to_all(edge_lists, "edge", split_axis=2, concat_axis=2, tiled=True)
    passes = [
        build(senders[number], arrived[:, number], edge_mask[number], atom_count, spec_hot)
        for number in range(EVALS)
    ]
    coords = positions
    moving = velocities
    energies, forces, stored = passes[0][0](coords, params)
    record = [stored]
    first_energy = energies
    for number in range(STEPS):
        half_speed = moving + 0.5 * STEP_DT * forces
        coords = coords + STEP_DT * half_speed
        energies, forces, stored = passes[number + 1][0](coords, params)
        record.append(stored)
        moving = half_speed + 0.5 * STEP_DT * forces
    local_sums = jnp.stack(
        [
            per_system(first_energy),
            per_system(energies),
            per_system(0.5 * jnp.sum(velocities * velocities, axis=0)),
            per_system(0.5 * jnp.sum(moving * moving, axis=0)),
        ]
    )
    totals = lax.psum(local_sums, "edge")
    drift = totals[1] + totals[3] - (totals[0] + totals[2])
    system_atoms = atom_count // SYS_LOC * lax.axis_size("edge")
    loss_local = jnp.sum(drift * drift) / system_atoms
    drift_grad = jnp.repeat(2.0 * drift / system_atoms, atom_count // SYS_LOC)
    speed_bar = drift_grad[None, :] * moving
    coord_bar = jnp.zeros_like(positions)
    force_next = jnp.zeros_like(positions)
    gradients = jax.tree.map(jnp.zeros_like, params)
    for number in reversed(range(STEPS)):
        later = number + 1
        force_bar = force_next + 0.5 * STEP_DT * speed_bar
        if later == STEPS:
            energy_bar = drift_grad
        else:
            energy_bar = jnp.zeros_like(drift_grad)
        coord_part, param_part = passes[later][1](record[later], params, energy_bar, force_bar)
        gradients = add_trees([gradients, param_part])
        coord_bar = coord_bar + coord_part
        half_bar = speed_bar + STEP_DT * coord_bar
        speed_bar = half_bar
        force_next = 0.5 * STEP_DT * half_bar
    _, param_part = passes[0][1](record[0], params, -drift_grad, force_next)
    gradients = add_trees([gradients, param_part])
    loss_term = loss_local * (lax.axis_index("edge") == 0).astype(jnp.float32)
    summed = lax.psum(
        (
            gradients[0],
            gradients[1],
            gradients[2],
            gradients[3],
            gradients[4],
            gradients[5],
            loss_term,
        ),
        ("sys", "edge"),
    )
    return update(summed, params, states)


def solution(mesh):
    placed = (
        P(None, ("sys", "edge")),
        P(None, ("sys", "edge")),
        P(("sys", "edge")),
        P(None, ("sys", "edge")),
        P(None, ("sys", "edge")),
        P(None, ("sys", "edge")),
        P(),
        P(),
        P(),
        P(),
        P(),
        P(),
        P(),
        P(),
        P(),
        P(),
        P(),
        P(),
        P(),
        P(),
        P(),
        P(),
        P(),
    )
    return jax.shard_map(
        on_device,
        mesh=mesh,
        in_specs=placed,
        out_specs=(
            P(),
            P(),
            P(),
            P(),
            P(),
            P(),
            P(),
            P(),
            P(),
            P(),
            P(),
            P(),
            P(),
            P(),
            P(),
            P(),
            P(),
            P(),
            P(),
            P(),
            P(),
            P(),
            P(),
            P(),
            P(),
            P(),
            P(),
            P(),
            P(),
            P(),
        ),
        check_vma=False,
    )
```

```python
from functools import reduce
import math

import jax
import jax.numpy as jnp
from jax import lax
from jax.experimental import pallas as pl
from jax.experimental.pallas import tpu as pltpu
from jax.sharding import PartitionSpec as P

NB = 8
SYS_LOC = 2
STEPS = 2
STEP_NUM = 10
EVALS = 3


PRECISE = lax.Precision.HIGHEST
SOFTEN = 0.25
CUTOFF = 5.0
INV_NEIGH = 0.2
STEP_DT = 0.5
RELATIVE = 0.3
EPS_SQUARE = 1e-30
ROOT3 = math.sqrt(3.0)
ROOT5 = math.sqrt(5.0)


def geometry(sender_pos, receiver_pos):
    offset_vec = sender_pos - receiver_pos
    radius = jnp.sqrt(jnp.sum(offset_vec * offset_vec, axis=0) + SOFTEN)
    direction = offset_vec / radius
    unit_x, unit_y, unit_z = (direction[0], direction[1], direction[2])
    first_harm = ROOT3 * direction
    second_harm = ROOT5 * jnp.stack(
        [
            ROOT3 * unit_x * unit_y,
            ROOT3 * unit_y * unit_z,
            0.5 * (3.0 * unit_z * unit_z - 1.0),
            ROOT3 * unit_x * unit_z,
            0.5 * ROOT3 * (unit_x * unit_x - unit_y * unit_y),
        ]
    )
    scaled = radius / CUTOFF
    envelope = 1.0 - 28.0 * scaled**6 + 48.0 * scaled**7 - 21.0 * scaled**8
    orders = jnp.arange(1, NB + 1).astype(jnp.float32)[:, None]
    bessel = (
        math.sqrt(2.0 / CUTOFF)
        * jnp.sin(orders * math.pi * scaled[None, :])
        / radius[None, :]
        * envelope[None, :]
    )
    return (first_harm, second_harm, bessel)


def radial(bessel, weight_in, weight_out):
    hidden = jax.nn.silu(jnp.einsum("nr,ne->re", weight_in, bessel, precision=PRECISE))
    return jnp.einsum("rk,re->ke", weight_out, hidden, precision=PRECISE)


def first_messages(
    first_harm, second_harm, bessel, sender_feat, edge_weight, weight_in, weight_out
):
    channels = sender_feat.shape[0]
    edge_weights = radial(bessel, weight_in, weight_out)
    scalar_part = (edge_weights[:channels] * sender_feat)[None]
    vector_part = (edge_weights[channels : 2 * channels] * sender_feat)[None] * first_harm[
        :, None, :
    ]
    tensor_part = (edge_weights[2 * channels :] * sender_feat)[None] * second_harm[:, None, :]
    return jnp.concatenate([scalar_part, vector_part, tensor_part], axis=0) * edge_weight


def node_first(summed, scalar_prev, mix_first, mix_square):
    gathered = summed * INV_NEIGH
    channels = scalar_prev.shape[0]
    mixed = jnp.einsum("cd,ca->da", mix_first, gathered[0], precision=PRECISE)
    vectors = jnp.einsum("mca,cd->mda", gathered[1:4], mix_square[0], precision=PRECISE)
    tensors = jnp.einsum("mca,cd->mda", gathered[4:9], mix_square[1], precision=PRECISE)
    scalars = scalar_prev + jax.nn.silu(mixed[:channels])
    vectors = jax.nn.sigmoid(mixed[channels : 2 * channels])[None] * vectors
    tensors = jax.nn.sigmoid(mixed[2 * channels :])[None] * tensors
    return jnp.concatenate([scalars[None], vectors, tensors], axis=0)


def second_messages(
    first_harm, second_harm, bessel, sender_feat, edge_weight, weight_in, weight_out
):
    channels = sender_feat.shape[1]
    edge_weights = radial(bessel, weight_in, weight_out)
    along_first = jnp.einsum("kce,ke->ce", sender_feat[1:4], first_harm, precision=PRECISE)
    along_second = jnp.einsum("kce,ke->ce", sender_feat[4:9], second_harm, precision=PRECISE)
    combined = (
        edge_weights[:channels] * sender_feat[0]
        + edge_weights[channels : 2 * channels] * along_first
        + edge_weights[2 * channels :] * along_second
    )
    return combined * edge_weight


def node_second(features, summed, mix_square, readout):
    scalars = features[0] + jax.nn.silu(
        jnp.einsum("cd,ca->da", mix_square[2], summed * INV_NEIGH, precision=PRECISE)
    )
    return jnp.einsum("c,ca->a", readout, scalars, precision=PRECISE)


def factored(gradient, weight, row_state, col_state):
    decay_rate = 1.0 - STEP_NUM ** (-0.8)
    squares = gradient * gradient + EPS_SQUARE
    row_new = decay_rate * row_state + (1.0 - decay_rate) * jnp.mean(squares, axis=-1)
    col_new = decay_rate * col_state + (1.0 - decay_rate) * jnp.mean(squares, axis=-2)
    second = (
        row_new[..., :, None]
        * col_new[..., None, :]
        / jnp.mean(row_new, axis=-1, keepdims=True)[..., None]
    )
    weight_rms = jnp.sqrt(jnp.mean(weight * weight, axis=(-2, -1), keepdims=True) + 1e-06)
    weight_new = weight - RELATIVE * weight_rms * gradient * lax.rsqrt(second)
    return (gradient, row_new, col_new, weight_new, weight_new.astype(jnp.bfloat16))


def unfactored(gradient, weight, second):
    decay_rate = 1.0 - STEP_NUM ** (-0.8)
    second_new = decay_rate * second + (1.0 - decay_rate) * (gradient * gradient + EPS_SQUARE)
    weight_rms = jnp.sqrt(jnp.mean(weight * weight) + 1e-06)
    weight_new = weight - RELATIVE * weight_rms * gradient * lax.rsqrt(second_new)
    return (gradient, second_new, weight_new, weight_new.astype(jnp.bfloat16))


def add_trees(trees):
    return reduce(lambda left, right: jax.tree.map(jnp.add, left, right), trees)


def per_system(values):
    return values.reshape(SYS_LOC, -1).sum(axis=1)


def build(send_row, arrived_lists, mask_row, atom_count, spec_hot):
    edge_weight = mask_row.astype(jnp.float32)
    arrived_row = arrived_lists[0]
    send_hot = (send_row[None, :] == jnp.arange(atom_count)[:, None]).astype(jnp.float32)
    inc_hot = (arrived_row[None, :] == jnp.arange(atom_count)[:, None]).astype(jnp.float32)

    def fetch_positions(coords):
        return lax.all_to_all(
            jnp.dot(coords, inc_hot, precision=PRECISE),
            "edge",
            split_axis=1,
            concat_axis=1,
            tiled=True,
        )

    def return_positions(cotangent):
        arrived = lax.all_to_all(cotangent, "edge", split_axis=1, concat_axis=1, tiled=True)
        return jnp.einsum("de,ae->da", arrived, inc_hot, precision=PRECISE)

    def collect(values):
        arrived = lax.all_to_all(values, "edge", split_axis=2, concat_axis=2, tiled=True)
        return jnp.einsum("mce,ae->mca", arrived, inc_hot, precision=PRECISE)

    def spread(values):
        per_slot = jnp.einsum("mca,ae->mce", values, inc_hot, precision=PRECISE)
        return lax.all_to_all(per_slot, "edge", split_axis=2, concat_axis=2, tiled=True)

    def scalar_start(params):
        return jnp.einsum("tc,ta->ca", params[0], spec_hot, precision=PRECISE)

    def give_back(aux_cot, recv_cot):
        return return_positions(aux_cot + recv_cot)

    def edge_first(coords, recv_pos, params):
        first_harm, second_harm, bessel = geometry(
            jnp.dot(coords, send_hot, precision=PRECISE), recv_pos
        )
        sender_feat = jnp.dot(scalar_start(params), send_hot, precision=PRECISE)
        return first_messages(
            first_harm, second_harm, bessel, sender_feat, edge_weight, params[1][0], params[2][0]
        )

    def collect_first(values):
        return collect(values)

    def spread_first(values):
        return spread(values)

    def node_one(summed, params):
        return node_first(summed, scalar_start(params), params[3], params[4])

    def edge_second(coords, recv_pos, features, params):
        first_harm, second_harm, bessel = geometry(
            jnp.dot(coords, send_hot, precision=PRECISE), recv_pos
        )
        sender_feat = jnp.einsum("mca,ae->mce", features, send_hot, precision=PRECISE)
        return second_messages(
            first_harm, second_harm, bessel, sender_feat, edge_weight, params[1][1], params[2][1]
        )[None]

    def node_two(features, summed, params):
        return node_second(features, summed[0], params[4], params[5])

    def back_node_two(features, summed, params):
        _, pullback = jax.vjp(
            lambda feature_in, summed_in: node_two(feature_in, summed_in, params), features, summed
        )
        return pullback(jnp.ones((atom_count,), jnp.float32))

    def back_edge_two(coords, recv_pos, features, params, cotangent):
        _, pullback = jax.vjp(
            lambda where_at, recv_at, feature_in: edge_second(
                where_at, recv_at, feature_in, params
            ),
            coords,
            recv_pos,
            features,
        )
        return pullback(cotangent)

    def back_node_one(summed, params, cotangent):
        _, pullback = jax.vjp(lambda summed_in: node_one(summed_in, params), summed)
        return pullback(cotangent)[0]

    def back_edge_one(coords, aux_pos, params, cotangent):
        _, pullback = jax.vjp(
            lambda where_at, aux_at: edge_first(where_at, aux_at, params), coords, aux_pos
        )
        return pullback(cotangent)

    def evaluate(coords, params):
        recv_pos = fetch_positions(coords)
        summed_one = collect_first(edge_first(coords, recv_pos, params))
        features = node_one(summed_one, params)
        summed_two = collect(edge_second(coords, recv_pos, features, params))
        energies = node_two(features, summed_two, params)
        feature_node, summed_two_bar = back_node_two(features, summed_two, params)
        second_bar = spread(summed_two_bar)
        coord_second, recv_second, feature_edge = back_edge_two(
            coords, recv_pos, features, params, second_bar
        )
        feature_bar = feature_node + feature_edge
        first_bar = spread_first(back_node_one(summed_one, params, feature_bar))
        coord_first, aux_first = back_edge_one(coords, recv_pos, params, first_bar)
        forces = -(coord_first + coord_second + give_back(aux_first, recv_second))
        stored = (
            coords,
            recv_pos,
            recv_pos,
            summed_one,
            features,
            summed_two,
            second_bar,
            feature_bar,
            first_bar,
        )
        return (energies, forces, stored)

    def reverse(stored, params, energy_bar, force_bar):
        (
            coords,
            recv_pos,
            aux_pos,
            summed_one,
            features,
            summed_two,
            second_bar,
            feature_bar,
            first_bar,
        ) = stored
        coord_cot = -force_bar
        recv_cot = fetch_positions(coord_cot)
        _, pullback = jax.vjp(back_edge_one, coords, aux_pos, params, first_bar)
        coord_one, aux_one, param_one, first_cot = pullback((coord_cot, recv_cot))
        _, pullback = jax.vjp(back_node_one, summed_one, params, feature_bar)
        summed_one_a, param_two, feature_cot = pullback(collect_first(first_cot))
        _, pullback = jax.vjp(back_edge_two, coords, recv_pos, features, params, second_bar)
        coord_two, recv_two, feature_one, param_three, second_cot = pullback(
            (coord_cot, recv_cot, feature_cot)
        )
        _, pullback = jax.vjp(back_node_two, features, summed_two, params)
        feature_two, summed_two_a, param_four = pullback((feature_cot, collect(second_cot)))
        _, pullback = jax.vjp(node_two, features, summed_two, params)
        feature_three, summed_two_b, param_five = pullback(energy_bar)
        _, pullback = jax.vjp(edge_second, coords, recv_pos, features, params)
        coord_three, recv_three, feature_four, param_six = pullback(
            spread(summed_two_a + summed_two_b)
        )
        _, pullback = jax.vjp(node_one, summed_one, params)
        summed_one_b, param_seven = pullback(
            feature_one + feature_two + feature_three + feature_four
        )
        _, pullback = jax.vjp(edge_first, coords, aux_pos, params)
        coord_four, aux_four, param_eight = pullback(spread_first(summed_one_a + summed_one_b))
        coord_total = (
            coord_one
            + coord_two
            + coord_three
            + coord_four
            + give_back(aux_one + aux_four, recv_two + recv_three)
        )
        param_total = add_trees(
            [
                param_one,
                param_two,
                param_three,
                param_four,
                param_five,
                param_six,
                param_seven,
                param_eight,
            ]
        )
        return (coord_total, param_total)

    return (evaluate, reverse)


def update(summed, params, states):
    embedding, radial_in, radial_out, mix_first, mix_square, readout = params
    (
        embedding_rows,
        embedding_cols,
        radial_in_rows,
        radial_in_cols,
        radial_out_rows,
        radial_out_cols,
        mix_first_rows,
        mix_first_cols,
        mix_square_rows,
        mix_square_cols,
        readout_second,
    ) = states
    emb = factored(summed[0], embedding, embedding_rows, embedding_cols)
    rin = factored(summed[1], radial_in, radial_in_rows, radial_in_cols)
    rout = factored(summed[2], radial_out, radial_out_rows, radial_out_cols)
    mfirst = factored(summed[3], mix_first, mix_first_rows, mix_first_cols)
    msquare = factored(summed[4], mix_square, mix_square_rows, mix_square_cols)
    rdout = unfactored(summed[5], readout, readout_second)
    return (
        summed[6],
        emb[0],
        emb[1],
        emb[2],
        emb[3],
        emb[4],
        rin[0],
        rin[1],
        rin[2],
        rin[3],
        rin[4],
        rout[0],
        rout[1],
        rout[2],
        rout[3],
        rout[4],
        mfirst[0],
        mfirst[1],
        mfirst[2],
        mfirst[3],
        mfirst[4],
        msquare[0],
        msquare[1],
        msquare[2],
        msquare[3],
        msquare[4],
        rdout[0],
        rdout[1],
        rdout[2],
        rdout[3],
    )


F32 = jnp.float32
BF = jnp.bfloat16
MESH = pl.DeviceIdType.MESH
ROOT15 = math.sqrt(15.0)
TILES = 2
CHUNK = 16
N_COMP = 9
PATHS = ((0, 3, 0), (3, 8, 1))
KIND_INIT, KIND_EDGES, KIND_MSG, KIND_COT, KIND_FORCE = 0, 1, 2, 3, 4
KIND_TMSG, KIND_TCOT, KIND_TFORCE, KIND_SCATTER, KIND_GATHER, KIND_SYS = 5, 6, 7, 8, 9, 10
KIND_PAIR, KIND_PASS = 11, 12
KINDS = 13


def dot_nn(left, right):
    return lax.dot_general(left, right, (((1,), (0,)), ((), ())), preferred_element_type=F32)


def dot_nt(left, right):
    return lax.dot_general(left, right, (((1,), (1,)), ((), ())), preferred_element_type=F32)


def two_parts(value):
    high = value.astype(BF)
    return high, (value - high.astype(F32)).astype(BF)


def two_parts_f32(value):
    high = value.astype(BF).astype(F32)
    return high, value - high


def three_parts_f32(value):
    high = value.astype(BF).astype(F32)
    rest = value - high
    middle = rest.astype(BF).astype(F32)
    return high, middle, rest - middle


def left_three(weight):
    high, low = two_parts_f32(weight)
    return jnp.concatenate([high, high, low], axis=1).astype(BF)


def right_three(value):
    high, low = two_parts(value)
    return jnp.concatenate([high, low, high], axis=0)


def right_three_small(value):
    high, low = two_parts_f32(value)
    return jnp.concatenate([high, low, high, jnp.zeros_like(high)], axis=0).astype(BF)


def stack_three(value):
    high, middle, low = three_parts_f32(value)
    return jnp.concatenate([high, middle, low, jnp.zeros_like(high)], axis=0).astype(BF)


def join_three(value):
    return value[0:8] + value[8:16] + value[16:24]


def outer_three(left, right):
    left_high, left_low = two_parts(left)
    right_high, right_low = two_parts(right)
    return (
        dot_nt(left_high, right_high)
        + dot_nt(left_low, right_high)
        + dot_nt(left_high, right_low)
    )


def logistic(value):
    return 1.0 / (1.0 + jnp.exp(jnp.minimum(-value, 80.0)))


def silu_slope(value, gate):
    return gate * (1.0 + value * (1.0 - gate))


def silu_bend(value, gate):
    return gate * (1.0 - gate) * (2.0 + value * (1.0 - 2.0 * gate))


def sin_cos_pi(turns):
    whole = jnp.floor(turns + 0.5)
    part = turns - whole
    sign = 1.0 - 2.0 * (whole - 2.0 * jnp.floor(0.5 * whole))
    square = part * part
    sine = 0.0
    for order in range(15, 0, -2):
        sine = sine * square + (-1.0) ** (order // 2) * math.pi**order / math.factorial(order)
    cosine = 0.0
    for order in range(16, -1, -2):
        cosine = cosine * square + (-1.0) ** (order // 2) * math.pi**order / math.factorial(order)
    return sign * (part * sine), sign * cosine


def sin_cos_multiples(sine, cosine):
    sines, cosines = [None, sine], [None, cosine]
    for order in range(2, 9):
        half, rest = order // 2, order - order // 2
        sines.append(sines[half] * cosines[rest] + cosines[half] * sines[rest])
        cosines.append(cosines[half] * cosines[rest] - sines[half] * sines[rest])
    return sines[1:], cosines[1:]


def second_slope(one, two, three, given):
    return (
        ROOT15 * (two * given[0] + three * given[3] + one * given[4]),
        ROOT15 * (one * given[0] + three * given[1] - two * given[4]),
        ROOT15 * (two * given[1] + one * given[3]) + 3.0 * ROOT5 * three * given[2],
    )


def rows_of(value, first, count):
    return [value[first + number : first + number + 1] for number in range(count)]


def step_kernel(
    n_edge,
    n_sys,
    pos_ref,
    vel_ref,
    spec_ref,
    send_ref,
    recv_ref,
    mask_ref,
    emb_ref,
    rin_ref,
    rout_ref,
    mfirst_ref,
    msquare_ref,
    readout_ref,
    total_ref,
    scratch,
):
    s = scratch
    channels = emb_ref.shape[1]
    wide = N_COMP * channels
    atoms = pos_ref.shape[1]
    tiles = TILES
    group = n_edge // tiles
    lanes = group * atoms
    chunks = channels // CHUNK
    me = lax.axis_index("edge")
    my_sys = lax.axis_index("sys")
    half = lax.div(me, group)
    core = lax.rem(me, 2)
    mate = me + 1 - 2 * core
    half_atoms = atoms // SYS_LOC

    def peer(distance):
        return lax.rem(me + distance, n_edge)

    def remote(source, target, kind, other):
        return pltpu.make_async_remote_copy(
            src_ref=source,
            dst_ref=target,
            send_sem=s.send_sem.at[kind, other],
            recv_sem=s.recv_sem.at[kind, me],
            device_id={"edge": other},
            device_id_type=MESH,
        )

    def landed(target, kind, other):
        pltpu.make_async_remote_copy(
            src_ref=target,
            dst_ref=target,
            send_sem=s.send_sem.at[kind, other],
            recv_sem=s.recv_sem.at[kind, other],
            device_id={"edge": other},
            device_id_type=MESH,
        ).wait_recv()

    def each_peer(action):
        def body(distance, carry):
            action(peer(distance))
            return carry

        lax.fori_loop(1, n_edge, body, 0)

    def each_tile(action):
        for index in range(tiles):
            action(index)

    def loop(count, action, unroll=False):
        def body(index, carry):
            action(index)
            return carry

        lax.fori_loop(0, count, body, 0, unroll=unroll)

    def chunk_at(base, index):
        return pl.ds(pl.multiple_of(base + index * CHUNK, CHUNK), CHUNK)

    barrier = pltpu.get_barrier_semaphore()

    def greet(other):
        pl.semaphore_signal(barrier, inc=1, device_id={"edge": other}, device_id_type=MESH)

    each_peer(greet)

    def greet_sys(distance, carry):
        other = lax.rem(my_sys + distance, n_sys)
        pl.semaphore_signal(barrier, inc=1, device_id={"sys": other}, device_id_type=MESH)
        return carry

    lax.fori_loop(1, n_sys, greet_sys, 0)

    s.start_float[me] = jnp.concatenate([pos_ref[...], vel_ref[...], pos_ref[0:2]], axis=0)
    species_rows = jnp.broadcast_to(spec_ref[...].reshape(1, atoms), (16 - 3 * EVALS, atoms))
    for other in range(n_edge):
        at = slice(other * atoms, (other + 1) * atoms)
        for part, ref in enumerate((send_ref, recv_ref, mask_ref)):
            s.lists_out[other, part * EVALS : (part + 1) * EVALS, :] = ref[:, at]
        s.lists_out[other, 3 * EVALS :, :] = species_rows

    pl.semaphore_wait(barrier, n_edge - 1 + n_sys - 1)

    def start_first(other):
        remote(s.start_float.at[me], s.start_float.at[me], KIND_INIT, other).start()
        remote(s.lists_out.at[other], s.lists_in.at[me], KIND_EDGES, other).start()

    each_peer(start_first)
    s.lists_in[me] = s.lists_out[me]

    for layer in range(2):
        w_in = rin_ref[layer]
        high, low = two_parts_f32(w_in)
        zero = jnp.zeros_like(high)
        s.w_in_left[layer] = jnp.concatenate([high, high, low, zero], axis=0).T.astype(BF)
        s.w_in_back[layer] = jnp.concatenate(
            [left_three(w_in), jnp.zeros((8, 3 * channels), BF)], axis=0
        )
        w_out = rout_ref[layer]
        s.w_out_left[layer] = left_three(w_out.T)
        s.w_out_back[layer] = left_three(w_out)
    s.mf_left[...] = left_three(mfirst_ref[...].T)
    s.mf_back[...] = left_three(mfirst_ref[...])
    for number in range(3):
        s.ms_left[number] = left_three(msquare_ref[number].T)
        s.ms_back[number] = left_three(msquare_ref[number])
    emb_pad = jnp.concatenate(
        [emb_ref[...], jnp.zeros((16 - emb_ref.shape[0], channels), F32)], axis=0
    )
    s.emb_left[...] = jnp.concatenate(list(three_parts_f32(emb_pad)), axis=0).T.astype(BF)
    s.readout_col[...] = jnp.broadcast_to(
        readout_ref[...].reshape(1, channels), (atoms, channels)
    ).T
    for ref in (
        s.grad_emb,
        s.grad_in,
        s.grad_out,
        s.grad_mf,
        s.grad_ms,
        s.grad_ro,
    ):
        ref[...] = jnp.zeros_like(ref)

    own_species = lax.broadcasted_iota(jnp.int32, (16, atoms), 0) == spec_ref[...].reshape(1, atoms)
    own_species = own_species.astype(F32).astype(BF)

    def species_values(hot):
        return dot_nn(s.emb_left[...], jnp.concatenate([hot, hot, hot], axis=0))

    s.start_scalar[...] = species_values(own_species)

    def first_landed(other):
        landed(s.start_float.at[other], KIND_INIT, other)
        landed(s.lists_in.at[other], KIND_EDGES, other)

    each_peer(first_landed)

    def first_sent(other):
        remote(s.start_float.at[me], s.start_float.at[me], KIND_INIT, other).wait_send()
        remote(s.lists_out.at[other], s.lists_in.at[me], KIND_EDGES, other).wait_send()

    each_peer(first_sent)
    s.rows[...] = jnp.zeros_like(s.rows)
    for axis in range(3):
        s.place[axis] = s.start_float[:, axis, :]
        s.speed[axis] = s.start_float[:, 3 + axis, :]

    def one_hots(number):
        atom_row = lax.broadcasted_iota(jnp.int32, (atoms, atoms), 0)

        def hot(row):
            return (atom_row == row).astype(F32).astype(BF)

        def put(ref, tile, at, value):
            ref[number, tile, 0:atoms, at] = value
            ref[number, tile, atoms:, at] = value

        def body(index):
            for part in range(group):
                other = index * group + part
                at = pl.ds(part * atoms, atoms)
                out_list = s.lists_out.at[other]
                in_list = s.lists_in.at[other]
                sender = out_list[pl.ds(number, 1), :]
                receiver = out_list[pl.ds(EVALS + number, 1), :]
                mask = out_list[pl.ds(2 * EVALS + number, 1), :]
                put(s.own_hot, index, at, hot(sender))
                put(s.far_hot, index, at, hot(jnp.where(mask == 0, -1, receiver)))
                sender = in_list[pl.ds(number, 1), :]
                receiver = in_list[pl.ds(EVALS + number, 1), :]
                mask = in_list[pl.ds(2 * EVALS + number, 1), :]
                sender_hot = hot(sender)
                put(s.own_hot, tiles + index, at, hot(jnp.where(mask == 0, -1, receiver)))
                put(s.far_hot, tiles + index, at, sender_hot)
                species = in_list[pl.ds(3 * EVALS, 1), :]
                kinds = lax.broadcasted_iota(jnp.int32, (16, atoms), 0)
                species_hot = (kinds == species).astype(F32).astype(BF)
                s.kind_hot[number, index, :, at] = dot_nn(species_hot, sender_hot).astype(BF)
            s.kind_value[number, index] = species_values(s.kind_hot[number, index])

        each_tile(body)

    def table(rows):
        for axis in range(3):
            s.rows[:, axis, :] = rows[axis]
        for other in range(n_edge):
            s.pieces[other] = stack_three(s.rows[other])

    def edge_difference(number, index):
        sign = jnp.where(index < tiles, 1.0, -1.0)
        own = dot_nn(s.pieces[me], s.own_hot[number, index, 0:atoms, :])
        first = lax.rem(index, tiles) * group
        far = [
            dot_nn(
                s.pieces[first + part],
                s.far_hot[number, index, 0:atoms, part * atoms : (part + 1) * atoms],
            )
            for part in range(group)
        ]
        return sign * join_three(own - jnp.concatenate(far, axis=1))

    def scatter_rows(number, target):
        parts = [stack_three(s.edge_rows[index]) for index in range(2 * tiles)]
        own = 0.0
        for index in range(2 * tiles):
            found = dot_nt(parts[index], s.own_hot[number, index, 0:atoms, :])
            own = own + found if index < tiles else own - found
        s.row_own[...] = join_three(own)
        for other in range(n_edge):
            index, part = other // group, other % group
            at = slice(part * atoms, (part + 1) * atoms)
            total = join_three(
                dot_nt(parts[tiles + index][:, at], s.far_hot[number, tiles + index, 0:atoms, at])
                - dot_nt(parts[index][:, at], s.far_hot[number, index, 0:atoms, at])
            )
            for axis in range(3):
                target[axis, other : other + 1, :] = total[axis : axis + 1]
        for axis in range(3):
            target[axis, pl.ds(me, 1), :] += s.row_own[axis : axis + 1, :]

    def geometry(number, index):
        offset = edge_difference(number, index)
        geo = s.geo.at[number, index]
        radius = jnp.sqrt(jnp.sum(offset * offset, axis=0, keepdims=True) + SOFTEN)
        inverse = 1.0 / radius
        unit = offset * inverse
        one, two, three = rows_of(unit, 0, 3)
        geo[0:3, :] = ROOT3 * unit[0:3]
        geo[3:4, :] = ROOT15 * one * two
        geo[4:5, :] = ROOT15 * two * three
        geo[5:6, :] = 0.5 * ROOT5 * (3.0 * three * three - 1.0)
        geo[6:7, :] = ROOT15 * one * three
        geo[7:8, :] = 0.5 * ROOT15 * (one * one - two * two)
        t = radius * (1.0 / CUTOFF)
        sines, cosines = sin_cos_multiples(*sin_cos_pi(t))
        sines = jnp.concatenate(sines, axis=0)
        cosines = jnp.concatenate(cosines, axis=0)
        t2 = t * t
        t4 = t2 * t2
        amount = math.sqrt(2.0 / CUTOFF) * inverse
        env = 1.0 - t4 * t2 * (28.0 - 48.0 * t + 21.0 * t2)
        env_one = -168.0 / CUTOFF * t4 * t * (1.0 - t) * (1.0 - t)
        env_two = -168.0 / CUTOFF**2 * t4 * (1.0 - t) * (5.0 - 7.0 * t)
        front = amount * env
        front_one = amount * (env_one - env * inverse)
        front_two = amount * (env_two - 2.0 * inverse * (env_one - env * inverse))
        waves = (lax.broadcasted_iota(jnp.int32, (NB, 1), 0) + 1).astype(F32) * (
            math.pi / CUTOFF
        )
        geo[8:16, :] = front * sines
        geo[16:24, :] = front_one * sines + front * waves * cosines
        geo[24:32, :] = (
            front_two * sines + 2.0 * front_one * waves * cosines - front * waves * waves * sines
        )
        geo[32:35, :] = unit[0:3]
        geo[35:36, :] = inverse

    def first_back(number, index):
        geo = s.geo.at[number, index]
        bars = s.geo_bar.at[number, index]
        ybar = rows_of(bars[0:8, :], 0, 8)
        slope = jnp.sum(bars[8:16, :] * geo[16:24, :], axis=0, keepdims=True)
        units = rows_of(geo[32:40, :], 0, 3)
        inverse = geo[35:36, :]
        extra = second_slope(*units, ybar[3:])
        back = [ROOT3 * ybar[axis] + extra[axis] for axis in range(3)]
        along = back[0] * units[0] + back[1] * units[1] + back[2] * units[2]
        rest = slope - along * inverse
        for axis in range(3):
            bars[16 + axis : 17 + axis, :] = back[axis]
            s.edge_rows[index, axis : axis + 1, :] = back[axis] * inverse + rest * units[axis]
        bars[19:20, :] = rest

    def geometry_tangent(number, index):
        move = edge_difference(number, index)
        geo = s.geo.at[number, index]
        out = s.geo_dot.at[index]
        inverse = geo[35:36, :]
        one, two, three = rows_of(geo[32:40, :], 0, 3)
        moves = rows_of(move, 0, 3)
        speed = one * moves[0] + two * moves[1] + three * moves[2]
        d_one, d_two, d_three = [
            (amount - unit * speed) * inverse for amount, unit in zip(moves, (one, two, three))
        ]
        out[0:1, :] = ROOT3 * d_one
        out[1:2, :] = ROOT3 * d_two
        out[2:3, :] = ROOT3 * d_three
        out[3:4, :] = ROOT15 * (d_one * two + one * d_two)
        out[4:5, :] = ROOT15 * (d_two * three + two * d_three)
        out[5:6, :] = 3.0 * ROOT5 * three * d_three
        out[6:7, :] = ROOT15 * (d_one * three + one * d_three)
        out[7:8, :] = ROOT15 * (one * d_one - two * d_two)
        out[8:16, :] = geo[16:24, :] * speed
        out[16:17, :] = d_one
        out[17:18, :] = d_two
        out[18:19, :] = d_three
        out[19:20, :] = speed
        out[20:23, :] = move[0:3]

    def second_back(number, index, hats):
        geo = s.geo.at[number, index]
        bars = s.geo_bar.at[number, index]
        dots = s.geo_dot.at[index]
        units = rows_of(geo[32:40, :], 0, 3)
        inverse = geo[35:36, :]
        turns = rows_of(dots[16:24, :], 0, 3)
        speed = dots[19:20, :]
        moves = rows_of(dots[16:24, :], 4, 3)
        back = rows_of(bars[16:24, :], 0, 3)
        rest = bars[19:20, :]
        yhat = rows_of(hats, 0, 8)
        ybar = rows_of(bars[0:8, :], 0, 8)
        extra = second_slope(*units, yhat[3:])
        more = second_slope(*turns, ybar[3:])
        radial_hat = jnp.sum(
            hats[8:16] * geo[16:24, :] + speed * (bars[8:16, :] * geo[24:32, :]),
            axis=0,
            keepdims=True,
        ) - inverse * (turns[0] * back[0] + turns[1] * back[1] + turns[2] * back[2])
        unit_hat = [
            ROOT3 * yhat[axis]
            + extra[axis]
            + more[axis]
            - speed * inverse * back[axis]
            + rest * moves[axis]
            for axis in range(3)
        ]
        along = unit_hat[0] * units[0] + unit_hat[1] * units[1] + unit_hat[2] * units[2]
        left = radial_hat - along * inverse
        for axis in range(3):
            s.edge_rows[index, axis : axis + 1, :] = unit_hat[axis] * inverse + left * units[axis]

    def radial_forward(layer, number, index, basis):
        before = dot_nn(s.w_in_left[layer], right_three_small(basis))
        s.hidden[layer, number, index] = before
        gate = logistic(before)
        s.radial[layer, number, index] = dot_nn(
            s.w_out_left[layer], right_three(before * gate)
        )

    def radial_tangent(layer, number, index, basis_dot):
        before = s.hidden[layer, number, index]
        before_dot = dot_nn(s.w_in_left[layer], right_three_small(basis_dot))
        s.hidden_dot[layer, index] = before_dot
        gate = logistic(before)
        s.radial_dot[layer, index] = dot_nn(
            s.w_out_left[layer], right_three(silu_slope(before, gate) * before_dot)
        )

    def radial_back(layer, number, index, high_ref, low_ref):
        high, low = high_ref[...], low_ref[...]
        hidden_bar = dot_nn(s.w_out_back[layer], jnp.concatenate([high, low, high], axis=0))
        s.hidden_bar[layer, number, index] = hidden_bar
        before = s.hidden[layer, number, index]
        before_bar = silu_slope(before, logistic(before)) * hidden_bar
        return dot_nn(s.w_in_back[layer], right_three(before_bar))[0:8]

    def radial_second(layer, number, index, basis, basis_dot):
        first_high, first_low = s.r_high[index], s.r_low[index]
        next_high, next_low = s.h_high[index], s.h_low[index]
        hidden_hat = dot_nn(
            s.w_out_back[layer], jnp.concatenate([next_high, next_low, next_high], axis=0)
        )
        before = s.hidden[layer, number, index]
        before_dot = s.hidden_dot[layer, index]
        hidden_bar = s.hidden_bar[layer, number, index]
        gate = logistic(before)
        slope = silu_slope(before, gate)
        before_hat = slope * hidden_hat + silu_bend(before, gate) * before_dot * hidden_bar
        before_bar = slope * hidden_bar
        out_high, out_low = two_parts(before * gate)
        dot_high, dot_low = two_parts(slope * before_dot)
        s.grad_out[layer] += (
            dot_nt(out_high, next_high)
            + dot_nt(out_low, next_high)
            + dot_nt(out_high, next_low)
            + dot_nt(dot_high, first_high)
            + dot_nt(dot_low, first_high)
            + dot_nt(dot_high, first_low)
        )
        s.grad_in[layer] += outer_three(basis, before_hat) + outer_three(basis_dot, before_bar)
        return dot_nn(s.w_in_back[layer], right_three(before_hat))[0:8]

    def put_pieces(high_ref, low_ref, at, value):
        high, low = two_parts(value)
        high_ref[at, :] = high
        low_ref[at, :] = low

    def add_scatter(index, hot):
        s.sum_wide[...] += dot_nt(s.m_high[index], hot) + dot_nt(s.m_low[index], hot)

    def harmonic_rows(ref):
        return [ref[row : row + 1, :] for row in range(8)]

    def fold(value):
        return value[0:8] + value[8:16]

    def sum_rows(parts):
        return jnp.concatenate([jnp.sum(part, axis=0, keepdims=True) for part in parts], axis=0)

    def first_forward(number, index):
        tile = tiles + index
        geo = s.geo.at[number, tile]
        radial_forward(0, number, index, geo[8:16, :])
        rad = s.radial.at[0, number, index]
        kind = s.kind_value.at[number, index]

        def body(c):
            value = kind[chunk_at(0, c), :]
            y = harmonic_rows(geo)
            put_pieces(s.m_high.at[index], s.m_low.at[index], chunk_at(0, c), rad[chunk_at(0, c), :] * value)
            vector = rad[chunk_at(channels, c), :] * value
            tensor = rad[chunk_at(2 * channels, c), :] * value
            for k in range(8):
                part = (vector if k < 3 else tensor) * y[k]
                put_pieces(s.m_high.at[index], s.m_low.at[index], chunk_at((k + 1) * channels, c), part)

        loop(chunks, body, True)
        add_scatter(index, s.own_hot[number, tile, 0:atoms, :])

    def first_tangent(number, index):
        tile = tiles + index
        geo = s.geo.at[number, tile]
        dots = s.geo_dot.at[tile]
        radial_tangent(0, number, index, dots[8:16, :])
        rad = s.radial.at[0, number, index]
        rad_dot = s.radial_dot.at[0, index]
        kind = s.kind_value.at[number, index]

        def body(c):
            value = kind[chunk_at(0, c), :]
            y = harmonic_rows(geo)
            y_dot = harmonic_rows(dots)
            put_pieces(s.m_high.at[index], s.m_low.at[index], chunk_at(0, c), rad_dot[chunk_at(0, c), :] * value)
            vector = rad[chunk_at(channels, c), :] * value
            tensor = rad[chunk_at(2 * channels, c), :] * value
            vector_dot = rad_dot[chunk_at(channels, c), :] * value
            tensor_dot = rad_dot[chunk_at(2 * channels, c), :] * value
            for k in range(8):
                base, move = (vector, vector_dot) if k < 3 else (tensor, tensor_dot)
                part = move * y[k] + base * y_dot[k]
                put_pieces(s.m_high.at[index], s.m_low.at[index], chunk_at((k + 1) * channels, c), part)

        loop(chunks, body, True)
        add_scatter(index, s.own_hot[number, tile, 0:atoms, :])

    def gather_wide(hot):
        return dot_nn(s.a_pair[...], hot)

    def first_reverse(number, index):
        tile = tiles + index
        geo = s.geo.at[number, tile]
        s.first_cot[number, index] = gather_wide(s.own_hot[number, tile])
        cot = s.first_cot.at[number, index]
        rad = s.radial.at[0, number, index]
        kind = s.kind_value.at[number, index]

        def body(c, sums):
            value = kind[chunk_at(0, c), :]
            y = harmonic_rows(geo)
            put_pieces(s.r_high.at[index], s.r_low.at[index], chunk_at(0, c), cot[chunk_at(0, c), :] * value)
            sums = list(sums)
            for first, last, path in ((0, 3, 1), (3, 8, 2)):
                base = rad[chunk_at(path * channels, c), :] * value
                total = 0.0
                for k in range(first, last):
                    given = cot[chunk_at((k + 1) * channels, c), :]
                    total = total + given * y[k]
                    sums[k] = sums[k] + fold(base * given)
                put_pieces(s.r_high.at[index], s.r_low.at[index], chunk_at(path * channels, c), total * value)
            return tuple(sums)

        sums = lax.fori_loop(
            0, chunks, body, (jnp.zeros((8, lanes), F32),) * 8, unroll=True
        )
        s.geo_bar[number, tile, 0:8, :] = sum_rows(sums)
        s.geo_bar[number, tile, 8:16, :] = radial_back(0, number, index, s.r_high.at[index], s.r_low.at[index])
        first_back(number, tile)

    def first_second(number, index):
        tile = tiles + index
        geo = s.geo.at[number, tile]
        dots = s.geo_dot.at[tile]
        s.wide_tile[index] = gather_wide(s.own_hot[number, tile])
        hat = s.wide_tile.at[index]
        cot = s.first_cot.at[number, index]
        rad = s.radial.at[0, number, index]
        rad_dot = s.radial_dot.at[0, index]
        kind = s.kind_value.at[number, index]

        def body(c, sums):
            value = kind[chunk_at(0, c), :]
            y = harmonic_rows(geo)
            y_dot = harmonic_rows(dots)
            sums = list(sums)
            total = cot[chunk_at(0, c), :]
            total_hat = hat[chunk_at(0, c), :]
            put_pieces(s.r_high.at[index], s.r_low.at[index], chunk_at(0, c), total * value)
            put_pieces(s.h_high.at[index], s.h_low.at[index], chunk_at(0, c), total_hat * value)
            value_hat = rad[chunk_at(0, c), :] * total_hat + rad_dot[chunk_at(0, c), :] * total
            for first, last, path in ((0, 3, 1), (3, 8, 2)):
                rad_here = rad[chunk_at(path * channels, c), :]
                rad_move = rad_dot[chunk_at(path * channels, c), :]
                base = rad_here * value
                move = rad_move * value
                total = 0.0
                total_hat = 0.0
                for k in range(first, last):
                    given = cot[chunk_at((k + 1) * channels, c), :]
                    given_hat = hat[chunk_at((k + 1) * channels, c), :]
                    total = total + given * y[k]
                    total_hat = total_hat + (given_hat * y[k] + given * y_dot[k])
                    sums[k] = sums[k] + fold(base * given_hat + move * given)
                put_pieces(s.r_high.at[index], s.r_low.at[index], chunk_at(path * channels, c), total * value)
                put_pieces(s.h_high.at[index], s.h_low.at[index], chunk_at(path * channels, c), total_hat * value)
                value_hat = value_hat + rad_here * total_hat + rad_move * total
            put_pieces(s.v_high.at[index], s.v_low.at[index], chunk_at(0, c), value_hat)
            return tuple(sums)

        sums = lax.fori_loop(
            0, chunks, body, (jnp.zeros((8, lanes), F32),) * 8, unroll=True
        )
        kinds = s.kind_hot[number, index]
        s.grad_emb[...] += dot_nt(kinds, s.v_high[index]) + dot_nt(kinds, s.v_low[index])
        basis_hat = radial_second(0, number, index, geo[8:16, :], dots[8:16, :])
        second_back(number, tile, jnp.concatenate([sum_rows(sums), basis_hat], axis=0))

    def gather_far(ref, number, index):
        found = []
        for part in range(group):
            pair = jnp.concatenate(two_parts(ref[index * group + part]), axis=1)
            hot = s.far_hot[number, index, :, part * atoms : (part + 1) * atoms]
            found.append(dot_nn(pair, hot))
        return jnp.concatenate(found, axis=1)

    def put_messages(number, index):
        for part in range(group):
            at = slice(part * atoms, (part + 1) * atoms)
            hot = s.far_hot[number, index, 0:atoms, at]
            s.msg_out[index * group + part] = dot_nt(s.v_high[index, :, at], hot) + dot_nt(
                s.v_low[index, :, at], hot
            )

    def to_mate(source, target, kind, place):
        return pltpu.make_async_remote_copy(
            src_ref=source,
            dst_ref=target,
            send_sem=s.send_sem.at[kind, place],
            recv_sem=s.recv_sem.at[kind, place],
            device_id={"edge": mate},
            device_id_type=MESH,
        )

    def near_peer(distance):
        return half * group + lax.rem(me + distance, group)

    def far_same(place):
        return (1 - half) * group + 2 * place + core

    def far_other(place):
        return (1 - half) * group + 2 * place + 1 - core

    def mate_part(place):
        return to_mate(s.msg_out.at[far_other(place)], s.pair_in.at[place], KIND_PAIR, place)

    def message_to(other, kind):
        return remote(s.msg_out.at[other], s.msg_in.at[me], kind, other)

    def exchange_messages(number, kind, make):
        make(number, 1 - half)
        put_messages(number, 1 - half)
        for place in range(group // 2):
            mate_part(place).start()
        make(number, half)
        put_messages(number, half)
        for distance in range(1, group):
            message_to(near_peer(distance), kind).start()
        for place in range(group // 2):
            mate_part(place).wait_recv()
            other = far_same(place)
            s.msg_out[other] = s.msg_out[other] + s.pair_in[place]
            message_to(other, kind).start()

    def second_forward(number, index):
        geo = s.geo.at[number, index]
        radial_forward(1, number, index, geo[8:16, :])
        s.feat[number, index] = gather_wide(s.own_hot[number, index])
        feat = s.feat.at[number, index]
        rad = s.radial.at[1, number, index]

        def body(c):
            y = harmonic_rows(geo)
            total = rad[chunk_at(0, c), :] * feat[chunk_at(0, c), :]
            for first, last, path in ((0, 3, 1), (3, 8, 2)):
                along = 0.0
                for k in range(first, last):
                    along = along + feat[chunk_at((k + 1) * channels, c), :] * y[k]
                s.along[number, index, chunk_at((path - 1) * channels, c), :] = along
                total = total + rad[chunk_at(path * channels, c), :] * along
            put_pieces(s.v_high.at[index], s.v_low.at[index], chunk_at(0, c), total)

        loop(chunks, body, True)

    def second_tangent(number, index):
        geo = s.geo.at[number, index]
        dots = s.geo_dot.at[index]
        radial_tangent(1, number, index, dots[8:16, :])
        s.feat_dot[index] = gather_wide(s.own_hot[number, index])
        feat = s.feat.at[number, index]
        feat_dot = s.feat_dot.at[index]
        rad = s.radial.at[1, number, index]
        rad_dot = s.radial_dot.at[1, index]

        def body(c):
            y = harmonic_rows(geo)
            y_dot = harmonic_rows(dots)
            at = chunk_at(0, c)
            total = rad_dot[at, :] * feat[at, :] + rad[at, :] * feat_dot[at, :]
            for first, last, path in ((0, 3, 1), (3, 8, 2)):
                move = 0.0
                for k in range(first, last):
                    here = chunk_at((k + 1) * channels, c)
                    move = move + (feat_dot[here, :] * y[k] + feat[here, :] * y_dot[k])
                here = chunk_at((path - 1) * channels, c)
                s.along_dot[index, here, :] = move
                here_rad = chunk_at(path * channels, c)
                total = total + (
                    rad_dot[here_rad, :] * s.along[number, index, here, :]
                    + rad[here_rad, :] * move
                )
            put_pieces(s.v_high.at[index], s.v_low.at[index], at, total)

        loop(chunks, body, True)

    def second_reverse(number, index):
        geo = s.geo.at[number, index]
        s.msg_cot[number, index] = gather_far(s.cot_all, number, index)
        cot = s.msg_cot.at[number, index]
        feat = s.feat.at[number, index]
        rad = s.radial.at[1, number, index]

        def body(c, sums):
            y = harmonic_rows(geo)
            at = chunk_at(0, c)
            given = cot[at, :]
            sums = list(sums)
            put_pieces(s.r_high.at[index], s.r_low.at[index], at, feat[at, :] * given)
            put_pieces(s.m_high.at[index], s.m_low.at[index], at, rad[at, :] * given)
            for first, last, path in ((0, 3, 1), (3, 8, 2)):
                here = chunk_at(path * channels, c)
                along = s.along[number, index, chunk_at((path - 1) * channels, c), :]
                put_pieces(s.r_high.at[index], s.r_low.at[index], here, along * given)
                base = rad[here, :] * given
                for k in range(first, last):
                    wide_at = chunk_at((k + 1) * channels, c)
                    put_pieces(s.m_high.at[index], s.m_low.at[index], wide_at, base * y[k])
                    sums[k] = sums[k] + fold(base * feat[wide_at, :])
            return tuple(sums)

        sums = lax.fori_loop(
            0, chunks, body, (jnp.zeros((8, lanes), F32),) * 8, unroll=True
        )
        s.geo_bar[number, index, 0:8, :] = sum_rows(sums)
        s.geo_bar[number, index, 8:16, :] = radial_back(1, number, index, s.r_high.at[index], s.r_low.at[index])
        first_back(number, index)
        add_scatter(index, s.own_hot[number, index, 0:atoms, :])

    def second_second(number, index):
        geo = s.geo.at[number, index]
        dots = s.geo_dot.at[index]
        s.msg_hat[index] = gather_far(s.cot_all, number, index)
        cot = s.msg_cot.at[number, index]
        feat = s.feat.at[number, index]
        feat_dot = s.feat_dot.at[index]
        rad = s.radial.at[1, number, index]
        rad_dot = s.radial_dot.at[1, index]

        def body(c, sums):
            y = harmonic_rows(geo)
            y_dot = harmonic_rows(dots)
            at = chunk_at(0, c)
            given = cot[at, :]
            given_hat = s.msg_hat[index, at, :]
            sums = list(sums)
            put_pieces(s.r_high.at[index], s.r_low.at[index], at, feat[at, :] * given)
            put_pieces(s.h_high.at[index], s.h_low.at[index], at, feat[at, :] * given_hat + feat_dot[at, :] * given)
            put_pieces(s.m_high.at[index], s.m_low.at[index], at, rad[at, :] * given_hat + rad_dot[at, :] * given)
            for first, last, path in ((0, 3, 1), (3, 8, 2)):
                here = chunk_at(path * channels, c)
                along_at = chunk_at((path - 1) * channels, c)
                along = s.along[number, index, along_at, :]
                along_dot = s.along_dot[index, along_at, :]
                put_pieces(s.r_high.at[index], s.r_low.at[index], here, along * given)
                put_pieces(s.h_high.at[index], s.h_low.at[index], here, along * given_hat + along_dot * given)
                base = rad[here, :] * given
                base_hat = rad[here, :] * given_hat + rad_dot[here, :] * given
                for k in range(first, last):
                    wide_at = chunk_at((k + 1) * channels, c)
                    put_pieces(s.m_high.at[index], s.m_low.at[index], wide_at, base_hat * y[k] + base * y_dot[k])
                    sums[k] = sums[k] + fold(
                        base_hat * feat[wide_at, :] + base * feat_dot[wide_at, :]
                    )
            return tuple(sums)

        sums = lax.fori_loop(
            0, chunks, body, (jnp.zeros((8, lanes), F32),) * 8, unroll=True
        )
        basis_hat = radial_second(1, number, index, geo[8:16, :], dots[8:16, :])
        second_back(number, index, jnp.concatenate([sum_rows(sums), basis_hat], axis=0))
        add_scatter(index, s.own_hot[number, index, 0:atoms, :])

    def part_of(ref, component):
        return ref[component * channels : (component + 1) * channels, :]

    def side_by_side(ref, first, last):
        return jnp.concatenate([part_of(ref, k + 1) for k in range(first, last)], axis=1)

    def linear(left, value):
        return dot_nn(left, right_three(value))

    def keep_wide(component, value):
        high, low = two_parts(value)
        at = slice(component * channels, (component + 1) * channels)
        s.a_pair[at, 0:atoms] = high
        s.a_pair[at, atoms:] = low

    def node_first_forward(number):
        s.agg[number] = INV_NEIGH * s.sum_wide[...]
        agg = s.agg.at[number]
        mixed = linear(s.mf_left[...], part_of(agg, 0))
        s.mixed[number] = mixed
        before, gate_one, gate_two = [mixed[i * channels : (i + 1) * channels] for i in range(3)]
        scalar = s.start_scalar[...] + before * logistic(before)
        s.scalar[number] = scalar
        keep_wide(0, scalar)
        gates = (logistic(gate_one), logistic(gate_two))
        for first, last, path in PATHS:
            raws = linear(s.ms_left[path], side_by_side(agg, first, last))
            for k in range(first, last):
                raw = raws[:, (k - first) * atoms : (k - first + 1) * atoms]
                s.raw[number, k * channels : (k + 1) * channels, :] = raw
                keep_wide(k + 1, gates[path] * raw)

    def node_first_tangent(number):
        s.agg_dot[...] = INV_NEIGH * s.sum_wide[...]
        mixed = s.mixed.at[number]
        mixed_dot = linear(s.mf_left[...], part_of(s.agg_dot, 0))
        s.mixed_dot[...] = mixed_dot
        before = part_of(mixed, 0)
        scalar_dot = silu_slope(before, logistic(before)) * mixed_dot[0:channels]
        s.scalar_dot[...] = scalar_dot
        keep_wide(0, scalar_dot)
        for first, last, path in PATHS:
            gate = logistic(part_of(mixed, path + 1))
            move = gate * (1.0 - gate) * mixed_dot[(path + 1) * channels : (path + 2) * channels]
            raws_dot = linear(s.ms_left[path], side_by_side(s.agg_dot, first, last))
            for k in range(first, last):
                raw_dot = raws_dot[:, (k - first) * atoms : (k - first + 1) * atoms]
                s.raw_dot[k * channels : (k + 1) * channels, :] = raw_dot
                raw = s.raw[number, k * channels : (k + 1) * channels, :]
                keep_wide(k + 1, move * raw + gate * raw_dot)

    def node_first_reverse(number):
        s.feat_bar[number] = s.sum_wide[...]
        s.feat_bar[number, 0:channels, :] += s.readout_col[...]
        bar = s.feat_bar.at[number]
        mixed = s.mixed.at[number]
        before = part_of(mixed, 0)
        s.mixed_bar[number, 0:channels, :] = silu_slope(before, logistic(before)) * part_of(bar, 0)
        for first, last, path in PATHS:
            gate = logistic(part_of(mixed, path + 1))
            total = 0.0
            bars = []
            for k in range(first, last):
                given = part_of(bar, k + 1)
                total = total + given * s.raw[number, k * channels : (k + 1) * channels, :]
                raw_bar = gate * given
                s.raw_bar[number, k * channels : (k + 1) * channels, :] = raw_bar
                bars.append(raw_bar)
            found = INV_NEIGH * linear(s.ms_back[path], jnp.concatenate(bars, axis=1))
            for k in range(first, last):
                keep_wide(k + 1, found[:, (k - first) * atoms : (k - first + 1) * atoms])
            s.mixed_bar[number, (path + 1) * channels : (path + 2) * channels, :] = (
                gate * (1.0 - gate) * total
            )
        keep_wide(0, INV_NEIGH * linear(s.mf_back[...], s.mixed_bar[number]))

    def node_first_second(number, energy_bar):
        s.sum_wide[0:channels, :] += s.readout_col[...] * energy_bar
        hat = s.sum_wide
        bar = s.feat_bar.at[number]
        mixed = s.mixed.at[number]
        before = part_of(mixed, 0)
        gate = logistic(before)
        scalar_hat = part_of(hat, 0)
        s.mixed_hat[0:channels, :] = silu_slope(before, gate) * scalar_hat + silu_bend(
            before, gate
        ) * s.mixed_dot[0:channels, :] * part_of(bar, 0)
        s.grad_emb[...] += dot_nt(own_species, two_parts(scalar_hat)[0]) + dot_nt(
            own_species, two_parts(scalar_hat)[1]
        )
        for first, last, path in PATHS:
            gate = logistic(part_of(mixed, path + 1))
            slope = gate * (1.0 - gate)
            bend = slope * (1.0 - 2.0 * gate)
            mixed_dot = s.mixed_dot[(path + 1) * channels : (path + 2) * channels, :]
            one = 0.0
            two = 0.0
            hats = []
            for k in range(first, last):
                at = slice(k * channels, (k + 1) * channels)
                given = part_of(bar, k + 1)
                given_hat = part_of(hat, k + 1)
                raw = s.raw[number, at, :]
                one = one + (given_hat * raw + given * s.raw_dot[at, :])
                two = two + given * raw
                hats.append(gate * given_hat + slope * mixed_dot * given)
            hats = jnp.concatenate(hats, axis=1)
            found = INV_NEIGH * linear(s.ms_back[path], hats)
            for k in range(first, last):
                keep_wide(k + 1, found[:, (k - first) * atoms : (k - first + 1) * atoms])
            bars = jnp.concatenate(
                [s.raw_bar[number, k * channels : (k + 1) * channels, :] for k in range(first, last)],
                axis=1,
            )
            s.grad_ms[path] += outer_three(
                side_by_side(s.agg.at[number], first, last), hats
            ) + outer_three(side_by_side(s.agg_dot, first, last), bars)
            s.mixed_hat[(path + 1) * channels : (path + 2) * channels, :] = (
                slope * one + bend * mixed_dot * two
            )
        keep_wide(0, INV_NEIGH * linear(s.mf_back[...], s.mixed_hat[...]))
        s.grad_mf[...] += outer_three(part_of(s.agg.at[number], 0), s.mixed_hat[...])
        s.grad_mf[...] += outer_three(part_of(s.agg_dot, 0), s.mixed_bar[number])

    def collect_messages(kind):
        total = s.msg_out[me]
        peers = [near_peer(distance) for distance in range(1, group)]
        peers += [far_same(place) for place in range(group // 2)]
        for other in peers:
            landed(s.msg_in.at[other], kind, other)
            total = total + s.msg_in[other]
        for other in peers:
            message_to(other, kind).wait_send()
        for place in range(group // 2):
            mate_part(place).wait_send()
        return INV_NEIGH * total

    def cotangent_to(other, kind):
        return remote(s.cot_all.at[me], s.cot_all.at[me], kind, other)

    def share_cotangent(value, kind):
        s.cot_all[me] = value
        for place in range(group // 2):
            cotangent_to(far_same(place), kind).start()
        for distance in range(1, group):
            cotangent_to(near_peer(distance), kind).start()

    def pass_on(other):
        return to_mate(s.cot_all.at[other], s.cot_all.at[other], KIND_PASS, other)

    def with_cotangents(number, kind, use):
        for distance in range(1, group):
            other = near_peer(distance)
            landed(s.cot_all.at[other], kind, other)
        use(number, half)
        for place in range(group // 2):
            other = far_same(place)
            landed(s.cot_all.at[other], kind, other)
            pass_on(other).start()
        for place in range(group // 2):
            pass_on(far_other(place)).wait_recv()
        use(number, 1 - half)
        for place in range(group // 2):
            other = far_same(place)
            pass_on(other).wait_send()
            cotangent_to(other, kind).wait_send()
        for distance in range(1, group):
            cotangent_to(near_peer(distance), kind).wait_send()

    def node_second_forward(number):
        agg = collect_messages(KIND_MSG)
        s.agg_two[number] = agg
        before = linear(s.ms_left[2], agg)
        s.last[number] = before
        gate = logistic(before)
        s.energy_row[...] = jnp.sum(
            s.readout_col[...] * (s.scalar[number] + before * gate), axis=0, keepdims=True
        )
        before_bar = s.readout_col[...] * silu_slope(before, gate)
        share_cotangent(INV_NEIGH * linear(s.ms_back[2], before_bar), KIND_COT)

    def node_second_second(number, energy_bar):
        agg_dot = collect_messages(KIND_TMSG)
        agg = s.agg_two[number]
        before = s.last[number]
        before_dot = linear(s.ms_left[2], agg_dot)
        gate = logistic(before)
        slope = silu_slope(before, gate)
        before_hat = s.readout_col[...] * (
            energy_bar * slope + silu_bend(before, gate) * before_dot
        )
        share_cotangent(INV_NEIGH * linear(s.ms_back[2], before_hat), KIND_TCOT)
        before_bar = s.readout_col[...] * slope
        s.grad_ms[2] += outer_three(agg, before_hat) + outer_three(agg_dot, before_bar)
        s.grad_ro[...] += energy_bar * (s.scalar[number] + before * gate) + (
            s.scalar_dot[...] + slope * before_dot
        )

    def share_rows(out_ref, in_ref, kind, meanwhile=None):
        def start(other):
            remote(out_ref, in_ref.at[me], kind, other).start()

        each_peer(start)
        in_ref[me] = out_ref[...]
        if meanwhile is not None:
            meanwhile()

        def wait(other):
            landed(in_ref.at[other], kind, other)
            remote(out_ref, in_ref.at[me], kind, other).wait_send()

        each_peer(wait)
        total = in_ref[0]
        for other in range(1, n_edge):
            total = total + in_ref[other]
        return total

    def evaluate(number):
        table(s.place)
        loop(2 * tiles, lambda index: geometry(number, index), True)
        s.sum_wide[...] = jnp.zeros_like(s.sum_wide)
        each_tile(lambda index: first_forward(number, index))
        node_first_forward(number)
        exchange_messages(number, KIND_MSG, second_forward)
        node_second_forward(number)
        s.sum_wide[...] = jnp.zeros_like(s.sum_wide)
        with_cotangents(number, KIND_COT, second_reverse)
        node_first_reverse(number)
        each_tile(lambda index: first_reverse(number, index))
        scatter_rows(number, s.force_out)
        s.force_out[3] = jnp.zeros((n_edge, atoms), F32)
        s.force_out[3, pl.ds(me, 1), :] = s.energy_row[...]

        def prepare():
            @pl.when(number < EVALS - 1)
            def _():
                one_hots(number + 1)

        total = share_rows(s.force_out, s.force_in, KIND_FORCE, prepare)
        force = -total[0:3]
        s.energy[number] = total[3]
        half_kick = 0.5 * STEP_DT * force

        @pl.when(number > 0)
        def _():
            s.speed[...] = s.speed[...] + half_kick

        @pl.when(number == 0)
        def _():
            s.start_kinetic[...] = 0.5 * jnp.sum(s.speed[...] * s.speed[...], axis=0)

        @pl.when(number < EVALS - 1)
        def _():
            s.speed[...] = s.speed[...] + half_kick
            s.place[...] = s.place[...] + STEP_DT * s.speed[...]

    one_hots(0)
    loop(EVALS, evaluate)

    kinetic = 0.5 * jnp.sum(s.speed[...] * s.speed[...], axis=0)
    change = (s.energy[EVALS - 1] + kinetic) - (s.energy[0] + s.start_kinetic[...])
    system_of = lax.broadcasted_iota(jnp.int32, (n_edge, atoms), 1) // half_atoms
    system_atoms = float(half_atoms * n_edge)
    loss = jnp.zeros((1, 1), F32)
    drift_grad = jnp.zeros((n_edge, atoms), F32)
    for number in range(SYS_LOC):
        mine = system_of == number
        drift = jnp.sum(jnp.where(mine, change, 0.0), axis=(0, 1), keepdims=True)
        loss = loss + drift * drift / system_atoms
        drift_grad = drift_grad + jnp.where(mine, 2.0 * drift / system_atoms, 0.0)
    s.drift_grad[...] = drift_grad
    s.place_bar[...] = jnp.zeros_like(s.place_bar)
    s.speed_bar[...] = drift_grad[None] * s.speed[...]
    loss = loss * jnp.where(me == 0, 1.0, 0.0)

    def reverse(step):
        number = EVALS - 1 - step
        sides = jnp.where(jnp.logical_or(number == 0, number == EVALS - 1), 1.0, 2.0)
        ends = jnp.where(number == 0, -1.0, jnp.where(number == EVALS - 1, 1.0, 0.0))
        s.move[...] = (-0.5 * STEP_DT * sides) * s.speed_bar[...]
        table(s.move)
        loop(2 * tiles, lambda index: geometry_tangent(number, index), True)
        energy_bar = ends * s.drift_grad[pl.ds(me, 1), :]
        s.sum_wide[...] = jnp.zeros_like(s.sum_wide)
        each_tile(lambda index: first_tangent(number, index))
        node_first_tangent(number)
        exchange_messages(number, KIND_TMSG, second_tangent)
        node_second_second(number, energy_bar)
        s.sum_wide[...] = jnp.zeros_like(s.sum_wide)
        with_cotangents(number, KIND_TCOT, second_second)
        node_first_second(number, energy_bar)
        each_tile(lambda index: first_second(number, index))

        @pl.when(number > 0)
        def _():
            scatter_rows(number, s.place_out)
            total = share_rows(s.place_out, s.place_in, KIND_TFORCE)
            s.place_bar[...] = s.place_bar[...] + total
            s.speed_bar[...] = s.speed_bar[...] + STEP_DT * s.place_bar[...]

    loop(EVALS, reverse)

    out = s.grad_all
    rows_each = out.shape[0] // n_edge
    blocks = []
    for layer in range(2):
        for path in range(3):
            blocks.append(s.grad_out[layer, :, path * channels : (path + 1) * channels])
    for path in range(3):
        blocks.append(s.grad_mf[:, path * channels : (path + 1) * channels])
    for number in range(3):
        blocks.append(s.grad_ms[number])
    for pair in range(6):
        out[pair * channels : (pair + 1) * channels, :] = jnp.concatenate(
            [blocks[2 * pair], blocks[2 * pair + 1]], axis=1
        )
    base = 6 * channels
    out[base : base + 8, :] = jnp.concatenate([s.grad_in[0], s.grad_in[1]], axis=1)
    ones = jnp.ones((8, atoms), BF)
    high, middle, low = three_parts_f32(s.grad_ro[...])
    ro_rows = (
        dot_nt(ones, high.astype(BF)) + dot_nt(ones, middle.astype(BF)) + dot_nt(ones, low.astype(BF))
    )
    row_of = lax.broadcasted_iota(jnp.int32, (8, channels), 0)
    ro_rows = jnp.where(row_of == 0, ro_rows, jnp.where(row_of == 1, loss, 0.0))
    out[base + 8 : base + 16, :] = jnp.concatenate([s.grad_emb[0:8, :], ro_rows], axis=1)
    rest = out.shape[0] - (base + 16)
    out[base + 16 :, :] = jnp.zeros((rest, out.shape[1]), F32)

    def part_rows(ref, other):
        return ref.at[pl.ds(pl.multiple_of(other * rows_each, 8), rows_each)]

    def start_scatter(other):
        remote(part_rows(out, other), s.part_in.at[me], KIND_SCATTER, other).start()

    each_peer(start_scatter)
    s.part_in[me] = part_rows(out, me)[...]

    def wait_scatter(other):
        landed(s.part_in.at[other], KIND_SCATTER, other)
        remote(part_rows(out, other), s.part_in.at[me], KIND_SCATTER, other).wait_send()

    each_peer(wait_scatter)
    total = s.part_in[0]
    for other in range(1, n_edge):
        total = total + s.part_in[other]
    s.sys_in[my_sys] = total

    def sys_copy(other):
        return pltpu.make_async_remote_copy(
            src_ref=s.sys_in.at[my_sys],
            dst_ref=s.sys_in.at[my_sys],
            send_sem=s.send_sem.at[KIND_SYS, other],
            recv_sem=s.recv_sem.at[KIND_SYS, my_sys],
            device_id={"sys": other},
            device_id_type=MESH,
        )

    def each_sys(action):
        def body(distance, carry):
            action(lax.rem(my_sys + distance, n_sys))
            return carry

        lax.fori_loop(1, n_sys, body, 0)

    each_sys(lambda other: sys_copy(other).start())

    def wait_sys(other):
        pltpu.make_async_remote_copy(
            src_ref=s.sys_in.at[other],
            dst_ref=s.sys_in.at[other],
            send_sem=s.send_sem.at[KIND_SYS, other],
            recv_sem=s.recv_sem.at[KIND_SYS, other],
            device_id={"sys": other},
            device_id_type=MESH,
        ).wait_recv()
        sys_copy(other).wait_send()

    each_sys(wait_sys)
    total = s.sys_in[0]
    for other in range(1, n_sys):
        total = total + s.sys_in[other]
    mine = part_rows(s.summed, me)
    mine[...] = total
    each_peer(lambda other: remote(mine, mine, KIND_GATHER, other).start())

    def wait_gather(other):
        landed(part_rows(s.summed, other), KIND_GATHER, other)
        remote(mine, mine, KIND_GATHER, other).wait_send()

    each_peer(wait_gather)
    total_ref[...] = s.summed[...]


class Scratch:
    pass


def step_scratch(n_edge, n_sys, channels, atoms, grad_rows):
    tiles = TILES
    lanes = n_edge // tiles * atoms
    wide = N_COMP * channels
    vm = lambda *shape: pltpu.VMEM(shape, F32)
    vb = lambda *shape: pltpu.VMEM(shape, BF)
    vi = lambda *shape: pltpu.VMEM(shape, jnp.int32)
    return {
        "send_sem": pltpu.SemaphoreType.DMA((KINDS, n_edge)),
        "recv_sem": pltpu.SemaphoreType.DMA((KINDS, n_edge)),
        "start_float": vm(n_edge, 8, atoms),
        "lists_out": vi(n_edge, 16, atoms),
        "lists_in": vi(n_edge, 16, atoms),
        "w_in_left": vb(2, channels, 32),
        "w_in_back": vb(2, 16, 3 * channels),
        "w_out_left": vb(2, 3 * channels, 3 * channels),
        "w_out_back": vb(2, channels, 9 * channels),
        "mf_left": vb(3 * channels, 3 * channels),
        "mf_back": vb(channels, 9 * channels),
        "ms_left": vb(3, channels, 3 * channels),
        "ms_back": vb(3, channels, 3 * channels),
        "emb_left": vb(channels, 48),
        "readout_col": vm(channels, atoms),
        "start_scalar": vm(channels, atoms),
        "place": vm(3, n_edge, atoms),
        "speed": vm(3, n_edge, atoms),
        "energy_row": vm(1, atoms),
        "energy": vm(EVALS, n_edge, atoms),
        "start_kinetic": vm(n_edge, atoms),
        "drift_grad": vm(n_edge, atoms),
        "place_bar": vm(3, n_edge, atoms),
        "speed_bar": vm(3, n_edge, atoms),
        "move": vm(3, n_edge, atoms),
        "own_hot": vb(EVALS, 2 * tiles, 2 * atoms, lanes),
        "far_hot": vb(EVALS, 2 * tiles, 2 * atoms, lanes),
        "kind_hot": vb(EVALS, tiles, 16, lanes),
        "kind_value": vm(EVALS, tiles, channels, lanes),
        "rows": vm(n_edge, 8, atoms),
        "pieces": vb(n_edge, 32, atoms),
        "row_own": vm(8, atoms),
        "edge_rows": vm(2 * tiles, 8, lanes),
        "geo": vm(EVALS, 2 * tiles, 40, lanes),
        "geo_bar": vm(EVALS, 2 * tiles, 24, lanes),
        "geo_dot": vm(2 * tiles, 24, lanes),
        "hidden": vm(2, EVALS, tiles, channels, lanes),
        "hidden_bar": vm(2, EVALS, tiles, channels, lanes),
        "hidden_dot": vm(2, tiles, channels, lanes),
        "radial": vm(2, EVALS, tiles, 3 * channels, lanes),
        "radial_dot": vm(2, tiles, 3 * channels, lanes),
        "m_high": vb(tiles, wide, lanes),
        "m_low": vb(tiles, wide, lanes),
        "r_high": vb(tiles, 3 * channels, lanes),
        "r_low": vb(tiles, 3 * channels, lanes),
        "h_high": vb(tiles, 3 * channels, lanes),
        "h_low": vb(tiles, 3 * channels, lanes),
        "v_high": vb(tiles, channels, lanes),
        "v_low": vb(tiles, channels, lanes),
        "a_pair": vb(wide, 2 * atoms),
        "sum_wide": vm(wide, atoms),
        "wide_tile": vm(tiles, wide, lanes),
        "first_cot": vm(EVALS, tiles, wide, lanes),
        "feat": vm(EVALS, tiles, wide, lanes),
        "feat_dot": vm(tiles, wide, lanes),
        "along": vm(EVALS, tiles, 2 * channels, lanes),
        "along_dot": vm(tiles, 2 * channels, lanes),
        "msg_cot": vm(EVALS, tiles, channels, lanes),
        "msg_hat": vm(tiles, channels, lanes),
        "agg": vm(EVALS, wide, atoms),
        "agg_dot": vm(wide, atoms),
        "mixed": vm(EVALS, 3 * channels, atoms),
        "mixed_dot": vm(3 * channels, atoms),
        "mixed_bar": vm(EVALS, 3 * channels, atoms),
        "mixed_hat": vm(3 * channels, atoms),
        "raw": vm(EVALS, 8 * channels, atoms),
        "raw_dot": vm(8 * channels, atoms),
        "raw_bar": vm(EVALS, 8 * channels, atoms),
        "scalar": vm(EVALS, channels, atoms),
        "scalar_dot": vm(channels, atoms),
        "feat_bar": vm(EVALS, wide, atoms),
        "agg_two": vm(EVALS, channels, atoms),
        "last": vm(EVALS, channels, atoms),
        "msg_out": vm(n_edge, channels, atoms),
        "pair_in": vm(n_edge // 4, channels, atoms),
        "msg_in": vm(n_edge, channels, atoms),
        "cot_all": vm(n_edge, channels, atoms),
        "force_out": vm(4, n_edge, atoms),
        "force_in": vm(n_edge, 4, n_edge, atoms),
        "place_out": vm(3, n_edge, atoms),
        "place_in": vm(n_edge, 3, n_edge, atoms),
        "grad_emb": vm(16, channels),
        "grad_in": vm(2, NB, channels),
        "grad_out": vm(2, channels, 3 * channels),
        "grad_mf": vm(channels, 3 * channels),
        "grad_ms": vm(3, channels, channels),
        "grad_ro": vm(channels, atoms),
        "grad_all": vm(grad_rows, 2 * channels),
        "part_in": vm(n_edge, grad_rows // n_edge, 2 * channels),
        "sys_in": vm(n_sys, grad_rows // n_edge, 2 * channels),
        "summed": vm(grad_rows, 2 * channels),
    }


def whole_step(positions, velocities, species, senders, receivers, edge_mask, params):
    n_edge, n_sys = lax.axis_size("edge"), lax.axis_size("sys")
    atoms = positions.shape[1]
    channels = params[0].shape[1]
    unit = 8 * n_edge
    grad_rows = -(-(6 * channels + 16) // unit) * unit
    shapes = step_scratch(n_edge, n_sys, channels, atoms, grad_rows)
    names = tuple(shapes)

    def kernel(*refs):
        scratch = Scratch()
        for name, ref in zip(names, refs[13:]):
            setattr(scratch, name, ref)
        step_kernel(n_edge, n_sys, *refs[:13], scratch)

    embedding, radial_in, radial_out, mix_first, mix_square, readout = params
    operands = (
        positions,
        velocities,
        species,
        senders,
        receivers,
        edge_mask,
        embedding,
        radial_in,
        radial_out,
        mix_first,
        mix_square,
        readout,
    )
    return pl.pallas_call(
        kernel,
        out_shape=jax.ShapeDtypeStruct((grad_rows, 2 * channels), F32),
        in_specs=[pl.BlockSpec(memory_space=pltpu.VMEM)] * len(operands),
        out_specs=pl.BlockSpec(memory_space=pltpu.VMEM),
        scratch_shapes=list(shapes.values()),
        compiler_params=pltpu.CompilerParams(
            collective_id=0, has_side_effects=True, vmem_limit_bytes=56 * 1024 * 1024
        ),
    )(*operands)


def to_column(row):
    count = row.shape[1]
    square = jnp.broadcast_to(row, (count, count))
    same = lax.broadcasted_iota(jnp.int32, (count, count), 0) == lax.broadcasted_iota(
        jnp.int32, (count, count), 1
    )
    return jnp.sum(jnp.where(same, square, 0.0), axis=1, keepdims=True)


def to_row(column):
    count = column.shape[0]
    square = jnp.broadcast_to(column, (count, count))
    same = lax.broadcasted_iota(jnp.int32, (count, count), 0) == lax.broadcasted_iota(
        jnp.int32, (count, count), 1
    )
    return jnp.sum(jnp.where(same, square, 0.0), axis=0, keepdims=True)


def total_mean(value):
    return jnp.sum(
        jnp.sum(value, axis=1, keepdims=True), axis=0, keepdims=True
    ) / float(value.shape[0] * value.shape[1])


def factored_rows(gradient, weight, row_state, col_state):
    decay_rate = 1.0 - STEP_NUM ** (-0.8)
    squares = gradient * gradient + EPS_SQUARE
    size_m, size_n = gradient.shape
    row_mean = jnp.sum(squares, axis=1, keepdims=True) / float(size_n)
    col_mean = jnp.sum(squares, axis=0, keepdims=True) / float(size_m)
    row_new = decay_rate * to_column(row_state) + (1.0 - decay_rate) * row_mean
    col_new = decay_rate * col_state + (1.0 - decay_rate) * col_mean
    second = row_new * col_new / total_mean(row_new)
    weight_rms = jnp.sqrt(total_mean(weight * weight) + 1e-06)
    weight_new = weight - RELATIVE * weight_rms * gradient * lax.rsqrt(second)
    return (gradient, to_row(row_new), col_new, weight_new, weight_new.astype(jnp.bfloat16))


def update_kernel(total_ref, *refs):
    weights, states, outs = refs[0:6], refs[6:17], refs[17:]
    kinds, channels = weights[0].shape

    def block(number):
        pair, side = number // 2, number % 2
        return total_ref[
            pair * channels : (pair + 1) * channels, side * channels : (side + 1) * channels
        ]

    base = 6 * channels
    gradients = (
        [total_ref[base + 8 : base + 8 + kinds, :channels]],
        [total_ref[base : base + 8, side * channels : (side + 1) * channels] for side in range(2)],
        [
            jnp.concatenate([block(3 * layer + path) for path in range(3)], axis=1)
            for layer in range(2)
        ],
        [jnp.concatenate([block(6 + path) for path in range(3)], axis=1)],
        [block(9 + number) for number in range(3)],
    )
    outs[0][...] = total_ref[base + 9 : base + 10, channels : channels + 1]
    for which, parts in enumerate(gradients):
        weight, rows, cols = weights[which], states[2 * which], states[2 * which + 1]
        results = outs[1 + 5 * which : 6 + 5 * which]
        stacked = len(weight.shape) == 3
        for number, gradient in enumerate(parts):
            if stacked:
                found = factored_rows(
                    gradient,
                    weight[number],
                    rows[number : number + 1, :],
                    cols[number : number + 1, :],
                )
                results[0][number] = found[0]
                results[1][number : number + 1, :] = found[1]
                results[2][number : number + 1, :] = found[2]
                results[3][number] = found[3]
                results[4][number] = found[4]
            else:
                size_m, size_n = weight.shape
                found = factored_rows(
                    gradient,
                    weight[...],
                    rows[...].reshape(1, size_m),
                    cols[...].reshape(1, size_n),
                )
                results[0][...] = found[0]
                results[1][...] = found[1].reshape(size_m)
                results[2][...] = found[2].reshape(size_n)
                results[3][...] = found[3]
                results[4][...] = found[4]
    gradient = total_ref[base + 8 : base + 9, channels:]
    decay_rate = 1.0 - STEP_NUM ** (-0.8)
    weight = weights[5][...].reshape(1, channels)
    second_new = decay_rate * states[10][...].reshape(1, channels) + (1.0 - decay_rate) * (
        gradient * gradient + EPS_SQUARE
    )
    weight_rms = jnp.sqrt(total_mean(weight * weight) + 1e-06)
    weight_new = weight - RELATIVE * weight_rms * gradient * lax.rsqrt(second_new)
    outs[26][...] = gradient.reshape(channels)
    outs[27][...] = second_new.reshape(channels)
    outs[28][...] = weight_new.reshape(channels)
    outs[29][...] = weight_new.astype(jnp.bfloat16).reshape(channels)


def whole_update(total, params, states):
    shapes = [jax.ShapeDtypeStruct((1, 1), F32)]
    for which in range(5):
        weight, rows, cols = params[which], states[2 * which], states[2 * which + 1]
        for like in (weight, rows, cols, weight):
            shapes.append(jax.ShapeDtypeStruct(like.shape, F32))
        shapes.append(jax.ShapeDtypeStruct(weight.shape, jnp.bfloat16))
    for kind in (F32, F32, F32, jnp.bfloat16):
        shapes.append(jax.ShapeDtypeStruct(params[5].shape, kind))
    operands = (total, *params, *states)
    results = pl.pallas_call(
        update_kernel,
        out_shape=shapes,
        in_specs=[pl.BlockSpec(memory_space=pltpu.VMEM)] * len(operands),
        out_specs=[pl.BlockSpec(memory_space=pltpu.VMEM)] * len(shapes),
        compiler_params=pltpu.CompilerParams(vmem_limit_bytes=8 * 1024 * 1024),
    )(*operands)
    return (results[0].reshape(()), *results[1:])


def fits_kernel(senders, atom_count):
    n_edge = lax.axis_size("edge")
    slots = senders.shape[1] // n_edge
    return slots == atom_count and atom_count % 128 == 0 and n_edge % 4 == 0


def on_device(
    positions,
    velocities,
    species,
    senders,
    receivers,
    edge_mask,
    embedding,
    radial_in,
    radial_out,
    mix_first,
    mix_square,
    readout,
    embedding_rows,
    embedding_cols,
    radial_in_rows,
    radial_in_cols,
    radial_out_rows,
    radial_out_cols,
    mix_first_rows,
    mix_first_cols,
    mix_square_rows,
    mix_square_cols,
    readout_second,
):
    params = (embedding, radial_in, radial_out, mix_first, mix_square, readout)
    atom_count = positions.shape[1]
    states = (
        embedding_rows,
        embedding_cols,
        radial_in_rows,
        radial_in_cols,
        radial_out_rows,
        radial_out_cols,
        mix_first_rows,
        mix_first_cols,
        mix_square_rows,
        mix_square_cols,
        readout_second,
    )
    if fits_kernel(senders, atom_count):
        total = whole_step(
            positions, velocities, species, senders, receivers, edge_mask, params
        )
        return whole_update(total, params, states)
    spec_hot = (species[None, :] == jnp.arange(embedding.shape[0])[:, None]).astype(jnp.float32)
    edge_lists = receivers[None]
    arrived = lax.all_to_all(edge_lists, "edge", split_axis=2, concat_axis=2, tiled=True)
    passes = [
        build(senders[number], arrived[:, number], edge_mask[number], atom_count, spec_hot)
        for number in range(EVALS)
    ]
    coords = positions
    moving = velocities
    energies, forces, stored = passes[0][0](coords, params)
    record = [stored]
    first_energy = energies
    for number in range(STEPS):
        half_speed = moving + 0.5 * STEP_DT * forces
        coords = coords + STEP_DT * half_speed
        energies, forces, stored = passes[number + 1][0](coords, params)
        record.append(stored)
        moving = half_speed + 0.5 * STEP_DT * forces
    local_sums = jnp.stack(
        [
            per_system(first_energy),
            per_system(energies),
            per_system(0.5 * jnp.sum(velocities * velocities, axis=0)),
            per_system(0.5 * jnp.sum(moving * moving, axis=0)),
        ]
    )
    totals = lax.psum(local_sums, "edge")
    drift = totals[1] + totals[3] - (totals[0] + totals[2])
    system_atoms = atom_count // SYS_LOC * lax.axis_size("edge")
    loss_local = jnp.sum(drift * drift) / system_atoms
    drift_grad = jnp.repeat(2.0 * drift / system_atoms, atom_count // SYS_LOC)
    speed_bar = drift_grad[None, :] * moving
    coord_bar = jnp.zeros_like(positions)
    force_next = jnp.zeros_like(positions)
    gradients = jax.tree.map(jnp.zeros_like, params)
    for number in reversed(range(STEPS)):
        later = number + 1
        force_bar = force_next + 0.5 * STEP_DT * speed_bar
        if later == STEPS:
            energy_bar = drift_grad
        else:
            energy_bar = jnp.zeros_like(drift_grad)
        coord_part, param_part = passes[later][1](record[later], params, energy_bar, force_bar)
        gradients = add_trees([gradients, param_part])
        coord_bar = coord_bar + coord_part
        half_bar = speed_bar + STEP_DT * coord_bar
        speed_bar = half_bar
        force_next = 0.5 * STEP_DT * half_bar
    _, param_part = passes[0][1](record[0], params, -drift_grad, force_next)
    gradients = add_trees([gradients, param_part])
    loss_term = loss_local * (lax.axis_index("edge") == 0).astype(jnp.float32)
    summed = lax.psum(
        (
            gradients[0],
            gradients[1],
            gradients[2],
            gradients[3],
            gradients[4],
            gradients[5],
            loss_term,
        ),
        ("sys", "edge"),
    )
    return update(summed, params, states)


def solution(mesh):
    placed = (
        P(None, ("sys", "edge")),
        P(None, ("sys", "edge")),
        P(("sys", "edge")),
        P(None, ("sys", "edge")),
        P(None, ("sys", "edge")),
        P(None, ("sys", "edge")),
        P(),
        P(),
        P(),
        P(),
        P(),
        P(),
        P(),
        P(),
        P(),
        P(),
        P(),
        P(),
        P(),
        P(),
        P(),
        P(),
        P(),
    )
    return jax.shard_map(
        on_device,
        mesh=mesh,
        in_specs=placed,
        out_specs=(
            P(),
            P(),
            P(),
            P(),
            P(),
            P(),
            P(),
            P(),
            P(),
            P(),
            P(),
            P(),
            P(),
            P(),
            P(),
            P(),
            P(),
            P(),
            P(),
            P(),
            P(),
            P(),
            P(),
            P(),
            P(),
            P(),
            P(),
            P(),
            P(),
            P(),
        ),
        check_vma=False,
    )
```

```python
from functools import reduce
import math

import jax
import jax.numpy as jnp
from jax import lax
from jax.experimental import pallas as pl
from jax.experimental.pallas import tpu as pltpu
from jax.sharding import PartitionSpec as P

NB = 8
SYS_LOC = 2
STEPS = 2
STEP_NUM = 10
EVALS = 3


PRECISE = lax.Precision.HIGHEST
SOFTEN = 0.25
CUTOFF = 5.0
INV_NEIGH = 0.2
STEP_DT = 0.5
RELATIVE = 0.3
EPS_SQUARE = 1e-30
ROOT3 = math.sqrt(3.0)
ROOT5 = math.sqrt(5.0)


def geometry(sender_pos, receiver_pos):
    offset_vec = sender_pos - receiver_pos
    radius = jnp.sqrt(jnp.sum(offset_vec * offset_vec, axis=0) + SOFTEN)
    direction = offset_vec / radius
    unit_x, unit_y, unit_z = (direction[0], direction[1], direction[2])
    first_harm = ROOT3 * direction
    second_harm = ROOT5 * jnp.stack(
        [
            ROOT3 * unit_x * unit_y,
            ROOT3 * unit_y * unit_z,
            0.5 * (3.0 * unit_z * unit_z - 1.0),
            ROOT3 * unit_x * unit_z,
            0.5 * ROOT3 * (unit_x * unit_x - unit_y * unit_y),
        ]
    )
    scaled = radius / CUTOFF
    envelope = 1.0 - 28.0 * scaled**6 + 48.0 * scaled**7 - 21.0 * scaled**8
    orders = jnp.arange(1, NB + 1).astype(jnp.float32)[:, None]
    bessel = (
        math.sqrt(2.0 / CUTOFF)
        * jnp.sin(orders * math.pi * scaled[None, :])
        / radius[None, :]
        * envelope[None, :]
    )
    return (first_harm, second_harm, bessel)


def radial(bessel, weight_in, weight_out):
    hidden = jax.nn.silu(jnp.einsum("nr,ne->re", weight_in, bessel, precision=PRECISE))
    return jnp.einsum("rk,re->ke", weight_out, hidden, precision=PRECISE)


def first_messages(
    first_harm, second_harm, bessel, sender_feat, edge_weight, weight_in, weight_out
):
    channels = sender_feat.shape[0]
    edge_weights = radial(bessel, weight_in, weight_out)
    scalar_part = (edge_weights[:channels] * sender_feat)[None]
    vector_part = (edge_weights[channels : 2 * channels] * sender_feat)[None] * first_harm[
        :, None, :
    ]
    tensor_part = (edge_weights[2 * channels :] * sender_feat)[None] * second_harm[:, None, :]
    return jnp.concatenate([scalar_part, vector_part, tensor_part], axis=0) * edge_weight


def node_first(summed, scalar_prev, mix_first, mix_square):
    gathered = summed * INV_NEIGH
    channels = scalar_prev.shape[0]
    mixed = jnp.einsum("cd,ca->da", mix_first, gathered[0], precision=PRECISE)
    vectors = jnp.einsum("mca,cd->mda", gathered[1:4], mix_square[0], precision=PRECISE)
    tensors = jnp.einsum("mca,cd->mda", gathered[4:9], mix_square[1], precision=PRECISE)
    scalars = scalar_prev + jax.nn.silu(mixed[:channels])
    vectors = jax.nn.sigmoid(mixed[channels : 2 * channels])[None] * vectors
    tensors = jax.nn.sigmoid(mixed[2 * channels :])[None] * tensors
    return jnp.concatenate([scalars[None], vectors, tensors], axis=0)


def second_messages(
    first_harm, second_harm, bessel, sender_feat, edge_weight, weight_in, weight_out
):
    channels = sender_feat.shape[1]
    edge_weights = radial(bessel, weight_in, weight_out)
    along_first = jnp.einsum("kce,ke->ce", sender_feat[1:4], first_harm, precision=PRECISE)
    along_second = jnp.einsum("kce,ke->ce", sender_feat[4:9], second_harm, precision=PRECISE)
    combined = (
        edge_weights[:channels] * sender_feat[0]
        + edge_weights[channels : 2 * channels] * along_first
        + edge_weights[2 * channels :] * along_second
    )
    return combined * edge_weight


def node_second(features, summed, mix_square, readout):
    scalars = features[0] + jax.nn.silu(
        jnp.einsum("cd,ca->da", mix_square[2], summed * INV_NEIGH, precision=PRECISE)
    )
    return jnp.einsum("c,ca->a", readout, scalars, precision=PRECISE)


def factored(gradient, weight, row_state, col_state):
    decay_rate = 1.0 - STEP_NUM ** (-0.8)
    squares = gradient * gradient + EPS_SQUARE
    row_new = decay_rate * row_state + (1.0 - decay_rate) * jnp.mean(squares, axis=-1)
    col_new = decay_rate * col_state + (1.0 - decay_rate) * jnp.mean(squares, axis=-2)
    second = (
        row_new[..., :, None]
        * col_new[..., None, :]
        / jnp.mean(row_new, axis=-1, keepdims=True)[..., None]
    )
    weight_rms = jnp.sqrt(jnp.mean(weight * weight, axis=(-2, -1), keepdims=True) + 1e-06)
    weight_new = weight - RELATIVE * weight_rms * gradient * lax.rsqrt(second)
    return (gradient, row_new, col_new, weight_new, weight_new.astype(jnp.bfloat16))


def unfactored(gradient, weight, second):
    decay_rate = 1.0 - STEP_NUM ** (-0.8)
    second_new = decay_rate * second + (1.0 - decay_rate) * (gradient * gradient + EPS_SQUARE)
    weight_rms = jnp.sqrt(jnp.mean(weight * weight) + 1e-06)
    weight_new = weight - RELATIVE * weight_rms * gradient * lax.rsqrt(second_new)
    return (gradient, second_new, weight_new, weight_new.astype(jnp.bfloat16))


def add_trees(trees):
    return reduce(lambda left, right: jax.tree.map(jnp.add, left, right), trees)


def per_system(values):
    return values.reshape(SYS_LOC, -1).sum(axis=1)


def build(send_row, arrived_lists, mask_row, atom_count, spec_hot):
    edge_weight = mask_row.astype(jnp.float32)
    arrived_row = arrived_lists[0]
    send_hot = (send_row[None, :] == jnp.arange(atom_count)[:, None]).astype(jnp.float32)
    inc_hot = (arrived_row[None, :] == jnp.arange(atom_count)[:, None]).astype(jnp.float32)

    def fetch_positions(coords):
        return lax.all_to_all(
            jnp.dot(coords, inc_hot, precision=PRECISE),
            "edge",
            split_axis=1,
            concat_axis=1,
            tiled=True,
        )

    def return_positions(cotangent):
        arrived = lax.all_to_all(cotangent, "edge", split_axis=1, concat_axis=1, tiled=True)
        return jnp.einsum("de,ae->da", arrived, inc_hot, precision=PRECISE)

    def collect(values):
        arrived = lax.all_to_all(values, "edge", split_axis=2, concat_axis=2, tiled=True)
        return jnp.einsum("mce,ae->mca", arrived, inc_hot, precision=PRECISE)

    def spread(values):
        per_slot = jnp.einsum("mca,ae->mce", values, inc_hot, precision=PRECISE)
        return lax.all_to_all(per_slot, "edge", split_axis=2, concat_axis=2, tiled=True)

    def scalar_start(params):
        return jnp.einsum("tc,ta->ca", params[0], spec_hot, precision=PRECISE)

    def give_back(aux_cot, recv_cot):
        return return_positions(aux_cot + recv_cot)

    def edge_first(coords, recv_pos, params):
        first_harm, second_harm, bessel = geometry(
            jnp.dot(coords, send_hot, precision=PRECISE), recv_pos
        )
        sender_feat = jnp.dot(scalar_start(params), send_hot, precision=PRECISE)
        return first_messages(
            first_harm, second_harm, bessel, sender_feat, edge_weight, params[1][0], params[2][0]
        )

    def collect_first(values):
        return collect(values)

    def spread_first(values):
        return spread(values)

    def node_one(summed, params):
        return node_first(summed, scalar_start(params), params[3], params[4])

    def edge_second(coords, recv_pos, features, params):
        first_harm, second_harm, bessel = geometry(
            jnp.dot(coords, send_hot, precision=PRECISE), recv_pos
        )
        sender_feat = jnp.einsum("mca,ae->mce", features, send_hot, precision=PRECISE)
        return second_messages(
            first_harm, second_harm, bessel, sender_feat, edge_weight, params[1][1], params[2][1]
        )[None]

    def node_two(features, summed, params):
        return node_second(features, summed[0], params[4], params[5])

    def back_node_two(features, summed, params):
        _, pullback = jax.vjp(
            lambda feature_in, summed_in: node_two(feature_in, summed_in, params), features, summed
        )
        return pullback(jnp.ones((atom_count,), jnp.float32))

    def back_edge_two(coords, recv_pos, features, params, cotangent):
        _, pullback = jax.vjp(
            lambda where_at, recv_at, feature_in: edge_second(
                where_at, recv_at, feature_in, params
            ),
            coords,
            recv_pos,
            features,
        )
        return pullback(cotangent)

    def back_node_one(summed, params, cotangent):
        _, pullback = jax.vjp(lambda summed_in: node_one(summed_in, params), summed)
        return pullback(cotangent)[0]

    def back_edge_one(coords, aux_pos, params, cotangent):
        _, pullback = jax.vjp(
            lambda where_at, aux_at: edge_first(where_at, aux_at, params), coords, aux_pos
        )
        return pullback(cotangent)

    def evaluate(coords, params):
        recv_pos = fetch_positions(coords)
        summed_one = collect_first(edge_first(coords, recv_pos, params))
        features = node_one(summed_one, params)
        summed_two = collect(edge_second(coords, recv_pos, features, params))
        energies = node_two(features, summed_two, params)
        feature_node, summed_two_bar = back_node_two(features, summed_two, params)
        second_bar = spread(summed_two_bar)
        coord_second, recv_second, feature_edge = back_edge_two(
            coords, recv_pos, features, params, second_bar
        )
        feature_bar = feature_node + feature_edge
        first_bar = spread_first(back_node_one(summed_one, params, feature_bar))
        coord_first, aux_first = back_edge_one(coords, recv_pos, params, first_bar)
        forces = -(coord_first + coord_second + give_back(aux_first, recv_second))
        stored = (
            coords,
            recv_pos,
            recv_pos,
            summed_one,
            features,
            summed_two,
            second_bar,
            feature_bar,
            first_bar,
        )
        return (energies, forces, stored)

    def reverse(stored, params, energy_bar, force_bar):
        (
            coords,
            recv_pos,
            aux_pos,
            summed_one,
            features,
            summed_two,
            second_bar,
            feature_bar,
            first_bar,
        ) = stored
        coord_cot = -force_bar
        recv_cot = fetch_positions(coord_cot)
        _, pullback = jax.vjp(back_edge_one, coords, aux_pos, params, first_bar)
        coord_one, aux_one, param_one, first_cot = pullback((coord_cot, recv_cot))
        _, pullback = jax.vjp(back_node_one, summed_one, params, feature_bar)
        summed_one_a, param_two, feature_cot = pullback(collect_first(first_cot))
        _, pullback = jax.vjp(back_edge_two, coords, recv_pos, features, params, second_bar)
        coord_two, recv_two, feature_one, param_three, second_cot = pullback(
            (coord_cot, recv_cot, feature_cot)
        )
        _, pullback = jax.vjp(back_node_two, features, summed_two, params)
        feature_two, summed_two_a, param_four = pullback((feature_cot, collect(second_cot)))
        _, pullback = jax.vjp(node_two, features, summed_two, params)
        feature_three, summed_two_b, param_five = pullback(energy_bar)
        _, pullback = jax.vjp(edge_second, coords, recv_pos, features, params)
        coord_three, recv_three, feature_four, param_six = pullback(
            spread(summed_two_a + summed_two_b)
        )
        _, pullback = jax.vjp(node_one, summed_one, params)
        summed_one_b, param_seven = pullback(
            feature_one + feature_two + feature_three + feature_four
        )
        _, pullback = jax.vjp(edge_first, coords, aux_pos, params)
        coord_four, aux_four, param_eight = pullback(spread_first(summed_one_a + summed_one_b))
        coord_total = (
            coord_one
            + coord_two
            + coord_three
            + coord_four
            + give_back(aux_one + aux_four, recv_two + recv_three)
        )
        param_total = add_trees(
            [
                param_one,
                param_two,
                param_three,
                param_four,
                param_five,
                param_six,
                param_seven,
                param_eight,
            ]
        )
        return (coord_total, param_total)

    return (evaluate, reverse)


def update(summed, params, states):
    embedding, radial_in, radial_out, mix_first, mix_square, readout = params
    (
        embedding_rows,
        embedding_cols,
        radial_in_rows,
        radial_in_cols,
        radial_out_rows,
        radial_out_cols,
        mix_first_rows,
        mix_first_cols,
        mix_square_rows,
        mix_square_cols,
        readout_second,
    ) = states
    emb = factored(summed[0], embedding, embedding_rows, embedding_cols)
    rin = factored(summed[1], radial_in, radial_in_rows, radial_in_cols)
    rout = factored(summed[2], radial_out, radial_out_rows, radial_out_cols)
    mfirst = factored(summed[3], mix_first, mix_first_rows, mix_first_cols)
    msquare = factored(summed[4], mix_square, mix_square_rows, mix_square_cols)
    rdout = unfactored(summed[5], readout, readout_second)
    return (
        summed[6],
        emb[0],
        emb[1],
        emb[2],
        emb[3],
        emb[4],
        rin[0],
        rin[1],
        rin[2],
        rin[3],
        rin[4],
        rout[0],
        rout[1],
        rout[2],
        rout[3],
        rout[4],
        mfirst[0],
        mfirst[1],
        mfirst[2],
        mfirst[3],
        mfirst[4],
        msquare[0],
        msquare[1],
        msquare[2],
        msquare[3],
        msquare[4],
        rdout[0],
        rdout[1],
        rdout[2],
        rdout[3],
    )


F32 = jnp.float32
BF = jnp.bfloat16
MESH = pl.DeviceIdType.MESH
ROOT15 = math.sqrt(15.0)
TILES = 2
CHUNK = 16
LANES_AT_ONCE = 256
N_COMP = 9
PATHS = ((0, 3, 0), (3, 8, 1))
KIND_INIT, KIND_EDGES, KIND_MSG, KIND_COT, KIND_FORCE = 0, 1, 2, 3, 4
KIND_TMSG, KIND_TCOT, KIND_TFORCE, KIND_SCATTER, KIND_GATHER, KIND_SYS = 5, 6, 7, 8, 9, 10
KIND_OWN, KIND_SCATTER_LATE = 11, 12
KINDS = 13


def dot_nn(left, right):
    return lax.dot_general(left, right, (((1,), (0,)), ((), ())), preferred_element_type=F32)


def dot_nt(left, right):
    return lax.dot_general(left, right, (((1,), (1,)), ((), ())), preferred_element_type=F32)


def two_parts(value):
    high = value.astype(BF)
    return high, (value - high.astype(F32)).astype(BF)


def two_parts_f32(value):
    high = value.astype(BF).astype(F32)
    return high, value - high


def three_parts_f32(value):
    high = value.astype(BF).astype(F32)
    rest = value - high
    middle = rest.astype(BF).astype(F32)
    return high, middle, rest - middle


def left_three(weight):
    high, low = two_parts_f32(weight)
    return jnp.concatenate([high, high, low], axis=1).astype(BF)


def right_three(value):
    high, low = two_parts(value)
    return jnp.concatenate([high, low, high], axis=0)


def right_three_small(value):
    high, low = two_parts_f32(value)
    return jnp.concatenate([high, low, high, jnp.zeros_like(high)], axis=0).astype(BF)


def stack_three(value):
    high, middle, low = three_parts_f32(value)
    return jnp.concatenate([high, middle, low, jnp.zeros_like(high)], axis=0).astype(BF)


def join_three(value):
    return value[0:8] + value[8:16] + value[16:24]


def outer_three(left, right):
    left_high, left_low = two_parts(left)
    right_high, right_low = two_parts(right)
    return (
        dot_nt(left_high, right_high)
        + dot_nt(left_low, right_high)
        + dot_nt(left_high, right_low)
    )


def logistic(value):
    return 1.0 / (1.0 + jnp.exp(jnp.minimum(-value, 80.0)))


def silu_slope(value, gate):
    return gate * (1.0 + value * (1.0 - gate))


def silu_bend(value, gate):
    return gate * (1.0 - gate) * (2.0 + value * (1.0 - 2.0 * gate))


def sin_cos_pi(turns):
    whole = jnp.floor(turns + 0.5)
    part = turns - whole
    sign = 1.0 - 2.0 * (whole - 2.0 * jnp.floor(0.5 * whole))
    square = part * part
    sine = 0.0
    for order in range(15, 0, -2):
        sine = sine * square + (-1.0) ** (order // 2) * math.pi**order / math.factorial(order)
    cosine = 0.0
    for order in range(16, -1, -2):
        cosine = cosine * square + (-1.0) ** (order // 2) * math.pi**order / math.factorial(order)
    return sign * (part * sine), sign * cosine


def sin_cos_multiples(sine, cosine):
    sines, cosines = [None, sine], [None, cosine]
    for order in range(2, 9):
        half, rest = order // 2, order - order // 2
        sines.append(sines[half] * cosines[rest] + cosines[half] * sines[rest])
        cosines.append(cosines[half] * cosines[rest] - sines[half] * sines[rest])
    return sines[1:], cosines[1:]


def second_slope(one, two, three, given):
    return (
        ROOT15 * (two * given[0] + three * given[3] + one * given[4]),
        ROOT15 * (one * given[0] + three * given[1] - two * given[4]),
        ROOT15 * (two * given[1] + one * given[3]) + 3.0 * ROOT5 * three * given[2],
    )


def rows_of(value, first, count):
    return [value[first + number : first + number + 1] for number in range(count)]


def step_kernel(
    n_edge,
    n_sys,
    pos_ref,
    vel_ref,
    spec_ref,
    send_ref,
    recv_ref,
    mask_ref,
    emb_ref,
    rin_ref,
    rout_ref,
    mfirst_ref,
    msquare_ref,
    readout_ref,
    total_ref,
    scratch,
):
    s = scratch
    channels = emb_ref.shape[1]
    wide = N_COMP * channels
    atoms = pos_ref.shape[1]
    tiles = TILES
    group = n_edge // tiles
    lanes = group * atoms
    chunks = channels // CHUNK
    held_group = lax.axis_index("sys")
    held_part = lax.axis_index("edge")
    my_group = lax.div(held_part, 2)
    core = lax.rem(held_part, 2)
    me = 2 * held_group + core
    half = lax.div(me, group)
    half_atoms = atoms // SYS_LOC

    def peer(distance):
        return lax.rem(me + distance, n_edge)

    def place_of(which_group, part):
        return {"sys": lax.div(part, 2), "edge": 2 * which_group + lax.rem(part, 2)}

    def remote(source, target, kind, other):
        return pltpu.make_async_remote_copy(
            src_ref=source,
            dst_ref=target,
            send_sem=s.send_sem.at[kind, other],
            recv_sem=s.recv_sem.at[kind, me],
            device_id=place_of(my_group, other),
            device_id_type=MESH,
        )

    def landed(target, kind, other):
        pltpu.make_async_remote_copy(
            src_ref=target,
            dst_ref=target,
            send_sem=s.send_sem.at[kind, other],
            recv_sem=s.recv_sem.at[kind, other],
            device_id=place_of(my_group, other),
            device_id_type=MESH,
        ).wait_recv()

    def each_peer(action):
        def body(distance, carry):
            action(peer(distance))
            return carry

        lax.fori_loop(1, n_edge, body, 0)

    def each_tile(action):
        for index in range(tiles):
            action(index)

    def loop(count, action, unroll=False):
        def body(index, carry):
            action(index)
            return carry

        lax.fori_loop(0, count, body, 0, unroll=unroll)

    def chunk_at(base, index):
        return slice(base + index * CHUNK, base + (index + 1) * CHUNK)

    barrier = pltpu.get_barrier_semaphore()

    def greet(device):
        pl.semaphore_signal(barrier, inc=1, device_id=device, device_id_type=MESH)

    stays = held_group == my_group

    def each_given(action):
        def body(part, carry):
            @pl.when(jnp.logical_not(jnp.logical_and(stays, part == held_part)))
            def _():
                action(part)

            return carry

        lax.fori_loop(0, n_edge, body, 0)

    def each_group(action):
        def body(distance, carry):
            action(lax.rem(my_group + distance, n_sys))
            return carry

        lax.fori_loop(1, n_sys, body, 0)

    each_given(lambda part: greet({"sys": my_group, "edge": part}))
    each_peer(lambda other: greet(place_of(my_group, other)))
    each_group(lambda other: greet({"edge": 2 * other + core}))

    s.start_out[...] = jnp.concatenate([pos_ref[...], vel_ref[...], pos_ref[0:2]], axis=0)
    species_rows = jnp.broadcast_to(spec_ref[...].reshape(1, atoms), (16 - 3 * EVALS, atoms))
    for other in range(n_edge):
        at = slice(other * atoms, (other + 1) * atoms)
        for part, ref in enumerate((send_ref, recv_ref, mask_ref)):
            s.lists_out[other, part * EVALS : (part + 1) * EVALS, :] = ref[:, at]
        s.lists_out[other, 3 * EVALS :, :] = species_rows

    pl.semaphore_wait(barrier, 2 * n_edge - 1 + n_sys - 1 - jnp.where(stays, 1, 0))

    def given(source, target, kind, part):
        return pltpu.make_async_remote_copy(
            src_ref=source,
            dst_ref=target,
            send_sem=s.send_sem.at[kind, part],
            recv_sem=s.recv_sem.at[kind, held_part],
            device_id=place_of(held_group, part),
            device_id_type=MESH,
        )

    def taken(target, kind, part):
        pltpu.make_async_remote_copy(
            src_ref=target,
            dst_ref=target,
            send_sem=s.send_sem.at[kind, part],
            recv_sem=s.recv_sem.at[kind, part],
            device_id={"sys": my_group, "edge": part},
            device_id_type=MESH,
        ).wait_recv()

    def give_atoms(part):
        return given(s.start_out, s.start_float.at[held_part], KIND_INIT, part)

    def give_slots(part):
        return given(s.lists_out.at[part], s.lists_in.at[held_part], KIND_EDGES, part)

    def give_lists():
        return given(s.lists_out, s.lists_own, KIND_OWN, held_part)

    def start_first(part):
        give_atoms(part).start()
        give_slots(part).start()

    each_given(start_first)

    @pl.when(jnp.logical_not(stays))
    def _():
        give_lists().start()

    @pl.when(stays)
    def _():
        s.start_float[me] = s.start_out[...]
        s.lists_in[me] = s.lists_out[me]
        s.lists_own[...] = s.lists_out[...]

    for layer in range(2):
        w_in = rin_ref[layer]
        high, low = two_parts_f32(w_in)
        zero = jnp.zeros_like(high)
        s.w_in_left[layer] = jnp.concatenate([high, high, low, zero], axis=0).T.astype(BF)
        s.w_in_back[layer] = jnp.concatenate(
            [
                jnp.concatenate([high, high], axis=1),
                jnp.concatenate([low, zero], axis=1),
            ],
            axis=0,
        ).astype(BF)
        w_out = rout_ref[layer]
        s.w_out_left[layer] = left_three(w_out.T)
        s.w_out_back[layer] = jnp.concatenate(two_parts_f32(w_out), axis=0).astype(BF)
    s.mf_left[...] = left_three(mfirst_ref[...].T)
    s.mf_back[...] = left_three(mfirst_ref[...])
    for number in range(3):
        s.ms_left[number] = left_three(msquare_ref[number].T)
        s.ms_back[number] = left_three(msquare_ref[number])
    emb_pad = jnp.concatenate(
        [emb_ref[...], jnp.zeros((16 - emb_ref.shape[0], channels), F32)], axis=0
    )
    s.emb_left[...] = jnp.concatenate(list(three_parts_f32(emb_pad)), axis=0).T.astype(BF)
    s.readout_col[...] = jnp.broadcast_to(
        readout_ref[...].reshape(1, channels), (atoms, channels)
    ).T
    for ref in (
        s.grad_emb,
        s.grad_in,
        s.grad_out,
        s.grad_mf,
        s.grad_ms,
        s.grad_ro,
        s.grad_second,
        s.grad_first,
    ):
        ref[...] = jnp.zeros_like(ref)

    def first_landed(part):
        taken(s.start_float.at[part], KIND_INIT, part)
        taken(s.lists_in.at[part], KIND_EDGES, part)

    each_given(first_landed)

    @pl.when(jnp.logical_not(stays))
    def _():
        taken(s.lists_own, KIND_OWN, me)

    def first_sent(part):
        give_atoms(part).wait_send()
        give_slots(part).wait_send()

    each_given(first_sent)

    @pl.when(jnp.logical_not(stays))
    def _():
        give_lists().wait_send()

    def species_values(hot):
        return dot_nn(s.emb_left[...], jnp.concatenate([hot, hot, hot], axis=0))

    own_species = s.lists_in[me, 3 * EVALS : 3 * EVALS + 1, :]
    own_species = lax.broadcasted_iota(jnp.int32, (16, atoms), 0) == own_species
    s.own_kind[...] = own_species.astype(F32).astype(BF)
    s.start_scalar[...] = species_values(s.own_kind[...])
    s.rows[...] = jnp.zeros_like(s.rows)
    for axis in range(3):
        s.place[axis] = s.start_float[:, axis, :]
        s.speed[axis] = s.start_float[:, 3 + axis, :]

    def one_hots(number):
        atom_row = lax.broadcasted_iota(jnp.int32, (atoms, atoms), 0)

        def hot(row):
            return (atom_row == row).astype(F32).astype(BF)

        def put_own(tile, at, value):
            s.own_hot[number, tile, 0:atoms, at] = value
            s.own_hot[number, tile, atoms:, at] = value

        def body(index):
            for part in range(group):
                other = index * group + part
                at = pl.ds(part * atoms, atoms)
                out_list = s.lists_own.at[other]
                in_list = s.lists_in.at[other]
                sender = out_list[pl.ds(number, 1), :]
                receiver = out_list[pl.ds(EVALS + number, 1), :]
                mask = out_list[pl.ds(2 * EVALS + number, 1), :]
                put_own(index, at, hot(sender))
                s.far_hot[number, index, :, at] = hot(jnp.where(mask == 0, -1, receiver))
                sender = in_list[pl.ds(number, 1), :]
                receiver = in_list[pl.ds(EVALS + number, 1), :]
                mask = in_list[pl.ds(2 * EVALS + number, 1), :]
                sender_hot = hot(sender)
                put_own(tiles + index, at, hot(jnp.where(mask == 0, -1, receiver)))
                s.far_hot[number, tiles + index, :, at] = sender_hot
                species = in_list[pl.ds(3 * EVALS, 1), :]
                kinds = lax.broadcasted_iota(jnp.int32, (16, atoms), 0)
                species_hot = (kinds == species).astype(F32).astype(BF)
                s.kind_hot[number, index, :, at] = dot_nn(species_hot, sender_hot).astype(BF)
            s.kind_value[number, index] = species_values(s.kind_hot[number, index])

        each_tile(body)

    def table(rows):
        for axis in range(3):
            s.rows[:, axis, :] = rows[axis]
        for other in range(n_edge):
            s.pieces[other] = stack_three(s.rows[other])

    def edge_difference(number, index):
        sign = jnp.where(index < tiles, 1.0, -1.0)
        own = dot_nn(s.pieces[me], s.own_hot[number, index, 0:atoms, :])
        first = lax.rem(index, tiles) * group
        far = [
            dot_nn(
                s.pieces[first + part],
                s.far_hot[number, index, :, part * atoms : (part + 1) * atoms],
            )
            for part in range(group)
        ]
        return sign * join_three(own - jnp.concatenate(far, axis=1))

    def scatter_rows(number, target):
        parts = [stack_three(s.edge_rows[index]) for index in range(2 * tiles)]
        own = 0.0
        for index in range(2 * tiles):
            found = dot_nt(parts[index], s.own_hot[number, index, 0:atoms, :])
            own = own + found if index < tiles else own - found
        s.row_own[...] = join_three(own)
        for other in range(n_edge):
            index, part = other // group, other % group
            at = slice(part * atoms, (part + 1) * atoms)
            total = join_three(
                dot_nt(parts[tiles + index][:, at], s.far_hot[number, tiles + index, :, at])
                - dot_nt(parts[index][:, at], s.far_hot[number, index, :, at])
            )
            for axis in range(3):
                target[axis, other : other + 1, :] = total[axis : axis + 1]
        for axis in range(3):
            target[axis, pl.ds(me, 1), :] += s.row_own[axis : axis + 1, :]

    def geometry(number, index):
        offset = edge_difference(number, index)
        geo = s.geo.at[number, index]
        radius = jnp.sqrt(jnp.sum(offset * offset, axis=0, keepdims=True) + SOFTEN)
        inverse = 1.0 / radius
        unit = offset * inverse
        one, two, three = rows_of(unit, 0, 3)
        geo[0:3, :] = ROOT3 * unit[0:3]
        geo[3:4, :] = ROOT15 * one * two
        geo[4:5, :] = ROOT15 * two * three
        geo[5:6, :] = 0.5 * ROOT5 * (3.0 * three * three - 1.0)
        geo[6:7, :] = ROOT15 * one * three
        geo[7:8, :] = 0.5 * ROOT15 * (one * one - two * two)
        t = radius * (1.0 / CUTOFF)
        sines, cosines = sin_cos_multiples(*sin_cos_pi(t))
        sines = jnp.concatenate(sines, axis=0)
        cosines = jnp.concatenate(cosines, axis=0)
        t2 = t * t
        t4 = t2 * t2
        amount = math.sqrt(2.0 / CUTOFF) * inverse
        env = 1.0 - t4 * t2 * (28.0 - 48.0 * t + 21.0 * t2)
        env_one = -168.0 / CUTOFF * t4 * t * (1.0 - t) * (1.0 - t)
        env_two = -168.0 / CUTOFF**2 * t4 * (1.0 - t) * (5.0 - 7.0 * t)
        front = amount * env
        front_one = amount * (env_one - env * inverse)
        front_two = amount * (env_two - 2.0 * inverse * (env_one - env * inverse))
        waves = (lax.broadcasted_iota(jnp.int32, (NB, 1), 0) + 1).astype(F32) * (
            math.pi / CUTOFF
        )
        geo[8:16, :] = front * sines
        geo[16:24, :] = front_one * sines + front * waves * cosines
        geo[24:32, :] = (
            front_two * sines + 2.0 * front_one * waves * cosines - front * waves * waves * sines
        )
        geo[32:35, :] = unit[0:3]
        geo[35:36, :] = inverse

    def first_back(number, index):
        geo = s.geo.at[number, index]
        bars = s.geo_bar.at[number, index]
        ybar = rows_of(bars[0:8, :], 0, 8)
        slope = jnp.sum(bars[8:16, :] * geo[16:24, :], axis=0, keepdims=True)
        units = rows_of(geo[32:40, :], 0, 3)
        inverse = geo[35:36, :]
        extra = second_slope(*units, ybar[3:])
        back = [ROOT3 * ybar[axis] + extra[axis] for axis in range(3)]
        along = back[0] * units[0] + back[1] * units[1] + back[2] * units[2]
        rest = slope - along * inverse
        for axis in range(3):
            bars[16 + axis : 17 + axis, :] = back[axis]
            s.edge_rows[index, axis : axis + 1, :] = back[axis] * inverse + rest * units[axis]
        bars[19:20, :] = rest

    def geometry_tangent(number, index):
        move = edge_difference(number, index)
        geo = s.geo.at[number, index]
        out = s.geo_dot.at[index]
        inverse = geo[35:36, :]
        one, two, three = rows_of(geo[32:40, :], 0, 3)
        moves = rows_of(move, 0, 3)
        speed = one * moves[0] + two * moves[1] + three * moves[2]
        d_one, d_two, d_three = [
            (amount - unit * speed) * inverse for amount, unit in zip(moves, (one, two, three))
        ]
        out[0:1, :] = ROOT3 * d_one
        out[1:2, :] = ROOT3 * d_two
        out[2:3, :] = ROOT3 * d_three
        out[3:4, :] = ROOT15 * (d_one * two + one * d_two)
        out[4:5, :] = ROOT15 * (d_two * three + two * d_three)
        out[5:6, :] = 3.0 * ROOT5 * three * d_three
        out[6:7, :] = ROOT15 * (d_one * three + one * d_three)
        out[7:8, :] = ROOT15 * (one * d_one - two * d_two)
        out[8:16, :] = geo[16:24, :] * speed
        out[16:17, :] = d_one
        out[17:18, :] = d_two
        out[18:19, :] = d_three
        out[19:20, :] = speed
        out[20:23, :] = move[0:3]

    def second_back(number, index, hats):
        geo = s.geo.at[number, index]
        bars = s.geo_bar.at[number, index]
        dots = s.geo_dot.at[index]
        units = rows_of(geo[32:40, :], 0, 3)
        inverse = geo[35:36, :]
        turns = rows_of(dots[16:24, :], 0, 3)
        speed = dots[19:20, :]
        moves = rows_of(dots[16:24, :], 4, 3)
        back = rows_of(bars[16:24, :], 0, 3)
        rest = bars[19:20, :]
        yhat = rows_of(hats, 0, 8)
        ybar = rows_of(bars[0:8, :], 0, 8)
        extra = second_slope(*units, yhat[3:])
        more = second_slope(*turns, ybar[3:])
        radial_hat = jnp.sum(
            hats[8:16] * geo[16:24, :] + speed * (bars[8:16, :] * geo[24:32, :]),
            axis=0,
            keepdims=True,
        ) - inverse * (turns[0] * back[0] + turns[1] * back[1] + turns[2] * back[2])
        unit_hat = [
            ROOT3 * yhat[axis]
            + extra[axis]
            + more[axis]
            - speed * inverse * back[axis]
            + rest * moves[axis]
            for axis in range(3)
        ]
        along = unit_hat[0] * units[0] + unit_hat[1] * units[1] + unit_hat[2] * units[2]
        left = radial_hat - along * inverse
        for axis in range(3):
            s.edge_rows[index, axis : axis + 1, :] = unit_hat[axis] * inverse + left * units[axis]

    def radial_forward(layer, number, index, basis):
        before = dot_nn(s.w_in_left[layer], right_three_small(basis))
        s.hidden[layer, number, index] = before
        gate = logistic(before)
        s.radial[layer, number, index] = dot_nn(
            s.w_out_left[layer], right_three(before * gate)
        )

    def radial_tangent(layer, number, index, basis_dot):
        before = s.hidden[layer, number, index]
        before_dot = dot_nn(s.w_in_left[layer], right_three_small(basis_dot))
        s.hidden_dot[layer, index] = before_dot
        gate = logistic(before)
        s.radial_dot[layer, index] = dot_nn(
            s.w_out_left[layer], right_three(silu_slope(before, gate) * before_dot)
        )

    def rows_pair(value):
        return jnp.concatenate(two_parts(value), axis=0)

    def hidden_back(layer, pair):
        half_rows = 3 * channels
        left = s.w_out_back[layer]
        found = dot_nn(left, pair[0:half_rows])
        return found[0:channels] + found[channels:] + dot_nn(left[0:channels], pair[half_rows:])

    def basis_back(layer, pair):
        found = dot_nn(s.w_in_back[layer], pair)
        return found[0:8] + found[8:16]

    def radial_back(layer, number, index):
        hidden_bar = hidden_back(layer, s.r_pair[layer, index])
        s.hidden_bar[layer, number, index] = hidden_bar
        before = s.hidden[layer, number, index]
        before_bar = silu_slope(before, logistic(before)) * hidden_bar
        return basis_back(layer, rows_pair(before_bar))

    def radial_second(layer, number, index, last):
        hidden_hat = hidden_back(layer, s.h_pair[layer, index])
        before = s.hidden[layer, number, index]
        before_dot = s.hidden_dot[layer, index]
        hidden_bar = s.hidden_bar[layer, number, index]
        gate = logistic(before)
        slope = silu_slope(before, gate)
        before_hat = slope * hidden_hat + silu_bend(before, gate) * before_dot * hidden_bar
        s.out_pair[layer, index] = rows_pair(before * gate)
        s.dot_pair[layer, index] = rows_pair(slope * before_dot)
        s.bar_pair[layer, index] = rows_pair(slope * hidden_bar)
        hat_pair = rows_pair(before_hat)
        s.hat_pair[layer, index] = hat_pair
        return None if last else basis_back(layer, hat_pair)

    def radial_gradients(layer, number):
        for index in range(tiles):
            s.grad_out[layer] += dot_nt(s.h_pair[layer, index], s.out_pair[layer, index]) + dot_nt(
                s.r_pair[layer, index], s.dot_pair[layer, index]
            )
            tile = index if layer == 1 else tiles + index
            basis = jnp.concatenate(two_parts_f32(s.geo[number, tile, 8:16, :]), axis=0)
            basis_dot = jnp.concatenate(two_parts_f32(s.geo_dot[tile, 8:16, :]), axis=0)
            s.grad_in[layer] += dot_nt(basis.astype(BF), s.hat_pair[layer, index]) + dot_nt(
                basis_dot.astype(BF), s.bar_pair[layer, index]
            )

    def kind_gradients(number):
        for index in range(tiles):
            kinds = s.kind_hot[number, index]
            s.grad_emb[...] += dot_nt(kinds, s.v_high[index]) + dot_nt(kinds, s.v_low[index])
        high, low = two_parts(s.scalar_hat[...])
        s.grad_emb[...] += dot_nt(s.own_kind[...], high) + dot_nt(s.own_kind[...], low)

    def node_gradients(number):
        agg = s.agg.at[number]
        for first, last, path in PATHS:
            hats = [s.raw_hat[k * channels : (k + 1) * channels, :] for k in range(first, last)]
            bars = [s.raw_bar[number, k * channels : (k + 1) * channels, :] for k in range(first, last)]
            s.grad_ms[path] += outer_three(
                side_by_side(agg, first, last), jnp.concatenate(hats, axis=1)
            ) + outer_three(side_by_side(s.agg_dot, first, last), jnp.concatenate(bars, axis=1))
        s.grad_ms[2] += outer_three(s.agg_two[number], s.last_hat[...]) + outer_three(
            s.agg_two_dot[...], s.last_bar[...]
        )
        s.grad_mf[...] += outer_three(s.mixed_hat[...], part_of(agg, 0)) + outer_three(
            s.mixed_bar[number], part_of(s.agg_dot, 0)
        )

    def put_pieces(high_ref, low_ref, lane, at, value):
        high, low = two_parts(value)
        high_ref[at, lane] = high
        low_ref[at, lane] = low

    def put_pair(ref, path, c, lane, value):
        high, low = two_parts(value)
        ref[chunk_at(path * channels, c), lane] = high
        ref[chunk_at((3 + path) * channels, c), lane] = low

    def add_scatter(index, hot):
        s.sum_wide[...] += dot_nt(s.m_high[index], hot) + dot_nt(s.m_low[index], hot)

    def harmonic_rows(ref, lane):
        return [ref[row : row + 1, lane] for row in range(8)]

    def lane_parts():
        return [slice(first, first + LANES_AT_ONCE) for first in range(0, lanes, LANES_AT_ONCE)]

    def over_chunks(body):
        for lane in lane_parts():
            for c in range(chunks):
                body(c, lane)

    def over_chunks_sum(body):
        found = []
        for lane in lane_parts():
            sums = (0.0,) * 8
            for c in range(chunks):
                sums = body(c, lane, sums)
            found.append(sum_rows(sums))
        return jnp.concatenate(found, axis=1)

    def fold(value):
        return value[0:8] + value[8:16]

    def sum_rows(parts):
        if not hasattr(parts[0], "shape"):
            return jnp.zeros((8, LANES_AT_ONCE), F32)
        return jnp.concatenate([jnp.sum(part, axis=0, keepdims=True) for part in parts], axis=0)

    def first_forward(number, index):
        tile = tiles + index
        geo = s.geo.at[number, tile]
        radial_forward(0, number, index, geo[8:16, :])
        rad = s.radial.at[0, number, index]
        kind = s.kind_value.at[number, index]

        def body(c, lane):
            value = kind[chunk_at(0, c), lane]
            y = harmonic_rows(geo, lane)
            put_pieces(s.m_high.at[index], s.m_low.at[index], lane, chunk_at(0, c), rad[chunk_at(0, c), lane] * value)
            vector = rad[chunk_at(channels, c), lane] * value
            tensor = rad[chunk_at(2 * channels, c), lane] * value
            for k in range(8):
                part = (vector if k < 3 else tensor) * y[k]
                put_pieces(s.m_high.at[index], s.m_low.at[index], lane, chunk_at((k + 1) * channels, c), part)

        over_chunks(body)
        add_scatter(index, s.own_hot[number, tile, 0:atoms, :])

    def first_tangent(number, index):
        tile = tiles + index
        geo = s.geo.at[number, tile]
        dots = s.geo_dot.at[tile]
        radial_tangent(0, number, index, dots[8:16, :])
        rad = s.radial.at[0, number, index]
        rad_dot = s.radial_dot.at[0, index]
        kind = s.kind_value.at[number, index]

        def body(c, lane):
            value = kind[chunk_at(0, c), lane]
            y = harmonic_rows(geo, lane)
            y_dot = harmonic_rows(dots, lane)
            put_pieces(s.m_high.at[index], s.m_low.at[index], lane, chunk_at(0, c), rad_dot[chunk_at(0, c), lane] * value)
            vector = rad[chunk_at(channels, c), lane] * value
            tensor = rad[chunk_at(2 * channels, c), lane] * value
            vector_dot = rad_dot[chunk_at(channels, c), lane] * value
            tensor_dot = rad_dot[chunk_at(2 * channels, c), lane] * value
            for k in range(8):
                base, move = (vector, vector_dot) if k < 3 else (tensor, tensor_dot)
                part = move * y[k] + base * y_dot[k]
                put_pieces(s.m_high.at[index], s.m_low.at[index], lane, chunk_at((k + 1) * channels, c), part)

        over_chunks(body)
        add_scatter(index, s.own_hot[number, tile, 0:atoms, :])

    def gather_wide(hot):
        return dot_nn(s.a_pair[...], hot)

    def first_reverse(number, index):
        tile = tiles + index
        geo = s.geo.at[number, tile]
        s.first_cot[number, index] = gather_wide(s.own_hot[number, tile])
        cot = s.first_cot.at[number, index]
        rad = s.radial.at[0, number, index]
        kind = s.kind_value.at[number, index]

        def body(c, lane, sums):
            value = kind[chunk_at(0, c), lane]
            y = harmonic_rows(geo, lane)
            put_pair(s.r_pair.at[0, index], 0, c, lane, cot[chunk_at(0, c), lane] * value)
            sums = list(sums)
            for first, last, path in ((0, 3, 1), (3, 8, 2)):
                base = rad[chunk_at(path * channels, c), lane] * value
                total = 0.0
                for k in range(first, last):
                    given = cot[chunk_at((k + 1) * channels, c), lane]
                    total = total + given * y[k]
                    sums[k] = sums[k] + fold(base * given)
                put_pair(s.r_pair.at[0, index], path, c, lane, total * value)
            return tuple(sums)

        sums = over_chunks_sum(body)
        s.geo_bar[number, tile, 0:8, :] = sums
        s.geo_bar[number, tile, 8:16, :] = radial_back(0, number, index)
        first_back(number, tile)

    def first_second(number, index, final):
        tile = tiles + index
        geo = s.geo.at[number, tile]
        dots = s.geo_dot.at[tile]
        s.feat_dot[index] = gather_wide(s.own_hot[number, tile])
        hat = s.feat_dot.at[index]
        cot = s.first_cot.at[number, index]
        rad = s.radial.at[0, number, index]
        rad_dot = s.radial_dot.at[0, index]
        kind = s.kind_value.at[number, index]

        def body(c, lane, sums):
            value = kind[chunk_at(0, c), lane]
            y = harmonic_rows(geo, lane)
            y_dot = harmonic_rows(dots, lane)
            sums = list(sums)
            total = cot[chunk_at(0, c), lane]
            total_hat = hat[chunk_at(0, c), lane]
            put_pair(s.r_pair.at[0, index], 0, c, lane, total * value)
            put_pair(s.h_pair.at[0, index], 0, c, lane, total_hat * value)
            value_hat = rad[chunk_at(0, c), lane] * total_hat + rad_dot[chunk_at(0, c), lane] * total
            for first, last, path in ((0, 3, 1), (3, 8, 2)):
                rad_here = rad[chunk_at(path * channels, c), lane]
                rad_move = rad_dot[chunk_at(path * channels, c), lane]
                base = rad_here * value
                move = rad_move * value
                total = 0.0
                total_hat = 0.0
                for k in range(first, last):
                    given = cot[chunk_at((k + 1) * channels, c), lane]
                    given_hat = hat[chunk_at((k + 1) * channels, c), lane]
                    total = total + given * y[k]
                    total_hat = total_hat + (given_hat * y[k] + given * y_dot[k])
                    if not final:
                        sums[k] = sums[k] + fold(base * given_hat + move * given)
                put_pair(s.r_pair.at[0, index], path, c, lane, total * value)
                put_pair(s.h_pair.at[0, index], path, c, lane, total_hat * value)
                value_hat = value_hat + rad_here * total_hat + rad_move * total
            put_pieces(s.v_high.at[index], s.v_low.at[index], lane, chunk_at(0, c), value_hat)
            return tuple(sums)

        sums = over_chunks_sum(body)
        basis_hat = radial_second(0, number, index, final)
        if not final:
            second_back(number, tile, jnp.concatenate([sums, basis_hat], axis=0))

    def gather_far(ref, number, index):
        found = []
        for part in range(group):
            pair = rows_pair(ref[index * group + part])
            here = dot_nn(pair, s.far_hot[number, index, :, part * atoms : (part + 1) * atoms])
            found.append(here[0:channels] + here[channels:])
        return jnp.concatenate(found, axis=1)

    def put_messages(number, index):
        for part in range(group):
            at = slice(part * atoms, (part + 1) * atoms)
            hot = s.far_hot[number, index, :, at]
            s.msg_out[index * group + part] = dot_nt(s.v_high[index, :, at], hot) + dot_nt(
                s.v_low[index, :, at], hot
            )

    def near_peer(distance):
        return half * group + lax.rem(me + distance, group)

    def far_peer(distance):
        return (1 - half) * group + lax.rem(me + distance, group)

    def message_to(other, kind):
        return remote(s.msg_out.at[other], s.msg_in.at[me], kind, other)

    def exchange_messages(number, kind, make):
        make(number, 1 - half)
        put_messages(number, 1 - half)
        for distance in range(group):
            message_to(far_peer(distance), kind).start()
        make(number, half)
        put_messages(number, half)
        for distance in range(group - 1, 0, -1):
            message_to(near_peer(distance), kind).start()

    def second_forward(number, index):
        geo = s.geo.at[number, index]
        radial_forward(1, number, index, geo[8:16, :])
        s.feat[number, index] = gather_wide(s.own_hot[number, index])
        feat = s.feat.at[number, index]
        rad = s.radial.at[1, number, index]

        def body(c, lane):
            y = harmonic_rows(geo, lane)
            total = rad[chunk_at(0, c), lane] * feat[chunk_at(0, c), lane]
            for first, last, path in ((0, 3, 1), (3, 8, 2)):
                along = 0.0
                for k in range(first, last):
                    along = along + feat[chunk_at((k + 1) * channels, c), lane] * y[k]
                s.along[number, index, chunk_at((path - 1) * channels, c), lane] = along
                total = total + rad[chunk_at(path * channels, c), lane] * along
            put_pieces(s.v_high.at[index], s.v_low.at[index], lane, chunk_at(0, c), total)

        over_chunks(body)

    def second_tangent(number, index):
        geo = s.geo.at[number, index]
        dots = s.geo_dot.at[index]
        radial_tangent(1, number, index, dots[8:16, :])
        s.feat_dot[index] = gather_wide(s.own_hot[number, index])
        feat = s.feat.at[number, index]
        feat_dot = s.feat_dot.at[index]
        rad = s.radial.at[1, number, index]
        rad_dot = s.radial_dot.at[1, index]

        def body(c, lane):
            y = harmonic_rows(geo, lane)
            y_dot = harmonic_rows(dots, lane)
            at = chunk_at(0, c)
            total = rad_dot[at, lane] * feat[at, lane] + rad[at, lane] * feat_dot[at, lane]
            for first, last, path in ((0, 3, 1), (3, 8, 2)):
                move = 0.0
                for k in range(first, last):
                    here = chunk_at((k + 1) * channels, c)
                    move = move + (feat_dot[here, lane] * y[k] + feat[here, lane] * y_dot[k])
                here = chunk_at((path - 1) * channels, c)
                s.along_dot[index, here, lane] = move
                here_rad = chunk_at(path * channels, c)
                total = total + (
                    rad_dot[here_rad, lane] * s.along[number, index, here, lane]
                    + rad[here_rad, lane] * move
                )
            put_pieces(s.v_high.at[index], s.v_low.at[index], lane, at, total)

        over_chunks(body)

    def second_reverse(number, index):
        geo = s.geo.at[number, index]
        s.msg_cot[number, index] = gather_far(s.cot_all, number, index)
        cot = s.msg_cot.at[number, index]
        feat = s.feat.at[number, index]
        rad = s.radial.at[1, number, index]

        def body(c, lane, sums):
            y = harmonic_rows(geo, lane)
            at = chunk_at(0, c)
            given = cot[at, lane]
            sums = list(sums)
            put_pair(s.r_pair.at[1, index], 0, c, lane, feat[at, lane] * given)
            put_pieces(s.m_high.at[index], s.m_low.at[index], lane, at, rad[at, lane] * given)
            for first, last, path in ((0, 3, 1), (3, 8, 2)):
                here = chunk_at(path * channels, c)
                along = s.along[number, index, chunk_at((path - 1) * channels, c), lane]
                put_pair(s.r_pair.at[1, index], path, c, lane, along * given)
                base = rad[here, lane] * given
                for k in range(first, last):
                    wide_at = chunk_at((k + 1) * channels, c)
                    put_pieces(s.m_high.at[index], s.m_low.at[index], lane, wide_at, base * y[k])
                    sums[k] = sums[k] + fold(base * feat[wide_at, lane])
            return tuple(sums)

        sums = over_chunks_sum(body)
        s.geo_bar[number, index, 0:8, :] = sums
        s.geo_bar[number, index, 8:16, :] = radial_back(1, number, index)
        first_back(number, index)
        add_scatter(index, s.own_hot[number, index, 0:atoms, :])

    def second_second(number, index, final):
        geo = s.geo.at[number, index]
        dots = s.geo_dot.at[index]
        s.msg_hat[index] = gather_far(s.cot_all, number, index)
        cot = s.msg_cot.at[number, index]
        feat = s.feat.at[number, index]
        feat_dot = s.feat_dot.at[index]
        rad = s.radial.at[1, number, index]
        rad_dot = s.radial_dot.at[1, index]

        def body(c, lane, sums):
            y = harmonic_rows(geo, lane)
            y_dot = harmonic_rows(dots, lane)
            at = chunk_at(0, c)
            given = cot[at, lane]
            given_hat = s.msg_hat[index, at, lane]
            sums = list(sums)
            put_pair(s.r_pair.at[1, index], 0, c, lane, feat[at, lane] * given)
            put_pair(s.h_pair.at[1, index], 0, c, lane, feat[at, lane] * given_hat + feat_dot[at, lane] * given)
            put_pieces(s.m_high.at[index], s.m_low.at[index], lane, at, rad[at, lane] * given_hat + rad_dot[at, lane] * given)
            for first, last, path in ((0, 3, 1), (3, 8, 2)):
                here = chunk_at(path * channels, c)
                along_at = chunk_at((path - 1) * channels, c)
                along = s.along[number, index, along_at, lane]
                along_dot = s.along_dot[index, along_at, lane]
                put_pair(s.r_pair.at[1, index], path, c, lane, along * given)
                put_pair(s.h_pair.at[1, index], path, c, lane, along * given_hat + along_dot * given)
                base = rad[here, lane] * given
                base_hat = rad[here, lane] * given_hat + rad_dot[here, lane] * given
                for k in range(first, last):
                    wide_at = chunk_at((k + 1) * channels, c)
                    put_pieces(s.m_high.at[index], s.m_low.at[index], lane, wide_at, base_hat * y[k] + base * y_dot[k])
                    if not final:
                        sums[k] = sums[k] + fold(
                            base_hat * feat[wide_at, lane] + base * feat_dot[wide_at, lane]
                        )
            return tuple(sums)

        sums = over_chunks_sum(body)
        basis_hat = radial_second(1, number, index, final)
        if not final:
            second_back(number, index, jnp.concatenate([sums, basis_hat], axis=0))
        add_scatter(index, s.own_hot[number, index, 0:atoms, :])

    def part_of(ref, component):
        return ref[component * channels : (component + 1) * channels, :]

    def side_by_side(ref, first, last):
        return jnp.concatenate([part_of(ref, k + 1) for k in range(first, last)], axis=1)

    def linear(left, value):
        return dot_nn(left, right_three(value))

    def keep_wide(component, value):
        high, low = two_parts(value)
        at = slice(component * channels, (component + 1) * channels)
        s.a_pair[at, 0:atoms] = high
        s.a_pair[at, atoms:] = low

    def node_first_forward(number):
        s.agg[number] = INV_NEIGH * s.sum_wide[...]
        agg = s.agg.at[number]
        mixed = linear(s.mf_left[...], part_of(agg, 0))
        s.mixed[number] = mixed
        before, gate_one, gate_two = [mixed[i * channels : (i + 1) * channels] for i in range(3)]
        scalar = s.start_scalar[...] + before * logistic(before)
        s.scalar[number] = scalar
        keep_wide(0, scalar)
        gates = (logistic(gate_one), logistic(gate_two))
        for first, last, path in PATHS:
            raws = linear(s.ms_left[path], side_by_side(agg, first, last))
            for k in range(first, last):
                raw = raws[:, (k - first) * atoms : (k - first + 1) * atoms]
                s.raw[number, k * channels : (k + 1) * channels, :] = raw
                keep_wide(k + 1, gates[path] * raw)

    def node_first_tangent(number):
        s.agg_dot[...] = INV_NEIGH * s.sum_wide[...]
        mixed = s.mixed.at[number]
        mixed_dot = linear(s.mf_left[...], part_of(s.agg_dot, 0))
        s.mixed_dot[...] = mixed_dot
        before = part_of(mixed, 0)
        scalar_dot = silu_slope(before, logistic(before)) * mixed_dot[0:channels]
        s.scalar_dot[...] = scalar_dot
        keep_wide(0, scalar_dot)
        for first, last, path in PATHS:
            gate = logistic(part_of(mixed, path + 1))
            move = gate * (1.0 - gate) * mixed_dot[(path + 1) * channels : (path + 2) * channels]
            raws_dot = linear(s.ms_left[path], side_by_side(s.agg_dot, first, last))
            for k in range(first, last):
                raw_dot = raws_dot[:, (k - first) * atoms : (k - first + 1) * atoms]
                s.raw_dot[k * channels : (k + 1) * channels, :] = raw_dot
                raw = s.raw[number, k * channels : (k + 1) * channels, :]
                keep_wide(k + 1, move * raw + gate * raw_dot)

    def node_first_reverse(number):
        s.feat_bar[number] = s.sum_wide[...]
        s.feat_bar[number, 0:channels, :] += s.readout_col[...]
        bar = s.feat_bar.at[number]
        mixed = s.mixed.at[number]
        before = part_of(mixed, 0)
        s.mixed_bar[number, 0:channels, :] = silu_slope(before, logistic(before)) * part_of(bar, 0)
        for first, last, path in PATHS:
            gate = logistic(part_of(mixed, path + 1))
            total = 0.0
            bars = []
            for k in range(first, last):
                given = part_of(bar, k + 1)
                total = total + given * s.raw[number, k * channels : (k + 1) * channels, :]
                raw_bar = gate * given
                s.raw_bar[number, k * channels : (k + 1) * channels, :] = raw_bar
                bars.append(raw_bar)
            found = INV_NEIGH * linear(s.ms_back[path], jnp.concatenate(bars, axis=1))
            for k in range(first, last):
                keep_wide(k + 1, found[:, (k - first) * atoms : (k - first + 1) * atoms])
            s.mixed_bar[number, (path + 1) * channels : (path + 2) * channels, :] = (
                gate * (1.0 - gate) * total
            )
        keep_wide(0, INV_NEIGH * linear(s.mf_back[...], s.mixed_bar[number]))

    def node_first_second(number, energy_bar):
        s.sum_wide[0:channels, :] += s.readout_col[...] * energy_bar
        hat = s.sum_wide
        bar = s.feat_bar.at[number]
        mixed = s.mixed.at[number]
        before = part_of(mixed, 0)
        gate = logistic(before)
        scalar_hat = part_of(hat, 0)
        s.mixed_hat[0:channels, :] = silu_slope(before, gate) * scalar_hat + silu_bend(
            before, gate
        ) * s.mixed_dot[0:channels, :] * part_of(bar, 0)
        s.scalar_hat[...] = scalar_hat
        for first, last, path in PATHS:
            gate = logistic(part_of(mixed, path + 1))
            slope = gate * (1.0 - gate)
            bend = slope * (1.0 - 2.0 * gate)
            mixed_dot = s.mixed_dot[(path + 1) * channels : (path + 2) * channels, :]
            one = 0.0
            two = 0.0
            hats = []
            for k in range(first, last):
                at = slice(k * channels, (k + 1) * channels)
                given = part_of(bar, k + 1)
                given_hat = part_of(hat, k + 1)
                raw = s.raw[number, at, :]
                one = one + (given_hat * raw + given * s.raw_dot[at, :])
                two = two + given * raw
                hats.append(gate * given_hat + slope * mixed_dot * given)
            for k in range(first, last):
                s.raw_hat[k * channels : (k + 1) * channels, :] = hats[k - first]
            found = INV_NEIGH * linear(s.ms_back[path], jnp.concatenate(hats, axis=1))
            for k in range(first, last):
                keep_wide(k + 1, found[:, (k - first) * atoms : (k - first + 1) * atoms])
            s.mixed_hat[(path + 1) * channels : (path + 2) * channels, :] = (
                slope * one + bend * mixed_dot * two
            )
        keep_wide(0, INV_NEIGH * linear(s.mf_back[...], s.mixed_hat[...]))

    def all_peers():
        return [far_peer(distance) for distance in range(group)] + [
            near_peer(distance) for distance in range(group - 1, 0, -1)
        ]

    def collect_messages(kind):
        total = s.msg_out[me]
        for other in all_peers():
            landed(s.msg_in.at[other], kind, other)
            total = total + s.msg_in[other]
        for other in all_peers():
            message_to(other, kind).wait_send()
        return INV_NEIGH * total

    def cotangent_to(other, kind):
        return remote(s.cot_all.at[me], s.cot_all.at[me], kind, other)

    def share_cotangent(value, kind):
        s.cot_all[me] = value
        for other in all_peers():
            cotangent_to(other, kind).start()

    def with_cotangents(number, kind, use):
        for distance in range(1, group):
            other = near_peer(distance)
            landed(s.cot_all.at[other], kind, other)
        use(number, half)
        for distance in range(group):
            other = far_peer(distance)
            landed(s.cot_all.at[other], kind, other)
        use(number, 1 - half)
        for other in all_peers():
            cotangent_to(other, kind).wait_send()

    def node_second_forward(number):
        agg = collect_messages(KIND_MSG)
        s.agg_two[number] = agg
        before = linear(s.ms_left[2], agg)
        s.last[number] = before
        gate = logistic(before)
        s.energy_row[...] = jnp.sum(
            s.readout_col[...] * (s.scalar[number] + before * gate), axis=0, keepdims=True
        )
        before_bar = s.readout_col[...] * silu_slope(before, gate)
        share_cotangent(INV_NEIGH * linear(s.ms_back[2], before_bar), KIND_COT)

    def node_second_second(number, energy_bar):
        agg_dot = collect_messages(KIND_TMSG)
        before = s.last[number]
        before_dot = linear(s.ms_left[2], agg_dot)
        gate = logistic(before)
        slope = silu_slope(before, gate)
        before_hat = s.readout_col[...] * (
            energy_bar * slope + silu_bend(before, gate) * before_dot
        )
        share_cotangent(INV_NEIGH * linear(s.ms_back[2], before_hat), KIND_TCOT)
        s.agg_two_dot[...] = agg_dot
        s.last_hat[...] = before_hat
        s.last_bar[...] = s.readout_col[...] * slope
        s.grad_ro[...] += energy_bar * (s.scalar[number] + before * gate) + (
            s.scalar_dot[...] + slope * before_dot
        )

    def share_rows(out_ref, in_ref, kind, meanwhile=None):
        def start(other):
            remote(out_ref, in_ref.at[me], kind, other).start()

        each_peer(start)
        in_ref[me] = out_ref[...]
        if meanwhile is not None:
            meanwhile()

        def wait(other):
            landed(in_ref.at[other], kind, other)
            remote(out_ref, in_ref.at[me], kind, other).wait_send()

        each_peer(wait)
        total = in_ref[0]
        for other in range(1, n_edge):
            total = total + in_ref[other]
        return total

    def evaluate(number):
        table(s.place)
        loop(2 * tiles, lambda index: geometry(number, index), True)
        s.sum_wide[...] = jnp.zeros_like(s.sum_wide)
        each_tile(lambda index: first_forward(number, index))
        node_first_forward(number)
        exchange_messages(number, KIND_MSG, second_forward)
        node_second_forward(number)
        s.sum_wide[...] = jnp.zeros_like(s.sum_wide)
        with_cotangents(number, KIND_COT, second_reverse)
        node_first_reverse(number)
        each_tile(lambda index: first_reverse(number, index))
        scatter_rows(number, s.force_out)
        s.force_out[3] = jnp.zeros((n_edge, atoms), F32)
        s.force_out[3, pl.ds(me, 1), :] = s.energy_row[...]

        def prepare():
            @pl.when(number < EVALS - 1)
            def _():
                one_hots(number + 1)

        total = share_rows(s.force_out, s.force_in, KIND_FORCE, prepare)
        force = -total[0:3]
        s.energy[number] = total[3]
        half_kick = 0.5 * STEP_DT * force

        @pl.when(number > 0)
        def _():
            s.speed[...] = s.speed[...] + half_kick

        @pl.when(number == 0)
        def _():
            s.start_kinetic[...] = 0.5 * jnp.sum(s.speed[...] * s.speed[...], axis=0)

        @pl.when(number < EVALS - 1)
        def _():
            s.speed[...] = s.speed[...] + half_kick
            s.place[...] = s.place[...] + STEP_DT * s.speed[...]

    one_hots(0)
    loop(EVALS, evaluate)

    kinetic = 0.5 * jnp.sum(s.speed[...] * s.speed[...], axis=0)
    change = (s.energy[EVALS - 1] + kinetic) - (s.energy[0] + s.start_kinetic[...])
    system_of = lax.broadcasted_iota(jnp.int32, (n_edge, atoms), 1) // half_atoms
    system_atoms = float(half_atoms * n_edge)
    loss = jnp.zeros((1, 1), F32)
    drift_grad = jnp.zeros((n_edge, atoms), F32)
    for number in range(SYS_LOC):
        mine = system_of == number
        drift = jnp.sum(jnp.where(mine, change, 0.0), axis=(0, 1), keepdims=True)
        loss = loss + drift * drift / system_atoms
        drift_grad = drift_grad + jnp.where(mine, 2.0 * drift / system_atoms, 0.0)
    s.drift_grad[...] = drift_grad
    s.place_bar[...] = jnp.zeros_like(s.place_bar)
    s.speed_bar[...] = drift_grad[None] * s.speed[...]
    s.loss_row[...] = jnp.broadcast_to(loss * jnp.where(me == 0, 1.0, 0.0), (1, channels))

    def reverse(step, last):
        number = EVALS - 1 - step
        sides = jnp.where(jnp.logical_or(number == 0, number == EVALS - 1), 1.0, 2.0)
        ends = jnp.where(number == 0, -1.0, jnp.where(number == EVALS - 1, 1.0, 0.0))
        s.move[...] = (-0.5 * STEP_DT * sides) * s.speed_bar[...]
        table(s.move)
        loop(2 * tiles, lambda index: geometry_tangent(number, index), True)
        energy_bar = ends * s.drift_grad[pl.ds(me, 1), :]
        s.sum_wide[...] = jnp.zeros_like(s.sum_wide)
        each_tile(lambda index: first_tangent(number, index))
        node_first_tangent(number)
        exchange_messages(number, KIND_TMSG, second_tangent)
        node_second_second(number, energy_bar)
        s.sum_wide[...] = jnp.zeros_like(s.sum_wide)
        with_cotangents(
            number, KIND_TCOT, lambda number, index: second_second(number, index, last)
        )
        node_first_second(number, energy_bar)
        if last:
            radial_gradients(1, number)
            node_gradients(number)
            pack_first()
            each_peer(lambda other: first_rows(other).start())
        each_tile(lambda index: first_second(number, index, last))
        if last:
            radial_gradients(0, number)
            kind_gradients(number)
            pack_second()
            each_peer(lambda other: second_rows(other).start())
        else:
            scatter_rows(number, s.place_out)

            def gradients():
                radial_gradients(1, number)
                node_gradients(number)
                radial_gradients(0, number)
                kind_gradients(number)

            total = share_rows(s.place_out, s.place_in, KIND_TFORCE, gradients)
            s.place_bar[...] = s.place_bar[...] + total
            s.speed_bar[...] = s.speed_bar[...] + STEP_DT * s.place_bar[...]

    first_each, second_each = [ref.shape[0] // n_edge for ref in (s.grad_first, s.grad_second)]

    def some_rows(ref, other, count):
        return ref.at[pl.ds(pl.multiple_of(other * count, 8), count)]

    def first_rows(other):
        return remote(
            some_rows(s.grad_first, other, first_each),
            s.part_in.at[me, 0:first_each],
            KIND_SCATTER,
            other,
        )

    def second_rows(other):
        return remote(
            some_rows(s.grad_second, other, second_each),
            s.part_in.at[me, first_each:],
            KIND_SCATTER_LATE,
            other,
        )

    def join_out(layer):
        found = s.grad_out[layer]
        rows = 3 * channels
        return found[0:rows, 0:channels] + found[0:rows, channels:] + found[rows:, 0:channels]

    def join_in(layer):
        found = s.grad_in[layer]
        return found[0:8, 0:channels] + found[0:8, channels:] + found[8:16, 0:channels]

    def pack_first():
        out = s.grad_first
        rows = 3 * channels
        out[0:rows, :] = jnp.concatenate([join_out(1), s.grad_mf[...]], axis=1)
        out[rows : rows + channels, :] = jnp.concatenate([s.grad_ms[0], s.grad_ms[1]], axis=1)
        ones = jnp.ones((8, atoms), BF)
        ro_rows = 0.0
        for piece in three_parts_f32(s.grad_ro[...]):
            ro_rows = ro_rows + dot_nt(ones, piece.astype(BF))
        rest = jnp.zeros((channels - 16, channels), F32)
        small = jnp.concatenate([ro_rows, join_in(1), rest], axis=0)
        out[rows + channels : rows + 2 * channels, :] = jnp.concatenate(
            [s.grad_ms[2], small], axis=1
        )

    def pack_second():
        out = s.grad_second
        rows = 3 * channels // 2
        found = join_out(0)
        out[0:rows, :] = jnp.concatenate([found[0:rows], found[rows:]], axis=1)
        out[rows : rows + 8, :] = jnp.concatenate([join_in(0), s.grad_emb[0:8, :]], axis=1)
        loss_rows = jnp.broadcast_to(s.loss_row[...], (8, channels))
        out[rows + 8 : rows + 16, :] = jnp.concatenate([loss_rows, loss_rows], axis=1)

    lax.fori_loop(0, EVALS - 1, lambda step, carry: (reverse(step, False), carry)[1], 0)
    reverse(EVALS - 1, True)

    s.part_in[me, 0:first_each, :] = some_rows(s.grad_first, me, first_each)[...]
    s.part_in[me, first_each:, :] = some_rows(s.grad_second, me, second_each)[...]

    def wait_scatter(other):
        landed(s.part_in.at[other, 0:first_each], KIND_SCATTER, other)
        landed(s.part_in.at[other, first_each:], KIND_SCATTER_LATE, other)
        first_rows(other).wait_send()
        second_rows(other).wait_send()

    each_peer(wait_scatter)
    total = s.part_in[0]
    for other in range(1, n_edge):
        total = total + s.part_in[other]
    s.sys_in[my_group] = total

    def line_copy(other, index):
        return pltpu.make_async_remote_copy(
            src_ref=s.sys_in.at[index],
            dst_ref=s.sys_in.at[index],
            send_sem=s.send_sem.at[KIND_SYS, other],
            recv_sem=s.recv_sem.at[KIND_SYS, index],
            device_id={"edge": 2 * other + core},
            device_id_type=MESH,
        )

    each_group(lambda other: line_copy(other, my_group).start())

    def wait_line(other):
        line_copy(other, other).wait_recv()
        line_copy(other, my_group).wait_send()

    each_group(wait_line)
    total = s.sys_in[0]
    for other in range(1, n_sys):
        total = total + s.sys_in[other]
    s.summed[me] = total
    mine = s.summed.at[me]
    each_peer(lambda other: remote(mine, mine, KIND_GATHER, other).start())

    def wait_gather(other):
        landed(s.summed.at[other], KIND_GATHER, other)
        remote(mine, mine, KIND_GATHER, other).wait_send()

    each_peer(wait_gather)
    first_total = s.grad_first.shape[0]
    for other in range(n_edge):
        total_ref[other * first_each : (other + 1) * first_each, :] = s.summed[other, 0:first_each, :]
        low_row = first_total + other * second_each
        total_ref[low_row : low_row + second_each, :] = s.summed[other, first_each:, :]


class Scratch:
    pass


def step_scratch(n_edge, n_sys, channels, atoms, first_rows, second_rows):
    tiles = TILES
    lanes = n_edge // tiles * atoms
    wide = N_COMP * channels
    vm = lambda *shape: pltpu.VMEM(shape, F32)
    vb = lambda *shape: pltpu.VMEM(shape, BF)
    vi = lambda *shape: pltpu.VMEM(shape, jnp.int32)
    return {
        "send_sem": pltpu.SemaphoreType.DMA((KINDS, n_edge)),
        "recv_sem": pltpu.SemaphoreType.DMA((KINDS, n_edge)),
        "start_out": vm(8, atoms),
        "start_float": vm(n_edge, 8, atoms),
        "lists_own": vi(n_edge, 16, atoms),
        "own_kind": vb(16, atoms),
        "lists_out": vi(n_edge, 16, atoms),
        "lists_in": vi(n_edge, 16, atoms),
        "w_in_left": vb(2, channels, 32),
        "w_in_back": vb(2, 16, 2 * channels),
        "w_out_left": vb(2, 3 * channels, 3 * channels),
        "w_out_back": vb(2, 2 * channels, 3 * channels),
        "mf_left": vb(3 * channels, 3 * channels),
        "mf_back": vb(channels, 9 * channels),
        "ms_left": vb(3, channels, 3 * channels),
        "ms_back": vb(3, channels, 3 * channels),
        "emb_left": vb(channels, 48),
        "readout_col": vm(channels, atoms),
        "start_scalar": vm(channels, atoms),
        "place": vm(3, n_edge, atoms),
        "speed": vm(3, n_edge, atoms),
        "energy_row": vm(1, atoms),
        "energy": vm(EVALS, n_edge, atoms),
        "start_kinetic": vm(n_edge, atoms),
        "drift_grad": vm(n_edge, atoms),
        "place_bar": vm(3, n_edge, atoms),
        "speed_bar": vm(3, n_edge, atoms),
        "move": vm(3, n_edge, atoms),
        "own_hot": vb(EVALS, 2 * tiles, 2 * atoms, lanes),
        "far_hot": vb(EVALS, 2 * tiles, atoms, lanes),
        "kind_hot": vb(EVALS, tiles, 16, lanes),
        "kind_value": vm(EVALS, tiles, channels, lanes),
        "rows": vm(n_edge, 8, atoms),
        "pieces": vb(n_edge, 32, atoms),
        "row_own": vm(8, atoms),
        "edge_rows": vm(2 * tiles, 8, lanes),
        "geo": vm(EVALS, 2 * tiles, 40, lanes),
        "geo_bar": vm(EVALS, 2 * tiles, 24, lanes),
        "geo_dot": vm(2 * tiles, 24, lanes),
        "hidden": vm(2, EVALS, tiles, channels, lanes),
        "hidden_bar": vm(2, EVALS, tiles, channels, lanes),
        "hidden_dot": vm(2, tiles, channels, lanes),
        "radial": vm(2, EVALS, tiles, 3 * channels, lanes),
        "radial_dot": vm(2, tiles, 3 * channels, lanes),
        "m_high": vb(tiles, wide, lanes),
        "m_low": vb(tiles, wide, lanes),
        "r_pair": vb(2, tiles, 6 * channels, lanes),
        "h_pair": vb(2, tiles, 6 * channels, lanes),
        "out_pair": vb(2, tiles, 2 * channels, lanes),
        "dot_pair": vb(2, tiles, 2 * channels, lanes),
        "bar_pair": vb(2, tiles, 2 * channels, lanes),
        "hat_pair": vb(2, tiles, 2 * channels, lanes),
        "scalar_hat": vm(channels, atoms),
        "raw_hat": vm(8 * channels, atoms),
        "last_hat": vm(channels, atoms),
        "last_bar": vm(channels, atoms),
        "agg_two_dot": vm(channels, atoms),
        "loss_row": vm(1, channels),
        "v_high": vb(tiles, channels, lanes),
        "v_low": vb(tiles, channels, lanes),
        "a_pair": vb(wide, 2 * atoms),
        "sum_wide": vm(wide, atoms),
        "first_cot": vm(EVALS, tiles, wide, lanes),
        "feat": vm(EVALS, tiles, wide, lanes),
        "feat_dot": vm(tiles, wide, lanes),
        "along": vm(EVALS, tiles, 2 * channels, lanes),
        "along_dot": vm(tiles, 2 * channels, lanes),
        "msg_cot": vm(EVALS, tiles, channels, lanes),
        "msg_hat": vm(tiles, channels, lanes),
        "agg": vm(EVALS, wide, atoms),
        "agg_dot": vm(wide, atoms),
        "mixed": vm(EVALS, 3 * channels, atoms),
        "mixed_dot": vm(3 * channels, atoms),
        "mixed_bar": vm(EVALS, 3 * channels, atoms),
        "mixed_hat": vm(3 * channels, atoms),
        "raw": vm(EVALS, 8 * channels, atoms),
        "raw_dot": vm(8 * channels, atoms),
        "raw_bar": vm(EVALS, 8 * channels, atoms),
        "scalar": vm(EVALS, channels, atoms),
        "scalar_dot": vm(channels, atoms),
        "feat_bar": vm(EVALS, wide, atoms),
        "agg_two": vm(EVALS, channels, atoms),
        "last": vm(EVALS, channels, atoms),
        "msg_out": vm(n_edge, channels, atoms),
        "msg_in": vm(n_edge, channels, atoms),
        "cot_all": vm(n_edge, channels, atoms),
        "force_out": vm(4, n_edge, atoms),
        "force_in": vm(n_edge, 4, n_edge, atoms),
        "place_out": vm(3, n_edge, atoms),
        "place_in": vm(n_edge, 3, n_edge, atoms),
        "grad_emb": vm(16, channels),
        "grad_in": vm(2, 2 * NB, 2 * channels),
        "grad_out": vm(2, 6 * channels, 2 * channels),
        "grad_mf": vm(3 * channels, channels),
        "grad_ms": vm(3, channels, channels),
        "grad_ro": vm(channels, atoms),
        "grad_first": vm(first_rows, 2 * channels),
        "grad_second": vm(second_rows, 2 * channels),
        "part_in": vm(n_edge, (first_rows + second_rows) // n_edge, 2 * channels),
        "sys_in": vm(n_sys, (first_rows + second_rows) // n_edge, 2 * channels),
        "summed": vm(n_edge, (first_rows + second_rows) // n_edge, 2 * channels),
    }


def gradient_rows(n_edge, channels):
    unit = 8 * n_edge
    return -(-(5 * channels) // unit) * unit, -(-(3 * channels // 2 + 16) // unit) * unit


def whole_step(positions, velocities, species, senders, receivers, edge_mask, params):
    n_edge, n_sys = lax.axis_size("edge"), lax.axis_size("sys")
    atoms = positions.shape[1]
    channels = params[0].shape[1]
    first_rows, second_rows = gradient_rows(n_edge, channels)
    shapes = step_scratch(n_edge, n_sys, channels, atoms, first_rows, second_rows)
    names = tuple(shapes)

    def kernel(*refs):
        scratch = Scratch()
        for name, ref in zip(names, refs[13:]):
            setattr(scratch, name, ref)
        step_kernel(n_edge, n_sys, *refs[:13], scratch)

    embedding, radial_in, radial_out, mix_first, mix_square, readout = params
    operands = (
        positions,
        velocities,
        species,
        senders,
        receivers,
        edge_mask,
        embedding,
        radial_in,
        radial_out,
        mix_first,
        mix_square,
        readout,
    )
    return pl.pallas_call(
        kernel,
        out_shape=jax.ShapeDtypeStruct((first_rows + second_rows, 2 * channels), F32),
        in_specs=[pl.BlockSpec(memory_space=pltpu.VMEM)] * len(operands),
        out_specs=pl.BlockSpec(memory_space=pltpu.VMEM),
        scratch_shapes=list(shapes.values()),
        compiler_params=pltpu.CompilerParams(
            collective_id=0, has_side_effects=True, vmem_limit_bytes=60 * 1024 * 1024
        ),
    )(*operands)


def to_column(row):
    count = row.shape[1]
    square = jnp.broadcast_to(row, (count, count))
    same = lax.broadcasted_iota(jnp.int32, (count, count), 0) == lax.broadcasted_iota(
        jnp.int32, (count, count), 1
    )
    return jnp.sum(jnp.where(same, square, 0.0), axis=1, keepdims=True)


def to_row(column):
    count = column.shape[0]
    square = jnp.broadcast_to(column, (count, count))
    same = lax.broadcasted_iota(jnp.int32, (count, count), 0) == lax.broadcasted_iota(
        jnp.int32, (count, count), 1
    )
    return jnp.sum(jnp.where(same, square, 0.0), axis=0, keepdims=True)


def total_mean(value):
    return jnp.sum(
        jnp.sum(value, axis=1, keepdims=True), axis=0, keepdims=True
    ) / float(value.shape[0] * value.shape[1])


def factored_rows(gradient, weight, row_state, col_state):
    decay_rate = 1.0 - STEP_NUM ** (-0.8)
    squares = gradient * gradient + EPS_SQUARE
    size_m, size_n = gradient.shape
    row_mean = jnp.sum(squares, axis=1, keepdims=True) / float(size_n)
    col_mean = jnp.sum(squares, axis=0, keepdims=True) / float(size_m)
    row_new = decay_rate * to_column(row_state) + (1.0 - decay_rate) * row_mean
    col_new = decay_rate * col_state + (1.0 - decay_rate) * col_mean
    second = row_new * col_new / total_mean(row_new)
    weight_rms = jnp.sqrt(total_mean(weight * weight) + 1e-06)
    weight_new = weight - RELATIVE * weight_rms * gradient * lax.rsqrt(second)
    return (gradient, to_row(row_new), col_new, weight_new, weight_new.astype(jnp.bfloat16))


def update_kernel(total_ref, *refs):
    weights, states, outs = refs[0:6], refs[6:17], refs[17:]
    kinds, channels = weights[0].shape

    rows = 3 * channels
    late = gradient_rows(lax.axis_size("edge"), channels)[0]
    small = rows + channels
    first_layer = jnp.concatenate(
        [
            total_ref[late : late + rows // 2, :channels],
            total_ref[late : late + rows // 2, channels:],
        ],
        axis=0,
    )
    below = late + rows // 2
    gradients = (
        [total_ref[below : below + kinds, channels:]],
        [total_ref[below : below + 8, :channels], total_ref[small + 8 : small + 16, channels:]],
        [first_layer.T, total_ref[0:rows, :channels].T],
        [total_ref[0:rows, channels:].T],
        [
            total_ref[rows:small, :channels],
            total_ref[rows:small, channels:],
            total_ref[small : small + channels, :channels],
        ],
    )
    outs[0][...] = total_ref[below + 8 : below + 9, 0:1]
    for which, parts in enumerate(gradients):
        weight, rows, cols = weights[which], states[2 * which], states[2 * which + 1]
        results = outs[1 + 5 * which : 6 + 5 * which]
        stacked = len(weight.shape) == 3
        for number, gradient in enumerate(parts):
            if stacked:
                found = factored_rows(
                    gradient,
                    weight[number],
                    rows[number : number + 1, :],
                    cols[number : number + 1, :],
                )
                results[0][number] = found[0]
                results[1][number : number + 1, :] = found[1]
                results[2][number : number + 1, :] = found[2]
                results[3][number] = found[3]
                results[4][number] = found[4]
            else:
                size_m, size_n = weight.shape
                found = factored_rows(
                    gradient,
                    weight[...],
                    rows[...].reshape(1, size_m),
                    cols[...].reshape(1, size_n),
                )
                results[0][...] = found[0]
                results[1][...] = found[1].reshape(size_m)
                results[2][...] = found[2].reshape(size_n)
                results[3][...] = found[3]
                results[4][...] = found[4]
    gradient = total_ref[small : small + 1, channels:]
    decay_rate = 1.0 - STEP_NUM ** (-0.8)
    weight = weights[5][...].reshape(1, channels)
    second_new = decay_rate * states[10][...].reshape(1, channels) + (1.0 - decay_rate) * (
        gradient * gradient + EPS_SQUARE
    )
    weight_rms = jnp.sqrt(total_mean(weight * weight) + 1e-06)
    weight_new = weight - RELATIVE * weight_rms * gradient * lax.rsqrt(second_new)
    outs[26][...] = gradient.reshape(channels)
    outs[27][...] = second_new.reshape(channels)
    outs[28][...] = weight_new.reshape(channels)
    outs[29][...] = weight_new.astype(jnp.bfloat16).reshape(channels)


def whole_update(total, params, states):
    shapes = [jax.ShapeDtypeStruct((1, 1), F32)]
    for which in range(5):
        weight, rows, cols = params[which], states[2 * which], states[2 * which + 1]
        for like in (weight, rows, cols, weight):
            shapes.append(jax.ShapeDtypeStruct(like.shape, F32))
        shapes.append(jax.ShapeDtypeStruct(weight.shape, jnp.bfloat16))
    for kind in (F32, F32, F32, jnp.bfloat16):
        shapes.append(jax.ShapeDtypeStruct(params[5].shape, kind))
    operands = (total, *params, *states)
    results = pl.pallas_call(
        update_kernel,
        out_shape=shapes,
        in_specs=[pl.BlockSpec(memory_space=pltpu.VMEM)] * len(operands),
        out_specs=[pl.BlockSpec(memory_space=pltpu.VMEM)] * len(shapes),
        compiler_params=pltpu.CompilerParams(vmem_limit_bytes=8 * 1024 * 1024),
    )(*operands)
    return (results[0].reshape(()), *results[1:])


def fits_kernel(senders, atom_count):
    n_edge = lax.axis_size("edge")
    slots = senders.shape[1] // n_edge
    whole = slots == atom_count and atom_count % 128 == 0
    return whole and n_edge == 2 * lax.axis_size("sys") and n_edge % TILES == 0


def on_device(
    positions,
    velocities,
    species,
    senders,
    receivers,
    edge_mask,
    embedding,
    radial_in,
    radial_out,
    mix_first,
    mix_square,
    readout,
    embedding_rows,
    embedding_cols,
    radial_in_rows,
    radial_in_cols,
    radial_out_rows,
    radial_out_cols,
    mix_first_rows,
    mix_first_cols,
    mix_square_rows,
    mix_square_cols,
    readout_second,
):
    params = (embedding, radial_in, radial_out, mix_first, mix_square, readout)
    atom_count = positions.shape[1]
    states = (
        embedding_rows,
        embedding_cols,
        radial_in_rows,
        radial_in_cols,
        radial_out_rows,
        radial_out_cols,
        mix_first_rows,
        mix_first_cols,
        mix_square_rows,
        mix_square_cols,
        readout_second,
    )
    if fits_kernel(senders, atom_count):
        total = whole_step(
            positions, velocities, species, senders, receivers, edge_mask, params
        )
        return whole_update(total, params, states)
    spec_hot = (species[None, :] == jnp.arange(embedding.shape[0])[:, None]).astype(jnp.float32)
    edge_lists = receivers[None]
    arrived = lax.all_to_all(edge_lists, "edge", split_axis=2, concat_axis=2, tiled=True)
    passes = [
        build(senders[number], arrived[:, number], edge_mask[number], atom_count, spec_hot)
        for number in range(EVALS)
    ]
    coords = positions
    moving = velocities
    energies, forces, stored = passes[0][0](coords, params)
    record = [stored]
    first_energy = energies
    for number in range(STEPS):
        half_speed = moving + 0.5 * STEP_DT * forces
        coords = coords + STEP_DT * half_speed
        energies, forces, stored = passes[number + 1][0](coords, params)
        record.append(stored)
        moving = half_speed + 0.5 * STEP_DT * forces
    local_sums = jnp.stack(
        [
            per_system(first_energy),
            per_system(energies),
            per_system(0.5 * jnp.sum(velocities * velocities, axis=0)),
            per_system(0.5 * jnp.sum(moving * moving, axis=0)),
        ]
    )
    totals = lax.psum(local_sums, "edge")
    drift = totals[1] + totals[3] - (totals[0] + totals[2])
    system_atoms = atom_count // SYS_LOC * lax.axis_size("edge")
    loss_local = jnp.sum(drift * drift) / system_atoms
    drift_grad = jnp.repeat(2.0 * drift / system_atoms, atom_count // SYS_LOC)
    speed_bar = drift_grad[None, :] * moving
    coord_bar = jnp.zeros_like(positions)
    force_next = jnp.zeros_like(positions)
    gradients = jax.tree.map(jnp.zeros_like, params)
    for number in reversed(range(STEPS)):
        later = number + 1
        force_bar = force_next + 0.5 * STEP_DT * speed_bar
        if later == STEPS:
            energy_bar = drift_grad
        else:
            energy_bar = jnp.zeros_like(drift_grad)
        coord_part, param_part = passes[later][1](record[later], params, energy_bar, force_bar)
        gradients = add_trees([gradients, param_part])
        coord_bar = coord_bar + coord_part
        half_bar = speed_bar + STEP_DT * coord_bar
        speed_bar = half_bar
        force_next = 0.5 * STEP_DT * half_bar
    _, param_part = passes[0][1](record[0], params, -drift_grad, force_next)
    gradients = add_trees([gradients, param_part])
    loss_term = loss_local * (lax.axis_index("edge") == 0).astype(jnp.float32)
    summed = lax.psum(
        (
            gradients[0],
            gradients[1],
            gradients[2],
            gradients[3],
            gradients[4],
            gradients[5],
            loss_term,
        ),
        ("sys", "edge"),
    )
    return update(summed, params, states)


def solution(mesh):
    placed = (
        P(None, ("sys", "edge")),
        P(None, ("sys", "edge")),
        P(("sys", "edge")),
        P(None, ("sys", "edge")),
        P(None, ("sys", "edge")),
        P(None, ("sys", "edge")),
        P(),
        P(),
        P(),
        P(),
        P(),
        P(),
        P(),
        P(),
        P(),
        P(),
        P(),
        P(),
        P(),
        P(),
        P(),
        P(),
        P(),
    )
    return jax.shard_map(
        on_device,
        mesh=mesh,
        in_specs=placed,
        out_specs=(
            P(),
            P(),
            P(),
            P(),
            P(),
            P(),
            P(),
            P(),
            P(),
            P(),
            P(),
            P(),
            P(),
            P(),
            P(),
            P(),
            P(),
            P(),
            P(),
            P(),
            P(),
            P(),
            P(),
            P(),
            P(),
            P(),
            P(),
            P(),
            P(),
            P(),
        ),
        check_vma=False,
    )
```

```python
from functools import reduce
import math

import jax
import jax.numpy as jnp
from jax import lax
from jax.experimental import pallas as pl
from jax.experimental.pallas import tpu as pltpu
from jax.sharding import PartitionSpec as P

NB = 8
SYS_LOC = 2
STEPS = 2
STEP_NUM = 10
EVALS = 3


PRECISE = lax.Precision.HIGHEST
SOFTEN = 0.25
CUTOFF = 5.0
INV_NEIGH = 0.2
STEP_DT = 0.5
RELATIVE = 0.3
EPS_SQUARE = 1e-30
ROOT3 = math.sqrt(3.0)
ROOT5 = math.sqrt(5.0)


def geometry(sender_pos, receiver_pos):
    offset_vec = sender_pos - receiver_pos
    radius = jnp.sqrt(jnp.sum(offset_vec * offset_vec, axis=0) + SOFTEN)
    direction = offset_vec / radius
    unit_x, unit_y, unit_z = (direction[0], direction[1], direction[2])
    first_harm = ROOT3 * direction
    second_harm = ROOT5 * jnp.stack(
        [
            ROOT3 * unit_x * unit_y,
            ROOT3 * unit_y * unit_z,
            0.5 * (3.0 * unit_z * unit_z - 1.0),
            ROOT3 * unit_x * unit_z,
            0.5 * ROOT3 * (unit_x * unit_x - unit_y * unit_y),
        ]
    )
    scaled = radius / CUTOFF
    envelope = 1.0 - 28.0 * scaled**6 + 48.0 * scaled**7 - 21.0 * scaled**8
    orders = jnp.arange(1, NB + 1).astype(jnp.float32)[:, None]
    bessel = (
        math.sqrt(2.0 / CUTOFF)
        * jnp.sin(orders * math.pi * scaled[None, :])
        / radius[None, :]
        * envelope[None, :]
    )
    return (first_harm, second_harm, bessel)


def radial(bessel, weight_in, weight_out):
    hidden = jax.nn.silu(jnp.einsum("nr,ne->re", weight_in, bessel, precision=PRECISE))
    return jnp.einsum("rk,re->ke", weight_out, hidden, precision=PRECISE)


def first_messages(
    first_harm, second_harm, bessel, sender_feat, edge_weight, weight_in, weight_out
):
    channels = sender_feat.shape[0]
    edge_weights = radial(bessel, weight_in, weight_out)
    scalar_part = (edge_weights[:channels] * sender_feat)[None]
    vector_part = (edge_weights[channels : 2 * channels] * sender_feat)[None] * first_harm[
        :, None, :
    ]
    tensor_part = (edge_weights[2 * channels :] * sender_feat)[None] * second_harm[:, None, :]
    return jnp.concatenate([scalar_part, vector_part, tensor_part], axis=0) * edge_weight


def node_first(summed, scalar_prev, mix_first, mix_square):
    gathered = summed * INV_NEIGH
    channels = scalar_prev.shape[0]
    mixed = jnp.einsum("cd,ca->da", mix_first, gathered[0], precision=PRECISE)
    vectors = jnp.einsum("mca,cd->mda", gathered[1:4], mix_square[0], precision=PRECISE)
    tensors = jnp.einsum("mca,cd->mda", gathered[4:9], mix_square[1], precision=PRECISE)
    scalars = scalar_prev + jax.nn.silu(mixed[:channels])
    vectors = jax.nn.sigmoid(mixed[channels : 2 * channels])[None] * vectors
    tensors = jax.nn.sigmoid(mixed[2 * channels :])[None] * tensors
    return jnp.concatenate([scalars[None], vectors, tensors], axis=0)


def second_messages(
    first_harm, second_harm, bessel, sender_feat, edge_weight, weight_in, weight_out
):
    channels = sender_feat.shape[1]
    edge_weights = radial(bessel, weight_in, weight_out)
    along_first = jnp.einsum("kce,ke->ce", sender_feat[1:4], first_harm, precision=PRECISE)
    along_second = jnp.einsum("kce,ke->ce", sender_feat[4:9], second_harm, precision=PRECISE)
    combined = (
        edge_weights[:channels] * sender_feat[0]
        + edge_weights[channels : 2 * channels] * along_first
        + edge_weights[2 * channels :] * along_second
    )
    return combined * edge_weight


def node_second(features, summed, mix_square, readout):
    scalars = features[0] + jax.nn.silu(
        jnp.einsum("cd,ca->da", mix_square[2], summed * INV_NEIGH, precision=PRECISE)
    )
    return jnp.einsum("c,ca->a", readout, scalars, precision=PRECISE)


def factored(gradient, weight, row_state, col_state):
    decay_rate = 1.0 - STEP_NUM ** (-0.8)
    squares = gradient * gradient + EPS_SQUARE
    row_new = decay_rate * row_state + (1.0 - decay_rate) * jnp.mean(squares, axis=-1)
    col_new = decay_rate * col_state + (1.0 - decay_rate) * jnp.mean(squares, axis=-2)
    second = (
        row_new[..., :, None]
        * col_new[..., None, :]
        / jnp.mean(row_new, axis=-1, keepdims=True)[..., None]
    )
    weight_rms = jnp.sqrt(jnp.mean(weight * weight, axis=(-2, -1), keepdims=True) + 1e-06)
    weight_new = weight - RELATIVE * weight_rms * gradient * lax.rsqrt(second)
    return (gradient, row_new, col_new, weight_new, weight_new.astype(jnp.bfloat16))


def unfactored(gradient, weight, second):
    decay_rate = 1.0 - STEP_NUM ** (-0.8)
    second_new = decay_rate * second + (1.0 - decay_rate) * (gradient * gradient + EPS_SQUARE)
    weight_rms = jnp.sqrt(jnp.mean(weight * weight) + 1e-06)
    weight_new = weight - RELATIVE * weight_rms * gradient * lax.rsqrt(second_new)
    return (gradient, second_new, weight_new, weight_new.astype(jnp.bfloat16))


def add_trees(trees):
    return reduce(lambda left, right: jax.tree.map(jnp.add, left, right), trees)


def per_system(values):
    return values.reshape(SYS_LOC, -1).sum(axis=1)


def build(send_row, arrived_lists, mask_row, atom_count, spec_hot):
    edge_weight = mask_row.astype(jnp.float32)
    arrived_row = arrived_lists[0]
    send_hot = (send_row[None, :] == jnp.arange(atom_count)[:, None]).astype(jnp.float32)
    inc_hot = (arrived_row[None, :] == jnp.arange(atom_count)[:, None]).astype(jnp.float32)

    def fetch_positions(coords):
        return lax.all_to_all(
            jnp.dot(coords, inc_hot, precision=PRECISE),
            "edge",
            split_axis=1,
            concat_axis=1,
            tiled=True,
        )

    def return_positions(cotangent):
        arrived = lax.all_to_all(cotangent, "edge", split_axis=1, concat_axis=1, tiled=True)
        return jnp.einsum("de,ae->da", arrived, inc_hot, precision=PRECISE)

    def collect(values):
        arrived = lax.all_to_all(values, "edge", split_axis=2, concat_axis=2, tiled=True)
        return jnp.einsum("mce,ae->mca", arrived, inc_hot, precision=PRECISE)

    def spread(values):
        per_slot = jnp.einsum("mca,ae->mce", values, inc_hot, precision=PRECISE)
        return lax.all_to_all(per_slot, "edge", split_axis=2, concat_axis=2, tiled=True)

    def scalar_start(params):
        return jnp.einsum("tc,ta->ca", params[0], spec_hot, precision=PRECISE)

    def give_back(aux_cot, recv_cot):
        return return_positions(aux_cot + recv_cot)

    def edge_first(coords, recv_pos, params):
        first_harm, second_harm, bessel = geometry(
            jnp.dot(coords, send_hot, precision=PRECISE), recv_pos
        )
        sender_feat = jnp.dot(scalar_start(params), send_hot, precision=PRECISE)
        return first_messages(
            first_harm, second_harm, bessel, sender_feat, edge_weight, params[1][0], params[2][0]
        )

    def collect_first(values):
        return collect(values)

    def spread_first(values):
        return spread(values)

    def node_one(summed, params):
        return node_first(summed, scalar_start(params), params[3], params[4])

    def edge_second(coords, recv_pos, features, params):
        first_harm, second_harm, bessel = geometry(
            jnp.dot(coords, send_hot, precision=PRECISE), recv_pos
        )
        sender_feat = jnp.einsum("mca,ae->mce", features, send_hot, precision=PRECISE)
        return second_messages(
            first_harm, second_harm, bessel, sender_feat, edge_weight, params[1][1], params[2][1]
        )[None]

    def node_two(features, summed, params):
        return node_second(features, summed[0], params[4], params[5])

    def back_node_two(features, summed, params):
        _, pullback = jax.vjp(
            lambda feature_in, summed_in: node_two(feature_in, summed_in, params), features, summed
        )
        return pullback(jnp.ones((atom_count,), jnp.float32))

    def back_edge_two(coords, recv_pos, features, params, cotangent):
        _, pullback = jax.vjp(
            lambda where_at, recv_at, feature_in: edge_second(
                where_at, recv_at, feature_in, params
            ),
            coords,
            recv_pos,
            features,
        )
        return pullback(cotangent)

    def back_node_one(summed, params, cotangent):
        _, pullback = jax.vjp(lambda summed_in: node_one(summed_in, params), summed)
        return pullback(cotangent)[0]

    def back_edge_one(coords, aux_pos, params, cotangent):
        _, pullback = jax.vjp(
            lambda where_at, aux_at: edge_first(where_at, aux_at, params), coords, aux_pos
        )
        return pullback(cotangent)

    def evaluate(coords, params):
        recv_pos = fetch_positions(coords)
        summed_one = collect_first(edge_first(coords, recv_pos, params))
        features = node_one(summed_one, params)
        summed_two = collect(edge_second(coords, recv_pos, features, params))
        energies = node_two(features, summed_two, params)
        feature_node, summed_two_bar = back_node_two(features, summed_two, params)
        second_bar = spread(summed_two_bar)
        coord_second, recv_second, feature_edge = back_edge_two(
            coords, recv_pos, features, params, second_bar
        )
        feature_bar = feature_node + feature_edge
        first_bar = spread_first(back_node_one(summed_one, params, feature_bar))
        coord_first, aux_first = back_edge_one(coords, recv_pos, params, first_bar)
        forces = -(coord_first + coord_second + give_back(aux_first, recv_second))
        stored = (
            coords,
            recv_pos,
            recv_pos,
            summed_one,
            features,
            summed_two,
            second_bar,
            feature_bar,
            first_bar,
        )
        return (energies, forces, stored)

    def reverse(stored, params, energy_bar, force_bar):
        (
            coords,
            recv_pos,
            aux_pos,
            summed_one,
            features,
            summed_two,
            second_bar,
            feature_bar,
            first_bar,
        ) = stored
        coord_cot = -force_bar
        recv_cot = fetch_positions(coord_cot)
        _, pullback = jax.vjp(back_edge_one, coords, aux_pos, params, first_bar)
        coord_one, aux_one, param_one, first_cot = pullback((coord_cot, recv_cot))
        _, pullback = jax.vjp(back_node_one, summed_one, params, feature_bar)
        summed_one_a, param_two, feature_cot = pullback(collect_first(first_cot))
        _, pullback = jax.vjp(back_edge_two, coords, recv_pos, features, params, second_bar)
        coord_two, recv_two, feature_one, param_three, second_cot = pullback(
            (coord_cot, recv_cot, feature_cot)
        )
        _, pullback = jax.vjp(back_node_two, features, summed_two, params)
        feature_two, summed_two_a, param_four = pullback((feature_cot, collect(second_cot)))
        _, pullback = jax.vjp(node_two, features, summed_two, params)
        feature_three, summed_two_b, param_five = pullback(energy_bar)
        _, pullback = jax.vjp(edge_second, coords, recv_pos, features, params)
        coord_three, recv_three, feature_four, param_six = pullback(
            spread(summed_two_a + summed_two_b)
        )
        _, pullback = jax.vjp(node_one, summed_one, params)
        summed_one_b, param_seven = pullback(
            feature_one + feature_two + feature_three + feature_four
        )
        _, pullback = jax.vjp(edge_first, coords, aux_pos, params)
        coord_four, aux_four, param_eight = pullback(spread_first(summed_one_a + summed_one_b))
        coord_total = (
            coord_one
            + coord_two
            + coord_three
            + coord_four
            + give_back(aux_one + aux_four, recv_two + recv_three)
        )
        param_total = add_trees(
            [
                param_one,
                param_two,
                param_three,
                param_four,
                param_five,
                param_six,
                param_seven,
                param_eight,
            ]
        )
        return (coord_total, param_total)

    return (evaluate, reverse)


def update(summed, params, states):
    embedding, radial_in, radial_out, mix_first, mix_square, readout = params
    (
        embedding_rows,
        embedding_cols,
        radial_in_rows,
        radial_in_cols,
        radial_out_rows,
        radial_out_cols,
        mix_first_rows,
        mix_first_cols,
        mix_square_rows,
        mix_square_cols,
        readout_second,
    ) = states
    emb = factored(summed[0], embedding, embedding_rows, embedding_cols)
    rin = factored(summed[1], radial_in, radial_in_rows, radial_in_cols)
    rout = factored(summed[2], radial_out, radial_out_rows, radial_out_cols)
    mfirst = factored(summed[3], mix_first, mix_first_rows, mix_first_cols)
    msquare = factored(summed[4], mix_square, mix_square_rows, mix_square_cols)
    rdout = unfactored(summed[5], readout, readout_second)
    return (
        summed[6],
        emb[0],
        emb[1],
        emb[2],
        emb[3],
        emb[4],
        rin[0],
        rin[1],
        rin[2],
        rin[3],
        rin[4],
        rout[0],
        rout[1],
        rout[2],
        rout[3],
        rout[4],
        mfirst[0],
        mfirst[1],
        mfirst[2],
        mfirst[3],
        mfirst[4],
        msquare[0],
        msquare[1],
        msquare[2],
        msquare[3],
        msquare[4],
        rdout[0],
        rdout[1],
        rdout[2],
        rdout[3],
    )


F32 = jnp.float32
BF = jnp.bfloat16
MESH = pl.DeviceIdType.MESH
ROOT15 = math.sqrt(15.0)
TILES = 2
CHUNK = 16
LANES_AT_ONCE = 256
N_COMP = 9
PATHS = ((0, 3, 0), (3, 8, 1))
KIND_INIT, KIND_EDGES, KIND_MSG, KIND_COT, KIND_FORCE = 0, 1, 2, 3, 4
KIND_TMSG, KIND_TCOT, KIND_TFORCE, KIND_SCATTER, KIND_GATHER, KIND_SYS = 5, 6, 7, 8, 9, 10
KIND_OWN, KIND_SCATTER_LATE = 11, 12
KINDS = 13


def dot_nn(left, right):
    return lax.dot_general(left, right, (((1,), (0,)), ((), ())), preferred_element_type=F32)


def dot_nt(left, right):
    return lax.dot_general(left, right, (((1,), (1,)), ((), ())), preferred_element_type=F32)


def two_parts(value):
    high = value.astype(BF)
    return high, (value - high.astype(F32)).astype(BF)


def two_parts_f32(value):
    high = value.astype(BF).astype(F32)
    return high, value - high


def three_parts_f32(value):
    high = value.astype(BF).astype(F32)
    rest = value - high
    middle = rest.astype(BF).astype(F32)
    return high, middle, rest - middle


def left_three(weight):
    high, low = two_parts_f32(weight)
    return jnp.concatenate([high, high, low], axis=1).astype(BF)


def right_three(value):
    high, low = two_parts(value)
    return jnp.concatenate([high, low, high], axis=0)


def right_three_small(value):
    high, low = two_parts_f32(value)
    return jnp.concatenate([high, low, high, jnp.zeros_like(high)], axis=0).astype(BF)


def stack_three(value):
    high, middle, low = three_parts_f32(value)
    return jnp.concatenate([high, middle, low, jnp.zeros_like(high)], axis=0).astype(BF)


def join_three(value):
    return value[0:8] + value[8:16] + value[16:24]


def outer_three(left, right):
    left_high, left_low = two_parts(left)
    right_high, right_low = two_parts(right)
    return (
        dot_nt(left_high, right_high)
        + dot_nt(left_low, right_high)
        + dot_nt(left_high, right_low)
    )


def logistic(value):
    return 1.0 / (1.0 + jnp.exp(jnp.minimum(-value, 80.0)))


def silu_slope(value, gate):
    return gate * (1.0 + value * (1.0 - gate))


def silu_bend(value, gate):
    return gate * (1.0 - gate) * (2.0 + value * (1.0 - 2.0 * gate))


def sin_cos_pi(turns):
    whole = jnp.floor(turns + 0.5)
    part = turns - whole
    sign = 1.0 - 2.0 * (whole - 2.0 * jnp.floor(0.5 * whole))
    square = part * part
    sine = 0.0
    for order in range(15, 0, -2):
        sine = sine * square + (-1.0) ** (order // 2) * math.pi**order / math.factorial(order)
    cosine = 0.0
    for order in range(16, -1, -2):
        cosine = cosine * square + (-1.0) ** (order // 2) * math.pi**order / math.factorial(order)
    return sign * (part * sine), sign * cosine


def sin_cos_multiples(sine, cosine):
    sines, cosines = [None, sine], [None, cosine]
    for order in range(2, 9):
        half, rest = order // 2, order - order // 2
        sines.append(sines[half] * cosines[rest] + cosines[half] * sines[rest])
        cosines.append(cosines[half] * cosines[rest] - sines[half] * sines[rest])
    return sines[1:], cosines[1:]


def second_slope(one, two, three, given):
    return (
        ROOT15 * (two * given[0] + three * given[3] + one * given[4]),
        ROOT15 * (one * given[0] + three * given[1] - two * given[4]),
        ROOT15 * (two * given[1] + one * given[3]) + 3.0 * ROOT5 * three * given[2],
    )


def rows_of(value, first, count):
    return [value[first + number : first + number + 1] for number in range(count)]


def step_kernel(
    n_edge,
    n_sys,
    pos_ref,
    vel_ref,
    spec_ref,
    send_ref,
    recv_ref,
    mask_ref,
    emb_ref,
    rin_ref,
    rout_ref,
    mfirst_ref,
    msquare_ref,
    readout_ref,
    total_ref,
    scratch,
):
    s = scratch
    channels = emb_ref.shape[1]
    wide = N_COMP * channels
    atoms = pos_ref.shape[1]
    tiles = TILES
    group = n_edge // tiles
    lanes = group * atoms
    chunks = channels // CHUNK
    held_group = lax.axis_index("sys")
    held_part = lax.axis_index("edge")
    my_group = lax.div(held_part, 2)
    core = lax.rem(held_part, 2)
    me = 2 * held_group + core
    half = lax.div(me, group)
    half_atoms = atoms // SYS_LOC

    def peer(distance):
        return jnp.bitwise_xor(me, distance)

    def place_of(which_group, part):
        return {"sys": lax.div(part, 2), "edge": 2 * which_group + lax.rem(part, 2)}

    def remote(source, target, kind, other):
        return pltpu.make_async_remote_copy(
            src_ref=source,
            dst_ref=target,
            send_sem=s.send_sem.at[kind, other],
            recv_sem=s.recv_sem.at[kind, me],
            device_id=place_of(my_group, other),
            device_id_type=MESH,
        )

    def landed(target, kind, other):
        pltpu.make_async_remote_copy(
            src_ref=target,
            dst_ref=target,
            send_sem=s.send_sem.at[kind, other],
            recv_sem=s.recv_sem.at[kind, other],
            device_id=place_of(my_group, other),
            device_id_type=MESH,
        ).wait_recv()

    def each_peer(action):
        def body(distance, carry):
            action(peer(distance))
            return carry

        lax.fori_loop(1, n_edge, body, 0)

    def each_tile(action):
        for index in range(tiles):
            action(index)

    def loop(count, action, unroll=False):
        def body(index, carry):
            action(index)
            return carry

        lax.fori_loop(0, count, body, 0, unroll=unroll)

    def chunk_at(base, index):
        return slice(base + index * CHUNK, base + (index + 1) * CHUNK)

    barrier = pltpu.get_barrier_semaphore()

    def greet(device):
        pl.semaphore_signal(barrier, inc=1, device_id=device, device_id_type=MESH)

    stays = held_group == my_group

    def each_given(action):
        def body(part, carry):
            @pl.when(jnp.logical_not(jnp.logical_and(stays, part == held_part)))
            def _():
                action(part)

            return carry

        lax.fori_loop(0, n_edge, body, 0)

    def each_group(action):
        def body(distance, carry):
            action(lax.rem(my_group + distance, n_sys))
            return carry

        lax.fori_loop(1, n_sys, body, 0)

    each_given(lambda part: greet({"sys": my_group, "edge": part}))
    each_peer(lambda other: greet(place_of(my_group, other)))
    each_group(lambda other: greet({"edge": 2 * other + core}))

    s.start_out[...] = jnp.concatenate([pos_ref[...], vel_ref[...], pos_ref[0:2]], axis=0)
    species_rows = jnp.broadcast_to(spec_ref[...].reshape(1, atoms), (16 - 3 * EVALS, atoms))
    for other in range(n_edge):
        at = slice(other * atoms, (other + 1) * atoms)
        for part, ref in enumerate((send_ref, recv_ref, mask_ref)):
            s.lists_out[other, part * EVALS : (part + 1) * EVALS, :] = ref[:, at]
        s.lists_out[other, 3 * EVALS :, :] = species_rows

    pl.semaphore_wait(barrier, 2 * n_edge - 1 + n_sys - 1 - jnp.where(stays, 1, 0))

    def given(source, target, kind, part):
        return pltpu.make_async_remote_copy(
            src_ref=source,
            dst_ref=target,
            send_sem=s.send_sem.at[kind, part],
            recv_sem=s.recv_sem.at[kind, held_part],
            device_id=place_of(held_group, part),
            device_id_type=MESH,
        )

    def taken(target, kind, part):
        pltpu.make_async_remote_copy(
            src_ref=target,
            dst_ref=target,
            send_sem=s.send_sem.at[kind, part],
            recv_sem=s.recv_sem.at[kind, part],
            device_id={"sys": my_group, "edge": part},
            device_id_type=MESH,
        ).wait_recv()

    def give_atoms(part):
        return given(s.start_out, s.start_float.at[held_part], KIND_INIT, part)

    def give_slots(part):
        return given(s.lists_out.at[part], s.lists_in.at[held_part], KIND_EDGES, part)

    def give_lists():
        return given(s.lists_out, s.lists_own, KIND_OWN, held_part)

    def start_first(part):
        give_atoms(part).start()
        give_slots(part).start()

    each_given(start_first)

    @pl.when(jnp.logical_not(stays))
    def _():
        give_lists().start()

    @pl.when(stays)
    def _():
        s.start_float[me] = s.start_out[...]
        s.lists_in[me] = s.lists_out[me]
        s.lists_own[...] = s.lists_out[...]

    for layer in range(2):
        w_in = rin_ref[layer]
        high, low = two_parts_f32(w_in)
        zero = jnp.zeros_like(high)
        s.w_in_left[layer] = jnp.concatenate([high, high, low, zero], axis=0).T.astype(BF)
        s.w_in_back[layer] = jnp.concatenate(
            [
                jnp.concatenate([high, high], axis=1),
                jnp.concatenate([low, zero], axis=1),
            ],
            axis=0,
        ).astype(BF)
        w_out = rout_ref[layer]
        s.w_out_left[layer] = left_three(w_out.T)
        s.w_out_back[layer] = jnp.concatenate(two_parts_f32(w_out), axis=0).astype(BF)
    s.mf_left[...] = left_three(mfirst_ref[...].T)
    s.mf_back[...] = left_three(mfirst_ref[...])
    for number in range(3):
        s.ms_left[number] = left_three(msquare_ref[number].T)
        s.ms_back[number] = left_three(msquare_ref[number])
    emb_pad = jnp.concatenate(
        [emb_ref[...], jnp.zeros((16 - emb_ref.shape[0], channels), F32)], axis=0
    )
    s.emb_left[...] = jnp.concatenate(list(three_parts_f32(emb_pad)), axis=0).T.astype(BF)
    s.readout_col[...] = jnp.broadcast_to(
        readout_ref[...].reshape(1, channels), (atoms, channels)
    ).T
    for ref in (
        s.grad_emb,
        s.grad_in,
        s.grad_out,
        s.grad_mf,
        s.grad_ms,
        s.grad_ro,
        s.grad_second,
        s.grad_first,
    ):
        ref[...] = jnp.zeros_like(ref)

    def first_landed(part):
        taken(s.start_float.at[part], KIND_INIT, part)
        taken(s.lists_in.at[part], KIND_EDGES, part)

    each_given(first_landed)

    @pl.when(jnp.logical_not(stays))
    def _():
        taken(s.lists_own, KIND_OWN, me)

    def first_sent(part):
        give_atoms(part).wait_send()
        give_slots(part).wait_send()

    each_given(first_sent)

    @pl.when(jnp.logical_not(stays))
    def _():
        give_lists().wait_send()

    def species_values(hot):
        return dot_nn(s.emb_left[...], jnp.concatenate([hot, hot, hot], axis=0))

    own_species = s.lists_in[me, 3 * EVALS : 3 * EVALS + 1, :]
    own_species = lax.broadcasted_iota(jnp.int32, (16, atoms), 0) == own_species
    s.own_kind[...] = own_species.astype(F32).astype(BF)
    s.start_scalar[...] = species_values(s.own_kind[...])
    s.rows[...] = jnp.zeros_like(s.rows)
    for axis in range(3):
        s.place[axis] = s.start_float[:, axis, :]
        s.speed[axis] = s.start_float[:, 3 + axis, :]

    def one_hots(number):
        atom_row = lax.broadcasted_iota(jnp.int32, (atoms, atoms), 0)

        def hot(row):
            return (atom_row == row).astype(F32).astype(BF)

        def put_own(tile, at, value):
            s.own_hot[number, tile, 0:atoms, at] = value
            s.own_hot[number, tile, atoms:, at] = value

        def body(index):
            for part in range(group):
                other = index * group + part
                at = pl.ds(part * atoms, atoms)
                out_list = s.lists_own.at[other]
                in_list = s.lists_in.at[other]
                sender = out_list[pl.ds(number, 1), :]
                receiver = out_list[pl.ds(EVALS + number, 1), :]
                mask = out_list[pl.ds(2 * EVALS + number, 1), :]
                put_own(index, at, hot(sender))
                s.far_hot[number, index, :, at] = hot(jnp.where(mask == 0, -1, receiver))
                sender = in_list[pl.ds(number, 1), :]
                receiver = in_list[pl.ds(EVALS + number, 1), :]
                mask = in_list[pl.ds(2 * EVALS + number, 1), :]
                sender_hot = hot(sender)
                put_own(tiles + index, at, hot(jnp.where(mask == 0, -1, receiver)))
                s.far_hot[number, tiles + index, :, at] = sender_hot
                species = in_list[pl.ds(3 * EVALS, 1), :]
                kinds = lax.broadcasted_iota(jnp.int32, (16, atoms), 0)
                species_hot = (kinds == species).astype(F32).astype(BF)
                s.kind_hot[number, index, :, at] = dot_nn(species_hot, sender_hot).astype(BF)
            s.kind_value[number, index] = species_values(s.kind_hot[number, index])

        each_tile(body)

    def table(rows):
        for axis in range(3):
            s.rows[:, axis, :] = rows[axis]
        for other in range(n_edge):
            s.pieces[other] = stack_three(s.rows[other])

    def edge_difference(number, index):
        sign = jnp.where(index < tiles, 1.0, -1.0)
        own = dot_nn(s.pieces[me], s.own_hot[number, index, 0:atoms, :])
        first = lax.rem(index, tiles) * group
        far = [
            dot_nn(
                s.pieces[first + part],
                s.far_hot[number, index, :, part * atoms : (part + 1) * atoms],
            )
            for part in range(group)
        ]
        return sign * join_three(own - jnp.concatenate(far, axis=1))

    def scatter_rows(number, target):
        parts = [stack_three(s.edge_rows[index]) for index in range(2 * tiles)]
        own = 0.0
        for index in range(2 * tiles):
            found = dot_nt(parts[index], s.own_hot[number, index, 0:atoms, :])
            own = own + found if index < tiles else own - found
        s.row_own[...] = join_three(own)
        for other in range(n_edge):
            index, part = other // group, other % group
            at = slice(part * atoms, (part + 1) * atoms)
            total = join_three(
                dot_nt(parts[tiles + index][:, at], s.far_hot[number, tiles + index, :, at])
                - dot_nt(parts[index][:, at], s.far_hot[number, index, :, at])
            )
            for axis in range(3):
                target[axis, other : other + 1, :] = total[axis : axis + 1]
        for axis in range(3):
            target[axis, pl.ds(me, 1), :] += s.row_own[axis : axis + 1, :]

    def geometry(number, index):
        offset = edge_difference(number, index)
        geo = s.geo.at[number, index]
        radius = jnp.sqrt(jnp.sum(offset * offset, axis=0, keepdims=True) + SOFTEN)
        inverse = 1.0 / radius
        unit = offset * inverse
        one, two, three = rows_of(unit, 0, 3)
        geo[0:3, :] = ROOT3 * unit[0:3]
        geo[3:4, :] = ROOT15 * one * two
        geo[4:5, :] = ROOT15 * two * three
        geo[5:6, :] = 0.5 * ROOT5 * (3.0 * three * three - 1.0)
        geo[6:7, :] = ROOT15 * one * three
        geo[7:8, :] = 0.5 * ROOT15 * (one * one - two * two)
        t = radius * (1.0 / CUTOFF)
        sines, cosines = sin_cos_multiples(*sin_cos_pi(t))
        sines = jnp.concatenate(sines, axis=0)
        cosines = jnp.concatenate(cosines, axis=0)
        t2 = t * t
        t4 = t2 * t2
        amount = math.sqrt(2.0 / CUTOFF) * inverse
        env = 1.0 - t4 * t2 * (28.0 - 48.0 * t + 21.0 * t2)
        env_one = -168.0 / CUTOFF * t4 * t * (1.0 - t) * (1.0 - t)
        env_two = -168.0 / CUTOFF**2 * t4 * (1.0 - t) * (5.0 - 7.0 * t)
        front = amount * env
        front_one = amount * (env_one - env * inverse)
        front_two = amount * (env_two - 2.0 * inverse * (env_one - env * inverse))
        waves = (lax.broadcasted_iota(jnp.int32, (NB, 1), 0) + 1).astype(F32) * (
            math.pi / CUTOFF
        )
        geo[8:16, :] = front * sines
        geo[16:24, :] = front_one * sines + front * waves * cosines
        geo[24:32, :] = (
            front_two * sines + 2.0 * front_one * waves * cosines - front * waves * waves * sines
        )
        geo[32:35, :] = unit[0:3]
        geo[35:36, :] = inverse

    def first_back(number, index):
        geo = s.geo.at[number, index]
        bars = s.geo_bar.at[number, index]
        ybar = rows_of(bars[0:8, :], 0, 8)
        slope = jnp.sum(bars[8:16, :] * geo[16:24, :], axis=0, keepdims=True)
        units = rows_of(geo[32:40, :], 0, 3)
        inverse = geo[35:36, :]
        extra = second_slope(*units, ybar[3:])
        back = [ROOT3 * ybar[axis] + extra[axis] for axis in range(3)]
        along = back[0] * units[0] + back[1] * units[1] + back[2] * units[2]
        rest = slope - along * inverse
        for axis in range(3):
            bars[16 + axis : 17 + axis, :] = back[axis]
            s.edge_rows[index, axis : axis + 1, :] = back[axis] * inverse + rest * units[axis]
        bars[19:20, :] = rest

    def geometry_tangent(number, index):
        move = edge_difference(number, index)
        geo = s.geo.at[number, index]
        out = s.geo_dot.at[index]
        inverse = geo[35:36, :]
        one, two, three = rows_of(geo[32:40, :], 0, 3)
        moves = rows_of(move, 0, 3)
        speed = one * moves[0] + two * moves[1] + three * moves[2]
        d_one, d_two, d_three = [
            (amount - unit * speed) * inverse for amount, unit in zip(moves, (one, two, three))
        ]
        out[0:1, :] = ROOT3 * d_one
        out[1:2, :] = ROOT3 * d_two
        out[2:3, :] = ROOT3 * d_three
        out[3:4, :] = ROOT15 * (d_one * two + one * d_two)
        out[4:5, :] = ROOT15 * (d_two * three + two * d_three)
        out[5:6, :] = 3.0 * ROOT5 * three * d_three
        out[6:7, :] = ROOT15 * (d_one * three + one * d_three)
        out[7:8, :] = ROOT15 * (one * d_one - two * d_two)
        out[8:16, :] = geo[16:24, :] * speed
        out[16:17, :] = d_one
        out[17:18, :] = d_two
        out[18:19, :] = d_three
        out[19:20, :] = speed
        out[20:23, :] = move[0:3]

    def second_back(number, index, hats):
        geo = s.geo.at[number, index]
        bars = s.geo_bar.at[number, index]
        dots = s.geo_dot.at[index]
        units = rows_of(geo[32:40, :], 0, 3)
        inverse = geo[35:36, :]
        turns = rows_of(dots[16:24, :], 0, 3)
        speed = dots[19:20, :]
        moves = rows_of(dots[16:24, :], 4, 3)
        back = rows_of(bars[16:24, :], 0, 3)
        rest = bars[19:20, :]
        yhat = rows_of(hats, 0, 8)
        ybar = rows_of(bars[0:8, :], 0, 8)
        extra = second_slope(*units, yhat[3:])
        more = second_slope(*turns, ybar[3:])
        radial_hat = jnp.sum(
            hats[8:16] * geo[16:24, :] + speed * (bars[8:16, :] * geo[24:32, :]),
            axis=0,
            keepdims=True,
        ) - inverse * (turns[0] * back[0] + turns[1] * back[1] + turns[2] * back[2])
        unit_hat = [
            ROOT3 * yhat[axis]
            + extra[axis]
            + more[axis]
            - speed * inverse * back[axis]
            + rest * moves[axis]
            for axis in range(3)
        ]
        along = unit_hat[0] * units[0] + unit_hat[1] * units[1] + unit_hat[2] * units[2]
        left = radial_hat - along * inverse
        for axis in range(3):
            s.edge_rows[index, axis : axis + 1, :] = unit_hat[axis] * inverse + left * units[axis]

    def radial_forward(layer, number, index, basis):
        before = dot_nn(s.w_in_left[layer], right_three_small(basis))
        s.hidden[layer, number, index] = before
        gate = logistic(before)
        s.radial[layer, number, index] = dot_nn(
            s.w_out_left[layer], right_three(before * gate)
        )

    def radial_tangent(layer, number, index, basis_dot):
        before = s.hidden[layer, number, index]
        before_dot = dot_nn(s.w_in_left[layer], right_three_small(basis_dot))
        s.hidden_dot[layer, index] = before_dot
        gate = logistic(before)
        s.radial_dot[layer, index] = dot_nn(
            s.w_out_left[layer], right_three(silu_slope(before, gate) * before_dot)
        )

    def rows_pair(value):
        return jnp.concatenate(two_parts(value), axis=0)

    def hidden_back(layer, pair):
        half_rows = 3 * channels
        left = s.w_out_back[layer]
        found = dot_nn(left, pair[0:half_rows])
        return found[0:channels] + found[channels:] + dot_nn(left[0:channels], pair[half_rows:])

    def basis_back(layer, pair):
        found = dot_nn(s.w_in_back[layer], pair)
        return found[0:8] + found[8:16]

    def radial_back(layer, number, index):
        hidden_bar = hidden_back(layer, s.r_pair[layer, index])
        s.hidden_bar[layer, number, index] = hidden_bar
        before = s.hidden[layer, number, index]
        before_bar = silu_slope(before, logistic(before)) * hidden_bar
        return basis_back(layer, rows_pair(before_bar))

    def radial_second(layer, number, index, last):
        hidden_hat = hidden_back(layer, s.h_pair[layer, index])
        before = s.hidden[layer, number, index]
        before_dot = s.hidden_dot[layer, index]
        hidden_bar = s.hidden_bar[layer, number, index]
        gate = logistic(before)
        slope = silu_slope(before, gate)
        before_hat = slope * hidden_hat + silu_bend(before, gate) * before_dot * hidden_bar
        s.out_pair[layer, index] = rows_pair(before * gate)
        hat_pair = rows_pair(before_hat)
        s.hat_pair[layer, index] = hat_pair
        return None if last else basis_back(layer, hat_pair)

    def radial_gradients(layer, number):
        for index in range(tiles):
            s.grad_out[layer] += dot_nt(s.h_pair[layer, index], s.out_pair[layer, index])
            tile = index if layer == 1 else tiles + index
            basis = jnp.concatenate(two_parts_f32(s.geo[number, tile, 8:16, :]), axis=0)
            s.grad_in[layer] += dot_nt(basis.astype(BF), s.hat_pair[layer, index])

    def early_gradients(layer, number, index):
        before = s.hidden[layer, number, index]
        slope = silu_slope(before, logistic(before))
        dot_pair = rows_pair(slope * s.hidden_dot[layer, index])
        bar_pair = rows_pair(slope * s.hidden_bar[layer, number, index])
        s.grad_out[layer] += dot_nt(s.r_pair[layer, index], dot_pair)
        tile = index if layer == 1 else tiles + index
        basis_dot = jnp.concatenate(two_parts_f32(s.geo_dot[tile, 8:16, :]), axis=0)
        s.grad_in[layer] += dot_nt(basis_dot.astype(BF), bar_pair)

    def first_early(number, index):
        geo = s.geo.at[number, tiles + index]
        cot = s.first_cot.at[number, index]
        kind = s.kind_value.at[number, index]

        def body(c, lane):
            value = kind[chunk_at(0, c), lane]
            y = harmonic_rows(geo, lane)
            put_pair(s.r_pair.at[0, index], 0, c, lane, cot[chunk_at(0, c), lane] * value)
            for first, last, path in ((0, 3, 1), (3, 8, 2)):
                total = 0.0
                for k in range(first, last):
                    total = total + cot[chunk_at((k + 1) * channels, c), lane] * y[k]
                put_pair(s.r_pair.at[0, index], path, c, lane, total * value)

        over_chunks(body)
        early_gradients(0, number, index)

    def second_early(number, index):
        cot = s.msg_cot.at[number, index]
        feat = s.feat.at[number, index]

        def body(c, lane):
            at = chunk_at(0, c)
            given = cot[at, lane]
            put_pair(s.r_pair.at[1, index], 0, c, lane, feat[at, lane] * given)
            for path in (1, 2):
                along = s.along[number, index, chunk_at((path - 1) * channels, c), lane]
                put_pair(s.r_pair.at[1, index], path, c, lane, along * given)

        over_chunks(body)
        early_gradients(1, number, index)

    def all_early(number):
        for index in range(tiles):
            second_early(number, index)
            first_early(number, index)
        for first, last, path in PATHS:
            bars = [s.raw_bar[number, k * channels : (k + 1) * channels, :] for k in range(first, last)]
            s.grad_ms[path] += outer_three(
                side_by_side(s.agg_dot, first, last), jnp.concatenate(bars, axis=1)
            )
        s.grad_mf[...] += outer_three(s.mixed_bar[number], part_of(s.agg_dot, 0))

    def kind_gradients(number):
        for index in range(tiles):
            kinds = s.kind_hot[number, index]
            s.grad_emb[...] += dot_nt(kinds, s.v_high[index]) + dot_nt(kinds, s.v_low[index])
        high, low = two_parts(s.scalar_hat[...])
        s.grad_emb[...] += dot_nt(s.own_kind[...], high) + dot_nt(s.own_kind[...], low)

    def node_gradients(number):
        agg = s.agg.at[number]
        for first, last, path in PATHS:
            hats = [s.raw_hat[k * channels : (k + 1) * channels, :] for k in range(first, last)]
            s.grad_ms[path] += outer_three(
                side_by_side(agg, first, last), jnp.concatenate(hats, axis=1)
            )
        s.grad_ms[2] += outer_three(s.agg_two[number], s.last_hat[...]) + outer_three(
            s.agg_two_dot[...], s.last_bar[...]
        )
        s.grad_mf[...] += outer_three(s.mixed_hat[...], part_of(agg, 0))

    def put_pieces(high_ref, low_ref, lane, at, value):
        high, low = two_parts(value)
        high_ref[at, lane] = high
        low_ref[at, lane] = low

    def put_pair(ref, path, c, lane, value):
        high, low = two_parts(value)
        ref[chunk_at(path * channels, c), lane] = high
        ref[chunk_at((3 + path) * channels, c), lane] = low

    def add_scatter(index, hot):
        s.sum_wide[...] += dot_nt(s.m_high[index], hot) + dot_nt(s.m_low[index], hot)

    def harmonic_rows(ref, lane):
        return [ref[row : row + 1, lane] for row in range(8)]

    def lane_parts():
        return [slice(first, first + LANES_AT_ONCE) for first in range(0, lanes, LANES_AT_ONCE)]

    def over_chunks(body):
        for lane in lane_parts():
            for c in range(chunks):
                body(c, lane)

    def over_chunks_sum(body):
        found = []
        for lane in lane_parts():
            sums = (0.0,) * 8
            for c in range(chunks):
                sums = body(c, lane, sums)
            found.append(sum_rows(sums))
        return jnp.concatenate(found, axis=1)

    def fold(value):
        return value[0:8] + value[8:16]

    def sum_rows(parts):
        if not hasattr(parts[0], "shape"):
            return jnp.zeros((8, LANES_AT_ONCE), F32)
        return jnp.concatenate([jnp.sum(part, axis=0, keepdims=True) for part in parts], axis=0)

    def first_forward(number, index):
        tile = tiles + index
        geo = s.geo.at[number, tile]
        radial_forward(0, number, index, geo[8:16, :])
        rad = s.radial.at[0, number, index]
        kind = s.kind_value.at[number, index]

        def body(c, lane):
            value = kind[chunk_at(0, c), lane]
            y = harmonic_rows(geo, lane)
            put_pieces(s.m_high.at[index], s.m_low.at[index], lane, chunk_at(0, c), rad[chunk_at(0, c), lane] * value)
            vector = rad[chunk_at(channels, c), lane] * value
            tensor = rad[chunk_at(2 * channels, c), lane] * value
            for k in range(8):
                part = (vector if k < 3 else tensor) * y[k]
                put_pieces(s.m_high.at[index], s.m_low.at[index], lane, chunk_at((k + 1) * channels, c), part)

        over_chunks(body)
        add_scatter(index, s.own_hot[number, tile, 0:atoms, :])

    def first_tangent(number, index):
        tile = tiles + index
        geo = s.geo.at[number, tile]
        dots = s.geo_dot.at[tile]
        radial_tangent(0, number, index, dots[8:16, :])
        rad = s.radial.at[0, number, index]
        rad_dot = s.radial_dot.at[0, index]
        kind = s.kind_value.at[number, index]

        def body(c, lane):
            value = kind[chunk_at(0, c), lane]
            y = harmonic_rows(geo, lane)
            y_dot = harmonic_rows(dots, lane)
            put_pieces(s.m_high.at[index], s.m_low.at[index], lane, chunk_at(0, c), rad_dot[chunk_at(0, c), lane] * value)
            vector = rad[chunk_at(channels, c), lane] * value
            tensor = rad[chunk_at(2 * channels, c), lane] * value
            vector_dot = rad_dot[chunk_at(channels, c), lane] * value
            tensor_dot = rad_dot[chunk_at(2 * channels, c), lane] * value
            for k in range(8):
                base, move = (vector, vector_dot) if k < 3 else (tensor, tensor_dot)
                part = move * y[k] + base * y_dot[k]
                put_pieces(s.m_high.at[index], s.m_low.at[index], lane, chunk_at((k + 1) * channels, c), part)

        over_chunks(body)
        add_scatter(index, s.own_hot[number, tile, 0:atoms, :])

    def gather_wide(hot):
        return dot_nn(s.a_pair[...], hot)

    def first_reverse(number, index):
        tile = tiles + index
        geo = s.geo.at[number, tile]
        s.first_cot[number, index] = gather_wide(s.own_hot[number, tile])
        cot = s.first_cot.at[number, index]
        rad = s.radial.at[0, number, index]
        kind = s.kind_value.at[number, index]

        def body(c, lane, sums):
            value = kind[chunk_at(0, c), lane]
            y = harmonic_rows(geo, lane)
            put_pair(s.r_pair.at[0, index], 0, c, lane, cot[chunk_at(0, c), lane] * value)
            sums = list(sums)
            for first, last, path in ((0, 3, 1), (3, 8, 2)):
                base = rad[chunk_at(path * channels, c), lane] * value
                total = 0.0
                for k in range(first, last):
                    given = cot[chunk_at((k + 1) * channels, c), lane]
                    total = total + given * y[k]
                    sums[k] = sums[k] + fold(base * given)
                put_pair(s.r_pair.at[0, index], path, c, lane, total * value)
            return tuple(sums)

        sums = over_chunks_sum(body)
        s.geo_bar[number, tile, 0:8, :] = sums
        s.geo_bar[number, tile, 8:16, :] = radial_back(0, number, index)
        first_back(number, tile)

    def first_second(number, index, final):
        tile = tiles + index
        geo = s.geo.at[number, tile]
        dots = s.geo_dot.at[tile]
        s.feat_dot[index] = gather_wide(s.own_hot[number, tile])
        hat = s.feat_dot.at[index]
        cot = s.first_cot.at[number, index]
        rad = s.radial.at[0, number, index]
        rad_dot = s.radial_dot.at[0, index]
        kind = s.kind_value.at[number, index]

        def body(c, lane, sums):
            value = kind[chunk_at(0, c), lane]
            y = harmonic_rows(geo, lane)
            y_dot = harmonic_rows(dots, lane)
            sums = list(sums)
            total = cot[chunk_at(0, c), lane]
            total_hat = hat[chunk_at(0, c), lane]
            put_pair(s.h_pair.at[0, index], 0, c, lane, total_hat * value)
            value_hat = rad[chunk_at(0, c), lane] * total_hat + rad_dot[chunk_at(0, c), lane] * total
            for first, last, path in ((0, 3, 1), (3, 8, 2)):
                rad_here = rad[chunk_at(path * channels, c), lane]
                rad_move = rad_dot[chunk_at(path * channels, c), lane]
                base = rad_here * value
                move = rad_move * value
                total = 0.0
                total_hat = 0.0
                for k in range(first, last):
                    given = cot[chunk_at((k + 1) * channels, c), lane]
                    given_hat = hat[chunk_at((k + 1) * channels, c), lane]
                    total = total + given * y[k]
                    total_hat = total_hat + (given_hat * y[k] + given * y_dot[k])
                    if not final:
                        sums[k] = sums[k] + fold(base * given_hat + move * given)
                put_pair(s.h_pair.at[0, index], path, c, lane, total_hat * value)
                value_hat = value_hat + rad_here * total_hat + rad_move * total
            put_pieces(s.v_high.at[index], s.v_low.at[index], lane, chunk_at(0, c), value_hat)
            return tuple(sums)

        sums = over_chunks_sum(body)
        basis_hat = radial_second(0, number, index, final)
        if not final:
            second_back(number, tile, jnp.concatenate([sums, basis_hat], axis=0))

    def gather_far(ref, number, index):
        found = []
        for part in range(group):
            pair = rows_pair(ref[index * group + part])
            here = dot_nn(pair, s.far_hot[number, index, :, part * atoms : (part + 1) * atoms])
            found.append(here[0:channels] + here[channels:])
        return jnp.concatenate(found, axis=1)

    def put_messages(number, index):
        for part in range(group):
            at = slice(part * atoms, (part + 1) * atoms)
            hot = s.far_hot[number, index, :, at]
            s.msg_out[index * group + part] = dot_nt(s.v_high[index, :, at], hot) + dot_nt(
                s.v_low[index, :, at], hot
            )

    def near_peer(distance):
        return half * group + jnp.bitwise_xor(lax.rem(me, group), distance)

    def far_peer(distance):
        return (1 - half) * group + jnp.bitwise_xor(lax.rem(me, group), group - 1 - distance)

    def message_to(other, kind):
        return remote(s.msg_out.at[other], s.msg_in.at[me], kind, other)

    def exchange_messages(number, kind, make):
        make(number, 1 - half)
        put_messages(number, 1 - half)
        for distance in range(group):
            message_to(far_peer(distance), kind).start()
        make(number, half)
        put_messages(number, half)
        for distance in range(group - 1, 0, -1):
            message_to(near_peer(distance), kind).start()

    def second_forward(number, index):
        geo = s.geo.at[number, index]
        radial_forward(1, number, index, geo[8:16, :])
        s.feat[number, index] = gather_wide(s.own_hot[number, index])
        feat = s.feat.at[number, index]
        rad = s.radial.at[1, number, index]

        def body(c, lane):
            y = harmonic_rows(geo, lane)
            total = rad[chunk_at(0, c), lane] * feat[chunk_at(0, c), lane]
            for first, last, path in ((0, 3, 1), (3, 8, 2)):
                along = 0.0
                for k in range(first, last):
                    along = along + feat[chunk_at((k + 1) * channels, c), lane] * y[k]
                s.along[number, index, chunk_at((path - 1) * channels, c), lane] = along
                total = total + rad[chunk_at(path * channels, c), lane] * along
            put_pieces(s.v_high.at[index], s.v_low.at[index], lane, chunk_at(0, c), total)

        over_chunks(body)

    def second_tangent(number, index):
        geo = s.geo.at[number, index]
        dots = s.geo_dot.at[index]
        radial_tangent(1, number, index, dots[8:16, :])
        s.feat_dot[index] = gather_wide(s.own_hot[number, index])
        feat = s.feat.at[number, index]
        feat_dot = s.feat_dot.at[index]
        rad = s.radial.at[1, number, index]
        rad_dot = s.radial_dot.at[1, index]

        def body(c, lane):
            y = harmonic_rows(geo, lane)
            y_dot = harmonic_rows(dots, lane)
            at = chunk_at(0, c)
            total = rad_dot[at, lane] * feat[at, lane] + rad[at, lane] * feat_dot[at, lane]
            for first, last, path in ((0, 3, 1), (3, 8, 2)):
                move = 0.0
                for k in range(first, last):
                    here = chunk_at((k + 1) * channels, c)
                    move = move + (feat_dot[here, lane] * y[k] + feat[here, lane] * y_dot[k])
                here = chunk_at((path - 1) * channels, c)
                s.along_dot[index, here, lane] = move
                here_rad = chunk_at(path * channels, c)
                total = total + (
                    rad_dot[here_rad, lane] * s.along[number, index, here, lane]
                    + rad[here_rad, lane] * move
                )
            put_pieces(s.v_high.at[index], s.v_low.at[index], lane, at, total)

        over_chunks(body)

    def second_reverse(number, index):
        geo = s.geo.at[number, index]
        s.msg_cot[number, index] = gather_far(s.cot_all, number, index)
        cot = s.msg_cot.at[number, index]
        feat = s.feat.at[number, index]
        rad = s.radial.at[1, number, index]

        def body(c, lane, sums):
            y = harmonic_rows(geo, lane)
            at = chunk_at(0, c)
            given = cot[at, lane]
            sums = list(sums)
            put_pair(s.r_pair.at[1, index], 0, c, lane, feat[at, lane] * given)
            put_pieces(s.m_high.at[index], s.m_low.at[index], lane, at, rad[at, lane] * given)
            for first, last, path in ((0, 3, 1), (3, 8, 2)):
                here = chunk_at(path * channels, c)
                along = s.along[number, index, chunk_at((path - 1) * channels, c), lane]
                put_pair(s.r_pair.at[1, index], path, c, lane, along * given)
                base = rad[here, lane] * given
                for k in range(first, last):
                    wide_at = chunk_at((k + 1) * channels, c)
                    put_pieces(s.m_high.at[index], s.m_low.at[index], lane, wide_at, base * y[k])
                    sums[k] = sums[k] + fold(base * feat[wide_at, lane])
            return tuple(sums)

        sums = over_chunks_sum(body)
        s.geo_bar[number, index, 0:8, :] = sums
        s.geo_bar[number, index, 8:16, :] = radial_back(1, number, index)
        first_back(number, index)
        add_scatter(index, s.own_hot[number, index, 0:atoms, :])

    def second_second(number, index, final):
        geo = s.geo.at[number, index]
        dots = s.geo_dot.at[index]
        s.msg_hat[index] = gather_far(s.cot_all, number, index)
        cot = s.msg_cot.at[number, index]
        feat = s.feat.at[number, index]
        feat_dot = s.feat_dot.at[index]
        rad = s.radial.at[1, number, index]
        rad_dot = s.radial_dot.at[1, index]

        def body(c, lane, sums):
            y = harmonic_rows(geo, lane)
            y_dot = harmonic_rows(dots, lane)
            at = chunk_at(0, c)
            given = cot[at, lane]
            given_hat = s.msg_hat[index, at, lane]
            sums = list(sums)
            put_pair(s.h_pair.at[1, index], 0, c, lane, feat[at, lane] * given_hat + feat_dot[at, lane] * given)
            put_pieces(s.m_high.at[index], s.m_low.at[index], lane, at, rad[at, lane] * given_hat + rad_dot[at, lane] * given)
            for first, last, path in ((0, 3, 1), (3, 8, 2)):
                here = chunk_at(path * channels, c)
                along_at = chunk_at((path - 1) * channels, c)
                along = s.along[number, index, along_at, lane]
                along_dot = s.along_dot[index, along_at, lane]
                put_pair(s.h_pair.at[1, index], path, c, lane, along * given_hat + along_dot * given)
                base = rad[here, lane] * given
                base_hat = rad[here, lane] * given_hat + rad_dot[here, lane] * given
                for k in range(first, last):
                    wide_at = chunk_at((k + 1) * channels, c)
                    put_pieces(s.m_high.at[index], s.m_low.at[index], lane, wide_at, base_hat * y[k] + base * y_dot[k])
                    if not final:
                        sums[k] = sums[k] + fold(
                            base_hat * feat[wide_at, lane] + base * feat_dot[wide_at, lane]
                        )
            return tuple(sums)

        sums = over_chunks_sum(body)
        basis_hat = radial_second(1, number, index, final)
        if not final:
            second_back(number, index, jnp.concatenate([sums, basis_hat], axis=0))
        add_scatter(index, s.own_hot[number, index, 0:atoms, :])

    def part_of(ref, component):
        return ref[component * channels : (component + 1) * channels, :]

    def side_by_side(ref, first, last):
        return jnp.concatenate([part_of(ref, k + 1) for k in range(first, last)], axis=1)

    def linear(left, value):
        return dot_nn(left, right_three(value))

    def keep_wide(component, value):
        high, low = two_parts(value)
        at = slice(component * channels, (component + 1) * channels)
        s.a_pair[at, 0:atoms] = high
        s.a_pair[at, atoms:] = low

    def node_first_forward(number):
        s.agg[number] = INV_NEIGH * s.sum_wide[...]
        agg = s.agg.at[number]
        mixed = linear(s.mf_left[...], part_of(agg, 0))
        s.mixed[number] = mixed
        before, gate_one, gate_two = [mixed[i * channels : (i + 1) * channels] for i in range(3)]
        scalar = s.start_scalar[...] + before * logistic(before)
        s.scalar[number] = scalar
        keep_wide(0, scalar)
        gates = (logistic(gate_one), logistic(gate_two))
        for first, last, path in PATHS:
            raws = linear(s.ms_left[path], side_by_side(agg, first, last))
            for k in range(first, last):
                raw = raws[:, (k - first) * atoms : (k - first + 1) * atoms]
                s.raw[number, k * channels : (k + 1) * channels, :] = raw
                keep_wide(k + 1, gates[path] * raw)

    def node_first_tangent(number):
        s.agg_dot[...] = INV_NEIGH * s.sum_wide[...]
        mixed = s.mixed.at[number]
        mixed_dot = linear(s.mf_left[...], part_of(s.agg_dot, 0))
        s.mixed_dot[...] = mixed_dot
        before = part_of(mixed, 0)
        scalar_dot = silu_slope(before, logistic(before)) * mixed_dot[0:channels]
        s.scalar_dot[...] = scalar_dot
        keep_wide(0, scalar_dot)
        for first, last, path in PATHS:
            gate = logistic(part_of(mixed, path + 1))
            move = gate * (1.0 - gate) * mixed_dot[(path + 1) * channels : (path + 2) * channels]
            raws_dot = linear(s.ms_left[path], side_by_side(s.agg_dot, first, last))
            for k in range(first, last):
                raw_dot = raws_dot[:, (k - first) * atoms : (k - first + 1) * atoms]
                s.raw_dot[k * channels : (k + 1) * channels, :] = raw_dot
                raw = s.raw[number, k * channels : (k + 1) * channels, :]
                keep_wide(k + 1, move * raw + gate * raw_dot)

    def node_first_reverse(number):
        s.feat_bar[number] = s.sum_wide[...]
        s.feat_bar[number, 0:channels, :] += s.readout_col[...]
        bar = s.feat_bar.at[number]
        mixed = s.mixed.at[number]
        before = part_of(mixed, 0)
        s.mixed_bar[number, 0:channels, :] = silu_slope(before, logistic(before)) * part_of(bar, 0)
        for first, last, path in PATHS:
            gate = logistic(part_of(mixed, path + 1))
            total = 0.0
            bars = []
            for k in range(first, last):
                given = part_of(bar, k + 1)
                total = total + given * s.raw[number, k * channels : (k + 1) * channels, :]
                raw_bar = gate * given
                s.raw_bar[number, k * channels : (k + 1) * channels, :] = raw_bar
                bars.append(raw_bar)
            found = INV_NEIGH * linear(s.ms_back[path], jnp.concatenate(bars, axis=1))
            for k in range(first, last):
                keep_wide(k + 1, found[:, (k - first) * atoms : (k - first + 1) * atoms])
            s.mixed_bar[number, (path + 1) * channels : (path + 2) * channels, :] = (
                gate * (1.0 - gate) * total
            )
        keep_wide(0, INV_NEIGH * linear(s.mf_back[...], s.mixed_bar[number]))

    def node_first_second(number, energy_bar):
        s.sum_wide[0:channels, :] += s.readout_col[...] * energy_bar
        hat = s.sum_wide
        bar = s.feat_bar.at[number]
        mixed = s.mixed.at[number]
        before = part_of(mixed, 0)
        gate = logistic(before)
        scalar_hat = part_of(hat, 0)
        s.mixed_hat[0:channels, :] = silu_slope(before, gate) * scalar_hat + silu_bend(
            before, gate
        ) * s.mixed_dot[0:channels, :] * part_of(bar, 0)
        s.scalar_hat[...] = scalar_hat
        for first, last, path in PATHS:
            gate = logistic(part_of(mixed, path + 1))
            slope = gate * (1.0 - gate)
            bend = slope * (1.0 - 2.0 * gate)
            mixed_dot = s.mixed_dot[(path + 1) * channels : (path + 2) * channels, :]
            one = 0.0
            two = 0.0
            hats = []
            for k in range(first, last):
                at = slice(k * channels, (k + 1) * channels)
                given = part_of(bar, k + 1)
                given_hat = part_of(hat, k + 1)
                raw = s.raw[number, at, :]
                one = one + (given_hat * raw + given * s.raw_dot[at, :])
                two = two + given * raw
                hats.append(gate * given_hat + slope * mixed_dot * given)
            for k in range(first, last):
                s.raw_hat[k * channels : (k + 1) * channels, :] = hats[k - first]
            found = INV_NEIGH * linear(s.ms_back[path], jnp.concatenate(hats, axis=1))
            for k in range(first, last):
                keep_wide(k + 1, found[:, (k - first) * atoms : (k - first + 1) * atoms])
            s.mixed_hat[(path + 1) * channels : (path + 2) * channels, :] = (
                slope * one + bend * mixed_dot * two
            )
        keep_wide(0, INV_NEIGH * linear(s.mf_back[...], s.mixed_hat[...]))

    def all_peers():
        return [far_peer(distance) for distance in range(group)] + [
            near_peer(distance) for distance in range(group - 1, 0, -1)
        ]

    def collect_messages(kind):
        total = s.msg_out[me]
        for other in all_peers():
            landed(s.msg_in.at[other], kind, other)
            total = total + s.msg_in[other]
        for other in all_peers():
            message_to(other, kind).wait_send()
        return INV_NEIGH * total

    def cotangent_to(other, kind):
        return remote(s.cot_all.at[me], s.cot_all.at[me], kind, other)

    def share_cotangent(value, kind):
        s.cot_all[me] = value
        for distance in range(1, group):
            cotangent_to(near_peer(distance), kind).start()
        for distance in range(group):
            cotangent_to(far_peer(distance), kind).start()

    def with_cotangents(number, kind, use):
        for distance in range(1, group):
            other = near_peer(distance)
            landed(s.cot_all.at[other], kind, other)
        use(number, half)
        for distance in range(group):
            other = far_peer(distance)
            landed(s.cot_all.at[other], kind, other)
        use(number, 1 - half)
        for other in all_peers():
            cotangent_to(other, kind).wait_send()

    def node_second_forward(number):
        agg = collect_messages(KIND_MSG)
        s.agg_two[number] = agg
        before = linear(s.ms_left[2], agg)
        s.last[number] = before
        gate = logistic(before)
        s.energy_row[...] = jnp.sum(
            s.readout_col[...] * (s.scalar[number] + before * gate), axis=0, keepdims=True
        )
        before_bar = s.readout_col[...] * silu_slope(before, gate)
        share_cotangent(INV_NEIGH * linear(s.ms_back[2], before_bar), KIND_COT)

    def node_second_second(number, energy_bar):
        all_early(number)
        agg_dot = collect_messages(KIND_TMSG)
        before = s.last[number]
        before_dot = linear(s.ms_left[2], agg_dot)
        gate = logistic(before)
        slope = silu_slope(before, gate)
        before_hat = s.readout_col[...] * (
            energy_bar * slope + silu_bend(before, gate) * before_dot
        )
        share_cotangent(INV_NEIGH * linear(s.ms_back[2], before_hat), KIND_TCOT)
        s.agg_two_dot[...] = agg_dot
        s.last_hat[...] = before_hat
        s.last_bar[...] = s.readout_col[...] * slope
        s.grad_ro[...] += energy_bar * (s.scalar[number] + before * gate) + (
            s.scalar_dot[...] + slope * before_dot
        )

    def share_rows(out_ref, in_ref, kind, meanwhile=None):
        def start(other):
            remote(out_ref, in_ref.at[me], kind, other).start()

        each_peer(start)
        in_ref[me] = out_ref[...]
        if meanwhile is not None:
            meanwhile()

        def wait(other):
            landed(in_ref.at[other], kind, other)
            remote(out_ref, in_ref.at[me], kind, other).wait_send()

        each_peer(wait)
        total = in_ref[0]
        for other in range(1, n_edge):
            total = total + in_ref[other]
        return total

    def evaluate(number):
        table(s.place)
        loop(2 * tiles, lambda index: geometry(number, index), True)
        s.sum_wide[...] = jnp.zeros_like(s.sum_wide)
        each_tile(lambda index: first_forward(number, index))
        node_first_forward(number)
        exchange_messages(number, KIND_MSG, second_forward)
        node_second_forward(number)
        s.sum_wide[...] = jnp.zeros_like(s.sum_wide)
        with_cotangents(number, KIND_COT, second_reverse)
        node_first_reverse(number)
        each_tile(lambda index: first_reverse(number, index))
        scatter_rows(number, s.force_out)
        s.force_out[3] = jnp.zeros((n_edge, atoms), F32)
        s.force_out[3, pl.ds(me, 1), :] = s.energy_row[...]

        def prepare():
            @pl.when(number < EVALS - 1)
            def _():
                one_hots(number + 1)

        total = share_rows(s.force_out, s.force_in, KIND_FORCE, prepare)
        force = -total[0:3]
        s.energy[number] = total[3]
        half_kick = 0.5 * STEP_DT * force

        @pl.when(number > 0)
        def _():
            s.speed[...] = s.speed[...] + half_kick

        @pl.when(number == 0)
        def _():
            s.start_kinetic[...] = 0.5 * jnp.sum(s.speed[...] * s.speed[...], axis=0)

        @pl.when(number < EVALS - 1)
        def _():
            s.speed[...] = s.speed[...] + half_kick
            s.place[...] = s.place[...] + STEP_DT * s.speed[...]

    one_hots(0)
    loop(EVALS, evaluate)

    kinetic = 0.5 * jnp.sum(s.speed[...] * s.speed[...], axis=0)
    change = (s.energy[EVALS - 1] + kinetic) - (s.energy[0] + s.start_kinetic[...])
    system_of = lax.broadcasted_iota(jnp.int32, (n_edge, atoms), 1) // half_atoms
    system_atoms = float(half_atoms * n_edge)
    loss = jnp.zeros((1, 1), F32)
    drift_grad = jnp.zeros((n_edge, atoms), F32)
    for number in range(SYS_LOC):
        mine = system_of == number
        drift = jnp.sum(jnp.where(mine, change, 0.0), axis=(0, 1), keepdims=True)
        loss = loss + drift * drift / system_atoms
        drift_grad = drift_grad + jnp.where(mine, 2.0 * drift / system_atoms, 0.0)
    s.drift_grad[...] = drift_grad
    s.place_bar[...] = jnp.zeros_like(s.place_bar)
    s.speed_bar[...] = drift_grad[None] * s.speed[...]
    s.loss_row[...] = jnp.broadcast_to(loss * jnp.where(me == 0, 1.0, 0.0), (1, channels))

    def reverse(step, last):
        number = EVALS - 1 - step
        sides = jnp.where(jnp.logical_or(number == 0, number == EVALS - 1), 1.0, 2.0)
        ends = jnp.where(number == 0, -1.0, jnp.where(number == EVALS - 1, 1.0, 0.0))
        s.move[...] = (-0.5 * STEP_DT * sides) * s.speed_bar[...]
        table(s.move)
        loop(2 * tiles, lambda index: geometry_tangent(number, index), True)
        energy_bar = ends * s.drift_grad[pl.ds(me, 1), :]
        s.sum_wide[...] = jnp.zeros_like(s.sum_wide)
        each_tile(lambda index: first_tangent(number, index))
        node_first_tangent(number)
        exchange_messages(number, KIND_TMSG, second_tangent)
        node_second_second(number, energy_bar)
        s.sum_wide[...] = jnp.zeros_like(s.sum_wide)
        with_cotangents(
            number, KIND_TCOT, lambda number, index: second_second(number, index, last)
        )
        node_first_second(number, energy_bar)
        if last:
            radial_gradients(1, number)
            node_gradients(number)
            pack_first()
            each_peer(lambda other: first_rows(other).start())
        each_tile(lambda index: first_second(number, index, last))
        if last:
            radial_gradients(0, number)
            kind_gradients(number)
            pack_second()
            each_peer(lambda other: second_rows(other).start())
        else:
            scatter_rows(number, s.place_out)

            def gradients():
                radial_gradients(1, number)
                node_gradients(number)
                radial_gradients(0, number)
                kind_gradients(number)

            total = share_rows(s.place_out, s.place_in, KIND_TFORCE, gradients)
            s.place_bar[...] = s.place_bar[...] + total
            s.speed_bar[...] = s.speed_bar[...] + STEP_DT * s.place_bar[...]

    first_each, second_each = [ref.shape[0] // n_edge for ref in (s.grad_first, s.grad_second)]

    def some_rows(ref, other, count):
        return ref.at[pl.ds(pl.multiple_of(other * count, 8), count)]

    def first_rows(other):
        return remote(
            some_rows(s.grad_first, other, first_each),
            s.part_in.at[me, 0:first_each],
            KIND_SCATTER,
            other,
        )

    def second_rows(other):
        return remote(
            some_rows(s.grad_second, other, second_each),
            s.part_in.at[me, first_each:],
            KIND_SCATTER_LATE,
            other,
        )

    def join_out(layer):
        found = s.grad_out[layer]
        rows = 3 * channels
        return found[0:rows, 0:channels] + found[0:rows, channels:] + found[rows:, 0:channels]

    def join_in(layer):
        found = s.grad_in[layer]
        return found[0:8, 0:channels] + found[0:8, channels:] + found[8:16, 0:channels]

    def pack_first():
        out = s.grad_first
        rows = 3 * channels
        out[0:rows, :] = jnp.concatenate([join_out(1), s.grad_mf[...]], axis=1)
        out[rows : rows + channels, :] = jnp.concatenate([s.grad_ms[0], s.grad_ms[1]], axis=1)
        ones = jnp.ones((8, atoms), BF)
        ro_rows = 0.0
        for piece in three_parts_f32(s.grad_ro[...]):
            ro_rows = ro_rows + dot_nt(ones, piece.astype(BF))
        rest = jnp.zeros((channels - 16, channels), F32)
        small = jnp.concatenate([ro_rows, join_in(1), rest], axis=0)
        out[rows + channels : rows + 2 * channels, :] = jnp.concatenate(
            [s.grad_ms[2], small], axis=1
        )

    def pack_second():
        out = s.grad_second
        rows = 3 * channels // 2
        found = join_out(0)
        out[0:rows, :] = jnp.concatenate([found[0:rows], found[rows:]], axis=1)
        out[rows : rows + 8, :] = jnp.concatenate([join_in(0), s.grad_emb[0:8, :]], axis=1)
        loss_rows = jnp.broadcast_to(s.loss_row[...], (8, channels))
        out[rows + 8 : rows + 16, :] = jnp.concatenate([loss_rows, loss_rows], axis=1)

    lax.fori_loop(0, EVALS - 1, lambda step, carry: (reverse(step, False), carry)[1], 0)
    reverse(EVALS - 1, True)

    s.part_in[me, 0:first_each, :] = some_rows(s.grad_first, me, first_each)[...]
    s.part_in[me, first_each:, :] = some_rows(s.grad_second, me, second_each)[...]

    def wait_scatter(other):
        landed(s.part_in.at[other, 0:first_each], KIND_SCATTER, other)
        landed(s.part_in.at[other, first_each:], KIND_SCATTER_LATE, other)
        first_rows(other).wait_send()
        second_rows(other).wait_send()

    each_peer(wait_scatter)
    total = s.part_in[0]
    for other in range(1, n_edge):
        total = total + s.part_in[other]
    s.sys_in[my_group] = total

    def line_copy(other, index):
        return pltpu.make_async_remote_copy(
            src_ref=s.sys_in.at[index],
            dst_ref=s.sys_in.at[index],
            send_sem=s.send_sem.at[KIND_SYS, other],
            recv_sem=s.recv_sem.at[KIND_SYS, index],
            device_id={"edge": 2 * other + core},
            device_id_type=MESH,
        )

    each_group(lambda other: line_copy(other, my_group).start())

    def wait_line(other):
        line_copy(other, other).wait_recv()
        line_copy(other, my_group).wait_send()

    each_group(wait_line)
    total = s.sys_in[0]
    for other in range(1, n_sys):
        total = total + s.sys_in[other]
    s.summed[me] = total
    mine = s.summed.at[me]
    each_peer(lambda other: remote(mine, mine, KIND_GATHER, other).start())

    def wait_gather(other):
        landed(s.summed.at[other], KIND_GATHER, other)
        remote(mine, mine, KIND_GATHER, other).wait_send()

    each_peer(wait_gather)
    first_total = s.grad_first.shape[0]
    for other in range(n_edge):
        total_ref[other * first_each : (other + 1) * first_each, :] = s.summed[other, 0:first_each, :]
        low_row = first_total + other * second_each
        total_ref[low_row : low_row + second_each, :] = s.summed[other, first_each:, :]


class Scratch:
    pass


def step_scratch(n_edge, n_sys, channels, atoms, first_rows, second_rows):
    tiles = TILES
    lanes = n_edge // tiles * atoms
    wide = N_COMP * channels
    vm = lambda *shape: pltpu.VMEM(shape, F32)
    vb = lambda *shape: pltpu.VMEM(shape, BF)
    vi = lambda *shape: pltpu.VMEM(shape, jnp.int32)
    return dict(
        send_sem=pltpu.SemaphoreType.DMA((KINDS, n_edge)),
        recv_sem=pltpu.SemaphoreType.DMA((KINDS, n_edge)),
        start_out=vm(8, atoms),
        start_float=vm(n_edge, 8, atoms),
        lists_own=vi(n_edge, 16, atoms),
        own_kind=vb(16, atoms),
        lists_out=vi(n_edge, 16, atoms),
        lists_in=vi(n_edge, 16, atoms),
        w_in_left=vb(2, channels, 32),
        w_in_back=vb(2, 16, 2 * channels),
        w_out_left=vb(2, 3 * channels, 3 * channels),
        w_out_back=vb(2, 2 * channels, 3 * channels),
        mf_left=vb(3 * channels, 3 * channels),
        mf_back=vb(channels, 9 * channels),
        ms_left=vb(3, channels, 3 * channels),
        ms_back=vb(3, channels, 3 * channels),
        emb_left=vb(channels, 48),
        readout_col=vm(channels, atoms),
        start_scalar=vm(channels, atoms),
        place=vm(3, n_edge, atoms),
        speed=vm(3, n_edge, atoms),
        energy_row=vm(1, atoms),
        energy=vm(EVALS, n_edge, atoms),
        start_kinetic=vm(n_edge, atoms),
        drift_grad=vm(n_edge, atoms),
        place_bar=vm(3, n_edge, atoms),
        speed_bar=vm(3, n_edge, atoms),
        move=vm(3, n_edge, atoms),
        own_hot=vb(EVALS, 2 * tiles, 2 * atoms, lanes),
        far_hot=vb(EVALS, 2 * tiles, atoms, lanes),
        kind_hot=vb(EVALS, tiles, 16, lanes),
        kind_value=vm(EVALS, tiles, channels, lanes),
        rows=vm(n_edge, 8, atoms),
        pieces=vb(n_edge, 32, atoms),
        row_own=vm(8, atoms),
        edge_rows=vm(2 * tiles, 8, lanes),
        geo=vm(EVALS, 2 * tiles, 40, lanes),
        geo_bar=vm(EVALS, 2 * tiles, 24, lanes),
        geo_dot=vm(2 * tiles, 24, lanes),
        hidden=vm(2, EVALS, tiles, channels, lanes),
        hidden_bar=vm(2, EVALS, tiles, channels, lanes),
        hidden_dot=vm(2, tiles, channels, lanes),
        radial=vm(2, EVALS, tiles, 3 * channels, lanes),
        radial_dot=vm(2, tiles, 3 * channels, lanes),
        m_high=vb(tiles, wide, lanes),
        m_low=vb(tiles, wide, lanes),
        r_pair=vb(2, tiles, 6 * channels, lanes),
        h_pair=vb(2, tiles, 6 * channels, lanes),
        out_pair=vb(2, tiles, 2 * channels, lanes),
        hat_pair=vb(2, tiles, 2 * channels, lanes),
        scalar_hat=vm(channels, atoms),
        raw_hat=vm(8 * channels, atoms),
        last_hat=vm(channels, atoms),
        last_bar=vm(channels, atoms),
        agg_two_dot=vm(channels, atoms),
        loss_row=vm(1, channels),
        v_high=vb(tiles, channels, lanes),
        v_low=vb(tiles, channels, lanes),
        a_pair=vb(wide, 2 * atoms),
        sum_wide=vm(wide, atoms),
        first_cot=vm(EVALS, tiles, wide, lanes),
        feat=vm(EVALS, tiles, wide, lanes),
        feat_dot=vm(tiles, wide, lanes),
        along=vm(EVALS, tiles, 2 * channels, lanes),
        along_dot=vm(tiles, 2 * channels, lanes),
        msg_cot=vm(EVALS, tiles, channels, lanes),
        msg_hat=vm(tiles, channels, lanes),
        agg=vm(EVALS, wide, atoms),
        agg_dot=vm(wide, atoms),
        mixed=vm(EVALS, 3 * channels, atoms),
        mixed_dot=vm(3 * channels, atoms),
        mixed_bar=vm(EVALS, 3 * channels, atoms),
        mixed_hat=vm(3 * channels, atoms),
        raw=vm(EVALS, 8 * channels, atoms),
        raw_dot=vm(8 * channels, atoms),
        raw_bar=vm(EVALS, 8 * channels, atoms),
        scalar=vm(EVALS, channels, atoms),
        scalar_dot=vm(channels, atoms),
        feat_bar=vm(EVALS, wide, atoms),
        agg_two=vm(EVALS, channels, atoms),
        last=vm(EVALS, channels, atoms),
        msg_out=vm(n_edge, channels, atoms),
        msg_in=vm(n_edge, channels, atoms),
        cot_all=vm(n_edge, channels, atoms),
        force_out=vm(4, n_edge, atoms),
        force_in=vm(n_edge, 4, n_edge, atoms),
        place_out=vm(3, n_edge, atoms),
        place_in=vm(n_edge, 3, n_edge, atoms),
        grad_emb=vm(16, channels),
        grad_in=vm(2, 2 * NB, 2 * channels),
        grad_out=vm(2, 6 * channels, 2 * channels),
        grad_mf=vm(3 * channels, channels),
        grad_ms=vm(3, channels, channels),
        grad_ro=vm(channels, atoms),
        grad_first=vm(first_rows, 2 * channels),
        grad_second=vm(second_rows, 2 * channels),
        part_in=vm(n_edge, (first_rows + second_rows) // n_edge, 2 * channels),
        sys_in=vm(n_sys, (first_rows + second_rows) // n_edge, 2 * channels),
        summed=vm(n_edge, (first_rows + second_rows) // n_edge, 2 * channels),
    )


def gradient_rows(n_edge, channels):
    unit = 8 * n_edge
    return -(-(5 * channels) // unit) * unit, -(-(3 * channels // 2 + 16) // unit) * unit


def whole_step(positions, velocities, species, senders, receivers, edge_mask, params):
    n_edge, n_sys = lax.axis_size("edge"), lax.axis_size("sys")
    atoms = positions.shape[1]
    channels = params[0].shape[1]
    first_rows, second_rows = gradient_rows(n_edge, channels)
    shapes = step_scratch(n_edge, n_sys, channels, atoms, first_rows, second_rows)
    names = tuple(shapes)

    def kernel(*refs):
        scratch = Scratch()
        for name, ref in zip(names, refs[13:]):
            setattr(scratch, name, ref)
        step_kernel(n_edge, n_sys, *refs[:13], scratch)

    embedding, radial_in, radial_out, mix_first, mix_square, readout = params
    operands = (
        positions,
        velocities,
        species,
        senders,
        receivers,
        edge_mask,
        embedding,
        radial_in,
        radial_out,
        mix_first,
        mix_square,
        readout,
    )
    return pl.pallas_call(
        kernel,
        out_shape=jax.ShapeDtypeStruct((first_rows + second_rows, 2 * channels), F32),
        in_specs=[pl.BlockSpec(memory_space=pltpu.VMEM)] * len(operands),
        out_specs=pl.BlockSpec(memory_space=pltpu.VMEM),
        scratch_shapes=list(shapes.values()),
        compiler_params=pltpu.CompilerParams(
            collective_id=0, has_side_effects=True, vmem_limit_bytes=60 * 1024 * 1024
        ),
    )(*operands)


def to_column(row):
    count = row.shape[1]
    square = jnp.broadcast_to(row, (count, count))
    same = lax.broadcasted_iota(jnp.int32, (count, count), 0) == lax.broadcasted_iota(
        jnp.int32, (count, count), 1
    )
    return jnp.sum(jnp.where(same, square, 0.0), axis=1, keepdims=True)


def to_row(column):
    count = column.shape[0]
    square = jnp.broadcast_to(column, (count, count))
    same = lax.broadcasted_iota(jnp.int32, (count, count), 0) == lax.broadcasted_iota(
        jnp.int32, (count, count), 1
    )
    return jnp.sum(jnp.where(same, square, 0.0), axis=0, keepdims=True)


def total_mean(value):
    return jnp.sum(
        jnp.sum(value, axis=1, keepdims=True), axis=0, keepdims=True
    ) / float(value.shape[0] * value.shape[1])


def factored_rows(gradient, weight, row_state, col_state):
    decay_rate = 1.0 - STEP_NUM ** (-0.8)
    squares = gradient * gradient + EPS_SQUARE
    size_m, size_n = gradient.shape
    row_mean = jnp.sum(squares, axis=1, keepdims=True) / float(size_n)
    col_mean = jnp.sum(squares, axis=0, keepdims=True) / float(size_m)
    row_new = decay_rate * to_column(row_state) + (1.0 - decay_rate) * row_mean
    col_new = decay_rate * col_state + (1.0 - decay_rate) * col_mean
    second = row_new * col_new / total_mean(row_new)
    weight_rms = jnp.sqrt(total_mean(weight * weight) + 1e-06)
    weight_new = weight - RELATIVE * weight_rms * gradient * lax.rsqrt(second)
    return (gradient, to_row(row_new), col_new, weight_new, weight_new.astype(jnp.bfloat16))


def update_kernel(total_ref, *refs):
    weights, states, outs = refs[0:6], refs[6:17], refs[17:]
    kinds, channels = weights[0].shape

    rows = 3 * channels
    late = gradient_rows(lax.axis_size("edge"), channels)[0]
    small = rows + channels
    first_layer = jnp.concatenate(
        [
            total_ref[late : late + rows // 2, :channels],
            total_ref[late : late + rows // 2, channels:],
        ],
        axis=0,
    )
    below = late + rows // 2
    gradients = (
        [total_ref[below : below + kinds, channels:]],
        [total_ref[below : below + 8, :channels], total_ref[small + 8 : small + 16, channels:]],
        [first_layer.T, total_ref[0:rows, :channels].T],
        [total_ref[0:rows, channels:].T],
        [
            total_ref[rows:small, :channels],
            total_ref[rows:small, channels:],
            total_ref[small : small + channels, :channels],
        ],
    )
    outs[0][...] = total_ref[below + 8 : below + 9, 0:1]
    for which, parts in enumerate(gradients):
        weight, rows, cols = weights[which], states[2 * which], states[2 * which + 1]
        results = outs[1 + 5 * which : 6 + 5 * which]
        stacked = len(weight.shape) == 3
        for number, gradient in enumerate(parts):
            if stacked:
                found = factored_rows(
                    gradient,
                    weight[number],
                    rows[number : number + 1, :],
                    cols[number : number + 1, :],
                )
                results[0][number] = found[0]
                results[1][number : number + 1, :] = found[1]
                results[2][number : number + 1, :] = found[2]
                results[3][number] = found[3]
                results[4][number] = found[4]
            else:
                size_m, size_n = weight.shape
                found = factored_rows(
                    gradient,
                    weight[...],
                    rows[...].reshape(1, size_m),
                    cols[...].reshape(1, size_n),
                )
                results[0][...] = found[0]
                results[1][...] = found[1].reshape(size_m)
                results[2][...] = found[2].reshape(size_n)
                results[3][...] = found[3]
                results[4][...] = found[4]
    gradient = total_ref[small : small + 1, channels:]
    decay_rate = 1.0 - STEP_NUM ** (-0.8)
    weight = weights[5][...].reshape(1, channels)
    second_new = decay_rate * states[10][...].reshape(1, channels) + (1.0 - decay_rate) * (
        gradient * gradient + EPS_SQUARE
    )
    weight_rms = jnp.sqrt(total_mean(weight * weight) + 1e-06)
    weight_new = weight - RELATIVE * weight_rms * gradient * lax.rsqrt(second_new)
    outs[26][...] = gradient.reshape(channels)
    outs[27][...] = second_new.reshape(channels)
    outs[28][...] = weight_new.reshape(channels)
    outs[29][...] = weight_new.astype(jnp.bfloat16).reshape(channels)


def whole_update(total, params, states):
    shapes = [jax.ShapeDtypeStruct((1, 1), F32)]
    for which in range(5):
        weight, rows, cols = params[which], states[2 * which], states[2 * which + 1]
        for like in (weight, rows, cols, weight):
            shapes.append(jax.ShapeDtypeStruct(like.shape, F32))
        shapes.append(jax.ShapeDtypeStruct(weight.shape, jnp.bfloat16))
    for kind in (F32, F32, F32, jnp.bfloat16):
        shapes.append(jax.ShapeDtypeStruct(params[5].shape, kind))
    operands = (total, *params, *states)
    results = pl.pallas_call(
        update_kernel,
        out_shape=shapes,
        in_specs=[pl.BlockSpec(memory_space=pltpu.VMEM)] * len(operands),
        out_specs=[pl.BlockSpec(memory_space=pltpu.VMEM)] * len(shapes),
        compiler_params=pltpu.CompilerParams(vmem_limit_bytes=8 * 1024 * 1024),
    )(*operands)
    return (results[0].reshape(()), *results[1:])


def fits_kernel(senders, atom_count):
    n_edge = lax.axis_size("edge")
    slots = senders.shape[1] // n_edge
    whole = slots == atom_count and atom_count % 128 == 0
    even = n_edge & (n_edge - 1) == 0 and n_edge >= 2 * TILES
    return whole and even and n_edge == 2 * lax.axis_size("sys")


def on_device(
    positions,
    velocities,
    species,
    senders,
    receivers,
    edge_mask,
    embedding,
    radial_in,
    radial_out,
    mix_first,
    mix_square,
    readout,
    embedding_rows,
    embedding_cols,
    radial_in_rows,
    radial_in_cols,
    radial_out_rows,
    radial_out_cols,
    mix_first_rows,
    mix_first_cols,
    mix_square_rows,
    mix_square_cols,
    readout_second,
):
    params = (embedding, radial_in, radial_out, mix_first, mix_square, readout)
    atom_count = positions.shape[1]
    states = (
        embedding_rows,
        embedding_cols,
        radial_in_rows,
        radial_in_cols,
        radial_out_rows,
        radial_out_cols,
        mix_first_rows,
        mix_first_cols,
        mix_square_rows,
        mix_square_cols,
        readout_second,
    )
    if fits_kernel(senders, atom_count):
        total = whole_step(
            positions, velocities, species, senders, receivers, edge_mask, params
        )
        return whole_update(total, params, states)
    spec_hot = (species[None, :] == jnp.arange(embedding.shape[0])[:, None]).astype(jnp.float32)
    edge_lists = receivers[None]
    arrived = lax.all_to_all(edge_lists, "edge", split_axis=2, concat_axis=2, tiled=True)
    passes = [
        build(senders[number], arrived[:, number], edge_mask[number], atom_count, spec_hot)
        for number in range(EVALS)
    ]
    coords = positions
    moving = velocities
    energies, forces, stored = passes[0][0](coords, params)
    record = [stored]
    first_energy = energies
    for number in range(STEPS):
        half_speed = moving + 0.5 * STEP_DT * forces
        coords = coords + STEP_DT * half_speed
        energies, forces, stored = passes[number + 1][0](coords, params)
        record.append(stored)
        moving = half_speed + 0.5 * STEP_DT * forces
    local_sums = jnp.stack(
        [
            per_system(first_energy),
            per_system(energies),
            per_system(0.5 * jnp.sum(velocities * velocities, axis=0)),
            per_system(0.5 * jnp.sum(moving * moving, axis=0)),
        ]
    )
    totals = lax.psum(local_sums, "edge")
    drift = totals[1] + totals[3] - (totals[0] + totals[2])
    system_atoms = atom_count // SYS_LOC * lax.axis_size("edge")
    loss_local = jnp.sum(drift * drift) / system_atoms
    drift_grad = jnp.repeat(2.0 * drift / system_atoms, atom_count // SYS_LOC)
    speed_bar = drift_grad[None, :] * moving
    coord_bar = jnp.zeros_like(positions)
    force_next = jnp.zeros_like(positions)
    gradients = jax.tree.map(jnp.zeros_like, params)
    for number in reversed(range(STEPS)):
        later = number + 1
        force_bar = force_next + 0.5 * STEP_DT * speed_bar
        if later == STEPS:
            energy_bar = drift_grad
        else:
            energy_bar = jnp.zeros_like(drift_grad)
        coord_part, param_part = passes[later][1](record[later], params, energy_bar, force_bar)
        gradients = add_trees([gradients, param_part])
        coord_bar = coord_bar + coord_part
        half_bar = speed_bar + STEP_DT * coord_bar
        speed_bar = half_bar
        force_next = 0.5 * STEP_DT * half_bar
    _, param_part = passes[0][1](record[0], params, -drift_grad, force_next)
    gradients = add_trees([gradients, param_part])
    loss_term = loss_local * (lax.axis_index("edge") == 0).astype(jnp.float32)
    summed = lax.psum(
        (
            gradients[0],
            gradients[1],
            gradients[2],
            gradients[3],
            gradients[4],
            gradients[5],
            loss_term,
        ),
        ("sys", "edge"),
    )
    return update(summed, params, states)


def solution(mesh):
    placed = (
        P(None, ("sys", "edge")),
        P(None, ("sys", "edge")),
        P(("sys", "edge")),
        P(None, ("sys", "edge")),
        P(None, ("sys", "edge")),
        P(None, ("sys", "edge")),
        P(),
        P(),
        P(),
        P(),
        P(),
        P(),
        P(),
        P(),
        P(),
        P(),
        P(),
        P(),
        P(),
        P(),
        P(),
        P(),
        P(),
    )
    return jax.shard_map(
        on_device,
        mesh=mesh,
        in_specs=placed,
        out_specs=(
            P(),
            P(),
            P(),
            P(),
            P(),
            P(),
            P(),
            P(),
            P(),
            P(),
            P(),
            P(),
            P(),
            P(),
            P(),
            P(),
            P(),
            P(),
            P(),
            P(),
            P(),
            P(),
            P(),
            P(),
            P(),
            P(),
            P(),
            P(),
            P(),
            P(),
        ),
        check_vma=False,
    )
```

```python
from functools import reduce
import math

import jax
import jax.numpy as jnp
from jax import lax
from jax.experimental import pallas as pl
from jax.experimental.pallas import tpu as pltpu
from jax.sharding import PartitionSpec as P

NB = 8
SYS_LOC = 2
STEPS = 2
STEP_NUM = 10
EVALS = 3


PRECISE = lax.Precision.HIGHEST
SOFTEN = 0.25
CUTOFF = 5.0
INV_NEIGH = 0.2
STEP_DT = 0.5
RELATIVE = 0.3
EPS_SQUARE = 1e-30
ROOT3 = math.sqrt(3.0)
ROOT5 = math.sqrt(5.0)


def geometry(sender_pos, receiver_pos):
    offset_vec = sender_pos - receiver_pos
    radius = jnp.sqrt(jnp.sum(offset_vec * offset_vec, axis=0) + SOFTEN)
    direction = offset_vec / radius
    unit_x, unit_y, unit_z = (direction[0], direction[1], direction[2])
    first_harm = ROOT3 * direction
    second_harm = ROOT5 * jnp.stack(
        [
            ROOT3 * unit_x * unit_y,
            ROOT3 * unit_y * unit_z,
            0.5 * (3.0 * unit_z * unit_z - 1.0),
            ROOT3 * unit_x * unit_z,
            0.5 * ROOT3 * (unit_x * unit_x - unit_y * unit_y),
        ]
    )
    scaled = radius / CUTOFF
    envelope = 1.0 - 28.0 * scaled**6 + 48.0 * scaled**7 - 21.0 * scaled**8
    orders = jnp.arange(1, NB + 1).astype(jnp.float32)[:, None]
    bessel = (
        math.sqrt(2.0 / CUTOFF)
        * jnp.sin(orders * math.pi * scaled[None, :])
        / radius[None, :]
        * envelope[None, :]
    )
    return (first_harm, second_harm, bessel)


def radial(bessel, weight_in, weight_out):
    hidden = jax.nn.silu(jnp.einsum("nr,ne->re", weight_in, bessel, precision=PRECISE))
    return jnp.einsum("rk,re->ke", weight_out, hidden, precision=PRECISE)


def first_messages(
    first_harm, second_harm, bessel, sender_feat, edge_weight, weight_in, weight_out
):
    channels = sender_feat.shape[0]
    edge_weights = radial(bessel, weight_in, weight_out)
    scalar_part = (edge_weights[:channels] * sender_feat)[None]
    vector_part = (edge_weights[channels : 2 * channels] * sender_feat)[None] * first_harm[
        :, None, :
    ]
    tensor_part = (edge_weights[2 * channels :] * sender_feat)[None] * second_harm[:, None, :]
    return jnp.concatenate([scalar_part, vector_part, tensor_part], axis=0) * edge_weight


def node_first(summed, scalar_prev, mix_first, mix_square):
    gathered = summed * INV_NEIGH
    channels = scalar_prev.shape[0]
    mixed = jnp.einsum("cd,ca->da", mix_first, gathered[0], precision=PRECISE)
    vectors = jnp.einsum("mca,cd->mda", gathered[1:4], mix_square[0], precision=PRECISE)
    tensors = jnp.einsum("mca,cd->mda", gathered[4:9], mix_square[1], precision=PRECISE)
    scalars = scalar_prev + jax.nn.silu(mixed[:channels])
    vectors = jax.nn.sigmoid(mixed[channels : 2 * channels])[None] * vectors
    tensors = jax.nn.sigmoid(mixed[2 * channels :])[None] * tensors
    return jnp.concatenate([scalars[None], vectors, tensors], axis=0)


def second_messages(
    first_harm, second_harm, bessel, sender_feat, edge_weight, weight_in, weight_out
):
    channels = sender_feat.shape[1]
    edge_weights = radial(bessel, weight_in, weight_out)
    along_first = jnp.einsum("kce,ke->ce", sender_feat[1:4], first_harm, precision=PRECISE)
    along_second = jnp.einsum("kce,ke->ce", sender_feat[4:9], second_harm, precision=PRECISE)
    combined = (
        edge_weights[:channels] * sender_feat[0]
        + edge_weights[channels : 2 * channels] * along_first
        + edge_weights[2 * channels :] * along_second
    )
    return combined * edge_weight


def node_second(features, summed, mix_square, readout):
    scalars = features[0] + jax.nn.silu(
        jnp.einsum("cd,ca->da", mix_square[2], summed * INV_NEIGH, precision=PRECISE)
    )
    return jnp.einsum("c,ca->a", readout, scalars, precision=PRECISE)


def factored(gradient, weight, row_state, col_state):
    decay_rate = 1.0 - STEP_NUM ** (-0.8)
    squares = gradient * gradient + EPS_SQUARE
    row_new = decay_rate * row_state + (1.0 - decay_rate) * jnp.mean(squares, axis=-1)
    col_new = decay_rate * col_state + (1.0 - decay_rate) * jnp.mean(squares, axis=-2)
    second = (
        row_new[..., :, None]
        * col_new[..., None, :]
        / jnp.mean(row_new, axis=-1, keepdims=True)[..., None]
    )
    weight_rms = jnp.sqrt(jnp.mean(weight * weight, axis=(-2, -1), keepdims=True) + 1e-06)
    weight_new = weight - RELATIVE * weight_rms * gradient * lax.rsqrt(second)
    return (gradient, row_new, col_new, weight_new, weight_new.astype(jnp.bfloat16))


def unfactored(gradient, weight, second):
    decay_rate = 1.0 - STEP_NUM ** (-0.8)
    second_new = decay_rate * second + (1.0 - decay_rate) * (gradient * gradient + EPS_SQUARE)
    weight_rms = jnp.sqrt(jnp.mean(weight * weight) + 1e-06)
    weight_new = weight - RELATIVE * weight_rms * gradient * lax.rsqrt(second_new)
    return (gradient, second_new, weight_new, weight_new.astype(jnp.bfloat16))


def add_trees(trees):
    return reduce(lambda left, right: jax.tree.map(jnp.add, left, right), trees)


def per_system(values):
    return values.reshape(SYS_LOC, -1).sum(axis=1)


def build(send_row, arrived_lists, mask_row, atom_count, spec_hot):
    edge_weight = mask_row.astype(jnp.float32)
    arrived_row = arrived_lists[0]
    send_hot = (send_row[None, :] == jnp.arange(atom_count)[:, None]).astype(jnp.float32)
    inc_hot = (arrived_row[None, :] == jnp.arange(atom_count)[:, None]).astype(jnp.float32)

    def fetch_positions(coords):
        return lax.all_to_all(
            jnp.dot(coords, inc_hot, precision=PRECISE),
            "edge",
            split_axis=1,
            concat_axis=1,
            tiled=True,
        )

    def return_positions(cotangent):
        arrived = lax.all_to_all(cotangent, "edge", split_axis=1, concat_axis=1, tiled=True)
        return jnp.einsum("de,ae->da", arrived, inc_hot, precision=PRECISE)

    def collect(values):
        arrived = lax.all_to_all(values, "edge", split_axis=2, concat_axis=2, tiled=True)
        return jnp.einsum("mce,ae->mca", arrived, inc_hot, precision=PRECISE)

    def spread(values):
        per_slot = jnp.einsum("mca,ae->mce", values, inc_hot, precision=PRECISE)
        return lax.all_to_all(per_slot, "edge", split_axis=2, concat_axis=2, tiled=True)

    def scalar_start(params):
        return jnp.einsum("tc,ta->ca", params[0], spec_hot, precision=PRECISE)

    def give_back(aux_cot, recv_cot):
        return return_positions(aux_cot + recv_cot)

    def edge_first(coords, recv_pos, params):
        first_harm, second_harm, bessel = geometry(
            jnp.dot(coords, send_hot, precision=PRECISE), recv_pos
        )
        sender_feat = jnp.dot(scalar_start(params), send_hot, precision=PRECISE)
        return first_messages(
            first_harm, second_harm, bessel, sender_feat, edge_weight, params[1][0], params[2][0]
        )

    def collect_first(values):
        return collect(values)

    def spread_first(values):
        return spread(values)

    def node_one(summed, params):
        return node_first(summed, scalar_start(params), params[3], params[4])

    def edge_second(coords, recv_pos, features, params):
        first_harm, second_harm, bessel = geometry(
            jnp.dot(coords, send_hot, precision=PRECISE), recv_pos
        )
        sender_feat = jnp.einsum("mca,ae->mce", features, send_hot, precision=PRECISE)
        return second_messages(
            first_harm, second_harm, bessel, sender_feat, edge_weight, params[1][1], params[2][1]
        )[None]

    def node_two(features, summed, params):
        return node_second(features, summed[0], params[4], params[5])

    def back_node_two(features, summed, params):
        _, pullback = jax.vjp(
            lambda feature_in, summed_in: node_two(feature_in, summed_in, params), features, summed
        )
        return pullback(jnp.ones((atom_count,), jnp.float32))

    def back_edge_two(coords, recv_pos, features, params, cotangent):
        _, pullback = jax.vjp(
            lambda where_at, recv_at, feature_in: edge_second(
                where_at, recv_at, feature_in, params
            ),
            coords,
            recv_pos,
            features,
        )
        return pullback(cotangent)

    def back_node_one(summed, params, cotangent):
        _, pullback = jax.vjp(lambda summed_in: node_one(summed_in, params), summed)
        return pullback(cotangent)[0]

    def back_edge_one(coords, aux_pos, params, cotangent):
        _, pullback = jax.vjp(
            lambda where_at, aux_at: edge_first(where_at, aux_at, params), coords, aux_pos
        )
        return pullback(cotangent)

    def evaluate(coords, params):
        recv_pos = fetch_positions(coords)
        summed_one = collect_first(edge_first(coords, recv_pos, params))
        features = node_one(summed_one, params)
        summed_two = collect(edge_second(coords, recv_pos, features, params))
        energies = node_two(features, summed_two, params)
        feature_node, summed_two_bar = back_node_two(features, summed_two, params)
        second_bar = spread(summed_two_bar)
        coord_second, recv_second, feature_edge = back_edge_two(
            coords, recv_pos, features, params, second_bar
        )
        feature_bar = feature_node + feature_edge
        first_bar = spread_first(back_node_one(summed_one, params, feature_bar))
        coord_first, aux_first = back_edge_one(coords, recv_pos, params, first_bar)
        forces = -(coord_first + coord_second + give_back(aux_first, recv_second))
        stored = (
            coords,
            recv_pos,
            recv_pos,
            summed_one,
            features,
            summed_two,
            second_bar,
            feature_bar,
            first_bar,
        )
        return (energies, forces, stored)

    def reverse(stored, params, energy_bar, force_bar):
        (
            coords,
            recv_pos,
            aux_pos,
            summed_one,
            features,
            summed_two,
            second_bar,
            feature_bar,
            first_bar,
        ) = stored
        coord_cot = -force_bar
        recv_cot = fetch_positions(coord_cot)
        _, pullback = jax.vjp(back_edge_one, coords, aux_pos, params, first_bar)
        coord_one, aux_one, param_one, first_cot = pullback((coord_cot, recv_cot))
        _, pullback = jax.vjp(back_node_one, summed_one, params, feature_bar)
        summed_one_a, param_two, feature_cot = pullback(collect_first(first_cot))
        _, pullback = jax.vjp(back_edge_two, coords, recv_pos, features, params, second_bar)
        coord_two, recv_two, feature_one, param_three, second_cot = pullback(
            (coord_cot, recv_cot, feature_cot)
        )
        _, pullback = jax.vjp(back_node_two, features, summed_two, params)
        feature_two, summed_two_a, param_four = pullback((feature_cot, collect(second_cot)))
        _, pullback = jax.vjp(node_two, features, summed_two, params)
        feature_three, summed_two_b, param_five = pullback(energy_bar)
        _, pullback = jax.vjp(edge_second, coords, recv_pos, features, params)
        coord_three, recv_three, feature_four, param_six = pullback(
            spread(summed_two_a + summed_two_b)
        )
        _, pullback = jax.vjp(node_one, summed_one, params)
        summed_one_b, param_seven = pullback(
            feature_one + feature_two + feature_three + feature_four
        )
        _, pullback = jax.vjp(edge_first, coords, aux_pos, params)
        coord_four, aux_four, param_eight = pullback(spread_first(summed_one_a + summed_one_b))
        coord_total = (
            coord_one
            + coord_two
            + coord_three
            + coord_four
            + give_back(aux_one + aux_four, recv_two + recv_three)
        )
        param_total = add_trees(
            [
                param_one,
                param_two,
                param_three,
                param_four,
                param_five,
                param_six,
                param_seven,
                param_eight,
            ]
        )
        return (coord_total, param_total)

    return (evaluate, reverse)


def update(summed, params, states):
    embedding, radial_in, radial_out, mix_first, mix_square, readout = params
    (
        embedding_rows,
        embedding_cols,
        radial_in_rows,
        radial_in_cols,
        radial_out_rows,
        radial_out_cols,
        mix_first_rows,
        mix_first_cols,
        mix_square_rows,
        mix_square_cols,
        readout_second,
    ) = states
    emb = factored(summed[0], embedding, embedding_rows, embedding_cols)
    rin = factored(summed[1], radial_in, radial_in_rows, radial_in_cols)
    rout = factored(summed[2], radial_out, radial_out_rows, radial_out_cols)
    mfirst = factored(summed[3], mix_first, mix_first_rows, mix_first_cols)
    msquare = factored(summed[4], mix_square, mix_square_rows, mix_square_cols)
    rdout = unfactored(summed[5], readout, readout_second)
    return (
        summed[6],
        emb[0],
        emb[1],
        emb[2],
        emb[3],
        emb[4],
        rin[0],
        rin[1],
        rin[2],
        rin[3],
        rin[4],
        rout[0],
        rout[1],
        rout[2],
        rout[3],
        rout[4],
        mfirst[0],
        mfirst[1],
        mfirst[2],
        mfirst[3],
        mfirst[4],
        msquare[0],
        msquare[1],
        msquare[2],
        msquare[3],
        msquare[4],
        rdout[0],
        rdout[1],
        rdout[2],
        rdout[3],
    )


F32 = jnp.float32
BF = jnp.bfloat16
MESH = pl.DeviceIdType.MESH
ROOT15 = math.sqrt(15.0)
TILES = 2
CHUNK = 16
LANES_AT_ONCE = 256
N_COMP = 9
PATHS = ((0, 3, 0), (3, 8, 1))
KIND_INIT, KIND_EDGES, KIND_MSG, KIND_COT, KIND_FORCE = 0, 1, 2, 3, 4
KIND_TMSG, KIND_TCOT, KIND_TFORCE, KIND_SCATTER, KIND_GATHER, KIND_SYS = 5, 6, 7, 8, 9, 10
KIND_OWN, KIND_SCATTER_LATE = 11, 12
KINDS = 13


def dot_nn(left, right):
    return lax.dot_general(left, right, (((1,), (0,)), ((), ())), preferred_element_type=F32)


def dot_nt(left, right):
    return lax.dot_general(left, right, (((1,), (1,)), ((), ())), preferred_element_type=F32)


def two_parts(value):
    high = value.astype(BF)
    return high, (value - high.astype(F32)).astype(BF)


def two_parts_f32(value):
    high = value.astype(BF).astype(F32)
    return high, value - high


def three_parts_f32(value):
    high = value.astype(BF).astype(F32)
    rest = value - high
    middle = rest.astype(BF).astype(F32)
    return high, middle, rest - middle


def left_three(weight):
    high, low = two_parts_f32(weight)
    return jnp.concatenate([high, high, low], axis=1).astype(BF)


def right_three(value):
    high, low = two_parts(value)
    return jnp.concatenate([high, low, high], axis=0)


def right_three_small(value):
    high, low = two_parts_f32(value)
    return jnp.concatenate([high, low, high, jnp.zeros_like(high)], axis=0).astype(BF)


def stack_three(value):
    high, middle, low = three_parts_f32(value)
    return jnp.concatenate([high, middle, low, jnp.zeros_like(high)], axis=0).astype(BF)


def join_three(value):
    return value[0:8] + value[8:16] + value[16:24]


def outer_three(left, right):
    left_high, left_low = two_parts(left)
    right_high, right_low = two_parts(right)
    return (
        dot_nt(left_high, right_high)
        + dot_nt(left_low, right_high)
        + dot_nt(left_high, right_low)
    )


def logistic(value):
    return 1.0 / (1.0 + jnp.exp(jnp.minimum(-value, 80.0)))


def silu_slope(value, gate):
    return gate * (1.0 + value * (1.0 - gate))


def silu_bend(value, gate):
    return gate * (1.0 - gate) * (2.0 + value * (1.0 - 2.0 * gate))


def sin_cos_pi(turns):
    whole = jnp.floor(turns + 0.5)
    part = turns - whole
    sign = 1.0 - 2.0 * (whole - 2.0 * jnp.floor(0.5 * whole))
    square = part * part
    sine = 0.0
    for order in range(15, 0, -2):
        sine = sine * square + (-1.0) ** (order // 2) * math.pi**order / math.factorial(order)
    cosine = 0.0
    for order in range(16, -1, -2):
        cosine = cosine * square + (-1.0) ** (order // 2) * math.pi**order / math.factorial(order)
    return sign * (part * sine), sign * cosine


def sin_cos_multiples(sine, cosine):
    sines, cosines = [None, sine], [None, cosine]
    for order in range(2, 9):
        half, rest = order // 2, order - order // 2
        sines.append(sines[half] * cosines[rest] + cosines[half] * sines[rest])
        cosines.append(cosines[half] * cosines[rest] - sines[half] * sines[rest])
    return sines[1:], cosines[1:]


def second_slope(one, two, three, given):
    return (
        ROOT15 * (two * given[0] + three * given[3] + one * given[4]),
        ROOT15 * (one * given[0] + three * given[1] - two * given[4]),
        ROOT15 * (two * given[1] + one * given[3]) + 3.0 * ROOT5 * three * given[2],
    )


def rows_of(value, first, count):
    return [value[first + number : first + number + 1] for number in range(count)]


def step_kernel(
    n_edge,
    n_sys,
    pos_ref,
    vel_ref,
    spec_ref,
    send_ref,
    recv_ref,
    mask_ref,
    emb_ref,
    rin_ref,
    rout_ref,
    mfirst_ref,
    msquare_ref,
    readout_ref,
    total_ref,
    scratch,
):
    s = scratch
    channels = emb_ref.shape[1]
    wide = N_COMP * channels
    atoms = pos_ref.shape[1]
    tiles = TILES
    group = n_edge // tiles
    lanes = group * atoms
    chunks = channels // CHUNK
    held_group = lax.axis_index("sys")
    held_part = lax.axis_index("edge")
    my_group = lax.div(held_part, 2)
    core = lax.rem(held_part, 2)
    me = 2 * held_group + core
    half = lax.div(me, group)
    half_atoms = atoms // SYS_LOC

    def peer(distance):
        return jnp.bitwise_xor(me, distance)

    def place_of(which_group, part):
        return {"sys": lax.div(part, 2), "edge": 2 * which_group + lax.rem(part, 2)}

    def remote(source, target, kind, other):
        return pltpu.make_async_remote_copy(
            src_ref=source,
            dst_ref=target,
            send_sem=s.send_sem.at[kind, other],
            recv_sem=s.recv_sem.at[kind, me],
            device_id=place_of(my_group, other),
            device_id_type=MESH,
        )

    def landed(target, kind, other):
        pltpu.make_async_remote_copy(
            src_ref=target,
            dst_ref=target,
            send_sem=s.send_sem.at[kind, other],
            recv_sem=s.recv_sem.at[kind, other],
            device_id=place_of(my_group, other),
            device_id_type=MESH,
        ).wait_recv()

    def each_peer(action):
        def body(distance, carry):
            action(peer(distance))
            return carry

        lax.fori_loop(1, n_edge, body, 0)

    def each_tile(action):
        for index in range(tiles):
            action(index)

    def loop(count, action, unroll=False):
        def body(index, carry):
            action(index)
            return carry

        lax.fori_loop(0, count, body, 0, unroll=unroll)

    def chunk_at(base, index):
        return slice(base + index * CHUNK, base + (index + 1) * CHUNK)

    barrier = pltpu.get_barrier_semaphore()

    def greet(device):
        pl.semaphore_signal(barrier, inc=1, device_id=device, device_id_type=MESH)

    stays = held_group == my_group

    def each_given(action):
        def body(part, carry):
            @pl.when(jnp.logical_not(jnp.logical_and(stays, part == held_part)))
            def _():
                action(part)

            return carry

        lax.fori_loop(0, n_edge, body, 0)

    def each_group(action):
        def body(distance, carry):
            action(lax.rem(my_group + distance, n_sys))
            return carry

        lax.fori_loop(1, n_sys, body, 0)

    each_given(lambda part: greet({"sys": my_group, "edge": part}))
    each_peer(lambda other: greet(place_of(my_group, other)))
    each_group(lambda other: greet({"edge": 2 * other + core}))

    s.start_out[...] = jnp.concatenate([pos_ref[...], vel_ref[...], pos_ref[0:2]], axis=0)
    species_rows = jnp.broadcast_to(spec_ref[...].reshape(1, atoms), (16 - 3 * EVALS, atoms))
    for other in range(n_edge):
        at = slice(other * atoms, (other + 1) * atoms)
        for part, ref in enumerate((send_ref, recv_ref, mask_ref)):
            s.lists_out[other, part * EVALS : (part + 1) * EVALS, :] = ref[:, at]
        s.lists_out[other, 3 * EVALS :, :] = species_rows

    pl.semaphore_wait(barrier, 2 * n_edge - 1 + n_sys - 1 - jnp.where(stays, 1, 0))

    def given(source, target, kind, part):
        return pltpu.make_async_remote_copy(
            src_ref=source,
            dst_ref=target,
            send_sem=s.send_sem.at[kind, part],
            recv_sem=s.recv_sem.at[kind, held_part],
            device_id=place_of(held_group, part),
            device_id_type=MESH,
        )

    def taken(target, kind, part):
        pltpu.make_async_remote_copy(
            src_ref=target,
            dst_ref=target,
            send_sem=s.send_sem.at[kind, part],
            recv_sem=s.recv_sem.at[kind, part],
            device_id={"sys": my_group, "edge": part},
            device_id_type=MESH,
        ).wait_recv()

    def give_atoms(part):
        return given(s.start_out, s.start_float.at[held_part], KIND_INIT, part)

    def give_slots(part):
        return given(s.lists_out.at[part], s.lists_in.at[held_part], KIND_EDGES, part)

    def give_lists():
        return given(s.lists_out, s.lists_own, KIND_OWN, held_part)

    def start_first(part):
        give_atoms(part).start()
        give_slots(part).start()

    each_given(start_first)

    @pl.when(jnp.logical_not(stays))
    def _():
        give_lists().start()

    @pl.when(stays)
    def _():
        s.start_float[me] = s.start_out[...]
        s.lists_in[me] = s.lists_out[me]
        s.lists_own[...] = s.lists_out[...]

    for layer in range(2):
        w_in = rin_ref[layer]
        high, low = two_parts_f32(w_in)
        zero = jnp.zeros_like(high)
        s.w_in_left[layer] = jnp.concatenate([high, high, low, zero], axis=0).T.astype(BF)
        s.w_in_back[layer] = jnp.concatenate(
            [
                jnp.concatenate([high, high], axis=1),
                jnp.concatenate([low, zero], axis=1),
            ],
            axis=0,
        ).astype(BF)
        w_out = rout_ref[layer]
        s.w_out_left[layer] = left_three(w_out.T)
        s.w_out_back[layer] = jnp.concatenate(two_parts_f32(w_out), axis=0).astype(BF)
    s.mf_left[...] = left_three(mfirst_ref[...].T)
    s.mf_back[...] = left_three(mfirst_ref[...])
    for number in range(3):
        s.ms_left[number] = left_three(msquare_ref[number].T)
        s.ms_back[number] = left_three(msquare_ref[number])
    emb_pad = jnp.concatenate(
        [emb_ref[...], jnp.zeros((16 - emb_ref.shape[0], channels), F32)], axis=0
    )
    s.emb_left[...] = jnp.concatenate(list(three_parts_f32(emb_pad)), axis=0).T.astype(BF)
    s.readout_col[...] = jnp.broadcast_to(
        readout_ref[...].reshape(1, channels), (atoms, channels)
    ).T
    for ref in (
        s.grad_emb,
        s.grad_in,
        s.grad_out,
        s.grad_mf,
        s.grad_ms,
        s.grad_ro,
        s.grad_second,
        s.grad_first,
    ):
        ref[...] = jnp.zeros_like(ref)

    def first_landed(part):
        taken(s.start_float.at[part], KIND_INIT, part)
        taken(s.lists_in.at[part], KIND_EDGES, part)

    each_given(first_landed)

    @pl.when(jnp.logical_not(stays))
    def _():
        taken(s.lists_own, KIND_OWN, me)

    def first_sent(part):
        give_atoms(part).wait_send()
        give_slots(part).wait_send()

    each_given(first_sent)

    @pl.when(jnp.logical_not(stays))
    def _():
        give_lists().wait_send()

    def species_values(hot):
        return dot_nn(s.emb_left[...], jnp.concatenate([hot, hot, hot], axis=0))

    own_species = s.lists_in[me, 3 * EVALS : 3 * EVALS + 1, :]
    own_species = lax.broadcasted_iota(jnp.int32, (16, atoms), 0) == own_species
    s.own_kind[...] = own_species.astype(F32).astype(BF)
    s.start_scalar[...] = species_values(s.own_kind[...])
    s.rows[...] = jnp.zeros_like(s.rows)
    for axis in range(3):
        s.place[axis] = s.start_float[:, axis, :]
        s.speed[axis] = s.start_float[:, 3 + axis, :]

    def one_hots(number):
        atom_row = lax.broadcasted_iota(jnp.int32, (atoms, atoms), 0)

        def hot(row):
            return (atom_row == row).astype(F32).astype(BF)

        def put_own(tile, at, value):
            s.own_hot[number, tile, 0:atoms, at] = value
            s.own_hot[number, tile, atoms:, at] = value

        def body(index):
            for part in range(group):
                other = index * group + part
                at = pl.ds(part * atoms, atoms)
                out_list = s.lists_own.at[other]
                in_list = s.lists_in.at[other]
                sender = out_list[pl.ds(number, 1), :]
                receiver = out_list[pl.ds(EVALS + number, 1), :]
                mask = out_list[pl.ds(2 * EVALS + number, 1), :]
                put_own(index, at, hot(sender))
                s.far_hot[number, index, :, at] = hot(jnp.where(mask == 0, -1, receiver))
                sender = in_list[pl.ds(number, 1), :]
                receiver = in_list[pl.ds(EVALS + number, 1), :]
                mask = in_list[pl.ds(2 * EVALS + number, 1), :]
                sender_hot = hot(sender)
                put_own(tiles + index, at, hot(jnp.where(mask == 0, -1, receiver)))
                s.far_hot[number, tiles + index, :, at] = sender_hot
                species = in_list[pl.ds(3 * EVALS, 1), :]
                kinds = lax.broadcasted_iota(jnp.int32, (16, atoms), 0)
                species_hot = (kinds == species).astype(F32).astype(BF)
                s.kind_hot[number, index, :, at] = dot_nn(species_hot, sender_hot).astype(BF)
            s.kind_value[number, index] = species_values(s.kind_hot[number, index])

        each_tile(body)

    def table(rows):
        for axis in range(3):
            s.rows[:, axis, :] = rows[axis]
        for other in range(n_edge):
            s.pieces[other] = stack_three(s.rows[other])

    def edge_difference(number, index):
        sign = jnp.where(index < tiles, 1.0, -1.0)
        own = dot_nn(s.pieces[me], s.own_hot[number, index, 0:atoms, :])
        first = lax.rem(index, tiles) * group
        far = [
            dot_nn(
                s.pieces[first + part],
                s.far_hot[number, index, :, part * atoms : (part + 1) * atoms],
            )
            for part in range(group)
        ]
        return sign * join_three(own - jnp.concatenate(far, axis=1))

    def scatter_rows(number, target):
        parts = [stack_three(s.edge_rows[index]) for index in range(2 * tiles)]
        own = 0.0
        for index in range(2 * tiles):
            found = dot_nt(parts[index], s.own_hot[number, index, 0:atoms, :])
            own = own + found if index < tiles else own - found
        s.row_own[...] = join_three(own)
        for other in range(n_edge):
            index, part = other // group, other % group
            at = slice(part * atoms, (part + 1) * atoms)
            total = join_three(
                dot_nt(parts[tiles + index][:, at], s.far_hot[number, tiles + index, :, at])
                - dot_nt(parts[index][:, at], s.far_hot[number, index, :, at])
            )
            for axis in range(3):
                target[axis, other : other + 1, :] = total[axis : axis + 1]
        for axis in range(3):
            target[axis, pl.ds(me, 1), :] += s.row_own[axis : axis + 1, :]

    def geometry(number, index):
        offset = edge_difference(number, index)
        geo = s.geo.at[number, index]
        radius = jnp.sqrt(jnp.sum(offset * offset, axis=0, keepdims=True) + SOFTEN)
        inverse = 1.0 / radius
        unit = offset * inverse
        one, two, three = rows_of(unit, 0, 3)
        geo[0:3, :] = ROOT3 * unit[0:3]
        geo[3:4, :] = ROOT15 * one * two
        geo[4:5, :] = ROOT15 * two * three
        geo[5:6, :] = 0.5 * ROOT5 * (3.0 * three * three - 1.0)
        geo[6:7, :] = ROOT15 * one * three
        geo[7:8, :] = 0.5 * ROOT15 * (one * one - two * two)
        t = radius * (1.0 / CUTOFF)
        sines, cosines = sin_cos_multiples(*sin_cos_pi(t))
        sines = jnp.concatenate(sines, axis=0)
        cosines = jnp.concatenate(cosines, axis=0)
        t2 = t * t
        t4 = t2 * t2
        amount = math.sqrt(2.0 / CUTOFF) * inverse
        env = 1.0 - t4 * t2 * (28.0 - 48.0 * t + 21.0 * t2)
        env_one = -168.0 / CUTOFF * t4 * t * (1.0 - t) * (1.0 - t)
        env_two = -168.0 / CUTOFF**2 * t4 * (1.0 - t) * (5.0 - 7.0 * t)
        front = amount * env
        front_one = amount * (env_one - env * inverse)
        front_two = amount * (env_two - 2.0 * inverse * (env_one - env * inverse))
        waves = (lax.broadcasted_iota(jnp.int32, (NB, 1), 0) + 1).astype(F32) * (
            math.pi / CUTOFF
        )
        geo[8:16, :] = front * sines
        geo[16:24, :] = front_one * sines + front * waves * cosines
        geo[24:32, :] = (
            front_two * sines + 2.0 * front_one * waves * cosines - front * waves * waves * sines
        )
        geo[32:35, :] = unit[0:3]
        geo[35:36, :] = inverse

    def first_back(number, index):
        geo = s.geo.at[number, index]
        bars = s.geo_bar.at[number, index]
        ybar = rows_of(bars[0:8, :], 0, 8)
        slope = jnp.sum(bars[8:16, :] * geo[16:24, :], axis=0, keepdims=True)
        units = rows_of(geo[32:40, :], 0, 3)
        inverse = geo[35:36, :]
        extra = second_slope(*units, ybar[3:])
        back = [ROOT3 * ybar[axis] + extra[axis] for axis in range(3)]
        along = back[0] * units[0] + back[1] * units[1] + back[2] * units[2]
        rest = slope - along * inverse
        for axis in range(3):
            bars[16 + axis : 17 + axis, :] = back[axis]
            s.edge_rows[index, axis : axis + 1, :] = back[axis] * inverse + rest * units[axis]
        bars[19:20, :] = rest

    def geometry_tangent(number, index):
        move = edge_difference(number, index)
        geo = s.geo.at[number, index]
        out = s.geo_dot.at[index]
        inverse = geo[35:36, :]
        one, two, three = rows_of(geo[32:40, :], 0, 3)
        moves = rows_of(move, 0, 3)
        speed = one * moves[0] + two * moves[1] + three * moves[2]
        d_one, d_two, d_three = [
            (amount - unit * speed) * inverse for amount, unit in zip(moves, (one, two, three))
        ]
        out[0:1, :] = ROOT3 * d_one
        out[1:2, :] = ROOT3 * d_two
        out[2:3, :] = ROOT3 * d_three
        out[3:4, :] = ROOT15 * (d_one * two + one * d_two)
        out[4:5, :] = ROOT15 * (d_two * three + two * d_three)
        out[5:6, :] = 3.0 * ROOT5 * three * d_three
        out[6:7, :] = ROOT15 * (d_one * three + one * d_three)
        out[7:8, :] = ROOT15 * (one * d_one - two * d_two)
        out[8:16, :] = geo[16:24, :] * speed
        out[16:17, :] = d_one
        out[17:18, :] = d_two
        out[18:19, :] = d_three
        out[19:20, :] = speed
        out[20:23, :] = move[0:3]

    def second_back(number, index, hats):
        geo = s.geo.at[number, index]
        bars = s.geo_bar.at[number, index]
        dots = s.geo_dot.at[index]
        units = rows_of(geo[32:40, :], 0, 3)
        inverse = geo[35:36, :]
        turns = rows_of(dots[16:24, :], 0, 3)
        speed = dots[19:20, :]
        moves = rows_of(dots[16:24, :], 4, 3)
        back = rows_of(bars[16:24, :], 0, 3)
        rest = bars[19:20, :]
        yhat = rows_of(hats, 0, 8)
        ybar = rows_of(bars[0:8, :], 0, 8)
        extra = second_slope(*units, yhat[3:])
        more = second_slope(*turns, ybar[3:])
        radial_hat = jnp.sum(
            hats[8:16] * geo[16:24, :] + speed * (bars[8:16, :] * geo[24:32, :]),
            axis=0,
            keepdims=True,
        ) - inverse * (turns[0] * back[0] + turns[1] * back[1] + turns[2] * back[2])
        unit_hat = [
            ROOT3 * yhat[axis]
            + extra[axis]
            + more[axis]
            - speed * inverse * back[axis]
            + rest * moves[axis]
            for axis in range(3)
        ]
        along = unit_hat[0] * units[0] + unit_hat[1] * units[1] + unit_hat[2] * units[2]
        left = radial_hat - along * inverse
        for axis in range(3):
            s.edge_rows[index, axis : axis + 1, :] = unit_hat[axis] * inverse + left * units[axis]

    def radial_forward(layer, number, index, basis):
        before = dot_nn(s.w_in_left[layer], right_three_small(basis))
        s.hidden[layer, number, index] = before
        gate = logistic(before)
        s.radial[layer, number, index] = dot_nn(
            s.w_out_left[layer], right_three(before * gate)
        )

    def radial_tangent(layer, number, index, basis_dot):
        before = s.hidden[layer, number, index]
        before_dot = dot_nn(s.w_in_left[layer], right_three_small(basis_dot))
        s.hidden_dot[layer, index] = before_dot
        gate = logistic(before)
        s.radial_dot[layer, index] = dot_nn(
            s.w_out_left[layer], right_three(silu_slope(before, gate) * before_dot)
        )

    def rows_pair(value):
        return jnp.concatenate(two_parts(value), axis=0)

    def hidden_back(layer, pair):
        half_rows = 3 * channels
        left = s.w_out_back[layer]
        found = dot_nn(left, pair[0:half_rows])
        return found[0:channels] + found[channels:] + dot_nn(left[0:channels], pair[half_rows:])

    def basis_back(layer, pair):
        found = dot_nn(s.w_in_back[layer], pair)
        return found[0:8] + found[8:16]

    def radial_back(layer, number, index):
        hidden_bar = hidden_back(layer, s.r_pair[layer, index])
        s.hidden_bar[layer, number, index] = hidden_bar
        before = s.hidden[layer, number, index]
        before_bar = silu_slope(before, logistic(before)) * hidden_bar
        return basis_back(layer, rows_pair(before_bar))

    def radial_second(layer, number, index, last):
        hidden_hat = hidden_back(layer, s.h_pair[layer, index])
        before = s.hidden[layer, number, index]
        before_dot = s.hidden_dot[layer, index]
        hidden_bar = s.hidden_bar[layer, number, index]
        gate = logistic(before)
        slope = silu_slope(before, gate)
        before_hat = slope * hidden_hat + silu_bend(before, gate) * before_dot * hidden_bar
        s.out_pair[layer, index] = rows_pair(before * gate)
        hat_pair = rows_pair(before_hat)
        s.hat_pair[layer, index] = hat_pair
        return None if last else basis_back(layer, hat_pair)

    def radial_gradients(layer, number):
        for index in range(tiles):
            s.grad_out[layer] += dot_nt(s.h_pair[layer, index], s.out_pair[layer, index])
            tile = index if layer == 1 else tiles + index
            basis = jnp.concatenate(two_parts_f32(s.geo[number, tile, 8:16, :]), axis=0)
            s.grad_in[layer] += dot_nt(basis.astype(BF), s.hat_pair[layer, index])

    def early_gradients(layer, number, index):
        before = s.hidden[layer, number, index]
        slope = silu_slope(before, logistic(before))
        dot_pair = rows_pair(slope * s.hidden_dot[layer, index])
        bar_pair = rows_pair(slope * s.hidden_bar[layer, number, index])
        s.grad_out[layer] += dot_nt(s.r_pair[layer, index], dot_pair)
        tile = index if layer == 1 else tiles + index
        basis_dot = jnp.concatenate(two_parts_f32(s.geo_dot[tile, 8:16, :]), axis=0)
        s.grad_in[layer] += dot_nt(basis_dot.astype(BF), bar_pair)

    def first_early(number, index):
        geo = s.geo.at[number, tiles + index]
        cot = s.first_cot.at[number, index]
        kind = s.kind_value.at[number, index]

        def body(c, lane):
            value = kind[chunk_at(0, c), lane]
            y = harmonic_rows(geo, lane)
            put_pair(s.r_pair.at[0, index], 0, c, lane, cot[chunk_at(0, c), lane] * value)
            for first, last, path in ((0, 3, 1), (3, 8, 2)):
                total = 0.0
                for k in range(first, last):
                    total = total + cot[chunk_at((k + 1) * channels, c), lane] * y[k]
                put_pair(s.r_pair.at[0, index], path, c, lane, total * value)

        over_chunks(body)
        early_gradients(0, number, index)

    def second_early(number, index):
        cot = s.msg_cot.at[number, index]
        feat = s.feat.at[number, index]

        def body(c, lane):
            at = chunk_at(0, c)
            given = cot[at, lane]
            put_pair(s.r_pair.at[1, index], 0, c, lane, feat[at, lane] * given)
            for path in (1, 2):
                along = s.along[number, index, chunk_at((path - 1) * channels, c), lane]
                put_pair(s.r_pair.at[1, index], path, c, lane, along * given)

        over_chunks(body)
        early_gradients(1, number, index)

    def all_early(number):
        for index in range(tiles):
            first_early(number, index)
        for first, last, path in PATHS:
            bars = [s.raw_bar[number, k * channels : (k + 1) * channels, :] for k in range(first, last)]
            s.grad_ms[path] += outer_three(
                side_by_side(s.agg_dot, first, last), jnp.concatenate(bars, axis=1)
            )
        s.grad_mf[...] += outer_three(s.mixed_bar[number], part_of(s.agg_dot, 0))

    def kind_gradients(number):
        for index in range(tiles):
            kinds = s.kind_hot[number, index]
            s.grad_emb[...] += dot_nt(kinds, s.v_high[index]) + dot_nt(kinds, s.v_low[index])
        high, low = two_parts(s.scalar_hat[...])
        s.grad_emb[...] += dot_nt(s.own_kind[...], high) + dot_nt(s.own_kind[...], low)

    def node_gradients(number):
        agg = s.agg.at[number]
        for first, last, path in PATHS:
            hats = [s.raw_hat[k * channels : (k + 1) * channels, :] for k in range(first, last)]
            s.grad_ms[path] += outer_three(
                side_by_side(agg, first, last), jnp.concatenate(hats, axis=1)
            )
        s.grad_ms[2] += outer_three(s.agg_two[number], s.last_hat[...]) + outer_three(
            s.agg_two_dot[...], s.last_bar[...]
        )
        s.grad_mf[...] += outer_three(s.mixed_hat[...], part_of(agg, 0))

    def put_pieces(high_ref, low_ref, lane, at, value):
        high, low = two_parts(value)
        high_ref[at, lane] = high
        low_ref[at, lane] = low

    def put_pair(ref, path, c, lane, value):
        high, low = two_parts(value)
        ref[chunk_at(path * channels, c), lane] = high
        ref[chunk_at((3 + path) * channels, c), lane] = low

    def add_scatter(index, hot):
        found = dot_nt(jnp.concatenate([s.m_high[index], s.m_low[index]], axis=0), hot)
        s.sum_wide[...] += found[0:wide] + found[wide:]

    def harmonic_rows(ref, lane):
        return [ref[row : row + 1, lane] for row in range(8)]

    def lane_parts():
        return [slice(first, first + LANES_AT_ONCE) for first in range(0, lanes, LANES_AT_ONCE)]

    def over_chunks(body):
        for lane in lane_parts():
            for c in range(chunks):
                body(c, lane)

    def over_chunks_sum(body):
        found = []
        for lane in lane_parts():
            sums = (0.0,) * 8
            for c in range(chunks):
                sums = body(c, lane, sums)
            found.append(sum_rows(sums))
        return jnp.concatenate(found, axis=1)

    def fold(value):
        return value[0:8] + value[8:16]

    def sum_rows(parts):
        if not hasattr(parts[0], "shape"):
            return jnp.zeros((8, LANES_AT_ONCE), F32)
        return jnp.concatenate([jnp.sum(part, axis=0, keepdims=True) for part in parts], axis=0)

    def first_forward(number, index):
        tile = tiles + index
        geo = s.geo.at[number, tile]
        radial_forward(0, number, index, geo[8:16, :])
        rad = s.radial.at[0, number, index]
        kind = s.kind_value.at[number, index]

        def body(c, lane):
            value = kind[chunk_at(0, c), lane]
            y = harmonic_rows(geo, lane)
            put_pieces(s.m_high.at[index], s.m_low.at[index], lane, chunk_at(0, c), rad[chunk_at(0, c), lane] * value)
            vector = rad[chunk_at(channels, c), lane] * value
            tensor = rad[chunk_at(2 * channels, c), lane] * value
            for k in range(8):
                part = (vector if k < 3 else tensor) * y[k]
                put_pieces(s.m_high.at[index], s.m_low.at[index], lane, chunk_at((k + 1) * channels, c), part)

        over_chunks(body)
        add_scatter(index, s.own_hot[number, tile, 0:atoms, :])

    def first_tangent(number, index):
        tile = tiles + index
        geo = s.geo.at[number, tile]
        dots = s.geo_dot.at[tile]
        radial_tangent(0, number, index, dots[8:16, :])
        rad = s.radial.at[0, number, index]
        rad_dot = s.radial_dot.at[0, index]
        kind = s.kind_value.at[number, index]

        def body(c, lane):
            value = kind[chunk_at(0, c), lane]
            y = harmonic_rows(geo, lane)
            y_dot = harmonic_rows(dots, lane)
            put_pieces(s.m_high.at[index], s.m_low.at[index], lane, chunk_at(0, c), rad_dot[chunk_at(0, c), lane] * value)
            vector = rad[chunk_at(channels, c), lane] * value
            tensor = rad[chunk_at(2 * channels, c), lane] * value
            vector_dot = rad_dot[chunk_at(channels, c), lane] * value
            tensor_dot = rad_dot[chunk_at(2 * channels, c), lane] * value
            for k in range(8):
                base, move = (vector, vector_dot) if k < 3 else (tensor, tensor_dot)
                part = move * y[k] + base * y_dot[k]
                put_pieces(s.m_high.at[index], s.m_low.at[index], lane, chunk_at((k + 1) * channels, c), part)

        over_chunks(body)
        add_scatter(index, s.own_hot[number, tile, 0:atoms, :])

    def gather_wide(hot):
        return dot_nn(s.a_pair[...], hot)

    def first_reverse(number, index):
        tile = tiles + index
        geo = s.geo.at[number, tile]
        s.first_cot[number, index] = gather_wide(s.own_hot[number, tile])
        cot = s.first_cot.at[number, index]
        rad = s.radial.at[0, number, index]
        kind = s.kind_value.at[number, index]

        def body(c, lane, sums):
            value = kind[chunk_at(0, c), lane]
            y = harmonic_rows(geo, lane)
            put_pair(s.r_pair.at[0, index], 0, c, lane, cot[chunk_at(0, c), lane] * value)
            sums = list(sums)
            for first, last, path in ((0, 3, 1), (3, 8, 2)):
                base = rad[chunk_at(path * channels, c), lane] * value
                total = 0.0
                for k in range(first, last):
                    given = cot[chunk_at((k + 1) * channels, c), lane]
                    total = total + given * y[k]
                    sums[k] = sums[k] + fold(base * given)
                put_pair(s.r_pair.at[0, index], path, c, lane, total * value)
            return tuple(sums)

        sums = over_chunks_sum(body)
        s.geo_bar[number, tile, 0:8, :] = sums
        s.geo_bar[number, tile, 8:16, :] = radial_back(0, number, index)
        first_back(number, tile)

    def first_second(number, index, final):
        tile = tiles + index
        geo = s.geo.at[number, tile]
        dots = s.geo_dot.at[tile]
        s.feat_dot[index] = gather_wide(s.own_hot[number, tile])
        hat = s.feat_dot.at[index]
        cot = s.first_cot.at[number, index]
        rad = s.radial.at[0, number, index]
        rad_dot = s.radial_dot.at[0, index]
        kind = s.kind_value.at[number, index]

        def body(c, lane, sums):
            value = kind[chunk_at(0, c), lane]
            y = harmonic_rows(geo, lane)
            y_dot = harmonic_rows(dots, lane)
            sums = list(sums)
            total = cot[chunk_at(0, c), lane]
            total_hat = hat[chunk_at(0, c), lane]
            put_pair(s.h_pair.at[0, index], 0, c, lane, total_hat * value)
            value_hat = rad[chunk_at(0, c), lane] * total_hat + rad_dot[chunk_at(0, c), lane] * total
            for first, last, path in ((0, 3, 1), (3, 8, 2)):
                rad_here = rad[chunk_at(path * channels, c), lane]
                rad_move = rad_dot[chunk_at(path * channels, c), lane]
                base = rad_here * value
                move = rad_move * value
                total = 0.0
                total_hat = 0.0
                for k in range(first, last):
                    given = cot[chunk_at((k + 1) * channels, c), lane]
                    given_hat = hat[chunk_at((k + 1) * channels, c), lane]
                    total = total + given * y[k]
                    total_hat = total_hat + (given_hat * y[k] + given * y_dot[k])
                    if not final:
                        sums[k] = sums[k] + fold(base * given_hat + move * given)
                put_pair(s.h_pair.at[0, index], path, c, lane, total_hat * value)
                value_hat = value_hat + rad_here * total_hat + rad_move * total
            put_pieces(s.v_high.at[index], s.v_low.at[index], lane, chunk_at(0, c), value_hat)
            return tuple(sums)

        sums = over_chunks_sum(body)
        basis_hat = radial_second(0, number, index, final)
        if not final:
            second_back(number, tile, jnp.concatenate([sums, basis_hat], axis=0))

    def gather_far(ref, number, index):
        found = []
        for part in range(group):
            pair = rows_pair(ref[index * group + part])
            here = dot_nn(pair, s.far_hot[number, index, :, part * atoms : (part + 1) * atoms])
            found.append(here[0:channels] + here[channels:])
        return jnp.concatenate(found, axis=1)

    def put_messages(number, index):
        for part in range(group):
            at = slice(part * atoms, (part + 1) * atoms)
            hot = s.far_hot[number, index, :, at]
            pair = jnp.concatenate([s.v_high[index, :, at], s.v_low[index, :, at]], axis=0)
            found = dot_nt(pair, hot)
            s.msg_out[index * group + part] = found[0:channels] + found[channels:]

    def near_peer(distance):
        return half * group + jnp.bitwise_xor(lax.rem(me, group), distance)

    def far_peer(distance):
        return (1 - half) * group + jnp.bitwise_xor(lax.rem(me, group), group - 1 - distance)

    def message_to(other, kind):
        return remote(s.msg_out.at[other], s.msg_in.at[me], kind, other)

    def exchange_messages(number, kind, make):
        make(number, 1 - half)
        put_messages(number, 1 - half)
        for distance in range(group):
            message_to(far_peer(distance), kind).start()
        make(number, half)
        put_messages(number, half)
        for distance in range(group - 1, 0, -1):
            message_to(near_peer(distance), kind).start()

    def second_forward(number, index):
        geo = s.geo.at[number, index]
        radial_forward(1, number, index, geo[8:16, :])
        s.feat[number, index] = gather_wide(s.own_hot[number, index])
        feat = s.feat.at[number, index]
        rad = s.radial.at[1, number, index]

        def body(c, lane):
            y = harmonic_rows(geo, lane)
            total = rad[chunk_at(0, c), lane] * feat[chunk_at(0, c), lane]
            for first, last, path in ((0, 3, 1), (3, 8, 2)):
                along = 0.0
                for k in range(first, last):
                    along = along + feat[chunk_at((k + 1) * channels, c), lane] * y[k]
                s.along[number, index, chunk_at((path - 1) * channels, c), lane] = along
                total = total + rad[chunk_at(path * channels, c), lane] * along
            put_pieces(s.v_high.at[index], s.v_low.at[index], lane, chunk_at(0, c), total)

        over_chunks(body)

    def second_tangent(number, index):
        geo = s.geo.at[number, index]
        dots = s.geo_dot.at[index]
        radial_tangent(1, number, index, dots[8:16, :])
        s.feat_dot[index] = gather_wide(s.own_hot[number, index])
        feat = s.feat.at[number, index]
        feat_dot = s.feat_dot.at[index]
        rad = s.radial.at[1, number, index]
        rad_dot = s.radial_dot.at[1, index]

        def body(c, lane):
            y = harmonic_rows(geo, lane)
            y_dot = harmonic_rows(dots, lane)
            at = chunk_at(0, c)
            total = rad_dot[at, lane] * feat[at, lane] + rad[at, lane] * feat_dot[at, lane]
            for first, last, path in ((0, 3, 1), (3, 8, 2)):
                move = 0.0
                for k in range(first, last):
                    here = chunk_at((k + 1) * channels, c)
                    move = move + (feat_dot[here, lane] * y[k] + feat[here, lane] * y_dot[k])
                here = chunk_at((path - 1) * channels, c)
                s.along_dot[index, here, lane] = move
                here_rad = chunk_at(path * channels, c)
                total = total + (
                    rad_dot[here_rad, lane] * s.along[number, index, here, lane]
                    + rad[here_rad, lane] * move
                )
            put_pieces(s.v_high.at[index], s.v_low.at[index], lane, at, total)

        over_chunks(body)

    def second_reverse(number, index):
        geo = s.geo.at[number, index]
        s.msg_cot[number, index] = gather_far(s.cot_all, number, index)
        cot = s.msg_cot.at[number, index]
        feat = s.feat.at[number, index]
        rad = s.radial.at[1, number, index]

        def body(c, lane, sums):
            y = harmonic_rows(geo, lane)
            at = chunk_at(0, c)
            given = cot[at, lane]
            sums = list(sums)
            put_pair(s.r_pair.at[1, index], 0, c, lane, feat[at, lane] * given)
            put_pieces(s.m_high.at[index], s.m_low.at[index], lane, at, rad[at, lane] * given)
            for first, last, path in ((0, 3, 1), (3, 8, 2)):
                here = chunk_at(path * channels, c)
                along = s.along[number, index, chunk_at((path - 1) * channels, c), lane]
                put_pair(s.r_pair.at[1, index], path, c, lane, along * given)
                base = rad[here, lane] * given
                for k in range(first, last):
                    wide_at = chunk_at((k + 1) * channels, c)
                    put_pieces(s.m_high.at[index], s.m_low.at[index], lane, wide_at, base * y[k])
                    sums[k] = sums[k] + fold(base * feat[wide_at, lane])
            return tuple(sums)

        sums = over_chunks_sum(body)
        s.geo_bar[number, index, 0:8, :] = sums
        s.geo_bar[number, index, 8:16, :] = radial_back(1, number, index)
        first_back(number, index)
        add_scatter(index, s.own_hot[number, index, 0:atoms, :])

    def second_second(number, index, final):
        geo = s.geo.at[number, index]
        dots = s.geo_dot.at[index]
        s.msg_hat[index] = gather_far(s.cot_all, number, index)
        cot = s.msg_cot.at[number, index]
        feat = s.feat.at[number, index]
        feat_dot = s.feat_dot.at[index]
        rad = s.radial.at[1, number, index]
        rad_dot = s.radial_dot.at[1, index]

        def body(c, lane, sums):
            y = harmonic_rows(geo, lane)
            y_dot = harmonic_rows(dots, lane)
            at = chunk_at(0, c)
            given = cot[at, lane]
            given_hat = s.msg_hat[index, at, lane]
            sums = list(sums)
            put_pair(s.h_pair.at[1, index], 0, c, lane, feat[at, lane] * given_hat + feat_dot[at, lane] * given)
            put_pieces(s.m_high.at[index], s.m_low.at[index], lane, at, rad[at, lane] * given_hat + rad_dot[at, lane] * given)
            for first, last, path in ((0, 3, 1), (3, 8, 2)):
                here = chunk_at(path * channels, c)
                along_at = chunk_at((path - 1) * channels, c)
                along = s.along[number, index, along_at, lane]
                along_dot = s.along_dot[index, along_at, lane]
                put_pair(s.h_pair.at[1, index], path, c, lane, along * given_hat + along_dot * given)
                base = rad[here, lane] * given
                base_hat = rad[here, lane] * given_hat + rad_dot[here, lane] * given
                for k in range(first, last):
                    wide_at = chunk_at((k + 1) * channels, c)
                    put_pieces(s.m_high.at[index], s.m_low.at[index], lane, wide_at, base_hat * y[k] + base * y_dot[k])
                    if not final:
                        sums[k] = sums[k] + fold(
                            base_hat * feat[wide_at, lane] + base * feat_dot[wide_at, lane]
                        )
            return tuple(sums)

        sums = over_chunks_sum(body)
        basis_hat = radial_second(1, number, index, final)
        if not final:
            second_back(number, index, jnp.concatenate([sums, basis_hat], axis=0))
        add_scatter(index, s.own_hot[number, index, 0:atoms, :])

    def part_of(ref, component):
        return ref[component * channels : (component + 1) * channels, :]

    def side_by_side(ref, first, last):
        return jnp.concatenate([part_of(ref, k + 1) for k in range(first, last)], axis=1)

    def linear(left, value):
        return dot_nn(left, right_three(value))

    def keep_wide(component, value):
        high, low = two_parts(value)
        at = slice(component * channels, (component + 1) * channels)
        s.a_pair[at, 0:atoms] = high
        s.a_pair[at, atoms:] = low

    def node_first_forward(number):
        s.agg[number] = INV_NEIGH * s.sum_wide[...]
        agg = s.agg.at[number]
        mixed = linear(s.mf_left[...], part_of(agg, 0))
        s.mixed[number] = mixed
        before, gate_one, gate_two = [mixed[i * channels : (i + 1) * channels] for i in range(3)]
        scalar = s.start_scalar[...] + before * logistic(before)
        s.scalar[number] = scalar
        keep_wide(0, scalar)
        gates = (logistic(gate_one), logistic(gate_two))
        for first, last, path in PATHS:
            raws = linear(s.ms_left[path], side_by_side(agg, first, last))
            for k in range(first, last):
                raw = raws[:, (k - first) * atoms : (k - first + 1) * atoms]
                s.raw[number, k * channels : (k + 1) * channels, :] = raw
                keep_wide(k + 1, gates[path] * raw)

    def node_first_tangent(number):
        s.agg_dot[...] = INV_NEIGH * s.sum_wide[...]
        mixed = s.mixed.at[number]
        mixed_dot = linear(s.mf_left[...], part_of(s.agg_dot, 0))
        s.mixed_dot[...] = mixed_dot
        before = part_of(mixed, 0)
        scalar_dot = silu_slope(before, logistic(before)) * mixed_dot[0:channels]
        s.scalar_dot[...] = scalar_dot
        keep_wide(0, scalar_dot)
        for first, last, path in PATHS:
            gate = logistic(part_of(mixed, path + 1))
            move = gate * (1.0 - gate) * mixed_dot[(path + 1) * channels : (path + 2) * channels]
            raws_dot = linear(s.ms_left[path], side_by_side(s.agg_dot, first, last))
            for k in range(first, last):
                raw_dot = raws_dot[:, (k - first) * atoms : (k - first + 1) * atoms]
                s.raw_dot[k * channels : (k + 1) * channels, :] = raw_dot
                raw = s.raw[number, k * channels : (k + 1) * channels, :]
                keep_wide(k + 1, move * raw + gate * raw_dot)

    def node_first_reverse(number):
        s.feat_bar[number] = s.sum_wide[...]
        s.feat_bar[number, 0:channels, :] += s.readout_col[...]
        bar = s.feat_bar.at[number]
        mixed = s.mixed.at[number]
        before = part_of(mixed, 0)
        s.mixed_bar[number, 0:channels, :] = silu_slope(before, logistic(before)) * part_of(bar, 0)
        for first, last, path in PATHS:
            gate = logistic(part_of(mixed, path + 1))
            total = 0.0
            bars = []
            for k in range(first, last):
                given = part_of(bar, k + 1)
                total = total + given * s.raw[number, k * channels : (k + 1) * channels, :]
                raw_bar = gate * given
                s.raw_bar[number, k * channels : (k + 1) * channels, :] = raw_bar
                bars.append(raw_bar)
            found = INV_NEIGH * linear(s.ms_back[path], jnp.concatenate(bars, axis=1))
            for k in range(first, last):
                keep_wide(k + 1, found[:, (k - first) * atoms : (k - first + 1) * atoms])
            s.mixed_bar[number, (path + 1) * channels : (path + 2) * channels, :] = (
                gate * (1.0 - gate) * total
            )
        keep_wide(0, INV_NEIGH * linear(s.mf_back[...], s.mixed_bar[number]))

    def node_first_second(number, energy_bar):
        s.sum_wide[0:channels, :] += s.readout_col[...] * energy_bar
        hat = s.sum_wide
        bar = s.feat_bar.at[number]
        mixed = s.mixed.at[number]
        before = part_of(mixed, 0)
        gate = logistic(before)
        scalar_hat = part_of(hat, 0)
        s.mixed_hat[0:channels, :] = silu_slope(before, gate) * scalar_hat + silu_bend(
            before, gate
        ) * s.mixed_dot[0:channels, :] * part_of(bar, 0)
        s.scalar_hat[...] = scalar_hat
        for first, last, path in PATHS:
            gate = logistic(part_of(mixed, path + 1))
            slope = gate * (1.0 - gate)
            bend = slope * (1.0 - 2.0 * gate)
            mixed_dot = s.mixed_dot[(path + 1) * channels : (path + 2) * channels, :]
            one = 0.0
            two = 0.0
            hats = []
            for k in range(first, last):
                at = slice(k * channels, (k + 1) * channels)
                given = part_of(bar, k + 1)
                given_hat = part_of(hat, k + 1)
                raw = s.raw[number, at, :]
                one = one + (given_hat * raw + given * s.raw_dot[at, :])
                two = two + given * raw
                hats.append(gate * given_hat + slope * mixed_dot * given)
            for k in range(first, last):
                s.raw_hat[k * channels : (k + 1) * channels, :] = hats[k - first]
            found = INV_NEIGH * linear(s.ms_back[path], jnp.concatenate(hats, axis=1))
            for k in range(first, last):
                keep_wide(k + 1, found[:, (k - first) * atoms : (k - first + 1) * atoms])
            s.mixed_hat[(path + 1) * channels : (path + 2) * channels, :] = (
                slope * one + bend * mixed_dot * two
            )
        keep_wide(0, INV_NEIGH * linear(s.mf_back[...], s.mixed_hat[...]))

    def all_peers():
        return [far_peer(distance) for distance in range(group)] + [
            near_peer(distance) for distance in range(group - 1, 0, -1)
        ]

    def collect_messages(kind):
        total = s.msg_out[me]
        for other in all_peers():
            landed(s.msg_in.at[other], kind, other)
            total = total + s.msg_in[other]
        for other in all_peers():
            message_to(other, kind).wait_send()
        return INV_NEIGH * total

    def cotangent_to(other, kind):
        return remote(s.cot_all.at[me], s.cot_all.at[me], kind, other)

    def share_cotangent(value, kind):
        s.cot_all[me] = value
        for distance in range(1, group):
            cotangent_to(near_peer(distance), kind).start()
        for distance in range(group):
            cotangent_to(far_peer(distance), kind).start()

    def with_cotangents(number, kind, use):
        for distance in range(1, group):
            other = near_peer(distance)
            landed(s.cot_all.at[other], kind, other)
        use(number, half)
        for distance in range(group):
            other = far_peer(distance)
            landed(s.cot_all.at[other], kind, other)
        use(number, 1 - half)
        for other in all_peers():
            cotangent_to(other, kind).wait_send()

    def node_second_forward(number):
        agg = collect_messages(KIND_MSG)
        s.agg_two[number] = agg
        before = linear(s.ms_left[2], agg)
        s.last[number] = before
        gate = logistic(before)
        s.energy_row[...] = jnp.sum(
            s.readout_col[...] * (s.scalar[number] + before * gate), axis=0, keepdims=True
        )
        before_bar = s.readout_col[...] * silu_slope(before, gate)
        share_cotangent(INV_NEIGH * linear(s.ms_back[2], before_bar), KIND_COT)

    def node_second_second(number, energy_bar):
        for index in range(tiles):
            second_early(number, index)
        agg_dot = collect_messages(KIND_TMSG)
        before = s.last[number]
        before_dot = linear(s.ms_left[2], agg_dot)
        gate = logistic(before)
        slope = silu_slope(before, gate)
        before_hat = s.readout_col[...] * (
            energy_bar * slope + silu_bend(before, gate) * before_dot
        )
        share_cotangent(INV_NEIGH * linear(s.ms_back[2], before_hat), KIND_TCOT)
        s.agg_two_dot[...] = agg_dot
        s.last_hat[...] = before_hat
        s.last_bar[...] = s.readout_col[...] * slope
        s.grad_ro[...] += energy_bar * (s.scalar[number] + before * gate) + (
            s.scalar_dot[...] + slope * before_dot
        )

    def share_rows(out_ref, in_ref, kind, meanwhile=None):
        def start(other):
            remote(out_ref, in_ref.at[me], kind, other).start()

        each_peer(start)
        in_ref[me] = out_ref[...]
        if meanwhile is not None:
            meanwhile()

        def wait(other):
            landed(in_ref.at[other], kind, other)
            remote(out_ref, in_ref.at[me], kind, other).wait_send()

        each_peer(wait)
        total = in_ref[0]
        for other in range(1, n_edge):
            total = total + in_ref[other]
        return total

    def evaluate(number):
        table(s.place)
        loop(2 * tiles, lambda index: geometry(number, index), True)
        s.sum_wide[...] = jnp.zeros_like(s.sum_wide)
        each_tile(lambda index: first_forward(number, index))
        node_first_forward(number)
        exchange_messages(number, KIND_MSG, second_forward)
        node_second_forward(number)
        s.sum_wide[...] = jnp.zeros_like(s.sum_wide)
        with_cotangents(number, KIND_COT, second_reverse)
        node_first_reverse(number)
        each_tile(lambda index: first_reverse(number, index))
        scatter_rows(number, s.force_out)
        s.force_out[3] = jnp.zeros((n_edge, atoms), F32)
        s.force_out[3, pl.ds(me, 1), :] = s.energy_row[...]

        def prepare():
            @pl.when(number < EVALS - 1)
            def _():
                one_hots(number + 1)

        total = share_rows(s.force_out, s.force_in, KIND_FORCE, prepare)
        force = -total[0:3]
        s.energy[number] = total[3]
        half_kick = 0.5 * STEP_DT * force

        @pl.when(number > 0)
        def _():
            s.speed[...] = s.speed[...] + half_kick

        @pl.when(number == 0)
        def _():
            s.start_kinetic[...] = 0.5 * jnp.sum(s.speed[...] * s.speed[...], axis=0)

        @pl.when(number < EVALS - 1)
        def _():
            s.speed[...] = s.speed[...] + half_kick
            s.place[...] = s.place[...] + STEP_DT * s.speed[...]

    one_hots(0)
    loop(EVALS, evaluate)

    kinetic = 0.5 * jnp.sum(s.speed[...] * s.speed[...], axis=0)
    change = (s.energy[EVALS - 1] + kinetic) - (s.energy[0] + s.start_kinetic[...])
    system_of = lax.broadcasted_iota(jnp.int32, (n_edge, atoms), 1) // half_atoms
    system_atoms = float(half_atoms * n_edge)
    loss = jnp.zeros((1, 1), F32)
    drift_grad = jnp.zeros((n_edge, atoms), F32)
    for number in range(SYS_LOC):
        mine = system_of == number
        drift = jnp.sum(jnp.where(mine, change, 0.0), axis=(0, 1), keepdims=True)
        loss = loss + drift * drift / system_atoms
        drift_grad = drift_grad + jnp.where(mine, 2.0 * drift / system_atoms, 0.0)
    s.drift_grad[...] = drift_grad
    s.place_bar[...] = jnp.zeros_like(s.place_bar)
    s.speed_bar[...] = drift_grad[None] * s.speed[...]
    s.loss_row[...] = jnp.broadcast_to(loss * jnp.where(me == 0, 1.0, 0.0), (1, channels))

    def reverse(step, last):
        number = EVALS - 1 - step
        sides = jnp.where(jnp.logical_or(number == 0, number == EVALS - 1), 1.0, 2.0)
        ends = jnp.where(number == 0, -1.0, jnp.where(number == EVALS - 1, 1.0, 0.0))
        s.move[...] = (-0.5 * STEP_DT * sides) * s.speed_bar[...]
        table(s.move)
        loop(2 * tiles, lambda index: geometry_tangent(number, index), True)
        energy_bar = ends * s.drift_grad[pl.ds(me, 1), :]
        s.sum_wide[...] = jnp.zeros_like(s.sum_wide)
        each_tile(lambda index: first_tangent(number, index))
        node_first_tangent(number)
        exchange_messages(number, KIND_TMSG, second_tangent)
        node_second_second(number, energy_bar)
        all_early(number)
        s.sum_wide[...] = jnp.zeros_like(s.sum_wide)
        with_cotangents(
            number, KIND_TCOT, lambda number, index: second_second(number, index, last)
        )
        node_first_second(number, energy_bar)
        if last:
            radial_gradients(1, number)
            node_gradients(number)
            pack_first()
            each_peer(lambda other: first_rows(other).start())
        each_tile(lambda index: first_second(number, index, last))
        if last:
            radial_gradients(0, number)
            kind_gradients(number)
            pack_second()
            each_peer(lambda other: second_rows(other).start())
        else:
            scatter_rows(number, s.place_out)

            def gradients():
                radial_gradients(1, number)
                node_gradients(number)
                radial_gradients(0, number)
                kind_gradients(number)

            total = share_rows(s.place_out, s.place_in, KIND_TFORCE, gradients)
            s.place_bar[...] = s.place_bar[...] + total
            s.speed_bar[...] = s.speed_bar[...] + STEP_DT * s.place_bar[...]

    first_each, second_each = [ref.shape[0] // n_edge for ref in (s.grad_first, s.grad_second)]

    def some_rows(ref, other, count):
        return ref.at[pl.ds(pl.multiple_of(other * count, 8), count)]

    def first_rows(other):
        return remote(
            some_rows(s.grad_first, other, first_each),
            s.part_in.at[me, 0:first_each],
            KIND_SCATTER,
            other,
        )

    def second_rows(other):
        return remote(
            some_rows(s.grad_second, other, second_each),
            s.part_in.at[me, first_each:],
            KIND_SCATTER_LATE,
            other,
        )

    def join_out(layer):
        found = s.grad_out[layer]
        rows = 3 * channels
        return found[0:rows, 0:channels] + found[0:rows, channels:] + found[rows:, 0:channels]

    def join_in(layer):
        found = s.grad_in[layer]
        return found[0:8, 0:channels] + found[0:8, channels:] + found[8:16, 0:channels]

    def pack_first():
        out = s.grad_first
        rows = 3 * channels
        out[0:rows, :] = jnp.concatenate([join_out(1), s.grad_mf[...]], axis=1)
        out[rows : rows + channels, :] = jnp.concatenate([s.grad_ms[0], s.grad_ms[1]], axis=1)
        ones = jnp.ones((8, atoms), BF)
        ro_rows = 0.0
        for piece in three_parts_f32(s.grad_ro[...]):
            ro_rows = ro_rows + dot_nt(ones, piece.astype(BF))
        rest = jnp.zeros((channels - 16, channels), F32)
        small = jnp.concatenate([ro_rows, join_in(1), rest], axis=0)
        out[rows + channels : rows + 2 * channels, :] = jnp.concatenate(
            [s.grad_ms[2], small], axis=1
        )

    def pack_second():
        out = s.grad_second
        rows = 3 * channels // 2
        found = join_out(0)
        out[0:rows, :] = jnp.concatenate([found[0:rows], found[rows:]], axis=1)
        out[rows : rows + 8, :] = jnp.concatenate([join_in(0), s.grad_emb[0:8, :]], axis=1)
        loss_rows = jnp.broadcast_to(s.loss_row[...], (8, channels))
        out[rows + 8 : rows + 16, :] = jnp.concatenate([loss_rows, loss_rows], axis=1)

    lax.fori_loop(0, EVALS - 1, lambda step, carry: (reverse(step, False), carry)[1], 0)
    reverse(EVALS - 1, True)

    s.part_in[me, 0:first_each, :] = some_rows(s.grad_first, me, first_each)[...]
    s.part_in[me, first_each:, :] = some_rows(s.grad_second, me, second_each)[...]

    def wait_scatter(other):
        landed(s.part_in.at[other, 0:first_each], KIND_SCATTER, other)
        landed(s.part_in.at[other, first_each:], KIND_SCATTER_LATE, other)
        first_rows(other).wait_send()
        second_rows(other).wait_send()

    each_peer(wait_scatter)
    total = s.part_in[0]
    for other in range(1, n_edge):
        total = total + s.part_in[other]
    s.sys_in[my_group] = total

    def line_copy(other, index):
        return pltpu.make_async_remote_copy(
            src_ref=s.sys_in.at[index],
            dst_ref=s.sys_in.at[index],
            send_sem=s.send_sem.at[KIND_SYS, other],
            recv_sem=s.recv_sem.at[KIND_SYS, index],
            device_id={"edge": 2 * other + core},
            device_id_type=MESH,
        )

    each_group(lambda other: line_copy(other, my_group).start())

    def wait_line(other):
        line_copy(other, other).wait_recv()
        line_copy(other, my_group).wait_send()

    each_group(wait_line)
    total = s.sys_in[0]
    for other in range(1, n_sys):
        total = total + s.sys_in[other]
    s.summed[me] = total
    mine = s.summed.at[me]
    each_peer(lambda other: remote(mine, mine, KIND_GATHER, other).start())

    def wait_gather(other):
        landed(s.summed.at[other], KIND_GATHER, other)
        remote(mine, mine, KIND_GATHER, other).wait_send()

    each_peer(wait_gather)
    first_total = s.grad_first.shape[0]
    for other in range(n_edge):
        total_ref[other * first_each : (other + 1) * first_each, :] = s.summed[other, 0:first_each, :]
        low_row = first_total + other * second_each
        total_ref[low_row : low_row + second_each, :] = s.summed[other, first_each:, :]


class Scratch:
    pass


def step_scratch(n_edge, n_sys, channels, atoms, first_rows, second_rows):
    tiles = TILES
    lanes = n_edge // tiles * atoms
    wide = N_COMP * channels
    vm = lambda *shape: pltpu.VMEM(shape, F32)
    vb = lambda *shape: pltpu.VMEM(shape, BF)
    vi = lambda *shape: pltpu.VMEM(shape, jnp.int32)
    return dict(
        send_sem=pltpu.SemaphoreType.DMA((KINDS, n_edge)),
        recv_sem=pltpu.SemaphoreType.DMA((KINDS, n_edge)),
        start_out=vm(8, atoms),
        start_float=vm(n_edge, 8, atoms),
        lists_own=vi(n_edge, 16, atoms),
        own_kind=vb(16, atoms),
        lists_out=vi(n_edge, 16, atoms),
        lists_in=vi(n_edge, 16, atoms),
        w_in_left=vb(2, channels, 32),
        w_in_back=vb(2, 16, 2 * channels),
        w_out_left=vb(2, 3 * channels, 3 * channels),
        w_out_back=vb(2, 2 * channels, 3 * channels),
        mf_left=vb(3 * channels, 3 * channels),
        mf_back=vb(channels, 9 * channels),
        ms_left=vb(3, channels, 3 * channels),
        ms_back=vb(3, channels, 3 * channels),
        emb_left=vb(channels, 48),
        readout_col=vm(channels, atoms),
        start_scalar=vm(channels, atoms),
        place=vm(3, n_edge, atoms),
        speed=vm(3, n_edge, atoms),
        energy_row=vm(1, atoms),
        energy=vm(EVALS, n_edge, atoms),
        start_kinetic=vm(n_edge, atoms),
        drift_grad=vm(n_edge, atoms),
        place_bar=vm(3, n_edge, atoms),
        speed_bar=vm(3, n_edge, atoms),
        move=vm(3, n_edge, atoms),
        own_hot=vb(EVALS, 2 * tiles, 2 * atoms, lanes),
        far_hot=vb(EVALS, 2 * tiles, atoms, lanes),
        kind_hot=vb(EVALS, tiles, 16, lanes),
        kind_value=vm(EVALS, tiles, channels, lanes),
        rows=vm(n_edge, 8, atoms),
        pieces=vb(n_edge, 32, atoms),
        row_own=vm(8, atoms),
        edge_rows=vm(2 * tiles, 8, lanes),
        geo=vm(EVALS, 2 * tiles, 40, lanes),
        geo_bar=vm(EVALS, 2 * tiles, 24, lanes),
        geo_dot=vm(2 * tiles, 24, lanes),
        hidden=vm(2, EVALS, tiles, channels, lanes),
        hidden_bar=vm(2, EVALS, tiles, channels, lanes),
        hidden_dot=vm(2, tiles, channels, lanes),
        radial=vm(2, EVALS, tiles, 3 * channels, lanes),
        radial_dot=vm(2, tiles, 3 * channels, lanes),
        m_high=vb(tiles, wide, lanes),
        m_low=vb(tiles, wide, lanes),
        r_pair=vb(2, tiles, 6 * channels, lanes),
        h_pair=vb(2, tiles, 6 * channels, lanes),
        out_pair=vb(2, tiles, 2 * channels, lanes),
        hat_pair=vb(2, tiles, 2 * channels, lanes),
        scalar_hat=vm(channels, atoms),
        raw_hat=vm(8 * channels, atoms),
        last_hat=vm(channels, atoms),
        last_bar=vm(channels, atoms),
        agg_two_dot=vm(channels, atoms),
        loss_row=vm(1, channels),
        v_high=vb(tiles, channels, lanes),
        v_low=vb(tiles, channels, lanes),
        a_pair=vb(wide, 2 * atoms),
        sum_wide=vm(wide, atoms),
        first_cot=vm(EVALS, tiles, wide, lanes),
        feat=vm(EVALS, tiles, wide, lanes),
        feat_dot=vm(tiles, wide, lanes),
        along=vm(EVALS, tiles, 2 * channels, lanes),
        along_dot=vm(tiles, 2 * channels, lanes),
        msg_cot=vm(EVALS, tiles, channels, lanes),
        msg_hat=vm(tiles, channels, lanes),
        agg=vm(EVALS, wide, atoms),
        agg_dot=vm(wide, atoms),
        mixed=vm(EVALS, 3 * channels, atoms),
        mixed_dot=vm(3 * channels, atoms),
        mixed_bar=vm(EVALS, 3 * channels, atoms),
        mixed_hat=vm(3 * channels, atoms),
        raw=vm(EVALS, 8 * channels, atoms),
        raw_dot=vm(8 * channels, atoms),
        raw_bar=vm(EVALS, 8 * channels, atoms),
        scalar=vm(EVALS, channels, atoms),
        scalar_dot=vm(channels, atoms),
        feat_bar=vm(EVALS, wide, atoms),
        agg_two=vm(EVALS, channels, atoms),
        last=vm(EVALS, channels, atoms),
        msg_out=vm(n_edge, channels, atoms),
        msg_in=vm(n_edge, channels, atoms),
        cot_all=vm(n_edge, channels, atoms),
        force_out=vm(4, n_edge, atoms),
        force_in=vm(n_edge, 4, n_edge, atoms),
        place_out=vm(3, n_edge, atoms),
        place_in=vm(n_edge, 3, n_edge, atoms),
        grad_emb=vm(16, channels),
        grad_in=vm(2, 2 * NB, 2 * channels),
        grad_out=vm(2, 6 * channels, 2 * channels),
        grad_mf=vm(3 * channels, channels),
        grad_ms=vm(3, channels, channels),
        grad_ro=vm(channels, atoms),
        grad_first=vm(first_rows, 2 * channels),
        grad_second=vm(second_rows, 2 * channels),
        part_in=vm(n_edge, (first_rows + second_rows) // n_edge, 2 * channels),
        sys_in=vm(n_sys, (first_rows + second_rows) // n_edge, 2 * channels),
        summed=vm(n_edge, (first_rows + second_rows) // n_edge, 2 * channels),
    )


def gradient_rows(n_edge, channels):
    unit = 8 * n_edge
    return -(-(5 * channels) // unit) * unit, -(-(3 * channels // 2 + 16) // unit) * unit


def whole_step(positions, velocities, species, senders, receivers, edge_mask, params):
    n_edge, n_sys = lax.axis_size("edge"), lax.axis_size("sys")
    atoms = positions.shape[1]
    channels = params[0].shape[1]
    first_rows, second_rows = gradient_rows(n_edge, channels)
    shapes = step_scratch(n_edge, n_sys, channels, atoms, first_rows, second_rows)
    names = tuple(shapes)

    def kernel(*refs):
        scratch = Scratch()
        for name, ref in zip(names, refs[13:]):
            setattr(scratch, name, ref)
        step_kernel(n_edge, n_sys, *refs[:13], scratch)

    embedding, radial_in, radial_out, mix_first, mix_square, readout = params
    operands = (
        positions,
        velocities,
        species,
        senders,
        receivers,
        edge_mask,
        embedding,
        radial_in,
        radial_out,
        mix_first,
        mix_square,
        readout,
    )
    return pl.pallas_call(
        kernel,
        out_shape=jax.ShapeDtypeStruct((first_rows + second_rows, 2 * channels), F32),
        in_specs=[pl.BlockSpec(memory_space=pltpu.VMEM)] * len(operands),
        out_specs=pl.BlockSpec(memory_space=pltpu.VMEM),
        scratch_shapes=list(shapes.values()),
        compiler_params=pltpu.CompilerParams(
            collective_id=0, has_side_effects=True, vmem_limit_bytes=60 * 1024 * 1024
        ),
    )(*operands)


def to_column(row):
    count = row.shape[1]
    square = jnp.broadcast_to(row, (count, count))
    same = lax.broadcasted_iota(jnp.int32, (count, count), 0) == lax.broadcasted_iota(
        jnp.int32, (count, count), 1
    )
    return jnp.sum(jnp.where(same, square, 0.0), axis=1, keepdims=True)


def to_row(column):
    count = column.shape[0]
    square = jnp.broadcast_to(column, (count, count))
    same = lax.broadcasted_iota(jnp.int32, (count, count), 0) == lax.broadcasted_iota(
        jnp.int32, (count, count), 1
    )
    return jnp.sum(jnp.where(same, square, 0.0), axis=0, keepdims=True)


def total_mean(value):
    return jnp.sum(
        jnp.sum(value, axis=1, keepdims=True), axis=0, keepdims=True
    ) / float(value.shape[0] * value.shape[1])


def factored_rows(gradient, weight, row_state, col_state):
    decay_rate = 1.0 - STEP_NUM ** (-0.8)
    squares = gradient * gradient + EPS_SQUARE
    size_m, size_n = gradient.shape
    row_mean = jnp.sum(squares, axis=1, keepdims=True) / float(size_n)
    col_mean = jnp.sum(squares, axis=0, keepdims=True) / float(size_m)
    row_new = decay_rate * to_column(row_state) + (1.0 - decay_rate) * row_mean
    col_new = decay_rate * col_state + (1.0 - decay_rate) * col_mean
    second = row_new * col_new / total_mean(row_new)
    weight_rms = jnp.sqrt(total_mean(weight * weight) + 1e-06)
    weight_new = weight - RELATIVE * weight_rms * gradient * lax.rsqrt(second)
    return (gradient, to_row(row_new), col_new, weight_new, weight_new.astype(jnp.bfloat16))


def update_kernel(total_ref, *refs):
    weights, states, outs = refs[0:6], refs[6:17], refs[17:]
    kinds, channels = weights[0].shape

    rows = 3 * channels
    late = gradient_rows(lax.axis_size("edge"), channels)[0]
    small = rows + channels
    first_layer = jnp.concatenate(
        [
            total_ref[late : late + rows // 2, :channels],
            total_ref[late : late + rows // 2, channels:],
        ],
        axis=0,
    )
    below = late + rows // 2
    gradients = (
        [total_ref[below : below + kinds, channels:]],
        [total_ref[below : below + 8, :channels], total_ref[small + 8 : small + 16, channels:]],
        [first_layer.T, total_ref[0:rows, :channels].T],
        [total_ref[0:rows, channels:].T],
        [
            total_ref[rows:small, :channels],
            total_ref[rows:small, channels:],
            total_ref[small : small + channels, :channels],
        ],
    )
    outs[0][...] = total_ref[below + 8 : below + 9, 0:1]
    for which, parts in enumerate(gradients):
        weight, rows, cols = weights[which], states[2 * which], states[2 * which + 1]
        results = outs[1 + 5 * which : 6 + 5 * which]
        stacked = len(weight.shape) == 3
        for number, gradient in enumerate(parts):
            if stacked:
                found = factored_rows(
                    gradient,
                    weight[number],
                    rows[number : number + 1, :],
                    cols[number : number + 1, :],
                )
                results[0][number] = found[0]
                results[1][number : number + 1, :] = found[1]
                results[2][number : number + 1, :] = found[2]
                results[3][number] = found[3]
                results[4][number] = found[4]
            else:
                size_m, size_n = weight.shape
                found = factored_rows(
                    gradient,
                    weight[...],
                    rows[...].reshape(1, size_m),
                    cols[...].reshape(1, size_n),
                )
                results[0][...] = found[0]
                results[1][...] = found[1].reshape(size_m)
                results[2][...] = found[2].reshape(size_n)
                results[3][...] = found[3]
                results[4][...] = found[4]
    gradient = total_ref[small : small + 1, channels:]
    decay_rate = 1.0 - STEP_NUM ** (-0.8)
    weight = weights[5][...].reshape(1, channels)
    second_new = decay_rate * states[10][...].reshape(1, channels) + (1.0 - decay_rate) * (
        gradient * gradient + EPS_SQUARE
    )
    weight_rms = jnp.sqrt(total_mean(weight * weight) + 1e-06)
    weight_new = weight - RELATIVE * weight_rms * gradient * lax.rsqrt(second_new)
    outs[26][...] = gradient.reshape(channels)
    outs[27][...] = second_new.reshape(channels)
    outs[28][...] = weight_new.reshape(channels)
    outs[29][...] = weight_new.astype(jnp.bfloat16).reshape(channels)


def whole_update(total, params, states):
    shapes = [jax.ShapeDtypeStruct((1, 1), F32)]
    for which in range(5):
        weight, rows, cols = params[which], states[2 * which], states[2 * which + 1]
        for like in (weight, rows, cols, weight):
            shapes.append(jax.ShapeDtypeStruct(like.shape, F32))
        shapes.append(jax.ShapeDtypeStruct(weight.shape, jnp.bfloat16))
    for kind in (F32, F32, F32, jnp.bfloat16):
        shapes.append(jax.ShapeDtypeStruct(params[5].shape, kind))
    operands = (total, *params, *states)
    results = pl.pallas_call(
        update_kernel,
        out_shape=shapes,
        in_specs=[pl.BlockSpec(memory_space=pltpu.VMEM)] * len(operands),
        out_specs=[pl.BlockSpec(memory_space=pltpu.VMEM)] * len(shapes),
        compiler_params=pltpu.CompilerParams(vmem_limit_bytes=8 * 1024 * 1024),
    )(*operands)
    return (results[0].reshape(()), *results[1:])


def fits_kernel(senders, atom_count):
    n_edge = lax.axis_size("edge")
    slots = senders.shape[1] // n_edge
    whole = slots == atom_count and atom_count % 128 == 0
    even = n_edge & (n_edge - 1) == 0 and n_edge >= 2 * TILES
    return whole and even and n_edge == 2 * lax.axis_size("sys")


def on_device(
    positions,
    velocities,
    species,
    senders,
    receivers,
    edge_mask,
    embedding,
    radial_in,
    radial_out,
    mix_first,
    mix_square,
    readout,
    embedding_rows,
    embedding_cols,
    radial_in_rows,
    radial_in_cols,
    radial_out_rows,
    radial_out_cols,
    mix_first_rows,
    mix_first_cols,
    mix_square_rows,
    mix_square_cols,
    readout_second,
):
    params = (embedding, radial_in, radial_out, mix_first, mix_square, readout)
    atom_count = positions.shape[1]
    states = (
        embedding_rows,
        embedding_cols,
        radial_in_rows,
        radial_in_cols,
        radial_out_rows,
        radial_out_cols,
        mix_first_rows,
        mix_first_cols,
        mix_square_rows,
        mix_square_cols,
        readout_second,
    )
    if fits_kernel(senders, atom_count):
        total = whole_step(
            positions, velocities, species, senders, receivers, edge_mask, params
        )
        return whole_update(total, params, states)
    spec_hot = (species[None, :] == jnp.arange(embedding.shape[0])[:, None]).astype(jnp.float32)
    edge_lists = receivers[None]
    arrived = lax.all_to_all(edge_lists, "edge", split_axis=2, concat_axis=2, tiled=True)
    passes = [
        build(senders[number], arrived[:, number], edge_mask[number], atom_count, spec_hot)
        for number in range(EVALS)
    ]
    coords = positions
    moving = velocities
    energies, forces, stored = passes[0][0](coords, params)
    record = [stored]
    first_energy = energies
    for number in range(STEPS):
        half_speed = moving + 0.5 * STEP_DT * forces
        coords = coords + STEP_DT * half_speed
        energies, forces, stored = passes[number + 1][0](coords, params)
        record.append(stored)
        moving = half_speed + 0.5 * STEP_DT * forces
    local_sums = jnp.stack(
        [
            per_system(first_energy),
            per_system(energies),
            per_system(0.5 * jnp.sum(velocities * velocities, axis=0)),
            per_system(0.5 * jnp.sum(moving * moving, axis=0)),
        ]
    )
    totals = lax.psum(local_sums, "edge")
    drift = totals[1] + totals[3] - (totals[0] + totals[2])
    system_atoms = atom_count // SYS_LOC * lax.axis_size("edge")
    loss_local = jnp.sum(drift * drift) / system_atoms
    drift_grad = jnp.repeat(2.0 * drift / system_atoms, atom_count // SYS_LOC)
    speed_bar = drift_grad[None, :] * moving
    coord_bar = jnp.zeros_like(positions)
    force_next = jnp.zeros_like(positions)
    gradients = jax.tree.map(jnp.zeros_like, params)
    for number in reversed(range(STEPS)):
        later = number + 1
        force_bar = force_next + 0.5 * STEP_DT * speed_bar
        if later == STEPS:
            energy_bar = drift_grad
        else:
            energy_bar = jnp.zeros_like(drift_grad)
        coord_part, param_part = passes[later][1](record[later], params, energy_bar, force_bar)
        gradients = add_trees([gradients, param_part])
        coord_bar = coord_bar + coord_part
        half_bar = speed_bar + STEP_DT * coord_bar
        speed_bar = half_bar
        force_next = 0.5 * STEP_DT * half_bar
    _, param_part = passes[0][1](record[0], params, -drift_grad, force_next)
    gradients = add_trees([gradients, param_part])
    loss_term = loss_local * (lax.axis_index("edge") == 0).astype(jnp.float32)
    summed = lax.psum(
        (
            gradients[0],
            gradients[1],
            gradients[2],
            gradients[3],
            gradients[4],
            gradients[5],
            loss_term,
        ),
        ("sys", "edge"),
    )
    return update(summed, params, states)


def solution(mesh):
    placed = (
        P(None, ("sys", "edge")),
        P(None, ("sys", "edge")),
        P(("sys", "edge")),
        P(None, ("sys", "edge")),
        P(None, ("sys", "edge")),
        P(None, ("sys", "edge")),
        P(),
        P(),
        P(),
        P(),
        P(),
        P(),
        P(),
        P(),
        P(),
        P(),
        P(),
        P(),
        P(),
        P(),
        P(),
        P(),
        P(),
    )
    return jax.shard_map(
        on_device,
        mesh=mesh,
        in_specs=placed,
        out_specs=(
            P(),
            P(),
            P(),
            P(),
            P(),
            P(),
            P(),
            P(),
            P(),
            P(),
            P(),
            P(),
            P(),
            P(),
            P(),
            P(),
            P(),
            P(),
            P(),
            P(),
            P(),
            P(),
            P(),
            P(),
            P(),
            P(),
            P(),
            P(),
            P(),
            P(),
        ),
        check_vma=False,
    )
```
